32 devices in a mesh: section: 2 (over core), row: 4 (over y, x), col: 4 (over z).
Axes of the slice: x: 2, y: 2, z: 4, core: 2. Of those that a mesh axis runs over, the one named last changes fastest.
Arguments:
- tokens: float32 [2, 2048, 1536], P(None, ('row', 'col')), may hold values from -6 to 6
- cotangent: float32 [2, 2048, 1536], P(None, ('row', 'col')), may hold values from -6 to 6
- doc_lengths: int32 [2, 4, 4], replicated, may hold values from 1 to 256, 512 in all within a row
- routes: int32 [2, 2, 2048, 6], P('section', None, ('row', 'col')), may hold values from 0 to 15, all different within a row; in each aligned block of 128 rows (0 to 127, 128 to 255, ..., all dimensions but the last counted through in order) at most 64 rows name the same one
- gates: float32 [2, 2, 2048, 6], P('section', None, ('row', 'col')), may hold values from 0.05 to 0.35
- norm_in: float32 [2, 1536], P('section'), may hold values from 0.5 to 1.5
- proj_gate: bfloat16 [2, 1536, 3072], P('section', 'row', 'col'), may hold values from -0.15625 to 0.15625
- proj_input: bfloat16 [2, 1536, 3072], P('section', 'row', 'col'), may hold values from -0.15625 to 0.15625
- proj_state: bfloat16 [2, 1536, 256], P('section', 'row'), may hold values from -0.15625 to 0.15625
- proj_step: bfloat16 [2, 1536, 48], P('section', 'row', 'col'), may hold values from -0.15625 to 0.15625
- step_bias: float32 [2, 48], P('section', 'col'), may hold values from -4 to -1
- decay_log: float32 [2, 48], P('section', 'col'), may hold values from 0 to 2.5
- skip_gain: float32 [2, 48], P('section', 'col'), may hold values from 0.5 to 1.5
- conv_input: float32 [2, 4, 3072], P('section', None, 'col'), may hold values from -3 to 3
- conv_state: float32 [2, 4, 256], P('section'), may hold values from -3 to 3
- gate_norm: float32 [2, 3072], P('section', 'col'), may hold values from 0.5 to 1.5
- proj_output: bfloat16 [2, 1536, 3072], P('section', 'row', 'col'), may hold values from -0.109375 to 0.109375
- norm_mid: float32 [2, 1536], P('section'), may hold values from 0.5 to 1.5
- expert_gate: bfloat16 [2, 16, 1536, 512], P('section', ('row', 'col')), may hold values from -0.15625 to 0.15625
- expert_up: bfloat16 [2, 16, 1536, 512], P('section', ('row', 'col')), may hold values from -0.15625 to 0.15625
- expert_down: bfloat16 [2, 16, 512, 1536], P('section', ('row', 'col')), may hold values from -0.25 to 0.25
- shared_gate: bfloat16 [2, 1536, 1024], P('section', 'row', 'col'), may hold values from -0.15625 to 0.15625
- shared_up: bfloat16 [2, 1536, 1024], P('section', 'row', 'col'), may hold values from -0.15625 to 0.15625
- shared_down: bfloat16 [2, 1536, 1024], P('section', 'row', 'col'), may hold values from -0.1875 to 0.1875
Outputs:
- layer_out: float32 [2, 2, 2048, 1536], P('section', None, ('row', 'col'))
- input_grad: float32 [2, 2, 2048, 1536], P('section', None, ('row', 'col'))
- grad_norm_in: float32 [2, 1536], P('section')
- grad_proj_gate: float32 [2, 1536, 3072], P('section', 'row', 'col')
- grad_proj_input: float32 [2, 1536, 3072], P('section', 'row', 'col')
- grad_proj_state: float32 [2, 1536, 256], P('section', 'row')
- grad_proj_step: float32 [2, 1536, 48], P('section', 'row', 'col')
- grad_step_bias: float32 [2, 48], P('section', 'col')
- grad_decay_log: float32 [2, 48], P('section', 'col')
- grad_skip_gain: float32 [2, 48], P('section', 'col')
- grad_conv_input: float32 [2, 4, 3072], P('section', None, 'col')
- grad_conv_state: float32 [2, 4, 256], P('section')
- grad_gate_norm: float32 [2, 3072], P('section', 'col')
- grad_proj_output: float32 [2, 1536, 3072], P('section', 'row', 'col')
- grad_norm_mid: float32 [2, 1536], P('section')
- grad_expert_gate: float32 [2, 16, 1536, 512], P('section', ('row', 'col'))
- grad_expert_up: float32 [2, 16, 1536, 512], P('section', ('row', 'col'))
- grad_expert_down: float32 [2, 16, 512, 1536], P('section', ('row', 'col'))
- grad_shared_gate: float32 [2, 1536, 1024], P('section', 'row', 'col')
- grad_shared_up: float32 [2, 1536, 1024], P('section', 'row', 'col')
- grad_shared_down: float32 [2, 1536, 1024], P('section', 'row', 'col')
The draws below stay inside these ranges and needn't reach their ends.
Inputs may be any that keep to these rules, and one draw needn't show every extreme that they name: `doc_lengths`: each sequence's 4 lengths sum to 512; its longest document has exactly 256 tokens. `routes`: a token's 6 experts are distinct; in each layer and micro-batch the 128 tokens of one device name any one expert at most 64 times, a bound that some block reaches.
All inputs are finite; a program needn't handle non-finite values.
Results may differ from the reference program's by a relative error of at most 0.039.
Values may be sent and summed in bfloat16 or wider, within the bound.
No kernel may reach another device: no remote copies, remote signals or barrier semaphores. Data moves between devices by JAX's collectives and lax.ppermute only.
A program may use at most 448 MiB of HBM per device.

```python
import math
import jax
import jax.numpy as jnp
import numpy as np
from jax import lax

D = 1536
HEADS = 48
STATE = 128
CONV = 4
EXP_FF = 512
SHARED_FF = 1024
TOP = 6
TOK_DEV = 128
MB = 2
DOCS = 4
BLOCK = 512
DI = 3072
EXPERTS = 16
TOKENS = 2048
SEQ = 512
SEQS = 4
CAP = 64
N_ROW = 4
N_COL = 4


def steps_of(rng, shape, shards, low, top_value):
    loudness = 1.0
    for dim, blocks in shards:
        draws = jax.random.uniform(jax.random.fold_in(jax.random.fold_in(rng, 6), dim), (blocks,), jnp.float32, low / len(shards), top_value / len(shards))
        loudness = loudness * jnp.repeat(jnp.exp(draws), shape[dim] // blocks).reshape((-1,) + (1,) * (len(shape) - 1 - dim))
    return loudness


def split_up(number_of, total, most, skew):
    portions = [(1 << 20) // math.isqrt(standing ** skew) + 1 for standing in range(2, number_of + 1)]
    surplus, counts = total - most - (number_of - 1), [1] * (number_of - 1)
    while surplus > 0:
        free = [i for i in range(number_of - 1) if counts[i] < most]
        pool, budget = sum([portions[i] for i in free]), surplus
        for i in free:
            extra = min(most - counts[i], max(1, budget * portions[i] // pool), surplus)
            counts[i] = counts[i] + extra
            surplus = surplus - extra
    return np.array([most] + counts)


def ragged_sizes(rng, number_of, total, most, slope):
    if number_of == 2:
        one = jax.random.randint(rng, (), max(1, total - most), min(most, total - 1) + 1)
        return jnp.stack([one, total - one])
    sizes = jnp.asarray(split_up(number_of, total, most, slope), jnp.int32)
    couples = (number_of - 1) // 2
    donor, taker = sizes[1:1 + 2 * couples:2], sizes[2:2 + 2 * couples:2]
    slack = jnp.minimum(donor - 1, most - taker)
    moved = jax.random.randint(jax.random.fold_in(rng, 1), (couples,), 0, 1 << 20) % (slack + 1)
    sizes = sizes.at[1:1 + 2 * couples:2].set(donor - moved).at[2:2 + 2 * couples:2].set(taker + moved)
    return sizes[jax.random.permutation(jax.random.fold_in(rng, 2), number_of)]


def deal_out(stream_key, own, number, rows, count, top, limit, lean):
    ranking = jax.random.permutation(stream_key, count)
    heavy_load, common = shares(count, rows * top, limit, lean, True), shares(count, rows * top, limit, lean, False)
    places = jnp.arange(count)

    def named(tallies, offset_by):
        used = int((tallies > 0).sum())
        fixed = max(1, used // 4)
        passed = fixed + (places - fixed + offset_by * (used - fixed)) % max(1, count - fixed)
        return jnp.zeros((count,), jnp.int32).at[ranking[jnp.where(places < fixed, places, passed)]].set(jnp.asarray(tallies, jnp.int32))

    tallies = jnp.where(number % 4 == 0, named(heavy_load, number // 4), named(common, number - number // 4 - 1))
    mixed = jax.random.permutation(jax.random.fold_in(own, 3), count)
    source_of, sink = mixed[0:count // 2 * 2:2], mixed[1:count // 2 * 2:2]
    room = jnp.minimum(tallies[source_of] - 1, limit - tallies[sink]) // 2
    room = jnp.where((source_of == ranking[0]) | (sink == ranking[0]) | (tallies[sink] == 0), 0, jnp.maximum(room, 0))
    passed = jax.random.randint(jax.random.fold_in(own, 4), (count // 2,), 0, 1 << 20) % (room + 1)
    tallies = tallies.at[source_of].add(-passed).at[sink].add(passed)
    items = jnp.searchsorted(jnp.cumsum(tallies), jnp.arange(rows * top), side="right").astype(jnp.int32)
    grid = items.reshape(top, rows).T
    grid = grid[jax.random.permutation(jax.random.fold_in(own, 1), rows)]
    offset_by = jax.random.randint(jax.random.fold_in(own, 2), (rows, 1), 0, top)
    return jnp.take_along_axis(grid, (jnp.arange(top)[None, :] + offset_by) % top, axis=1)


def shares(count, total, most, skew, full):
    loads = [(1 << 20) // math.isqrt(grade ** skew) + 1 for grade in range(1, count + 1)]
    largest = most if full else min(most, max(-(-total // count), total * loads[0] // sum(loads)))
    least = 1 if total - largest >= count - 1 else 0
    holding, surplus = [largest] + [least] * (count - 1), total - largest - least * (count - 1)
    while surplus > 0:
        free = [i for i in range(1, count) if holding[i] < largest] or [i for i in range(1, count) if holding[i] < most]
        whole, budget = sum([loads[i] for i in free]), surplus
        for i in free:
            extra = min(most - holding[i], max(1, budget * loads[i] // whole), surplus)
            holding[i] = holding[i] + extra
            surplus = surplus - extra
    return np.array(holding)


def gaussian(stream_key, dims, spread, most, cuts=(), kind=jnp.bfloat16):
    values = spread * jax.random.normal(stream_key, dims, jnp.float32)
    if cuts:
        values = values * steps_of(stream_key, dims, cuts, -0.22, 0.18)
    return jnp.clip(values, -most, most).astype(kind)


def setup_inputs(seed: int = 0) -> dict:
    streams_of = jax.random.split(jax.random.key(seed), 25)
    tokens = gaussian(streams_of[0], (MB, TOKENS, D), 1.0, 6.0, ((1, 16),), jnp.float32)
    cotangent = gaussian(streams_of[1], (MB, TOKENS, D), 1.0, 6.0, ((1, 16),), jnp.float32)
    doc_lengths = jax.vmap(lambda own: ragged_sizes(own, DOCS, SEQ, SEQ // 2, 2))(jax.random.split(streams_of[2], MB * SEQS)).reshape((MB, SEQS, DOCS)).astype(jnp.int32)
    routes_keys = jax.random.split(jax.random.fold_in(streams_of[3], 1), 2 * MB * TOKENS // TOK_DEV)
    routes_turns = jax.random.permutation(jax.random.fold_in(streams_of[3], 3), 2 * MB * TOKENS // TOK_DEV)
    routes = jax.vmap(lambda own, number: deal_out(jax.random.fold_in(streams_of[3], 2), own, number, TOK_DEV, EXPERTS, TOP, CAP, 2))(routes_keys, routes_turns).reshape((2, MB, TOKENS, TOP))
    gates = jnp.clip(jnp.exp(math.log(0.35) - 1.9459101 * jax.random.uniform(streams_of[4], (2, MB, TOKENS, TOP), jnp.float32) ** steps_of(streams_of[4], (2, MB, TOKENS, TOP), ((0, 2), (2, 16)), -0.2, 0.2)), 0.05, 0.35)
    norm_in = jnp.clip(1.0 + 0.1 * jax.random.normal(streams_of[5], (2, D), jnp.float32), 0.5, 1.5)
    proj_gate = gaussian(streams_of[6], (2, D, DI), D ** -0.5, 0.15625, ((0, 2), (1, 4), (2, 4)))
    proj_input = gaussian(streams_of[7], (2, D, DI), D ** -0.5, 0.15625, ((0, 2), (1, 4), (2, 4)))
    proj_state = gaussian(streams_of[8], (2, D, 2 * STATE), D ** -0.5, 0.15625, ((0, 2), (1, 4)))
    proj_step = gaussian(streams_of[9], (2, D, HEADS), D ** -0.5, 0.15625, ((0, 2), (1, 4), (2, 4)))
    step_bias = jnp.clip(-4.0 + 3.0 * jax.random.uniform(streams_of[10], (2, HEADS), jnp.float32) ** steps_of(streams_of[10], (2, HEADS), ((0, 2), (1, 4)), -0.2, 0.2), -4.0, -1.0)
    decay_log = jnp.clip(2.5 * jax.random.uniform(streams_of[11], (2, HEADS), jnp.float32) ** steps_of(streams_of[11], (2, HEADS), ((0, 2), (1, 4)), -0.2, 0.2), 0.0, 2.5)
    skip_gain = jnp.clip(0.5 + 1.0 * jax.random.uniform(streams_of[12], (2, HEADS), jnp.float32) ** steps_of(streams_of[12], (2, HEADS), ((0, 2), (1, 4)), -0.2, 0.2), 0.5, 1.5)
    conv_input = gaussian(streams_of[13], (2, CONV, DI), CONV ** -0.5, 3.0, ((0, 2), (2, 4)), jnp.float32)
    conv_state = gaussian(streams_of[14], (2, CONV, 2 * STATE), CONV ** -0.5, 3.0, ((0, 2),), jnp.float32)
    gate_norm = jnp.clip(1.0 + 0.1 * jax.random.normal(streams_of[15], (2, DI), jnp.float32), 0.5, 1.5)
    proj_output = gaussian(streams_of[16], (2, D, DI), DI ** -0.5, 0.109375, ((0, 2), (1, 4), (2, 4)))
    norm_mid = jnp.clip(1.0 + 0.1 * jax.random.normal(streams_of[17], (2, D), jnp.float32), 0.5, 1.5)
    expert_gate = gaussian(streams_of[18], (2, EXPERTS, D, EXP_FF), D ** -0.5, 0.15625, ((0, 2), (1, 16)))
    expert_up = gaussian(streams_of[19], (2, EXPERTS, D, EXP_FF), D ** -0.5, 0.15625, ((0, 2), (1, 16)))
    expert_down = gaussian(streams_of[20], (2, EXPERTS, EXP_FF, D), EXP_FF ** -0.5, 0.25, ((0, 2), (1, 16)))
    shared_gate = gaussian(streams_of[21], (2, D, SHARED_FF), D ** -0.5, 0.15625, ((0, 2), (1, 4), (2, 4)))
    shared_up = gaussian(streams_of[22], (2, D, SHARED_FF), D ** -0.5, 0.15625, ((0, 2), (1, 4), (2, 4)))
    shared_down = gaussian(streams_of[23], (2, D, SHARED_FF), SHARED_FF ** -0.5, 0.1875, ((0, 2), (1, 4), (2, 4)))
    return {"tokens": tokens, "cotangent": cotangent, "doc_lengths": doc_lengths, "routes": routes, "gates": gates, "norm_in": norm_in, "proj_gate": proj_gate, "proj_input": proj_input, "proj_state": proj_state, "proj_step": proj_step, "step_bias": step_bias, "decay_log": decay_log, "skip_gain": skip_gain, "conv_input": conv_input, "conv_state": conv_state, "gate_norm": gate_norm, "proj_output": proj_output, "norm_mid": norm_mid, "expert_gate": expert_gate, "expert_up": expert_up, "expert_down": expert_down, "shared_gate": shared_gate, "shared_up": shared_up, "shared_down": shared_down}


@jax.custom_vjp
def low(v):
    return lax.optimization_barrier(v.astype(jnp.bfloat16)).astype(jnp.float32)

@jax.custom_vjp
def low_back(v):
    return v

def low_keep(v):
    return (low(v), None)

def low_pass(kept, grad):
    return (grad,)

def back_keep(v):
    return (v, None)

def back_low(kept, grad):
    return (low(grad),)
low.defvjp(low_keep, low_pass)
low_back.defvjp(back_keep, back_low)
EPS = 1e-05
HIGH = lax.Precision.HIGHEST

def exact_dot(left, right):
    return jnp.dot(left, right, precision=HIGH)

def rms_norm(value, gain):
    return value * lax.rsqrt(lax.optimization_barrier(jnp.mean(value * value, axis=-1, keepdims=True)) + EPS) * gain

def doc_ids(lengths):
    bounds = jnp.cumsum(lengths, axis=1).astype(jnp.int32)[:, :-1]
    place = jnp.arange(SEQ, dtype=jnp.int32)
    inner = lax.optimization_barrier(jnp.sum((place[None, :, None] >= bounds[:, None, :]).astype(jnp.int32), axis=2)).astype(jnp.int32)
    first = jnp.arange(lengths.shape[0], dtype=jnp.int32)[:, None] * lengths.shape[1]
    return (inner + first).reshape(-1).astype(jnp.int32)

def causal_conv(values, weight, docs):
    width = weight.shape[0]
    result = values * weight[width - 1]
    for back in range(1, width):
        moved = jnp.pad(values, ((back, 0), (0, 0)))[:-back]
        prior = jnp.pad(docs, (back, 0), constant_values=-1)[:-back]
        same = (prior == docs).astype(values.dtype)[:, None]
        result = result + moved * same * weight[width - 1 - back]
    return result

def ssd_scan(inputs, step_size, rate, state_in, state_out, docs, skip_gain):
    length, heads, width = inputs.shape
    count = length // BLOCK
    order = jnp.arange(BLOCK, dtype=jnp.int32)
    causal = order[:, None] >= order[None, :]

    def advance(carry, block):
        state, previous = carry
        values, sizes, keys, queries, labels = block
        logs = sizes * rate[None, :]
        running = jnp.cumsum(logs, axis=0)
        same = causal & (labels[:, None] == labels[None, :])
        spread_log = running[:, None, :] - running[None, :, :]
        decay = jnp.exp(jnp.where(same[:, :, None], spread_log, -1e+30))
        scores = jnp.dot(queries, keys.T, precision=HIGH)
        mixing = decay * scores[:, :, None] * sizes[None, :, :]
        inner = jnp.einsum('tsh,shp->thp', mixing, values, precision=HIGH)
        carried = (labels == previous).astype(values.dtype)
        reach = jnp.exp(running) * carried[:, None]
        outer = jnp.einsum('tn,hpn->thp', queries, state, precision=HIGH) * reach[:, :, None]
        final = labels[BLOCK - 1].astype(jnp.int32)
        tail = jnp.exp(running[BLOCK - 1][None, :] - running) * sizes * (labels == final).astype(values.dtype)[:, None]
        kept = jnp.exp(running[BLOCK - 1]) * (final == previous).astype(values.dtype)
        fresh = jnp.einsum('sh,shp,sn->hpn', tail, values, keys, precision=HIGH)
        new_state = state * kept[:, None, None] + fresh
        output = inner + outer + skip_gain[None, :, None] * values
        return ((new_state, final), output)
    blocks = (inputs.reshape(count, BLOCK, heads, width), step_size.reshape(count, BLOCK, heads), state_in.reshape(count, BLOCK, -1), state_out.reshape(count, BLOCK, -1), docs.astype(jnp.int32).reshape(count, BLOCK))
    start = (jnp.zeros((heads, width, state_in.shape[1]), inputs.dtype), jnp.array(-1, jnp.int32))
    _, result = lax.scan(jax.checkpoint(advance), start, blocks)
    return result.reshape(length, heads, width)

def mamba_core(gate_pre, input_pre, state_pre, step_pre, conv_input, conv_state, step_bias, decay_log, skip_gain, docs):
    heads = step_pre.shape[1]
    length = input_pre.shape[0]
    mixed_input = jax.nn.silu(causal_conv(input_pre, conv_input, docs))
    mixed_state = jax.nn.silu(causal_conv(state_pre, conv_state, docs))
    half = state_pre.shape[1] // 2
    step_size = jax.nn.softplus(step_pre + step_bias)
    rate = -jnp.exp(decay_log)
    result = ssd_scan(mixed_input.reshape(length, heads, -1), step_size, rate, mixed_state[:, :half], mixed_state[:, half:], docs, skip_gain)
    return result.reshape(length, -1) * jax.nn.silu(gate_pre)

def gated_scale(values, total, gain):
    return values * lax.rsqrt(total[:, None] / DI + EPS) * gain

def route_slots(routes, experts, capacity):
    flat = routes.reshape(-1).astype(jnp.int32)
    hits = (flat[:, None] == jnp.arange(experts, dtype=jnp.int32)[None, :]).astype(jnp.int32)
    before = lax.optimization_barrier(jnp.sum((jnp.cumsum(hits, axis=0).astype(jnp.int32) - 1) * hits, axis=1)).astype(jnp.int32)
    return (flat * capacity + before).astype(jnp.int32)

def slot_sources(places, slots):
    count = places.shape[0]
    return jnp.full((slots,), count, jnp.int32).at[places].set(jnp.arange(count, dtype=jnp.int32))

def routed_block(normed, routes, gates, expert_gate, expert_up, expert_down):
    blocks = N_ROW * N_COL
    width = normed.shape[1]
    places = jax.vmap(lambda table: route_slots(table, EXPERTS, CAP))(routes.reshape(blocks, TOK_DEV, TOP))
    sources = jax.vmap(lambda chosen: slot_sources(chosen, EXPERTS * CAP))(places)
    padded = jnp.concatenate([normed.reshape(blocks, TOK_DEV, width), jnp.zeros((blocks, 1, width), normed.dtype)], axis=1)
    sent = jax.vmap(lambda table, chosen: table[chosen])(padded, sources // TOP)
    sent = low_back(sent)
    grouped = sent.reshape(blocks, EXPERTS, CAP, width).transpose(1, 0, 2, 3).reshape(EXPERTS, blocks * CAP, width)

    def expert(operands):
        rows_in, gate_weight, up_weight, down_weight = operands
        gate_pre = low_back(exact_dot(rows_in, gate_weight))
        lift_pre = low_back(exact_dot(rows_in, up_weight))
        active = low(jax.nn.silu(gate_pre) * lift_pre)
        return low_back(low(exact_dot(active, down_weight)))
    result = lax.map(jax.checkpoint(expert), (grouped, expert_gate, expert_up, expert_down))
    result = result.reshape(EXPERTS, blocks, CAP, width).transpose(1, 0, 2, 3).reshape(blocks, EXPERTS * CAP, width)
    picked = jax.vmap(lambda table, chosen: table[chosen])(result, places)
    weighted = picked.reshape(blocks, TOK_DEV, TOP, width) * gates.reshape(blocks, TOK_DEV, TOP)[:, :, :, None]
    return lax.optimization_barrier(jnp.sum(weighted, axis=2)).reshape(-1, width)

def layer(resid, weights, labels, routes, gates):
    norm_in, proj_gate, proj_input, proj_state, proj_step, step_bias, decay_log, skip_gain, conv_input, conv_state, gate_norm, proj_output, norm_mid, expert_gate, expert_up, expert_down, shared_gate, shared_up, shared_down = weights
    normed_in = low(rms_norm(resid, norm_in))
    gate_pre = low_back(exact_dot(normed_in, proj_gate))
    input_pre = low_back(exact_dot(normed_in, proj_input))
    state_pre = low_back(exact_dot(normed_in, proj_state))
    step_pre = low_back(exact_dot(normed_in, proj_step))
    gated = mamba_core(gate_pre, input_pre, state_pre, step_pre, conv_input, conv_state, step_bias, decay_log, skip_gain, labels)
    total = lax.optimization_barrier(jnp.sum(gated * gated, axis=1))
    scaled = low(gated_scale(gated, total, gate_norm))
    middle = resid + low_back(exact_dot(scaled, proj_output.T))
    normed = low(rms_norm(middle, norm_mid))
    shared_pre = low_back(exact_dot(normed, shared_gate))
    lift_pre = low_back(exact_dot(normed, shared_up))
    shared_act = low(jax.nn.silu(shared_pre) * lift_pre)
    shared_out = low_back(exact_dot(shared_act, shared_down.T))
    routed = routed_block(normed, routes, gates, expert_gate, expert_up, expert_down)
    return middle + shared_out + routed

def reference(tokens, cotangent, doc_lengths, routes, gates, norm_in, proj_gate, proj_input, proj_state, proj_step, step_bias, decay_log, skip_gain, conv_input, conv_state, gate_norm, proj_output, norm_mid, expert_gate, expert_up, expert_down, shared_gate, shared_up, shared_down):
    stacked = (norm_in, proj_gate, proj_input, proj_state, proj_step, step_bias, decay_log, skip_gain, conv_input, conv_state, gate_norm, proj_output, norm_mid, expert_gate, expert_up, expert_down, shared_gate, shared_up, shared_down)
    sections = [tuple((item[index].astype(jnp.float32) for item in stacked)) for index in range(2)]

    def one_batch(carry, operands):
        layer_in, grad_top, lengths, route_pair, gate_pair = operands
        labels = doc_ids(lengths)

        def first_layer(value, weights):
            return layer(value, weights, labels, route_pair[0], gate_pair[0])

        def second_layer(value, weights):
            return layer(value, weights, labels, route_pair[1], gate_pair[1])
        middle, pull_first = jax.vjp(first_layer, layer_in, sections[0])
        final, pull_second = jax.vjp(second_layer, middle, sections[1])
        grad_middle, grads_second = pull_second(grad_top)
        grad_in, grads_first = pull_first(grad_middle)
        carry = (jax.tree.map(jnp.add, carry[0], grads_first), jax.tree.map(jnp.add, carry[1], grads_second))
        return (carry, (middle, final, grad_in, grad_middle))
    zeros = (jax.tree.map(jnp.zeros_like, sections[0]), jax.tree.map(jnp.zeros_like, sections[1]))
    operands = (tokens.astype(jnp.float32), cotangent.astype(jnp.float32), doc_lengths.astype(jnp.int32), jnp.swapaxes(routes, 0, 1).astype(jnp.int32), jnp.swapaxes(gates, 0, 1).astype(jnp.float32))
    totals, (middles, finals, grad_ins, grad_middles) = lax.scan(one_batch, zeros, operands)
    layer_out = jnp.stack([middles, finals])
    input_grad = jnp.stack([grad_ins, grad_middles])
    grads = [jnp.stack([totals[0][index], totals[1][index]]) for index in range(len(stacked))]
    return (layer_out, input_grad, grads[0], grads[1], grads[2], grads[3], grads[4], grads[5], grads[6], grads[7], grads[8], grads[9], grads[10], grads[11], grads[12], grads[13], grads[14], grads[15], grads[16], grads[17], grads[18])
```

```python
import jax
import jax.numpy as jnp
from jax import lax
from jax.sharding import PartitionSpec as P

BLOCK = 512
DI = 3072


EPS = 1e-05
HIGH = lax.Precision.HIGHEST
FLOAT = jnp.float32
HALF = jnp.bfloat16


def shifted(block, axis, distance):
    count = lax.axis_size(axis)
    if distance % count == 0:
        return block
    return lax.ppermute(block, axis, [(i, (i + distance) % count) for i in range(count)])


def swapped(block):
    return lax.ppermute(block, "section", [(0, 1), (1, 0)])


def rms_norm(value, gain):
    return value * lax.rsqrt(jnp.mean(value * value, axis=-1, keepdims=True) + EPS) * gain


def causal_conv(values, weight, docs):
    width = weight.shape[0]
    result = values * weight[width - 1]
    for back in range(1, width):
        moved = jnp.pad(values, ((back, 0), (0, 0)))[:-back]
        prior = jnp.pad(docs, (back, 0), constant_values=-1)[:-back]
        same = (prior == docs).astype(values.dtype)[:, None]
        result = result + moved * same * weight[width - 1 - back]
    return result


def ssd_scan(inputs, step_size, rate, state_in, state_out, docs, skip_gain):
    length, heads, width = inputs.shape
    count = length // BLOCK
    order = jnp.arange(BLOCK, dtype=jnp.int32)
    causal = order[:, None] >= order[None, :]

    def advance(carry, block):
        state, previous = carry
        values, sizes, keys, queries, labels = block
        logs = sizes * rate[None, :]
        running = jnp.cumsum(logs, axis=0)
        same = causal & (labels[:, None] == labels[None, :])
        spread_log = running[:, None, :] - running[None, :, :]
        decay = jnp.exp(jnp.where(same[:, :, None], spread_log, -1e30))
        scores = jnp.dot(queries, keys.T, precision=HIGH)
        mixing = decay * scores[:, :, None] * sizes[None, :, :]
        inner = jnp.einsum("tsh,shp->thp", mixing, values, precision=HIGH)
        carried = (labels == previous).astype(values.dtype)
        reach = jnp.exp(running) * carried[:, None]
        outer = jnp.einsum("tn,hpn->thp", queries, state, precision=HIGH) * reach[:, :, None]
        final = labels[BLOCK - 1]
        tail = (
            jnp.exp(running[BLOCK - 1][None, :] - running)
            * sizes
            * (labels == final).astype(values.dtype)[:, None]
        )
        kept = jnp.exp(running[BLOCK - 1]) * (final == previous).astype(values.dtype)
        fresh = jnp.einsum("sh,shp,sn->hpn", tail, values, keys, precision=HIGH)
        new_state = state * kept[:, None, None] + fresh
        output = inner + outer + skip_gain[None, :, None] * values
        return ((new_state, final), output)

    blocks = (
        inputs.reshape(count, BLOCK, heads, width),
        step_size.reshape(count, BLOCK, heads),
        state_in.reshape(count, BLOCK, -1),
        state_out.reshape(count, BLOCK, -1),
        docs.reshape(count, BLOCK),
    )
    start = (jnp.zeros((heads, width, state_in.shape[1]), inputs.dtype), jnp.array(-1, jnp.int32))
    _, result = lax.scan(jax.checkpoint(advance), start, blocks)
    return result.reshape(length, heads, width)


def mamba_core(
    gate_pre,
    input_pre,
    state_pre,
    step_pre,
    conv_input,
    conv_state,
    step_bias,
    decay_log,
    skip_gain,
    docs,
):
    heads = step_pre.shape[1]
    length = input_pre.shape[0]
    mixed_input = jax.nn.silu(causal_conv(input_pre, conv_input, docs))
    mixed_state = jax.nn.silu(causal_conv(state_pre, conv_state, docs))
    half = state_pre.shape[1] // 2
    step_size = jax.nn.softplus(step_pre + step_bias)
    rate = -jnp.exp(decay_log)
    result = ssd_scan(
        mixed_input.reshape(length, heads, -1),
        step_size,
        rate,
        mixed_state[:, :half],
        mixed_state[:, half:],
        docs,
        skip_gain,
    )
    return result.reshape(length, -1) * jax.nn.silu(gate_pre)


def local_docs(lengths, row_now, length):
    bounds = jnp.cumsum(lengths)[:-1]
    place = jnp.arange(length, dtype=jnp.int32)
    inner = jnp.sum((place[:, None] >= bounds[None, :]).astype(jnp.int32), axis=1)
    return inner + row_now * lengths.shape[0]


def project(left, right):
    return jnp.dot(left, right, preferred_element_type=FLOAT)


def project_back(left, right):
    return lax.dot_general(left, right, (((1,), (1,)), ((), ())), preferred_element_type=FLOAT)


def outer(left, right):
    return lax.dot_general(left, right, (((0,), (0,)), ((), ())), preferred_element_type=FLOAT)


def silu_slope(value):
    sigma = jax.nn.sigmoid(value)
    return sigma * (1.0 + value * (1.0 - sigma))


def groups():
    count = lax.axis_size("col")
    return count if count <= 4 else 1


def spread(block):
    if groups() == 1:
        return [lax.all_gather(block, "col", axis=0, tiled=True)]
    return [shifted(block, "col", back) for back in range(lax.axis_size("col"))]


def in_order(blocks):
    count = len(blocks)
    if count == 1:
        return blocks[0]
    rows = blocks[0].shape[0]
    line = jnp.concatenate(blocks[::-1] + blocks[:0:-1], axis=0)
    start = (count - 1 - lax.axis_index("col")) * rows
    return lax.dynamic_slice_in_dim(line, start, count * rows, axis=0)


def gathered_sum(parts):
    if len(parts) == 1:
        return lax.psum_scatter(parts[0], "col", scatter_dimension=0, tiled=True).astype(FLOAT)
    total = parts[0].astype(FLOAT)
    for back in range(1, len(parts)):
        total = total + shifted(parts[back], "col", -back).astype(FLOAT)
    return total


def block_of(values, back, rows):
    if groups() == 1:
        return values
    count = lax.axis_size("col")
    index = lax.rem(lax.axis_index("col") - back + count, count)
    return lax.dynamic_slice_in_dim(values, index * rows, rows, axis=0)


def route_tables(meta, top, capacity):
    n_row, n_col = lax.axis_size("row"), lax.axis_size("col")
    row_now, col_now = lax.axis_index("row"), lax.axis_index("col")
    tables = []
    blocks = meta.shape[0] // groups()
    slots = blocks * capacity
    for back in range(groups()):
        block = lax.rem(col_now - back + n_col, n_col) if blocks == 1 else 0
        now = lax.dynamic_slice_in_dim(meta, block, blocks, axis=0).reshape(-1, 2 * top)
        routes, gates = now[:, :top], now[:, top:]
        count = routes.shape[0]
        experts = (lax.rem(row_now + jnp.arange(n_row), n_row) * n_col + col_now).astype(FLOAT)
        match = routes[None, :, :] == experts[:, None, None]
        hit = jnp.any(match, axis=2)
        weight = jnp.sum(jnp.where(match, gates[None], 0.0), axis=2)
        place = jnp.cumsum(hit.astype(jnp.int32), axis=1) - 1
        slot = jnp.arange(slots, dtype=jnp.int32)
        chosen = (place[:, None, :] == slot[None, :, None]) & hit[:, None, :]
        plain = chosen.astype(HALF).reshape(n_row * slots, count)
        scaled = jnp.where(chosen, weight[:, None, :], 0.0).astype(HALF)
        tables.append((plain, scaled.reshape(n_row * slots, count)))
    return tables


def dispatch(table, block):
    n_row = lax.axis_size("row")
    rows = project(table, block).astype(HALF)
    rows = rows.reshape(n_row, rows.shape[0] // n_row, rows.shape[1])
    return jnp.concatenate([shifted(rows[ahead], "row", ahead) for ahead in range(n_row)], axis=0)


def give_back(rows):
    n_row = lax.axis_size("row")
    rows = rows.astype(HALF).reshape(n_row, rows.shape[0] // n_row, rows.shape[1])
    return jnp.concatenate([shifted(rows[ahead], "row", -ahead) for ahead in range(n_row)], axis=0)


def layer_forward(resid, params, dense, labels, tables):
    (
        norm_in,
        step_bias,
        decay_log,
        skip_gain,
        conv_input,
        conv_state,
        gate_norm,
        norm_mid,
    ) = params
    proj, proj_output, shared, expert_gate, expert_up, expert_down = dense
    count = resid.shape[0]
    inner = gate_norm.shape[0]
    state = conv_state.shape[1]
    hidden = shared.shape[1] // 3
    wide_in = in_order(spread(rms_norm(resid, norm_in).astype(HALF)))
    pre = project(wide_in, proj)
    gate_pre = pre[:, :inner]
    input_pre = pre[:, inner : 2 * inner]
    state_pre = pre[:, 2 * inner : 2 * inner + state]
    step_pre = pre[:, 2 * inner + state :]

    def core(*inputs):
        return mamba_core(*inputs, labels)

    gated, pull_core = jax.vjp(
        core,
        gate_pre,
        input_pre,
        state_pre,
        step_pre,
        conv_input,
        conv_state,
        step_bias,
        decay_log,
        skip_gain,
    )
    total_part = jnp.sum(gated * gated, axis=1, keepdims=True)
    scaled = (gated * gate_norm).astype(HALF)
    backs = range(groups())
    total = gathered_sum([block_of(total_part, back, count) for back in backs])
    mixed = gathered_sum(
        [project_back(block_of(scaled, back, count), proj_output).astype(HALF) for back in backs]
    )
    rr = lax.rsqrt(total / DI + EPS)
    middle = resid + mixed * rr
    normed = rms_norm(middle, norm_mid).astype(HALF)
    wide_mid = spread(normed)
    shared_pre, lift_pre, shared_act, arrived, expert_pre, active, parts = [], [], [], [], [], [], []
    for back in backs:
        rows = dispatch(tables[back][0], wide_mid[back])
        gate_e = project(rows, expert_gate)
        lift_e = project(rows, expert_up)
        act_e = (jax.nn.silu(gate_e) * lift_e).astype(HALF)
        result = give_back(project(act_e, expert_down))
        arrived.append(rows)
        expert_pre.append((gate_e, lift_e))
        active.append(act_e)
        both = project(wide_mid[back], shared[:, : 2 * hidden])
        gate_s, lift_s = both[:, :hidden], both[:, hidden:]
        act_s = (jax.nn.silu(gate_s) * lift_s).astype(HALF)
        shared_pre.append(gate_s)
        lift_pre.append(lift_s)
        shared_act.append(act_s)
        part = outer(tables[back][1], result) + project_back(act_s, shared[:, 2 * hidden :])
        parts.append(part.astype(HALF))
    saved = (
        resid,
        middle,
        mixed,
        rr,
        wide_in,
        gated,
        pull_core,
        wide_mid,
        shared_pre,
        lift_pre,
        shared_act,
        arrived,
        expert_pre,
        active,
    )
    return (middle + gathered_sum(parts), saved)


def layer_backward(grad_out, saved, params, dense, tables):
    (
        norm_in,
        step_bias,
        decay_log,
        skip_gain,
        conv_input,
        conv_state,
        gate_norm,
        norm_mid,
    ) = params
    proj, proj_output, shared, expert_gate, expert_up, expert_down = dense
    (
        resid,
        middle,
        mixed,
        rr,
        wide_in,
        gated,
        pull_core,
        wide_mid,
        shared_pre,
        lift_pre,
        shared_act,
        arrived,
        expert_pre,
        active,
    ) = saved
    count = resid.shape[0]
    hidden = shared.shape[1] // 3
    backs = range(groups())
    wide_out = spread(grad_out.astype(HALF))
    parts, rows_grad, gate_grads, lift_grads, shared_grads = [], [], [], [], []
    for back in backs:
        rows = dispatch(tables[back][1], wide_out[back])
        gate_e, lift_e = expert_pre[back]
        grad_act = project_back(rows, expert_down)
        grad_gate_e = (grad_act * lift_e * silu_slope(gate_e)).astype(HALF)
        grad_lift_e = (grad_act * jax.nn.silu(gate_e)).astype(HALF)
        result = give_back(
            project_back(grad_gate_e, expert_gate) + project_back(grad_lift_e, expert_up)
        )
        rows_grad.append(rows)
        gate_grads.append(grad_gate_e)
        lift_grads.append(grad_lift_e)
        gate_s, lift_s = shared_pre[back], lift_pre[back]
        grad_act_s = project(wide_out[back], shared[:, 2 * hidden :])
        grad_gate_s = grad_act_s * lift_s * silu_slope(gate_s)
        grad_lift_s = grad_act_s * jax.nn.silu(gate_s)
        grad_s = jnp.concatenate([grad_gate_s, grad_lift_s], axis=1).astype(HALF)
        shared_grads.append(grad_s)
        part = outer(tables[back][0], result) + project_back(grad_s, shared[:, : 2 * hidden])
        parts.append(part.astype(HALF))
    grad_normed = gathered_sum(parts)
    rows_in = jnp.concatenate(arrived, axis=0)
    rows_out = jnp.concatenate(rows_grad, axis=0)
    expert_grads = (
        outer(rows_in, jnp.concatenate(gate_grads, axis=0)),
        outer(rows_in, jnp.concatenate(lift_grads, axis=0)),
        outer(jnp.concatenate(active, axis=0), rows_out),
    )
    mids, outs = jnp.concatenate(wide_mid, axis=0), jnp.concatenate(wide_out, axis=0)
    grad_shared = jnp.concatenate(
        [
            outer(mids, jnp.concatenate(shared_grads, axis=0)).astype(HALF),
            outer(outs, jnp.concatenate(shared_act, axis=0)).astype(HALF),
        ],
        axis=1,
    )
    _, pull_mid = jax.vjp(rms_norm, middle, norm_mid)
    grad_middle, grad_norm_mid = pull_mid(grad_normed)
    grad_middle = grad_middle + grad_out
    along = jnp.sum(grad_middle * mixed, axis=1, keepdims=True)
    wide_mix = in_order(spread(grad_middle.astype(HALF)))
    sides = in_order(spread(jnp.concatenate([rr, along], axis=1)))
    rr_all, along_all = sides[:, :1], sides[:, 1:]
    grad_scaled = project(wide_mix, proj_output)
    normed_gate = gated * rr_all
    grad_proj_output = outer(wide_mix, (normed_gate * gate_norm).astype(HALF)).astype(HALF)
    grad_gate_norm = jnp.sum(grad_scaled * normed_gate, axis=0)
    grad_gated = rr_all * gate_norm * grad_scaled - gated * rr_all**3 * along_all / DI
    (
        grad_gate_pre,
        grad_input_pre,
        grad_state_pre,
        grad_step_pre,
        grad_conv_input,
        grad_conv_state,
        grad_step_bias,
        grad_decay_log,
        grad_skip_gain,
    ) = pull_core(grad_gated)
    grad_pre = jnp.concatenate(
        [
            grad_gate_pre.astype(HALF),
            grad_input_pre.astype(HALF),
            grad_state_pre.astype(HALF),
            grad_step_pre.astype(HALF),
        ],
        axis=1,
    )
    grad_proj = outer(wide_in, grad_pre).astype(HALF)
    grad_normed_in = gathered_sum(
        [project_back(block_of(grad_pre, back, count), proj).astype(HALF) for back in backs]
    )
    _, pull_in = jax.vjp(rms_norm, resid, norm_in)
    grad_resid, grad_norm_in = pull_in(grad_normed_in)
    small = (
        grad_norm_in,
        grad_norm_mid,
        grad_conv_state,
        grad_conv_input,
        grad_gate_norm,
        grad_step_bias,
        grad_decay_log,
        grad_skip_gain,
    )
    return (grad_resid + grad_middle, small, (grad_proj, grad_proj_output, grad_shared), expert_grads)


def flat(parts):
    return jnp.concatenate([part.reshape(-1) for part in parts])


def unflat(vector, shapes):
    result, start = [], 0
    for shape in shapes:
        size = 1
        for entry in shape:
            size *= entry
        result.append(vector[start : start + size].reshape(shape))
        start += size
    return result


def shards(
    tokens,
    cotangent,
    doc_lengths,
    routes,
    gates,
    norm_in,
    proj_gate,
    proj_input,
    proj_state,
    proj_step,
    step_bias,
    decay_log,
    skip_gain,
    conv_input,
    conv_state,
    gate_norm,
    proj_output,
    norm_mid,
    expert_gate,
    expert_up,
    expert_down,
    shared_gate,
    shared_up,
    shared_down,
):
    section_now = lax.axis_index("section")
    first = section_now == 0
    row_now = lax.axis_index("row")
    n_row, n_col = lax.axis_size("row"), lax.axis_size("col")
    count = tokens.shape[1]
    top = routes.shape[3]
    capacity = count * top * 4 // (3 * n_row * n_col)
    width = tokens.shape[2]

    def pair(own, other):
        return (jnp.where(first, own, other), jnp.where(first, other, own))

    small_in = (
        norm_in[0],
        step_bias[0],
        decay_log[0],
        skip_gain[0],
        conv_input[0],
        conv_state[0],
        gate_norm[0],
        norm_mid[0],
    )
    vector = flat(small_in)
    params = [unflat(part, [v.shape for v in small_in]) for part in pair(vector, swapped(vector))]

    def both_layers(weight):
        whole = lax.all_gather(weight, ("section", "row"), axis=0, tiled=True)
        return whole.reshape(2, n_row * weight.shape[0], weight.shape[1])

    proj = both_layers(
        jnp.concatenate([proj_gate[0], proj_input[0], proj_state[0], proj_step[0]], axis=1)
    )
    proj_out = both_layers(proj_output[0])
    shared = both_layers(jnp.concatenate([shared_gate[0], shared_up[0], shared_down[0]], axis=1))
    gate_all = lax.all_gather(expert_gate[0, 0], "section")
    up_all = lax.all_gather(expert_up[0, 0], "section")
    down_all = lax.all_gather(expert_down[0, 0], "section")
    dense = [
        (proj[s], proj_out[s], shared[s], gate_all[s], up_all[s], down_all[s]) for s in range(2)
    ]

    meta = jnp.concatenate([routes.astype(FLOAT), gates], axis=3)[0]
    keep = lax.dynamic_index_in_dim(meta, section_now, 0, keepdims=False)
    give = lax.dynamic_index_in_dim(meta, 1 - section_now, 0, keepdims=False)
    meta = jnp.concatenate(pair(keep, swapped(give)), axis=1)
    meta = lax.all_gather(meta, "col", axis=0)
    tables = [
        route_tables(meta[:, :, : 2 * top], top, capacity),
        route_tables(meta[:, :, 2 * top :], top, capacity),
    ]
    lengths = lax.dynamic_slice(
        doc_lengths, (section_now, row_now, 0), (1, 1, doc_lengths.shape[2])
    )
    labels = local_docs(lengths[0, 0], row_now, n_col * count)

    resid = lax.dynamic_index_in_dim(tokens, section_now, 0, keepdims=False)
    grad = lax.dynamic_index_in_dim(cotangent, section_now, 0, keepdims=False)
    outputs, stored = [], []
    for s in range(2):
        resid, saved = layer_forward(resid, params[s], dense[s], labels, tables[s])
        outputs.append(resid)
        stored.append(saved)
    grads = [None, None]
    backs = [None, None]
    for s in (1, 0):
        grad, small, dense_grads, expert_grads = layer_backward(
            grad, stored[s], params[s], dense[s], tables[s]
        )
        backs[s] = grad
        grads[s] = (small, dense_grads, expert_grads)

    def own_layer(first_value, second_value):
        keep = jnp.where(first, first_value, second_value)
        give = jnp.where(first, second_value, first_value).astype(HALF)
        return keep.astype(FLOAT) + swapped(give).astype(FLOAT)

    def own_rows(index):
        both = jnp.concatenate([grads[0][1][index], grads[1][1][index]], axis=0)
        return lax.psum_scatter(both, ("section", "row"), scatter_dimension=0, tiled=True)

    grad_proj, grad_out, grad_shared = [own_rows(index) for index in range(3)]
    expert_out = [own_layer(a, b) for a, b in zip(grads[0][2], grads[1][2])]
    shapes = [part.shape for part in grads[0][0]]
    vector = jnp.stack([flat(grads[0][0]), flat(grads[1][0])])
    vector = lax.psum(vector, ("section", "row"))
    vector = lax.dynamic_index_in_dim(vector, section_now, 0, keepdims=False)
    wide = 2 * width + conv_state.shape[1] * conv_state.shape[2]
    inner = gate_norm.shape[1]
    state = conv_state.shape[2]
    state_grad = grad_proj[:, 2 * inner : 2 * inner + state]
    shared_sum, state_grad = lax.psum((vector[:wide], state_grad), "col")
    (
        out_norm_in,
        out_norm_mid,
        out_conv_state,
        out_conv_input,
        out_gate_norm,
        out_step_bias,
        out_decay_log,
        out_skip_gain,
    ) = unflat(jnp.concatenate([shared_sum, vector[wide:]]), shapes)

    def per_micro(first_value, second_value):
        keep = jnp.where(first, first_value, second_value)
        other = swapped(jnp.where(first, second_value, first_value).astype(HALF)).astype(FLOAT)
        return jnp.stack(pair(keep, other))[None]

    hidden = shared_gate.shape[2]
    grad_proj, grad_out, grad_shared, state_grad = [
        part.astype(FLOAT)[None] for part in (grad_proj, grad_out, grad_shared, state_grad)
    ]
    return (
        per_micro(outputs[0], outputs[1]),
        per_micro(backs[0], backs[1]),
        out_norm_in[None],
        grad_proj[:, :, :inner],
        grad_proj[:, :, inner : 2 * inner],
        state_grad,
        grad_proj[:, :, 2 * inner + state :],
        out_step_bias[None],
        out_decay_log[None],
        out_skip_gain[None],
        out_conv_input[None],
        out_conv_state[None],
        out_gate_norm[None],
        grad_out,
        out_norm_mid[None],
        expert_out[0][None, None],
        expert_out[1][None, None],
        expert_out[2][None, None],
        grad_shared[:, :, :hidden],
        grad_shared[:, :, hidden : 2 * hidden],
        grad_shared[:, :, 2 * hidden :],
    )


def solution(mesh):
    in_specs = (
        P(None, ("row", "col"), None),
        P(None, ("row", "col"), None),
        P(),
        P("section", None, ("row", "col"), None),
        P("section", None, ("row", "col"), None),
        P("section", None),
        P("section", "row", "col"),
        P("section", "row", "col"),
        P("section", "row", None),
        P("section", "row", "col"),
        P("section", "col"),
        P("section", "col"),
        P("section", "col"),
        P("section", None, "col"),
        P("section", None, None),
        P("section", "col"),
        P("section", "row", "col"),
        P("section", None),
        P("section", ("row", "col"), None, None),
        P("section", ("row", "col"), None, None),
        P("section", ("row", "col"), None, None),
        P("section", "row", "col"),
        P("section", "row", "col"),
        P("section", "row", "col"),
    )
    out_specs = (
        P("section", None, ("row", "col"), None),
        P("section", None, ("row", "col"), None),
        P("section", None),
        P("section", "row", "col"),
        P("section", "row", "col"),
        P("section", "row", None),
        P("section", "row", "col"),
        P("section", "col"),
        P("section", "col"),
        P("section", "col"),
        P("section", None, "col"),
        P("section", None, None),
        P("section", "col"),
        P("section", "row", "col"),
        P("section", None),
        P("section", ("row", "col"), None, None),
        P("section", ("row", "col"), None, None),
        P("section", ("row", "col"), None, None),
        P("section", "row", "col"),
        P("section", "row", "col"),
        P("section", "row", "col"),
    )
    return jax.shard_map(shards, mesh=mesh, in_specs=in_specs, out_specs=out_specs, check_vma=False)
```

```python
import functools

import jax
import jax.numpy as jnp
from jax import lax
from jax.experimental import pallas as pl
from jax.experimental.pallas import tpu as pltpu
from jax.sharding import PartitionSpec as P

DI = 3072
HEAD = 64
LANES = 128
CHUNK = 256
VMEM_BYTES = 48 * 2**20

EPS = 1e-05
HIGH = lax.Precision.HIGHEST
FLOAT = jnp.float32
HALF = jnp.bfloat16


def shifted(block, axis, distance):
    count = lax.axis_size(axis)
    if distance % count == 0:
        return block
    return lax.ppermute(block, axis, [(i, (i + distance) % count) for i in range(count)])


def swapped(block):
    return lax.ppermute(block, "section", [(0, 1), (1, 0)])


def after(value, *others):
    return lax.optimization_barrier((value, *others))[0]


def rms_norm(value, gain):
    return value * lax.rsqrt(jnp.mean(value * value, axis=-1, keepdims=True) + EPS) * gain


def local_docs(lengths, row_now, length):
    bounds = jnp.cumsum(lengths)[:-1]
    place = jnp.arange(length, dtype=jnp.int32)
    inner = jnp.sum((place[:, None] >= bounds[None, :]).astype(jnp.int32), axis=1)
    return inner + row_now * lengths.shape[0]


def project(left, right):
    return jnp.dot(left, right, preferred_element_type=FLOAT)


def project_back(left, right):
    return lax.dot_general(left, right, (((1,), (1,)), ((), ())), preferred_element_type=FLOAT)


def outer(left, right):
    return lax.dot_general(left, right, (((0,), (0,)), ((), ())), preferred_element_type=FLOAT)


def silu_slope(value):
    sigma = jax.nn.sigmoid(value)
    return sigma * (1.0 + value * (1.0 - sigma))


def groups():
    count = lax.axis_size("col")
    return count if count <= 4 else 1


def chunks():
    count = groups()
    order = [0] + [step * side for step in range(1, count // 2 + 1) for side in (1, -1)]
    order = [back % count for back in order]
    order = list(dict.fromkeys(order))
    return [tuple(order[at : at + 2]) for at in range(0, count, 2)]


def spread(block, staged=False):
    count = groups()
    if count == 1:
        return [lax.all_gather(block, "col", axis=0, tiled=True)]
    result = [block] * count
    result[1] = shifted(block, "col", 1)
    source = after(block, result[1]) if staged else block
    for back in range(count - 1, 1, -1):
        result[back] = shifted(source, "col", back)
    return result


def joined(blocks):
    return blocks[0] if len(blocks) == 1 else jnp.concatenate(blocks, axis=0)


def in_order(blocks, axis):
    count = len(blocks)
    if count == 1:
        return blocks[0]
    rows = blocks[0].shape[0]
    line = jnp.concatenate(blocks[::-1] + blocks[:0:-1], axis=0)
    start = (count - 1 - lax.axis_index(axis)) * rows
    return lax.dynamic_slice_in_dim(line, start, count * rows, axis=0)


def gathered_sum(parts):
    if len(parts) == 1:
        return lax.psum_scatter(parts[0], "col", scatter_dimension=0, tiled=True).astype(FLOAT)
    total = parts[0].astype(FLOAT)
    for back in range(1, len(parts)):
        total = total + shifted(parts[back], "col", -back).astype(FLOAT)
    return total


def block_of(values, back):
    rows = values.shape[0] // groups()
    return values[back * rows : (back + 1) * rows]


def turn():
    place = lax.axis_index("col") if groups() > 1 else jnp.int32(0)
    return place.astype(jnp.int32).reshape(1)


def route_tables(blocks, top, capacity, layers):
    n_row, n_col = lax.axis_size("row"), lax.axis_size("col")
    slots = len(chunks()[0]) * (n_col // groups()) * capacity
    experts = (jnp.arange(n_row) * n_col + lax.axis_index("col")).astype(FLOAT)
    now = jnp.stack([joined([blocks[back] for back in chunk]) for chunk in chunks()])
    parts, count = now.shape[:2]
    now = now.reshape(parts, count, layers, 2, top).transpose(2, 0, 3, 4, 1)
    match = now[:, :, 0, None] == experts[None, None, :, None, None]
    hit = jnp.any(match, axis=3)
    weight = jnp.sum(jnp.where(match, now[:, :, 1, None], 0.0), axis=3)
    order = jnp.arange(count, dtype=jnp.int32)
    triangle = (order[:, None] <= order[None, :]).astype(HALF)
    place = project(hit.astype(HALF).reshape(-1, count), triangle).reshape(hit.shape)
    slot = jnp.arange(1, slots + 1, dtype=jnp.int32).astype(FLOAT)
    chosen = (place[:, :, :, None, :] == slot[:, None]) & hit[:, :, :, None, :]
    shape = (layers, parts, n_row * slots, count)
    plain = chosen.astype(HALF).reshape(shape)
    scaled = jnp.where(chosen, weight[:, :, :, None, :], 0.0).astype(HALF).reshape(shape)
    return [[(plain[s, i], scaled[s, i]) for i in range(parts)] for s in range(layers)]


def to_experts(rows):
    return lax.all_to_all(rows.astype(HALF), "row", split_axis=0, concat_axis=0, tiled=True)


def summed_rows(values, reverse):
    step = min(values.shape[0], CHUNK)
    count = values.shape[0] // step
    place = lax.broadcasted_iota(jnp.int32, (step, step), 0)
    other = lax.broadcasted_iota(jnp.int32, (step, step), 1)
    before = (place <= other) if reverse else (place >= other)
    triangle = before.astype(FLOAT)
    carry = jnp.zeros((1, values.shape[1]), FLOAT)
    parts = [None] * count
    for index in reversed(range(count)) if reverse else range(count):
        part = values[index * step : (index + 1) * step]
        run = jnp.dot(triangle, part, precision=HIGH, preferred_element_type=FLOAT) + carry
        carry = run[:1] if reverse else run[step - 1 :]
        parts[index] = run
    return parts[0] if count == 1 else jnp.concatenate(parts, axis=0)


def head_columns(rows, columns, head_width):
    head = lax.broadcasted_iota(jnp.int32, (rows, columns), 0) * head_width
    column = lax.broadcasted_iota(jnp.int32, (rows, columns), 1)
    return ((column >= head) & (column < head + head_width)).astype(FLOAT)


def sigmoid(value):
    return 1.0 / (1.0 + jnp.exp(-value))


def step_sizes(step_pre, step_row_ref):
    shifted_pre = step_pre + step_row_ref[0:1, :]
    sizes = jnp.maximum(shifted_pre, 0.0) + jnp.log1p(jnp.exp(-jnp.abs(shifted_pre)))
    return shifted_pre, sizes, -jnp.exp(step_row_ref[1:2, :])


def conv_rows(values, weight_ref, columns, marks_ref):
    width = weight_ref.shape[0]
    result = values * weight_ref[width - 1 : width, columns]
    for back in range(1, width):
        moved = pltpu.roll(values, back, 0) * marks_ref[:, back : back + 1]
        result = result + moved * weight_ref[width - 1 - back : width - back, columns]
    return result


def conv_rows_back(grad, values, weight_ref, columns, marks_ref, weight_grad_ref):
    width = weight_ref.shape[0]
    rows = values.shape[0]
    result = grad * weight_ref[width - 1 : width, columns]
    weight_grad_ref[width - 1 : width, columns] = jnp.sum(grad * values, axis=0, keepdims=True)
    for back in range(1, width):
        kept = grad * marks_ref[:, back : back + 1]
        taps = jnp.sum(kept * pltpu.roll(values, back, 0), axis=0, keepdims=True)
        weight_grad_ref[width - 1 - back : width - back, columns] = taps
        moved = pltpu.roll(kept, rows - back, 0)
        result = result + moved * weight_ref[width - 1 - back : width - back, columns]
    return result


def copy_in_order(source_ref, target_ref, place_ref, parts):
    if parts == 1:
        return source_ref
    rows = source_ref.shape[0] // parts
    for index in range(parts):
        target_ref[index * rows : (index + 1) * rows, :] = source_ref[
            block_rows(index, rows, place_ref, parts), :
        ]
    return target_ref


def block_rows(index, rows, place_ref, parts):
    if parts == 1:
        return slice(0, rows)
    back = lax.rem(place_ref[0] - index + parts, parts)
    return pl.ds(pl.multiple_of(back * rows, rows), rows)


def mixer_forward_kernel(
    heads,
    parts,
    pre_in_ref,
    conv_input_ref,
    conv_state_ref,
    step_row_ref,
    wide_row_ref,
    marks_ref,
    labels_ref,
    place_ref,
    y_ref,
    scaled_ref,
    total_ref,
    pre_ref,
    x_ref,
    dosed_ref,
    keys_ref,
    queries_ref,
):
    length, wide = y_ref.shape
    states = conv_state_ref.shape[1] // 2
    state_at, step_at = 2 * wide, 2 * wide + 2 * states
    head_width = HEAD
    pre_ref = copy_in_order(pre_in_ref, pre_ref, place_ref, parts)
    _, sizes, rate = step_sizes(pre_ref[:, step_at : step_at + LANES], step_row_ref)
    running = summed_rows(sizes * rate, False)
    running_t = running.T
    expand = head_columns(LANES, wide, head_width)
    for start in range(0, wide, LANES):
        columns = slice(start, start + LANES)
        conv = conv_rows(
            pre_ref[:, wide + start : wide + start + LANES], conv_input_ref, columns, marks_ref
        )
        x = conv * sigmoid(conv)
        x_ref[:, columns] = x
        dose = jnp.dot(sizes, expand[:, columns], precision=HIGH, preferred_element_type=FLOAT)
        dosed_ref[:, columns] = (x * dose).astype(HALF)
    for part, target in ((0, keys_ref), (1, queries_ref)):
        columns = slice(part * states, (part + 1) * states)
        conv = conv_rows(
            pre_ref[:, state_at + part * states : state_at + (part + 1) * states],
            conv_state_ref,
            columns,
            marks_ref,
        )
        target[...] = (conv * sigmoid(conv)).astype(HALF)
    block = min(length, CHUNK)
    place = lax.broadcasted_iota(jnp.int32, (block, block), 0)
    other = lax.broadcasted_iota(jnp.int32, (block, block), 1)
    for late in range(length // block):
        rows = slice(late * block, (late + 1) * block)
        for early in range(late + 1):
            past = slice(early * block, (early + 1) * block)
            same = marks_ref[rows, 0:1] == labels_ref[:, past]
            if late == early:
                same = same & (place >= other)
            mask = jnp.where(same, 0.0, -1e30)
            scores = lax.dot_general(
                queries_ref[rows, :],
                keys_ref[past, :],
                (((1,), (1,)), ((), ())),
                preferred_element_type=FLOAT,
            )
            for head in range(heads):
                columns = slice(head * head_width, (head + 1) * head_width)
                spread_log = running[rows, head : head + 1] - running_t[head : head + 1, past]
                mixing = (jnp.exp(spread_log + mask) * scores).astype(HALF)
                inner = jnp.dot(mixing, dosed_ref[past, columns], preferred_element_type=FLOAT)
                if early == 0:
                    y_ref[rows, columns] = inner
                else:
                    y_ref[rows, columns] += inner
    total = jnp.zeros((length, 1), FLOAT)
    for start in range(0, wide, LANES):
        columns = slice(start, start + LANES)
        y = y_ref[:, columns]
        if heads * head_width < start + LANES:
            lane = lax.broadcasted_iota(jnp.int32, y.shape, 1) + start
            y = jnp.where(lane < heads * head_width, y, 0.0)
        y = y + wide_row_ref[1:2, columns] * x_ref[:, columns]
        gate = pre_ref[:, columns]
        gated = y * gate * sigmoid(gate)
        y_ref[:, columns] = y
        scaled = (gated * wide_row_ref[0:1, columns]).astype(HALF)
        each = length // parts
        for index in range(parts):
            block_at = block_rows(index, each, place_ref, parts)
            scaled_ref[block_at, columns] = scaled[index * each : (index + 1) * each]
        total = total + jnp.sum(gated * gated, axis=1, keepdims=True)
    each = length // parts
    for index in range(parts):
        block_at = block_rows(index, each, place_ref, parts)
        total_ref[block_at, :] = total[index * each : (index + 1) * each]


def mixer_backward_kernel(
    heads,
    parts,
    inner_all,
    pre_in_ref,
    y_ref,
    grad_in_ref,
    sides_in_ref,
    conv_input_ref,
    conv_state_ref,
    step_row_ref,
    wide_row_ref,
    marks_ref,
    labels_ref,
    place_ref,
    grad_pre_ref,
    wide_grad_ref,
    conv_input_grad_ref,
    conv_state_grad_ref,
    step_grad_ref,
    pre_ref,
    grad_ref,
    sides_ref,
    x_ref,
    dosed_ref,
    dose_ref,
    slope_ref,
    dy_ref,
    z_ref,
    bc_ref,
    bc_slope_ref,
    bc_grad_ref,
):
    length, wide = y_ref.shape
    states = conv_state_ref.shape[1] // 2
    state_at, step_at = 2 * wide, 2 * wide + 2 * states
    head_width = HEAD
    each = length // parts
    pre_ref = copy_in_order(pre_in_ref, pre_ref, place_ref, parts)
    grad_ref = copy_in_order(grad_in_ref, grad_ref, place_ref, parts)
    sides_ref = copy_in_order(sides_in_ref, sides_ref, place_ref, parts)

    def put(value, start):
        for index in range(parts):
            grad_pre_ref[block_rows(index, each, place_ref, parts), start : start + LANES] = value[
                index * each : (index + 1) * each
            ]

    shifted_pre, sizes, rate = step_sizes(pre_ref[:, step_at : step_at + LANES], step_row_ref)
    running = summed_rows(sizes * rate, False)
    running_t = running.T
    expand = head_columns(LANES, wide, head_width)
    rr = sides_ref[:, 0:1]
    pull = rr * rr * rr * sides_ref[:, 1:2] * (1.0 / inner_all)
    for start in range(0, wide, LANES):
        columns = slice(start, start + LANES)
        gate = pre_ref[:, columns]
        y = y_ref[:, columns]
        grad = grad_ref[:, columns]
        gain = wide_row_ref[0:1, columns]
        sigma = sigmoid(gate)
        silu = gate * sigma
        gated = y * silu
        normed = gated * rr
        wide_grad_ref[0:1, columns] = jnp.sum(grad * normed, axis=0, keepdims=True)
        grad_gated = rr * gain * grad - gated * pull
        slope = sigma * (1.0 + gate * (1.0 - sigma))
        put((grad_gated * y * slope).astype(HALF), start)
        dy = grad_gated * silu
        dy_ref[:, columns] = dy
        conv = conv_rows(
            pre_ref[:, wide + start : wide + start + LANES], conv_input_ref, columns, marks_ref
        )
        sigma = sigmoid(conv)
        x = conv * sigma
        x_ref[:, columns] = x
        slope_ref[:, columns] = sigma * (1.0 + conv * (1.0 - sigma))
        dose = jnp.dot(sizes, expand[:, columns], precision=HIGH, preferred_element_type=FLOAT)
        dose_ref[:, columns] = dose
        dosed_ref[:, columns] = (x * dose).astype(HALF)
        wide_grad_ref[1:2, columns] = jnp.sum(dy * x, axis=0, keepdims=True)
    for start in range(0, 2 * states, LANES):
        columns = slice(start, start + LANES)
        conv = conv_rows(
            pre_ref[:, state_at + start : state_at + start + LANES],
            conv_state_ref,
            columns,
            marks_ref,
        )
        sigma = sigmoid(conv)
        bc_ref[:, columns] = (conv * sigma).astype(HALF)
        bc_slope_ref[:, columns] = sigma * (1.0 + conv * (1.0 - sigma))
    block = min(length, CHUNK)
    place = lax.broadcasted_iota(jnp.int32, (block, block), 0)
    other = lax.broadcasted_iota(jnp.int32, (block, block), 1)
    z_ref[...] = jnp.zeros(z_ref.shape, FLOAT)
    bc_grad_ref[...] = jnp.zeros(bc_grad_ref.shape, FLOAT)
    for late in range(length // block):
        rows = slice(late * block, (late + 1) * block)
        for early in range(late + 1):
            past = slice(early * block, (early + 1) * block)
            same = marks_ref[past, 0:1] == labels_ref[:, rows]
            if late == early:
                same = same & (place <= other)
            mask = jnp.where(same, 0.0, -1e30)
            keys = bc_ref[past, :states]
            queries = bc_ref[rows, states:]
            scores = lax.dot_general(
                keys, queries, (((1,), (1,)), ((), ())), preferred_element_type=FLOAT
            )
            mixed = jnp.zeros((block, block), FLOAT)
            for head in range(heads):
                columns = slice(head * head_width, (head + 1) * head_width)
                spread_log = running_t[head : head + 1, rows] - running[past, head : head + 1]
                decay = jnp.exp(spread_log + mask)
                mixing = (decay * scores).astype(HALF)
                dy = dy_ref[rows, columns].astype(HALF)
                z_ref[past, columns] += jnp.dot(mixing, dy, preferred_element_type=FLOAT)
                along = lax.dot_general(
                    dosed_ref[past, columns],
                    dy,
                    (((1,), (1,)), ((), ())),
                    preferred_element_type=FLOAT,
                )
                mixed = mixed + decay * along
            mixed = mixed.astype(HALF)
            bc_grad_ref[past, :states] += jnp.dot(mixed, queries, preferred_element_type=FLOAT)
            bc_grad_ref[rows, states:] += lax.dot_general(
                mixed, keys, (((0,), (0,)), ((), ())), preferred_element_type=FLOAT
            )
    direct = jnp.zeros((length, LANES), FLOAT)
    balance = jnp.zeros((length, LANES), FLOAT)
    for start in range(0, wide, LANES):
        columns = slice(start, start + LANES)
        x, z, dy = x_ref[:, columns], z_ref[:, columns], dy_ref[:, columns]
        skip = wide_row_ref[1:2, columns]
        collapse = (((1,), (1,)), ((), ()))
        both = dy.astype(HALF).astype(FLOAT) * (y_ref[:, columns] - skip * x)
        both = both - dosed_ref[:, columns].astype(FLOAT) * z
        heads_of = expand[:, columns]
        direct = direct + lax.dot_general(
            x * z, heads_of, collapse, precision=HIGH, preferred_element_type=FLOAT
        )
        balance = balance + lax.dot_general(
            both, heads_of, collapse, precision=HIGH, preferred_element_type=FLOAT
        )
        grad_conv = (dose_ref[:, columns] * z + skip * dy) * slope_ref[:, columns]
        grad_in = conv_rows_back(
            grad_conv,
            pre_ref[:, wide + start : wide + start + LANES],
            conv_input_ref,
            columns,
            marks_ref,
            conv_input_grad_ref,
        )
        put(grad_in.astype(HALF), wide + start)
    for start in range(0, 2 * states, LANES):
        columns = slice(start, start + LANES)
        grad_in = conv_rows_back(
            bc_grad_ref[:, columns] * bc_slope_ref[:, columns],
            pre_ref[:, state_at + start : state_at + start + LANES],
            conv_state_ref,
            columns,
            marks_ref,
            conv_state_grad_ref,
        )
        put(grad_in.astype(HALF), state_at + start)
    crossing = summed_rows(balance, True)
    grad_step = (direct + rate * crossing) * sigmoid(shifted_pre)
    put(grad_step.astype(HALF), step_at)
    step_grad_ref[0:1, :] = jnp.sum(grad_step, axis=0, keepdims=True)
    step_grad_ref[1:2, :] = rate * jnp.sum(sizes * crossing, axis=0, keepdims=True)


def ordered_copy(shape):
    return pltpu.VMEM(shape if groups() > 1 else (8, LANES), FLOAT)


def whole_call(kernel, inputs, results, scratch, name):
    whole = pl.BlockSpec(memory_space=pltpu.VMEM)
    place = pl.BlockSpec(memory_space=pltpu.SMEM)
    return pl.pallas_call(
        kernel,
        in_specs=[whole] * (inputs - 1) + [place],
        out_shape=results,
        scratch_shapes=scratch,
        compiler_params=pltpu.CompilerParams(vmem_limit_bytes=VMEM_BYTES),
        name=name,
    )


def mixer_forward(pre, heads, wide, mixer):
    length = pre.shape[0]
    kernel = functools.partial(mixer_forward_kernel, heads, groups())
    states = mixer[1].shape[1] // 2
    return whole_call(
        kernel,
        1 + len(mixer),
        (
            jax.ShapeDtypeStruct((length, wide), FLOAT),
            jax.ShapeDtypeStruct((length, wide), HALF),
            jax.ShapeDtypeStruct((length, 1), FLOAT),
        ),
        [
            ordered_copy(pre.shape),
            pltpu.VMEM((length, wide), FLOAT),
            pltpu.VMEM((length, wide), HALF),
            pltpu.VMEM((length, states), HALF),
            pltpu.VMEM((length, states), HALF),
        ],
        "mixer_forward",
    )(pre, *mixer)


def mixer_backward(pre, y, grad, sides, heads, mixer):
    length, wide = y.shape
    kernel = functools.partial(mixer_backward_kernel, heads, groups(), DI)
    double = mixer[1].shape[1]
    square = pltpu.VMEM((length, wide), FLOAT)
    return whole_call(
        kernel,
        4 + len(mixer),
        (
            jax.ShapeDtypeStruct(pre.shape, HALF),
            jax.ShapeDtypeStruct((2, wide), FLOAT),
            jax.ShapeDtypeStruct((4, wide), FLOAT),
            jax.ShapeDtypeStruct((4, double), FLOAT),
            jax.ShapeDtypeStruct((2, LANES), FLOAT),
        ),
        [
            ordered_copy(pre.shape),
            ordered_copy(y.shape),
            ordered_copy(sides.shape),
            square,
            pltpu.VMEM((length, wide), HALF),
            square,
            square,
            square,
            square,
            pltpu.VMEM((length, double), HALF),
            pltpu.VMEM((length, double), FLOAT),
            pltpu.VMEM((length, double), FLOAT),
        ],
        "mixer_backward",
    )(pre, y, grad, sides, *mixer)


def layer_forward(resid, params, dense, mixer, tables):
    norm_in, norm_mid = params
    proj, proj_output, shared, expert_gate, expert_up, expert_down = dense
    wide = mixer[0].shape[1]
    heads = mixer[-1]
    hidden = shared.shape[1] // 3
    backs = range(groups())
    wide_in = joined(spread(rms_norm(resid, norm_in).astype(HALF)))
    pre = project(wide_in, proj)
    y, scaled, total_part = mixer_forward(pre, heads, wide, mixer[:-1])
    total = gathered_sum([block_of(total_part, back) for back in backs])
    mixed = gathered_sum(
        [project_back(block_of(scaled, back), proj_output).astype(HALF) for back in backs]
    )
    if callable(tables):
        tables = tables(scaled)
    rr = lax.rsqrt(total / DI + EPS)
    middle = resid + mixed * rr
    wide_mid = spread(rms_norm(middle, norm_mid).astype(HALF), staged=True)
    shared_pre, shared_act, arrived, expert_pre, active = [], [], [], [], []
    parts = [None] * groups()
    for index, chunk in enumerate(chunks()):
        tokens = joined([wide_mid[back] for back in chunk])
        plain, scaling = tables[0][index]
        rows = to_experts(project(plain, tokens))
        gate_e = project(rows, expert_gate)
        lift_e = project(rows, expert_up)
        act_e = (jax.nn.silu(gate_e) * lift_e).astype(HALF)
        result = to_experts(project(act_e, expert_down))
        arrived.append(rows)
        expert_pre.append((gate_e, lift_e))
        active.append(act_e)
        gate_s = project(tokens, shared[:, :hidden])
        lift_s = project(tokens, shared[:, hidden : 2 * hidden])
        act_s = (jax.nn.silu(gate_s) * lift_s).astype(HALF)
        shared_pre.append((gate_s, lift_s))
        shared_act.append(act_s)
        part = outer(scaling, result) + project_back(act_s, shared[:, 2 * hidden :])
        part = part.astype(HALF)
        rows_each = part.shape[0] // len(chunk)
        for at, back in enumerate(chunk):
            parts[back] = part[at * rows_each : (at + 1) * rows_each]
    saved = (
        resid,
        middle,
        mixed,
        rr,
        wide_in,
        pre,
        y,
        scaled,
        wide_mid,
        shared_pre,
        shared_act,
        arrived,
        expert_pre,
        active,
    )
    return (middle + gathered_sum(parts), saved, tables)


def layer_backward(grad_out, saved, params, dense, mixer, tables, pending):
    norm_in, norm_mid = params
    proj, proj_output, shared, expert_gate, expert_up, expert_down = dense
    (
        resid,
        middle,
        mixed,
        rr,
        wide_in,
        pre,
        y,
        scaled,
        wide_mid,
        shared_pre,
        shared_act,
        arrived,
        expert_pre,
        active,
    ) = saved
    heads = mixer[-1]
    hidden = shared.shape[1] // 3
    backs = range(groups())
    wide_out = spread(grad_out.astype(HALF), staged=True)
    parts = [None] * groups()
    rows_grad, gate_grads, lift_grads, shared_grads = [], [], [], []
    for index, chunk in enumerate(chunks()):
        tokens = joined([wide_out[back] for back in chunk])
        plain, scaling = tables[index]
        rows = to_experts(project(scaling, tokens))
        gate_e, lift_e = expert_pre[index]
        grad_act = project_back(rows, expert_down)
        grad_gate_e = (grad_act * lift_e * silu_slope(gate_e)).astype(HALF)
        grad_lift_e = (grad_act * jax.nn.silu(gate_e)).astype(HALF)
        result = to_experts(
            project_back(grad_gate_e, expert_gate) + project_back(grad_lift_e, expert_up)
        )
        rows_grad.append(rows)
        gate_grads.append(grad_gate_e)
        lift_grads.append(grad_lift_e)
        gate_s, lift_s = shared_pre[index]
        grad_act_s = project(tokens, shared[:, 2 * hidden :])
        grad_gate_s = (grad_act_s * lift_s * silu_slope(gate_s)).astype(HALF)
        grad_lift_s = (grad_act_s * jax.nn.silu(gate_s)).astype(HALF)
        shared_grads.append((grad_gate_s, grad_lift_s))
        part = (
            outer(plain, result)
            + project_back(grad_gate_s, shared[:, :hidden])
            + project_back(grad_lift_s, shared[:, hidden : 2 * hidden])
        )
        part = part.astype(HALF)
        rows_each = part.shape[0] // len(chunk)
        for at, back in enumerate(chunk):
            parts[back] = part[at * rows_each : (at + 1) * rows_each]
    grad_normed = gathered_sum(parts)
    _, pull_mid = jax.vjp(rms_norm, middle, norm_mid)
    grad_middle, grad_norm_mid = pull_mid(grad_normed)
    grad_middle = grad_middle + grad_out
    along = jnp.sum(grad_middle * mixed, axis=1, keepdims=True)
    wide_mix = joined(spread(grad_middle.astype(HALF)))
    sides = joined(spread(jnp.concatenate([rr, along], axis=1)))
    rows_in, rows_out = joined(arrived), joined(rows_grad)
    expert_grads = (
        outer(rows_in, joined(gate_grads)),
        outer(rows_in, joined(lift_grads)),
        outer(joined(active), rows_out),
    )
    order = [back for chunk in chunks() for back in chunk]
    mids, outs = joined([wide_mid[back] for back in order]), joined([wide_out[back] for back in order])
    grad_shared = (
        outer(mids, joined([pair[0] for pair in shared_grads])).astype(HALF),
        outer(mids, joined([pair[1] for pair in shared_grads])).astype(HALF),
        outer(outs, joined(shared_act)).astype(HALF),
    )
    expert_grads, grad_shared = pending(expert_grads, grad_shared)
    wide_mix = after(wide_mix, expert_grads, grad_shared)
    grad_proj_output = outer((wide_mix * sides[:, :1]).astype(HALF), scaled).astype(HALF)
    grad_scaled = project(wide_mix, proj_output)
    grad_pre, wide_grads, grad_conv_input, grad_conv_state, step_grads = mixer_backward(
        pre, y, grad_scaled, sides, heads, mixer[:-1]
    )
    grad_normed_in = gathered_sum(
        [project_back(block_of(grad_pre, back), proj).astype(HALF) for back in backs]
    )
    grad_proj = outer(wide_in, grad_pre).astype(HALF)
    _, pull_in = jax.vjp(rms_norm, resid, norm_in)
    grad_resid, grad_norm_in = pull_in(grad_normed_in)
    small = (
        grad_norm_in,
        grad_norm_mid,
        grad_conv_state,
        grad_conv_input,
        wide_grads,
        step_grads,
    )
    return (grad_resid + grad_middle, small, (grad_proj, grad_proj_output, grad_shared), expert_grads)


def flat(parts):
    return jnp.concatenate([part.reshape(-1) for part in parts])


def unflat(vector, shapes):
    result, start = [], 0
    for shape in shapes:
        size = 1
        for entry in shape:
            size *= entry
        result.append(vector[start : start + size].reshape(shape))
        start += size
    return result


def widened(value, columns):
    return jnp.pad(value, ((0, 0), (0, columns - value.shape[1])))


def shards(
    tokens,
    cotangent,
    doc_lengths,
    routes,
    gates,
    norm_in,
    proj_gate,
    proj_input,
    proj_state,
    proj_step,
    step_bias,
    decay_log,
    skip_gain,
    conv_input,
    conv_state,
    gate_norm,
    proj_output,
    norm_mid,
    expert_gate,
    expert_up,
    expert_down,
    shared_gate,
    shared_up,
    shared_down,
):
    section_now = lax.axis_index("section")
    first = section_now == 0
    row_now = lax.axis_index("row")
    n_row, n_col = lax.axis_size("row"), lax.axis_size("col")
    count = tokens.shape[1]
    top = routes.shape[3]
    capacity = count * top * 4 // (3 * n_row * n_col)
    width = tokens.shape[2]
    heads = step_bias.shape[1]
    inner = gate_norm.shape[1]
    state = conv_state.shape[2]
    wide = -(-inner // LANES) * LANES

    def pair(own, other):
        return (jnp.where(first, own, other), jnp.where(first, other, own))

    small_in = (
        norm_in[0],
        norm_mid[0],
        widened(conv_input[0], wide),
        conv_state[0],
        widened(jnp.concatenate([step_bias, decay_log], axis=0), LANES),
        widened(jnp.concatenate([gate_norm, jnp.repeat(skip_gain, HEAD, axis=1)], axis=0), wide),
    )
    vector = flat(small_in)
    small_all = [unflat(part, [v.shape for v in small_in]) for part in pair(vector, swapped(vector))]

    def both_layers(weight):
        whole = lax.all_gather(weight, ("section", "row"), axis=0, tiled=True)
        return whole.reshape(2, n_row * weight.shape[0], weight.shape[1])

    proj = both_layers(
        jnp.concatenate(
            [
                widened(proj_gate[0], wide),
                widened(proj_input[0], wide),
                proj_state[0],
                widened(proj_step[0], LANES),
            ],
            axis=1,
        )
    )
    proj_out = both_layers(widened(proj_output[0], wide))
    gate_all = lax.all_gather(expert_gate[0, 0], "section")
    up_all = lax.all_gather(expert_up[0, 0], "section")
    down_all = lax.all_gather(expert_down[0, 0], "section")
    shared = both_layers(jnp.concatenate([shared_gate[0], shared_up[0], shared_down[0]], axis=1))
    dense = [
        (proj[s], proj_out[s], shared[s], gate_all[s], up_all[s], down_all[s]) for s in range(2)
    ]

    meta = jnp.concatenate([routes.astype(FLOAT), gates], axis=3)[0]
    keep = lax.dynamic_index_in_dim(meta, section_now, 0, keepdims=False)
    give = lax.dynamic_index_in_dim(meta, 1 - section_now, 0, keepdims=False)
    meta = jnp.concatenate(pair(keep, swapped(give)), axis=1)

    def tables_once(scaled):
        return route_tables(spread(after(meta, scaled)), top, capacity, 2)

    lengths = lax.dynamic_slice(
        doc_lengths, (section_now, row_now, 0), (1, 1, doc_lengths.shape[2])
    )
    labels = local_docs(lengths[0, 0], row_now, n_col * count)
    marks = [labels.astype(FLOAT)]
    for back in range(1, conv_input.shape[1]):
        prior = jnp.pad(labels, (back, 0), constant_values=-1)[:-back]
        marks.append((prior == labels).astype(FLOAT))
    marks = jnp.stack(marks, axis=1)
    label_row = labels.astype(FLOAT)[None]
    place = turn()
    mixers = [
        (conv_in, conv_st, step_row, wide_row, marks, label_row, place, heads)
        for _, _, conv_in, conv_st, step_row, wide_row in small_all
    ]
    params = [part[:2] for part in small_all]

    resid = lax.dynamic_index_in_dim(tokens, section_now, 0, keepdims=False)
    grad = lax.dynamic_index_in_dim(cotangent, section_now, 0, keepdims=False)
    outputs, stored = [], []
    tables = tables_once
    for s in range(2):
        resid, saved, tables = layer_forward(
            resid, params[s], dense[s], mixers[s], tables if s == 0 else both_tables[1:]
        )
        outputs.append(resid)
        stored.append(saved)
        if s == 0:
            both_tables = tables

    def own_layer(first_value, second_value):
        keep = jnp.where(first, first_value, second_value)
        give = jnp.where(first, second_value, first_value).astype(HALF)
        return keep + swapped(give).astype(FLOAT)

    def row_sums(halves):
        both = jnp.concatenate(halves, axis=0)
        return lax.psum_scatter(both, ("section", "row"), scatter_dimension=0, tiled=True)

    def own_halves(first_value, second_value):
        keep = jnp.where(first, first_value, second_value)
        give = jnp.where(first, second_value, first_value)
        return pair(keep, swapped(give))

    held = {}

    def keep_first(expert_grads, grad_shared):
        held["experts"] = expert_grads
        return expert_grads, grad_shared

    def settle(expert_grads, grad_shared):
        return [own_layer(a, b) for a, b in zip(expert_grads, held["experts"])], grad_shared

    grads = [None, None]
    backs = [None, None]
    sums = [None, None]
    for s in (1, 0):
        grad, small, (grad_proj, grad_out, grad_shared), expert_grads = layer_backward(
            grad,
            stored[s],
            params[s],
            dense[s],
            mixers[s],
            both_tables[s],
            keep_first if s else settle,
        )
        backs[s] = grad
        grads[s] = small
        mixed = jnp.concatenate([*grad_shared, grad_out], axis=1)
        middle = mixed.shape[1] // 2
        tail = grad_proj[:, 2 * wide :]
        half = tail.shape[1] // 2
        sums[s] = (
            row_sums([mixed[:, :middle], mixed[:, middle:]]),
            row_sums(
                [
                    jnp.concatenate([grad_proj[:, :wide], tail[:, :half]], axis=1),
                    jnp.concatenate([grad_proj[:, wide : 2 * wide], tail[:, half:]], axis=1),
                ]
            ),
        )
    expert_out = expert_grads
    grad_mixed = jnp.concatenate(own_halves(sums[0][0], sums[1][0]), axis=1)
    first_half, second_half = own_halves(sums[0][1], sums[1][1])
    tail = jnp.concatenate([first_half[:, wide:], second_half[:, wide:]], axis=1)
    state_grad = lax.psum(tail[:, :state], "col")

    shapes = [part.shape for part in grads[0]]
    vector = own_layer(flat(grads[0]), flat(grads[1]))
    lines = [shifted(vector[None], "row", back) for back in range(n_row)]
    vector = jnp.sum(in_order(lines, "row"), axis=0)
    common = 2 * width + conv_state.shape[1] * state
    if groups() > 1:
        lines = [shifted(vector[None, :common], "col", back) for back in range(n_col)]
        shared_sum = jnp.sum(in_order(lines, "col"), axis=0)
    else:
        shared_sum = lax.psum(vector[:common], "col")
    (
        out_norm_in,
        out_norm_mid,
        out_conv_state,
        out_conv_input,
        out_wide,
        out_step,
    ) = unflat(jnp.concatenate([shared_sum, vector[common:]]), shapes)

    def per_micro(first_value, second_value):
        keep = jnp.where(first, first_value, second_value)
        other = swapped(jnp.where(first, second_value, first_value).astype(HALF)).astype(FLOAT)
        return jnp.stack(pair(keep, other))[None]

    hidden = shared_gate.shape[2]

    def out(value):
        return value.astype(FLOAT)[None]

    return (
        per_micro(outputs[0], outputs[1]),
        per_micro(backs[0], backs[1]),
        out_norm_in[None],
        out(first_half[:, :inner]),
        out(second_half[:, :inner]),
        out(state_grad),
        out(tail[:, state : state + heads]),
        out_step[:1, :heads],
        out_step[1:, :heads],
        jnp.sum(out_wide[1, :inner].reshape(heads, HEAD), axis=1)[None],
        out_conv_input[None, :, :inner],
        out_conv_state[None],
        out_wide[:1, :inner],
        out(grad_mixed[:, 3 * hidden : 3 * hidden + inner]),
        out_norm_mid[None],
        expert_out[0][None, None],
        expert_out[1][None, None],
        expert_out[2][None, None],
        out(grad_mixed[:, :hidden]),
        out(grad_mixed[:, hidden : 2 * hidden]),
        out(grad_mixed[:, 2 * hidden : 3 * hidden]),
    )


def solution(mesh):
    in_specs = (
        P(None, ("row", "col"), None),
        P(None, ("row", "col"), None),
        P(),
        P("section", None, ("row", "col"), None),
        P("section", None, ("row", "col"), None),
        P("section", None),
        P("section", "row", "col"),
        P("section", "row", "col"),
        P("section", "row", None),
        P("section", "row", "col"),
        P("section", "col"),
        P("section", "col"),
        P("section", "col"),
        P("section", None, "col"),
        P("section", None, None),
        P("section", "col"),
        P("section", "row", "col"),
        P("section", None),
        P("section", ("row", "col"), None, None),
        P("section", ("row", "col"), None, None),
        P("section", ("row", "col"), None, None),
        P("section", "row", "col"),
        P("section", "row", "col"),
        P("section", "row", "col"),
    )
    out_specs = (
        P("section", None, ("row", "col"), None),
        P("section", None, ("row", "col"), None),
        P("section", None),
        P("section", "row", "col"),
        P("section", "row", "col"),
        P("section", "row", None),
        P("section", "row", "col"),
        P("section", "col"),
        P("section", "col"),
        P("section", "col"),
        P("section", None, "col"),
        P("section", None, None),
        P("section", "col"),
        P("section", "row", "col"),
        P("section", None),
        P("section", ("row", "col"), None, None),
        P("section", ("row", "col"), None, None),
        P("section", ("row", "col"), None, None),
        P("section", "row", "col"),
        P("section", "row", "col"),
        P("section", "row", "col"),
    )
    return jax.shard_map(shards, mesh=mesh, in_specs=in_specs, out_specs=out_specs, check_vma=False)
```

```python
import functools

import jax
import jax.numpy as jnp
from jax import lax
from jax.experimental import pallas as pl
from jax.experimental.pallas import tpu as pltpu
from jax.sharding import PartitionSpec as P

DI = 3072
HEAD = 64
LANES = 128
CHUNK = 256
VMEM_BYTES = 48 * 2**20

EPS = 1e-05
HIGH = lax.Precision.HIGHEST
FLOAT = jnp.float32
HALF = jnp.bfloat16


def shifted(block, axis, distance):
    count = lax.axis_size(axis)
    if distance % count == 0:
        return block
    return lax.ppermute(block, axis, [(i, (i + distance) % count) for i in range(count)])


def swapped(block):
    return lax.ppermute(block, "section", [(0, 1), (1, 0)])


def after(value, *others):
    return lax.optimization_barrier((value, *others))[0]


def rms_norm(value, gain):
    return value * lax.rsqrt(jnp.mean(value * value, axis=-1, keepdims=True) + EPS) * gain


def local_docs(lengths, row_now, length):
    bounds = jnp.cumsum(lengths)[:-1]
    place = jnp.arange(length, dtype=jnp.int32)
    inner = jnp.sum((place[:, None] >= bounds[None, :]).astype(jnp.int32), axis=1)
    return inner + row_now * lengths.shape[0]


def project(left, right):
    return jnp.dot(left, right, preferred_element_type=FLOAT)


def project_back(left, right):
    return lax.dot_general(left, right, (((1,), (1,)), ((), ())), preferred_element_type=FLOAT)


def outer(left, right):
    return lax.dot_general(left, right, (((0,), (0,)), ((), ())), preferred_element_type=FLOAT)


def silu_slope(value):
    sigma = jax.nn.sigmoid(value)
    return sigma * (1.0 + value * (1.0 - sigma))


def groups():
    count = lax.axis_size("col")
    return count if count <= 4 else 1


def chunks():
    count = groups()
    return {1: [(0,)], 2: [(0,), (1,)], 3: [(0,), (1, 2)], 4: [(0,), (1, 3), (2,)]}[count]


def spread(block, staged=False):
    count = groups()
    if count == 1:
        return [lax.all_gather(block, "col", axis=0, tiled=True)]
    result = [block] * count
    for back in (1, count - 1):
        result[back] = shifted(block, "col", back)
    source = after(block, result[1], result[-1]) if staged else block
    for back in range(2, count - 1):
        result[back] = shifted(source, "col", back)
    return result


def joined(blocks):
    return blocks[0] if len(blocks) == 1 else jnp.concatenate(blocks, axis=0)


def in_order(blocks, axis):
    count = len(blocks)
    if count == 1:
        return blocks[0]
    rows = blocks[0].shape[0]
    line = jnp.concatenate(blocks[::-1] + blocks[:0:-1], axis=0)
    start = (count - 1 - lax.axis_index(axis)) * rows
    return lax.dynamic_slice_in_dim(line, start, count * rows, axis=0)


def gathered_sum(parts):
    if len(parts) == 1:
        return lax.psum_scatter(parts[0], "col", scatter_dimension=0, tiled=True).astype(FLOAT)
    total = parts[0].astype(FLOAT)
    for back in range(1, len(parts)):
        total = total + shifted(parts[back], "col", -back).astype(FLOAT)
    return total


def block_of(values, back):
    rows = values.shape[0] // groups()
    return values[back * rows : (back + 1) * rows]


def turn():
    place = lax.axis_index("col") if groups() > 1 else jnp.int32(0)
    return place.astype(jnp.int32).reshape(1)


def route_tables(blocks, top, capacity, layers):
    n_row, n_col = lax.axis_size("row"), lax.axis_size("col")
    experts = (jnp.arange(n_row) * n_col + lax.axis_index("col")).astype(FLOAT)
    tables = [[] for _ in range(layers)]
    for chunk in chunks():
        now = joined([blocks[back] for back in chunk])
        count = now.shape[0]
        slots = len(chunk) * (n_col // groups()) * capacity
        now = now.reshape(count, layers, 2, top).transpose(1, 2, 3, 0)
        match = now[:, None, 0] == experts[None, :, None, None]
        hit = jnp.any(match, axis=2)
        weight = jnp.sum(jnp.where(match, now[:, None, 1], 0.0), axis=2)
        order = jnp.arange(count, dtype=jnp.int32)
        triangle = (order[:, None] <= order[None, :]).astype(HALF)
        place = project(hit.astype(HALF).reshape(-1, count), triangle).reshape(hit.shape)
        slot = jnp.arange(1, slots + 1, dtype=jnp.int32).astype(FLOAT)
        chosen = (place[:, :, None, :] == slot[:, None]) & hit[:, :, None, :]
        shape = (layers, n_row * slots, count)
        plain = chosen.astype(HALF).reshape(shape)
        scaled = jnp.where(chosen, weight[:, :, None, :], 0.0).astype(HALF).reshape(shape)
        for s in range(layers):
            tables[s].append((plain[s], scaled[s]))
    return tables


def to_experts(rows):
    return lax.all_to_all(rows.astype(HALF), "row", split_axis=0, concat_axis=0, tiled=True)


def summed_rows(values, reverse):
    step = min(values.shape[0], CHUNK)
    count = values.shape[0] // step
    place = lax.broadcasted_iota(jnp.int32, (step, step), 0)
    other = lax.broadcasted_iota(jnp.int32, (step, step), 1)
    before = (place <= other) if reverse else (place >= other)
    triangle = before.astype(FLOAT)
    carry = jnp.zeros((1, values.shape[1]), FLOAT)
    parts = [None] * count
    for index in reversed(range(count)) if reverse else range(count):
        part = values[index * step : (index + 1) * step]
        run = jnp.dot(triangle, part, precision=HIGH, preferred_element_type=FLOAT) + carry
        carry = run[:1] if reverse else run[step - 1 :]
        parts[index] = run
    return parts[0] if count == 1 else jnp.concatenate(parts, axis=0)


def head_columns(rows, columns, head_width):
    head = lax.broadcasted_iota(jnp.int32, (rows, columns), 0) * head_width
    column = lax.broadcasted_iota(jnp.int32, (rows, columns), 1)
    return ((column >= head) & (column < head + head_width)).astype(FLOAT)


def sigmoid(value):
    return 1.0 / (1.0 + jnp.exp(-value))


def step_sizes(step_pre, step_row_ref):
    shifted_pre = step_pre + step_row_ref[0:1, :]
    sizes = jnp.maximum(shifted_pre, 0.0) + jnp.log1p(jnp.exp(-jnp.abs(shifted_pre)))
    return shifted_pre, sizes, -jnp.exp(step_row_ref[1:2, :])


def conv_rows(values, weight_ref, columns, marks_ref):
    width = weight_ref.shape[0]
    result = values * weight_ref[width - 1 : width, columns]
    for back in range(1, width):
        moved = pltpu.roll(values, back, 0) * marks_ref[:, back : back + 1]
        result = result + moved * weight_ref[width - 1 - back : width - back, columns]
    return result


def conv_rows_back(grad, values, weight_ref, columns, marks_ref, weight_grad_ref):
    width = weight_ref.shape[0]
    rows = values.shape[0]
    result = grad * weight_ref[width - 1 : width, columns]
    weight_grad_ref[width - 1 : width, columns] = jnp.sum(grad * values, axis=0, keepdims=True)
    for back in range(1, width):
        kept = grad * marks_ref[:, back : back + 1]
        taps = jnp.sum(kept * pltpu.roll(values, back, 0), axis=0, keepdims=True)
        weight_grad_ref[width - 1 - back : width - back, columns] = taps
        moved = pltpu.roll(kept, rows - back, 0)
        result = result + moved * weight_ref[width - 1 - back : width - back, columns]
    return result


def copy_in_order(source_ref, target_ref, place_ref, parts):
    if parts == 1:
        return source_ref
    rows = source_ref.shape[0] // parts
    for index in range(parts):
        target_ref[index * rows : (index + 1) * rows, :] = source_ref[
            block_rows(index, rows, place_ref, parts), :
        ]
    return target_ref


def block_rows(index, rows, place_ref, parts):
    if parts == 1:
        return slice(0, rows)
    back = lax.rem(place_ref[0] - index + parts, parts)
    return pl.ds(pl.multiple_of(back * rows, rows), rows)


def mixer_forward_kernel(
    heads,
    parts,
    pre_in_ref,
    conv_input_ref,
    conv_state_ref,
    step_row_ref,
    wide_row_ref,
    marks_ref,
    labels_ref,
    place_ref,
    y_ref,
    scaled_ref,
    total_ref,
    pre_ref,
    x_ref,
    dosed_ref,
    keys_ref,
    queries_ref,
):
    length, wide = y_ref.shape
    states = conv_state_ref.shape[1] // 2
    state_at, step_at = 2 * wide, 2 * wide + 2 * states
    head_width = HEAD
    pre_ref = copy_in_order(pre_in_ref, pre_ref, place_ref, parts)
    _, sizes, rate = step_sizes(pre_ref[:, step_at : step_at + LANES], step_row_ref)
    running = summed_rows(sizes * rate, False)
    running_t = running.T
    expand = head_columns(LANES, wide, head_width)
    for start in range(0, wide, LANES):
        columns = slice(start, start + LANES)
        conv = conv_rows(
            pre_ref[:, wide + start : wide + start + LANES], conv_input_ref, columns, marks_ref
        )
        x = conv * sigmoid(conv)
        x_ref[:, columns] = x
        dose = jnp.dot(sizes, expand[:, columns], precision=HIGH, preferred_element_type=FLOAT)
        dosed_ref[:, columns] = (x * dose).astype(HALF)
    for part, target in ((0, keys_ref), (1, queries_ref)):
        columns = slice(part * states, (part + 1) * states)
        conv = conv_rows(
            pre_ref[:, state_at + part * states : state_at + (part + 1) * states],
            conv_state_ref,
            columns,
            marks_ref,
        )
        target[...] = (conv * sigmoid(conv)).astype(HALF)
    block = min(length, CHUNK)
    place = lax.broadcasted_iota(jnp.int32, (block, block), 0)
    other = lax.broadcasted_iota(jnp.int32, (block, block), 1)
    for late in range(length // block):
        rows = slice(late * block, (late + 1) * block)
        for early in range(late + 1):
            past = slice(early * block, (early + 1) * block)
            same = marks_ref[rows, 0:1] == labels_ref[:, past]
            if late == early:
                same = same & (place >= other)
            mask = jnp.where(same, 0.0, -1e30)
            scores = lax.dot_general(
                queries_ref[rows, :],
                keys_ref[past, :],
                (((1,), (1,)), ((), ())),
                preferred_element_type=FLOAT,
            )
            for head in range(heads):
                columns = slice(head * head_width, (head + 1) * head_width)
                spread_log = running[rows, head : head + 1] - running_t[head : head + 1, past]
                mixing = (jnp.exp(spread_log + mask) * scores).astype(HALF)
                inner = jnp.dot(mixing, dosed_ref[past, columns], preferred_element_type=FLOAT)
                if early == 0:
                    y_ref[rows, columns] = inner
                else:
                    y_ref[rows, columns] += inner
    total = jnp.zeros((length, 1), FLOAT)
    for start in range(0, wide, LANES):
        columns = slice(start, start + LANES)
        y = y_ref[:, columns]
        if heads * head_width < start + LANES:
            lane = lax.broadcasted_iota(jnp.int32, y.shape, 1) + start
            y = jnp.where(lane < heads * head_width, y, 0.0)
        y = y + wide_row_ref[1:2, columns] * x_ref[:, columns]
        gate = pre_ref[:, columns]
        gated = y * gate * sigmoid(gate)
        y_ref[:, columns] = y
        scaled = (gated * wide_row_ref[0:1, columns]).astype(HALF)
        each = length // parts
        for index in range(parts):
            block_at = block_rows(index, each, place_ref, parts)
            scaled_ref[block_at, columns] = scaled[index * each : (index + 1) * each]
        total = total + jnp.sum(gated * gated, axis=1, keepdims=True)
    each = length // parts
    for index in range(parts):
        block_at = block_rows(index, each, place_ref, parts)
        total_ref[block_at, :] = total[index * each : (index + 1) * each]


def mixer_backward_kernel(
    heads,
    parts,
    inner_all,
    pre_in_ref,
    y_ref,
    grad_in_ref,
    sides_in_ref,
    conv_input_ref,
    conv_state_ref,
    step_row_ref,
    wide_row_ref,
    marks_ref,
    labels_ref,
    place_ref,
    grad_pre_ref,
    wide_grad_ref,
    conv_input_grad_ref,
    conv_state_grad_ref,
    step_grad_ref,
    pre_ref,
    grad_ref,
    sides_ref,
    x_ref,
    dosed_ref,
    dose_ref,
    slope_ref,
    dy_ref,
    z_ref,
    bc_ref,
    bc_slope_ref,
    bc_grad_ref,
):
    length, wide = y_ref.shape
    states = conv_state_ref.shape[1] // 2
    state_at, step_at = 2 * wide, 2 * wide + 2 * states
    head_width = HEAD
    each = length // parts
    pre_ref = copy_in_order(pre_in_ref, pre_ref, place_ref, parts)
    grad_ref = copy_in_order(grad_in_ref, grad_ref, place_ref, parts)
    sides_ref = copy_in_order(sides_in_ref, sides_ref, place_ref, parts)

    def put(value, start):
        for index in range(parts):
            grad_pre_ref[block_rows(index, each, place_ref, parts), start : start + LANES] = value[
                index * each : (index + 1) * each
            ]

    shifted_pre, sizes, rate = step_sizes(pre_ref[:, step_at : step_at + LANES], step_row_ref)
    running = summed_rows(sizes * rate, False)
    running_t = running.T
    expand = head_columns(LANES, wide, head_width)
    rr = sides_ref[:, 0:1]
    pull = rr * rr * rr * sides_ref[:, 1:2] * (1.0 / inner_all)
    for start in range(0, wide, LANES):
        columns = slice(start, start + LANES)
        gate = pre_ref[:, columns]
        y = y_ref[:, columns]
        grad = grad_ref[:, columns]
        gain = wide_row_ref[0:1, columns]
        sigma = sigmoid(gate)
        silu = gate * sigma
        gated = y * silu
        normed = gated * rr
        wide_grad_ref[0:1, columns] = jnp.sum(grad * normed, axis=0, keepdims=True)
        grad_gated = rr * gain * grad - gated * pull
        slope = sigma * (1.0 + gate * (1.0 - sigma))
        put((grad_gated * y * slope).astype(HALF), start)
        dy = grad_gated * silu
        dy_ref[:, columns] = dy
        conv = conv_rows(
            pre_ref[:, wide + start : wide + start + LANES], conv_input_ref, columns, marks_ref
        )
        sigma = sigmoid(conv)
        x = conv * sigma
        x_ref[:, columns] = x
        slope_ref[:, columns] = sigma * (1.0 + conv * (1.0 - sigma))
        dose = jnp.dot(sizes, expand[:, columns], precision=HIGH, preferred_element_type=FLOAT)
        dose_ref[:, columns] = dose
        dosed_ref[:, columns] = (x * dose).astype(HALF)
        wide_grad_ref[1:2, columns] = jnp.sum(dy * x, axis=0, keepdims=True)
    for start in range(0, 2 * states, LANES):
        columns = slice(start, start + LANES)
        conv = conv_rows(
            pre_ref[:, state_at + start : state_at + start + LANES],
            conv_state_ref,
            columns,
            marks_ref,
        )
        sigma = sigmoid(conv)
        bc_ref[:, columns] = (conv * sigma).astype(HALF)
        bc_slope_ref[:, columns] = sigma * (1.0 + conv * (1.0 - sigma))
    block = min(length, CHUNK)
    place = lax.broadcasted_iota(jnp.int32, (block, block), 0)
    other = lax.broadcasted_iota(jnp.int32, (block, block), 1)
    z_ref[...] = jnp.zeros(z_ref.shape, FLOAT)
    bc_grad_ref[...] = jnp.zeros(bc_grad_ref.shape, FLOAT)
    for late in range(length // block):
        rows = slice(late * block, (late + 1) * block)
        for early in range(late + 1):
            past = slice(early * block, (early + 1) * block)
            same = marks_ref[past, 0:1] == labels_ref[:, rows]
            if late == early:
                same = same & (place <= other)
            mask = jnp.where(same, 0.0, -1e30)
            keys = bc_ref[past, :states]
            queries = bc_ref[rows, states:]
            scores = lax.dot_general(
                keys, queries, (((1,), (1,)), ((), ())), preferred_element_type=FLOAT
            )
            mixed = jnp.zeros((block, block), FLOAT)
            for head in range(heads):
                columns = slice(head * head_width, (head + 1) * head_width)
                spread_log = running_t[head : head + 1, rows] - running[past, head : head + 1]
                decay = jnp.exp(spread_log + mask)
                mixing = (decay * scores).astype(HALF)
                dy = dy_ref[rows, columns].astype(HALF)
                z_ref[past, columns] += jnp.dot(mixing, dy, preferred_element_type=FLOAT)
                along = lax.dot_general(
                    dosed_ref[past, columns],
                    dy,
                    (((1,), (1,)), ((), ())),
                    preferred_element_type=FLOAT,
                )
                mixed = mixed + decay * along
            mixed = mixed.astype(HALF)
            bc_grad_ref[past, :states] += jnp.dot(mixed, queries, preferred_element_type=FLOAT)
            bc_grad_ref[rows, states:] += lax.dot_general(
                mixed, keys, (((0,), (0,)), ((), ())), preferred_element_type=FLOAT
            )
    direct = jnp.zeros((length, LANES), FLOAT)
    balance = jnp.zeros((length, LANES), FLOAT)
    for start in range(0, wide, LANES):
        columns = slice(start, start + LANES)
        x, z, dy = x_ref[:, columns], z_ref[:, columns], dy_ref[:, columns]
        skip = wide_row_ref[1:2, columns]
        collapse = (((1,), (1,)), ((), ()))
        both = dy.astype(HALF).astype(FLOAT) * (y_ref[:, columns] - skip * x)
        both = both - dosed_ref[:, columns].astype(FLOAT) * z
        heads_of = expand[:, columns]
        direct = direct + lax.dot_general(
            x * z, heads_of, collapse, precision=HIGH, preferred_element_type=FLOAT
        )
        balance = balance + lax.dot_general(
            both, heads_of, collapse, precision=HIGH, preferred_element_type=FLOAT
        )
        grad_conv = (dose_ref[:, columns] * z + skip * dy) * slope_ref[:, columns]
        grad_in = conv_rows_back(
            grad_conv,
            pre_ref[:, wide + start : wide + start + LANES],
            conv_input_ref,
            columns,
            marks_ref,
            conv_input_grad_ref,
        )
        put(grad_in.astype(HALF), wide + start)
    for start in range(0, 2 * states, LANES):
        columns = slice(start, start + LANES)
        grad_in = conv_rows_back(
            bc_grad_ref[:, columns] * bc_slope_ref[:, columns],
            pre_ref[:, state_at + start : state_at + start + LANES],
            conv_state_ref,
            columns,
            marks_ref,
            conv_state_grad_ref,
        )
        put(grad_in.astype(HALF), state_at + start)
    crossing = summed_rows(balance, True)
    grad_step = (direct + rate * crossing) * sigmoid(shifted_pre)
    put(grad_step.astype(HALF), step_at)
    step_grad_ref[0:1, :] = jnp.sum(grad_step, axis=0, keepdims=True)
    step_grad_ref[1:2, :] = rate * jnp.sum(sizes * crossing, axis=0, keepdims=True)


def ordered_copy(shape):
    return pltpu.VMEM(shape if groups() > 1 else (8, LANES), FLOAT)


def whole_call(kernel, inputs, results, scratch, name):
    whole = pl.BlockSpec(memory_space=pltpu.VMEM)
    place = pl.BlockSpec(memory_space=pltpu.SMEM)
    return pl.pallas_call(
        kernel,
        in_specs=[whole] * (inputs - 1) + [place],
        out_shape=results,
        scratch_shapes=scratch,
        compiler_params=pltpu.CompilerParams(vmem_limit_bytes=VMEM_BYTES),
        name=name,
    )


def mixer_forward(pre, heads, wide, mixer):
    length = pre.shape[0]
    kernel = functools.partial(mixer_forward_kernel, heads, groups())
    states = mixer[1].shape[1] // 2
    return whole_call(
        kernel,
        1 + len(mixer),
        (
            jax.ShapeDtypeStruct((length, wide), FLOAT),
            jax.ShapeDtypeStruct((length, wide), HALF),
            jax.ShapeDtypeStruct((length, 1), FLOAT),
        ),
        [
            ordered_copy(pre.shape),
            pltpu.VMEM((length, wide), FLOAT),
            pltpu.VMEM((length, wide), HALF),
            pltpu.VMEM((length, states), HALF),
            pltpu.VMEM((length, states), HALF),
        ],
        "mixer_forward",
    )(pre, *mixer)


def mixer_backward(pre, y, grad, sides, heads, mixer):
    length, wide = y.shape
    kernel = functools.partial(mixer_backward_kernel, heads, groups(), DI)
    double = mixer[1].shape[1]
    square = pltpu.VMEM((length, wide), FLOAT)
    return whole_call(
        kernel,
        4 + len(mixer),
        (
            jax.ShapeDtypeStruct(pre.shape, HALF),
            jax.ShapeDtypeStruct((2, wide), FLOAT),
            jax.ShapeDtypeStruct((4, wide), FLOAT),
            jax.ShapeDtypeStruct((4, double), FLOAT),
            jax.ShapeDtypeStruct((2, LANES), FLOAT),
        ),
        [
            ordered_copy(pre.shape),
            ordered_copy(y.shape),
            ordered_copy(sides.shape),
            square,
            pltpu.VMEM((length, wide), HALF),
            square,
            square,
            square,
            square,
            pltpu.VMEM((length, double), HALF),
            pltpu.VMEM((length, double), FLOAT),
            pltpu.VMEM((length, double), FLOAT),
        ],
        "mixer_backward",
    )(pre, y, grad, sides, *mixer)


def through_experts(blocks, tables, expert, beside):
    tokens = [joined([blocks[back] for back in chunk]) for chunk in chunks()]
    count = len(tokens)
    sent = [project(table, values).astype(HALF) for table, values in zip(tables, tokens)]
    parts = [None] * groups()
    arrived = []
    rows = to_experts(sent[0])
    for index, chunk in enumerate(chunks()):
        if index and index + 1 < count:
            rows = after(rows, sent[index + 1])
        arrived.append(rows)
        answer = expert(index, rows)
        if index + 1 < count:
            following = sent[index + 1] if index else after(sent[1], answer)
            rows = to_experts(following)
        part = beside(index, tokens[index], to_experts(answer))
        rows_each = part.shape[0] // len(chunk)
        for at, back in enumerate(chunk):
            parts[back] = part[at * rows_each : (at + 1) * rows_each]
    return parts, arrived


def layer_forward(resid, params, dense, mixer, tables):
    norm_in, norm_mid = params
    proj, proj_output, shared, expert_gate, expert_up, expert_down = dense
    wide = mixer[0].shape[1]
    heads = mixer[-1]
    hidden = shared.shape[1] // 3
    backs = range(groups())
    wide_in = joined(spread(rms_norm(resid, norm_in).astype(HALF)))
    pre = project(wide_in, proj)
    y, scaled, total_part = mixer_forward(pre, heads, wide, mixer[:-1])
    total = gathered_sum([block_of(total_part, back) for back in backs])
    mixed = gathered_sum(
        [project_back(block_of(scaled, back), proj_output).astype(HALF) for back in backs]
    )
    if callable(tables):
        tables = tables(scaled)
    rr = lax.rsqrt(total / DI + EPS)
    middle = resid + mixed * rr
    wide_mid = spread(rms_norm(middle, norm_mid).astype(HALF), staged=True)
    shared_pre, shared_act, expert_pre, active, returned = [], [], [], [], []

    def expert(index, rows):
        gate_e = project(rows, expert_gate)
        lift_e = project(rows, expert_up)
        act_e = (jax.nn.silu(gate_e) * lift_e).astype(HALF)
        expert_pre.append((gate_e, lift_e))
        active.append(act_e)
        return project(act_e, expert_down).astype(HALF)

    def beside(index, tokens, result):
        gate_s = project(tokens, shared[:, :hidden])
        lift_s = project(tokens, shared[:, hidden : 2 * hidden])
        act_s = (jax.nn.silu(gate_s) * lift_s).astype(HALF)
        shared_pre.append((gate_s, lift_s))
        shared_act.append(act_s)
        part = outer(tables[0][index][1], result) + project_back(act_s, shared[:, 2 * hidden :])
        return part.astype(HALF)

    parts, arrived = through_experts(wide_mid, [table[0] for table in tables[0]], expert, beside)
    saved = (
        resid,
        middle,
        mixed,
        rr,
        wide_in,
        pre,
        y,
        scaled,
        wide_mid,
        shared_pre,
        shared_act,
        arrived,
        expert_pre,
        active,
    )
    return (middle + gathered_sum(parts), saved, tables)


def layer_backward(grad_out, saved, params, dense, mixer, tables, pending):
    norm_in, norm_mid = params
    proj, proj_output, shared, expert_gate, expert_up, expert_down = dense
    (
        resid,
        middle,
        mixed,
        rr,
        wide_in,
        pre,
        y,
        scaled,
        wide_mid,
        shared_pre,
        shared_act,
        arrived,
        expert_pre,
        active,
    ) = saved
    wide, heads = mixer[0].shape[1], mixer[-1]
    hidden = shared.shape[1] // 3
    backs = range(groups())
    wide_out = spread(grad_out.astype(HALF), staged=True)
    gate_grads, lift_grads, shared_grads = [], [], []

    def expert(index, rows):
        gate_e, lift_e = expert_pre[index]
        grad_act = project_back(rows, expert_down)
        grad_gate_e = (grad_act * lift_e * silu_slope(gate_e)).astype(HALF)
        grad_lift_e = (grad_act * jax.nn.silu(gate_e)).astype(HALF)
        gate_grads.append(grad_gate_e)
        lift_grads.append(grad_lift_e)
        back = project_back(grad_gate_e, expert_gate) + project_back(grad_lift_e, expert_up)
        return back.astype(HALF)

    def beside(index, tokens, result):
        gate_s, lift_s = shared_pre[index]
        grad_act_s = project(tokens, shared[:, 2 * hidden :])
        grad_gate_s = (grad_act_s * lift_s * silu_slope(gate_s)).astype(HALF)
        grad_lift_s = (grad_act_s * jax.nn.silu(gate_s)).astype(HALF)
        shared_grads.append((grad_gate_s, grad_lift_s))
        part = (
            outer(tables[index][0], result)
            + project_back(grad_gate_s, shared[:, :hidden])
            + project_back(grad_lift_s, shared[:, hidden : 2 * hidden])
        )
        return part.astype(HALF)

    parts, rows_grad = through_experts(wide_out, [table[1] for table in tables], expert, beside)
    grad_normed = gathered_sum(parts)
    _, pull_mid = jax.vjp(rms_norm, middle, norm_mid)
    grad_middle, grad_norm_mid = pull_mid(grad_normed)
    grad_middle = grad_middle + grad_out
    along = jnp.sum(grad_middle * mixed, axis=1, keepdims=True)
    wide_mix = joined(spread(grad_middle.astype(HALF)))
    sides = joined(spread(jnp.concatenate([rr, along], axis=1)))
    rows_in, rows_out = joined(arrived), joined(rows_grad)
    expert_grads = (
        outer(rows_in, joined(gate_grads)),
        outer(rows_in, joined(lift_grads)),
        outer(joined(active), rows_out),
    )
    order = [back for chunk in chunks() for back in chunk]
    mids, outs = joined([wide_mid[back] for back in order]), joined([wide_out[back] for back in order])
    grad_shared = (
        section_half(mids, *[joined(list(part)) for part in zip(*shared_grads)]),
        section_half(outs, *two_halves(joined(shared_act))),
    )
    expert_grads = pending(expert_grads)
    wide_mix = after(wide_mix, expert_grads, grad_shared)
    grad_proj_output = section_half((wide_mix * sides[:, :1]).astype(HALF), *two_halves(scaled))
    grad_scaled = project(wide_mix, proj_output)
    grad_pre, wide_grads, grad_conv_input, grad_conv_state, step_grads = mixer_backward(
        pre, y, grad_scaled, sides, heads, mixer[:-1]
    )
    grad_normed_in = gathered_sum(
        [project_back(block_of(grad_pre, back), proj).astype(HALF) for back in backs]
    )
    grad_proj = section_half(wide_in, grad_pre[:, :wide], grad_pre[:, wide : 2 * wide])
    grad_tail = outer(wide_in, grad_pre[:, 2 * wide :]).astype(HALF)
    _, pull_in = jax.vjp(rms_norm, resid, norm_in)
    grad_resid, grad_norm_in = pull_in(grad_normed_in)
    small = (
        grad_norm_in,
        grad_norm_mid,
        grad_conv_state,
        grad_conv_input,
        wide_grads,
        step_grads,
    )
    dense_grads = (grad_proj, grad_proj_output, *grad_shared)
    return (grad_resid + grad_middle, small, dense_grads, grad_tail, expert_grads)


def two_halves(values):
    middle = values.shape[1] // 2
    return values[:, :middle], values[:, middle:]


def section_half(left, first_right, second_right):
    first = lax.axis_index("section") == 0
    give = outer(left, jnp.where(first, second_right, first_right)).astype(HALF)
    keep = outer(left, jnp.where(first, first_right, second_right))
    return (keep + swapped(give).astype(FLOAT)).astype(HALF)


def row_share(values):
    n_row = lax.axis_size("row")
    rows = values.shape[0] // n_row
    total = None
    for ahead in range(n_row):
        index = lax.rem(lax.axis_index("row") + ahead, n_row)
        part = lax.dynamic_slice_in_dim(values, index * rows, rows, axis=0)
        part = shifted(part, "row", ahead).astype(FLOAT)
        total = part if total is None else total + part
    return total.astype(HALF)


def col_sum(values):
    n_col = lax.axis_size("col")
    if groups() == 1:
        return lax.psum(values, "col")
    rows = values.shape[0] // n_col
    total = None
    for ahead in range(n_col):
        index = lax.rem(lax.axis_index("col") + ahead, n_col)
        part = lax.dynamic_slice_in_dim(values, index * rows, rows, axis=0)
        part = shifted(part, "col", ahead).astype(FLOAT)
        total = part if total is None else total + part
    total = total.astype(values.dtype)
    return in_order([shifted(total, "col", back) for back in range(n_col)], "col")


def flat(parts):
    return jnp.concatenate([part.reshape(-1) for part in parts])


def unflat(vector, shapes):
    result, start = [], 0
    for shape in shapes:
        size = 1
        for entry in shape:
            size *= entry
        result.append(vector[start : start + size].reshape(shape))
        start += size
    return result


def widened(value, columns):
    return jnp.pad(value, ((0, 0), (0, columns - value.shape[1])))


def shards(
    tokens,
    cotangent,
    doc_lengths,
    routes,
    gates,
    norm_in,
    proj_gate,
    proj_input,
    proj_state,
    proj_step,
    step_bias,
    decay_log,
    skip_gain,
    conv_input,
    conv_state,
    gate_norm,
    proj_output,
    norm_mid,
    expert_gate,
    expert_up,
    expert_down,
    shared_gate,
    shared_up,
    shared_down,
):
    section_now = lax.axis_index("section")
    first = section_now == 0
    row_now = lax.axis_index("row")
    n_row, n_col = lax.axis_size("row"), lax.axis_size("col")
    count = tokens.shape[1]
    top = routes.shape[3]
    capacity = count * top * 4 // (3 * n_row * n_col)
    width = tokens.shape[2]
    heads = step_bias.shape[1]
    inner = gate_norm.shape[1]
    state = conv_state.shape[2]
    wide = -(-inner // LANES) * LANES

    def pair(own, other):
        return (jnp.where(first, own, other), jnp.where(first, other, own))

    small_in = (
        norm_in[0],
        norm_mid[0],
        widened(conv_input[0], wide),
        conv_state[0],
        widened(jnp.concatenate([step_bias, decay_log], axis=0), LANES),
        widened(jnp.concatenate([gate_norm, jnp.repeat(skip_gain, HEAD, axis=1)], axis=0), wide),
    )
    vector = flat(small_in)
    small_all = [unflat(part, [v.shape for v in small_in]) for part in pair(vector, swapped(vector))]

    def both_layers(weight):
        whole = lax.all_gather(weight, ("section", "row"), axis=0, tiled=True)
        return whole.reshape(2, n_row * weight.shape[0], weight.shape[1])

    proj = both_layers(
        jnp.concatenate(
            [
                widened(proj_gate[0], wide),
                widened(proj_input[0], wide),
                proj_state[0],
                widened(proj_step[0], LANES),
            ],
            axis=1,
        )
    )
    proj_out = both_layers(widened(proj_output[0], wide))
    gate_all = lax.all_gather(expert_gate[0, 0], "section")
    up_all = lax.all_gather(expert_up[0, 0], "section")
    down_all = lax.all_gather(expert_down[0, 0], "section")
    shared = both_layers(jnp.concatenate([shared_gate[0], shared_up[0], shared_down[0]], axis=1))
    dense = [
        (proj[s], proj_out[s], shared[s], gate_all[s], up_all[s], down_all[s]) for s in range(2)
    ]

    meta = jnp.concatenate([routes.astype(FLOAT), gates], axis=3)[0]
    keep = lax.dynamic_index_in_dim(meta, section_now, 0, keepdims=False)
    give = lax.dynamic_index_in_dim(meta, 1 - section_now, 0, keepdims=False)
    meta = jnp.concatenate(pair(keep, swapped(give)), axis=1)

    def tables_once(scaled):
        return route_tables(spread(after(meta, scaled)), top, capacity, 2)

    lengths = lax.dynamic_slice(
        doc_lengths, (section_now, row_now, 0), (1, 1, doc_lengths.shape[2])
    )
    labels = local_docs(lengths[0, 0], row_now, n_col * count)
    marks = [labels.astype(FLOAT)]
    for back in range(1, conv_input.shape[1]):
        prior = jnp.pad(labels, (back, 0), constant_values=-1)[:-back]
        marks.append((prior == labels).astype(FLOAT))
    marks = jnp.stack(marks, axis=1)
    label_row = labels.astype(FLOAT)[None]
    place = turn()
    mixers = [
        (conv_in, conv_st, step_row, wide_row, marks, label_row, place, heads)
        for _, _, conv_in, conv_st, step_row, wide_row in small_all
    ]
    params = [part[:2] for part in small_all]

    resid = lax.dynamic_index_in_dim(tokens, section_now, 0, keepdims=False)
    grad = lax.dynamic_index_in_dim(cotangent, section_now, 0, keepdims=False)
    outputs, stored = [], []
    tables = tables_once
    for s in range(2):
        resid, saved, tables = layer_forward(
            resid, params[s], dense[s], mixers[s], tables if s == 0 else both_tables[1:]
        )
        outputs.append(resid)
        stored.append(saved)
        if s == 0:
            both_tables = tables

    def own_layer(first_value, second_value):
        keep = jnp.where(first, first_value, second_value)
        give = jnp.where(first, second_value, first_value).astype(HALF)
        return keep.astype(FLOAT) + swapped(give).astype(FLOAT)

    def row_sums(value):
        return lax.psum_scatter(value, "row", scatter_dimension=0, tiled=True)

    def own_halves(first_value, second_value):
        keep = jnp.where(first, first_value, second_value)
        give = jnp.where(first, second_value, first_value)
        return pair(keep, swapped(give))

    held = {}

    def keep_first(expert_grads):
        held["experts"] = [grad.astype(HALF) for grad in expert_grads]
        return held["experts"]

    def settle(expert_grads):
        return [
            own_layer(a.astype(HALF), b).astype(FLOAT)
            for a, b in zip(expert_grads, held["experts"])
        ]

    grads = [None, None]
    backs = [None, None]
    sums = [None, None]
    tails = [None, None]
    for s in (1, 0):
        grad, small, (grad_proj, *others), tails[s], expert_out = layer_backward(
            grad,
            stored[s],
            params[s],
            dense[s],
            mixers[s],
            both_tables[s],
            keep_first if s else settle,
        )
        backs[s] = grad
        grads[s] = small
        sums[s] = [
            row_sums(grad_proj) if s else row_share(grad_proj),
            *[row_sums(value) for value in others],
        ]
    tail = row_share(own_layer(tails[0], tails[1]).astype(HALF))
    state_grad = col_sum(tail[:, :state])
    grad_gates, grad_out, grad_shared, grad_down = [own_halves(a, b) for a, b in zip(*sums)]
    grad_out, grad_down = [jnp.concatenate(both, axis=1) for both in (grad_out, grad_down)]

    shapes = [part.shape for part in grads[0]]
    vector = own_layer(flat(grads[0]), flat(grads[1]))
    lines = [shifted(vector[None], "row", back) for back in range(n_row)]
    vector = jnp.sum(in_order(lines, "row"), axis=0)
    common = 2 * width + conv_state.shape[1] * state
    if groups() > 1:
        lines = [shifted(vector[None, :common], "col", back) for back in range(n_col)]
        shared_sum = jnp.sum(in_order(lines, "col"), axis=0)
    else:
        shared_sum = lax.psum(vector[:common], "col")
    (
        out_norm_in,
        out_norm_mid,
        out_conv_state,
        out_conv_input,
        out_wide,
        out_step,
    ) = unflat(jnp.concatenate([shared_sum, vector[common:]]), shapes)

    def per_micro(first_value, second_value):
        keep = jnp.where(first, first_value, second_value)
        other = swapped(jnp.where(first, second_value, first_value).astype(HALF)).astype(FLOAT)
        return jnp.stack(pair(keep, other))[None]

    def out(value):
        return value.astype(FLOAT)[None]

    return (
        per_micro(outputs[0], outputs[1]),
        per_micro(backs[0], backs[1]),
        out_norm_in[None],
        out(grad_gates[0][:, :inner]),
        out(grad_gates[1][:, :inner]),
        out(state_grad),
        out(tail[:, state : state + heads]),
        out_step[:1, :heads],
        out_step[1:, :heads],
        jnp.sum(out_wide[1, :inner].reshape(heads, HEAD), axis=1)[None],
        out_conv_input[None, :, :inner],
        out_conv_state[None],
        out_wide[:1, :inner],
        out(grad_out[:, :inner]),
        out_norm_mid[None],
        expert_out[0][None, None],
        expert_out[1][None, None],
        expert_out[2][None, None],
        out(grad_shared[0]),
        out(grad_shared[1]),
        out(grad_down),
    )


def solution(mesh):
    in_specs = (
        P(None, ("row", "col"), None),
        P(None, ("row", "col"), None),
        P(),
        P("section", None, ("row", "col"), None),
        P("section", None, ("row", "col"), None),
        P("section", None),
        P("section", "row", "col"),
        P("section", "row", "col"),
        P("section", "row", None),
        P("section", "row", "col"),
        P("section", "col"),
        P("section", "col"),
        P("section", "col"),
        P("section", None, "col"),
        P("section", None, None),
        P("section", "col"),
        P("section", "row", "col"),
        P("section", None),
        P("section", ("row", "col"), None, None),
        P("section", ("row", "col"), None, None),
        P("section", ("row", "col"), None, None),
        P("section", "row", "col"),
        P("section", "row", "col"),
        P("section", "row", "col"),
    )
    out_specs = (
        P("section", None, ("row", "col"), None),
        P("section", None, ("row", "col"), None),
        P("section", None),
        P("section", "row", "col"),
        P("section", "row", "col"),
        P("section", "row", None),
        P("section", "row", "col"),
        P("section", "col"),
        P("section", "col"),
        P("section", "col"),
        P("section", None, "col"),
        P("section", None, None),
        P("section", "col"),
        P("section", "row", "col"),
        P("section", None),
        P("section", ("row", "col"), None, None),
        P("section", ("row", "col"), None, None),
        P("section", ("row", "col"), None, None),
        P("section", "row", "col"),
        P("section", "row", "col"),
        P("section", "row", "col"),
    )
    return jax.shard_map(shards, mesh=mesh, in_specs=in_specs, out_specs=out_specs, check_vma=False)
```

```python
import functools

import jax
import jax.numpy as jnp
from jax import lax
from jax.experimental import pallas as pl
from jax.experimental.pallas import tpu as pltpu
from jax.sharding import PartitionSpec as P

DI = 3072
HEAD = 64
LANES = 128
CHUNK = 256
VMEM_BYTES = 48 * 2**20

EPS = 1e-05
HIGH = lax.Precision.HIGHEST
FLOAT = jnp.float32
HALF = jnp.bfloat16


def shifted(block, axis, distance):
    count = lax.axis_size(axis)
    if distance % count == 0:
        return block
    return lax.ppermute(block, axis, [(i, (i + distance) % count) for i in range(count)])


def swapped(block):
    return lax.ppermute(block, "section", [(0, 1), (1, 0)])


def after(value, *others):
    return lax.optimization_barrier((value, *others))[0]


def rms_norm(value, gain):
    return value * lax.rsqrt(jnp.mean(value * value, axis=-1, keepdims=True) + EPS) * gain


def local_docs(lengths, row_now, length):
    bounds = jnp.cumsum(lengths)[:-1]
    place = jnp.arange(length, dtype=jnp.int32)
    inner = jnp.sum((place[:, None] >= bounds[None, :]).astype(jnp.int32), axis=1)
    return inner + row_now * lengths.shape[0]


def project(left, right):
    return jnp.dot(left, right, preferred_element_type=FLOAT)


def project_back(left, right):
    return lax.dot_general(left, right, (((1,), (1,)), ((), ())), preferred_element_type=FLOAT)


def outer(left, right):
    return lax.dot_general(left, right, (((0,), (0,)), ((), ())), preferred_element_type=FLOAT)


def silu_slope(value):
    sigma = jax.nn.sigmoid(value)
    return sigma * (1.0 + value * (1.0 - sigma))


def groups():
    count = lax.axis_size("col")
    return count if count <= 4 else 1


def chunks():
    count = groups()
    return {1: [(0,)], 2: [(0,), (1,)], 3: [(0,), (1, 2)], 4: [(0,), (1, 3), (2,)]}[count]


def spread(block):
    if groups() == 1:
        return [lax.all_gather(block, "col", axis=0, tiled=True)]
    return [shifted(block, "col", back) for back in range(groups())]


def joined(blocks):
    return blocks[0] if len(blocks) == 1 else jnp.concatenate(blocks, axis=0)


def in_order(blocks, axis):
    count = len(blocks)
    if count == 1:
        return blocks[0]
    rows = blocks[0].shape[0]
    line = jnp.concatenate(blocks[::-1] + blocks[:0:-1], axis=0)
    start = (count - 1 - lax.axis_index(axis)) * rows
    return lax.dynamic_slice_in_dim(line, start, count * rows, axis=0)


def gathered_sum(parts):
    if len(parts) == 1:
        return lax.psum_scatter(parts[0], "col", scatter_dimension=0, tiled=True).astype(FLOAT)
    total = parts[0].astype(FLOAT)
    for back in range(1, len(parts)):
        total = total + shifted(parts[back], "col", -back).astype(FLOAT)
    return total


def block_of(values, back):
    rows = values.shape[0] // groups()
    return values[back * rows : (back + 1) * rows]


def turn():
    place = lax.axis_index("col") if groups() > 1 else jnp.int32(0)
    return place.astype(jnp.int32).reshape(1)


def route_tables(blocks, top, capacity, layers):
    n_row, n_col = lax.axis_size("row"), lax.axis_size("col")
    experts = (jnp.arange(n_row) * n_col + lax.axis_index("col")).astype(FLOAT)
    tables = [[] for _ in range(layers)]
    for chunk in chunks():
        now = joined([blocks[back] for back in chunk])
        count = now.shape[0]
        slots = len(chunk) * (n_col // groups()) * capacity
        now = now.reshape(count, layers, 2, top).transpose(1, 2, 3, 0)
        match = now[:, None, 0] == experts[None, :, None, None]
        hit = jnp.any(match, axis=2)
        weight = jnp.sum(jnp.where(match, now[:, None, 1], 0.0), axis=2)
        order = jnp.arange(count, dtype=jnp.int32)
        triangle = (order[:, None] <= order[None, :]).astype(HALF)
        place = project(hit.astype(HALF).reshape(-1, count), triangle).reshape(hit.shape)
        slot = jnp.arange(1, slots + 1, dtype=jnp.int32).astype(FLOAT)
        chosen = (place[:, :, None, :] == slot[:, None]) & hit[:, :, None, :]
        shape = (layers, n_row * slots, count)
        plain = chosen.astype(HALF).reshape(shape)
        scaled = jnp.where(chosen, weight[:, :, None, :], 0.0).astype(HALF).reshape(shape)
        for s in range(layers):
            tables[s].append((plain[s], scaled[s]))
    return tables


def to_experts(rows):
    return lax.all_to_all(rows.astype(HALF), "row", split_axis=0, concat_axis=0, tiled=True)


def summed_rows(values, reverse):
    step = min(values.shape[0], CHUNK)
    count = values.shape[0] // step
    place = lax.broadcasted_iota(jnp.int32, (step, step), 0)
    other = lax.broadcasted_iota(jnp.int32, (step, step), 1)
    before = (place <= other) if reverse else (place >= other)
    triangle = before.astype(FLOAT)
    carry = jnp.zeros((1, values.shape[1]), FLOAT)
    parts = [None] * count
    for index in reversed(range(count)) if reverse else range(count):
        part = values[index * step : (index + 1) * step]
        run = jnp.dot(triangle, part, precision=HIGH, preferred_element_type=FLOAT) + carry
        carry = run[:1] if reverse else run[step - 1 :]
        parts[index] = run
    return parts[0] if count == 1 else jnp.concatenate(parts, axis=0)


def head_columns(rows, columns, head_width):
    head = lax.broadcasted_iota(jnp.int32, (rows, columns), 0) * head_width
    column = lax.broadcasted_iota(jnp.int32, (rows, columns), 1)
    return ((column >= head) & (column < head + head_width)).astype(FLOAT)


def sigmoid(value):
    return 1.0 / (1.0 + jnp.exp(-value))


def step_sizes(step_pre, step_row_ref):
    shifted_pre = step_pre + step_row_ref[0:1, :]
    sizes = jnp.maximum(shifted_pre, 0.0) + jnp.log1p(jnp.exp(-jnp.abs(shifted_pre)))
    return shifted_pre, sizes, -jnp.exp(step_row_ref[1:2, :])


def conv_rows(values, weight_ref, columns, marks_ref):
    width = weight_ref.shape[0]
    result = values * weight_ref[width - 1 : width, columns]
    for back in range(1, width):
        moved = pltpu.roll(values, back, 0) * marks_ref[:, back : back + 1]
        result = result + moved * weight_ref[width - 1 - back : width - back, columns]
    return result


def conv_rows_back(grad, values, weight_ref, columns, marks_ref, weight_grad_ref):
    width = weight_ref.shape[0]
    rows = values.shape[0]
    result = grad * weight_ref[width - 1 : width, columns]
    weight_grad_ref[width - 1 : width, columns] = jnp.sum(grad * values, axis=0, keepdims=True)
    for back in range(1, width):
        kept = grad * marks_ref[:, back : back + 1]
        taps = jnp.sum(kept * pltpu.roll(values, back, 0), axis=0, keepdims=True)
        weight_grad_ref[width - 1 - back : width - back, columns] = taps
        moved = pltpu.roll(kept, rows - back, 0)
        result = result + moved * weight_ref[width - 1 - back : width - back, columns]
    return result


def copy_in_order(source_ref, target_ref, place_ref, parts):
    if parts == 1:
        return source_ref
    rows = source_ref.shape[0] // parts
    for index in range(parts):
        target_ref[index * rows : (index + 1) * rows, :] = source_ref[
            block_rows(index, rows, place_ref, parts), :
        ]
    return target_ref


def block_rows(index, rows, place_ref, parts):
    if parts == 1:
        return slice(0, rows)
    back = lax.rem(place_ref[0] - index + parts, parts)
    return pl.ds(pl.multiple_of(back * rows, rows), rows)


def mixer_forward_kernel(
    heads,
    parts,
    pre_in_ref,
    pre_other_in_ref,
    conv_input_ref,
    conv_state_ref,
    step_row_ref,
    wide_row_ref,
    marks_ref,
    labels_ref,
    place_ref,
    y_ref,
    scaled_ref,
    total_ref,
    pre_ref,
    pre_other_ref,
    x_ref,
    dosed_ref,
    keys_ref,
    queries_ref,
):
    length, wide = y_ref.shape
    states = conv_state_ref.shape[1] // 2
    state_at, step_at = wide, wide
    head_width = HEAD
    pre_ref = copy_in_order(pre_in_ref, pre_ref, place_ref, parts)
    pre_other_ref = copy_in_order(pre_other_in_ref, pre_other_ref, place_ref, parts)
    _, sizes, rate = step_sizes(pre_other_ref[:, step_at : step_at + LANES], step_row_ref)
    running = summed_rows(sizes * rate, False)
    running_t = running.T
    expand = head_columns(LANES, wide, head_width)
    for start in range(0, wide, LANES):
        columns = slice(start, start + LANES)
        conv = conv_rows(
            pre_other_ref[:, columns], conv_input_ref, columns, marks_ref
        )
        x = conv * sigmoid(conv)
        x_ref[:, columns] = x
        dose = jnp.dot(sizes, expand[:, columns], precision=HIGH, preferred_element_type=FLOAT)
        dosed_ref[:, columns] = (x * dose).astype(HALF)
    for part, target in ((0, keys_ref), (1, queries_ref)):
        columns = slice(part * states, (part + 1) * states)
        conv = conv_rows(
            pre_ref[:, state_at + part * states : state_at + (part + 1) * states],
            conv_state_ref,
            columns,
            marks_ref,
        )
        target[...] = (conv * sigmoid(conv)).astype(HALF)
    block = min(length, CHUNK)
    place = lax.broadcasted_iota(jnp.int32, (block, block), 0)
    other = lax.broadcasted_iota(jnp.int32, (block, block), 1)
    for late in range(length // block):
        rows = slice(late * block, (late + 1) * block)
        for early in range(late + 1):
            past = slice(early * block, (early + 1) * block)
            same = marks_ref[rows, 0:1] == labels_ref[:, past]
            if late == early:
                same = same & (place >= other)
            mask = jnp.where(same, 0.0, -1e30)
            scores = lax.dot_general(
                queries_ref[rows, :],
                keys_ref[past, :],
                (((1,), (1,)), ((), ())),
                preferred_element_type=FLOAT,
            )
            for head in range(heads):
                columns = slice(head * head_width, (head + 1) * head_width)
                spread_log = running[rows, head : head + 1] - running_t[head : head + 1, past]
                mixing = (jnp.exp(spread_log + mask) * scores).astype(HALF)
                inner = jnp.dot(mixing, dosed_ref[past, columns], preferred_element_type=FLOAT)
                if early == 0:
                    y_ref[rows, columns] = inner
                else:
                    y_ref[rows, columns] += inner
    total = jnp.zeros((length, 1), FLOAT)
    for start in range(0, wide, LANES):
        columns = slice(start, start + LANES)
        y = y_ref[:, columns]
        if heads * head_width < start + LANES:
            lane = lax.broadcasted_iota(jnp.int32, y.shape, 1) + start
            y = jnp.where(lane < heads * head_width, y, 0.0)
        y = y + wide_row_ref[1:2, columns] * x_ref[:, columns]
        gate = pre_ref[:, columns]
        gated = y * gate * sigmoid(gate)
        y_ref[:, columns] = y
        scaled = (gated * wide_row_ref[0:1, columns]).astype(HALF)
        each = length // parts
        for index in range(parts):
            block_at = block_rows(index, each, place_ref, parts)
            scaled_ref[block_at, columns] = scaled[index * each : (index + 1) * each]
        total = total + jnp.sum(gated * gated, axis=1, keepdims=True)
    each = length // parts
    for index in range(parts):
        block_at = block_rows(index, each, place_ref, parts)
        total_ref[block_at, :] = total[index * each : (index + 1) * each]


def mixer_backward_kernel(
    heads,
    parts,
    inner_all,
    pre_in_ref,
    pre_other_in_ref,
    y_ref,
    grad_in_ref,
    sides_in_ref,
    conv_input_ref,
    conv_state_ref,
    step_row_ref,
    wide_row_ref,
    marks_ref,
    labels_ref,
    place_ref,
    grad_pre_ref,
    grad_pre_other_ref,
    wide_grad_ref,
    conv_input_grad_ref,
    conv_state_grad_ref,
    step_grad_ref,
    pre_ref,
    pre_other_ref,
    grad_ref,
    sides_ref,
    x_ref,
    dosed_ref,
    dose_ref,
    slope_ref,
    dy_ref,
    z_ref,
    bc_ref,
    bc_slope_ref,
    bc_grad_ref,
):
    length, wide = y_ref.shape
    states = conv_state_ref.shape[1] // 2
    state_at, step_at = wide, wide
    head_width = HEAD
    each = length // parts
    pre_ref = copy_in_order(pre_in_ref, pre_ref, place_ref, parts)
    pre_other_ref = copy_in_order(pre_other_in_ref, pre_other_ref, place_ref, parts)
    grad_ref = copy_in_order(grad_in_ref, grad_ref, place_ref, parts)
    sides_ref = copy_in_order(sides_in_ref, sides_ref, place_ref, parts)

    def put(target_ref, value, start):
        for index in range(parts):
            target_ref[block_rows(index, each, place_ref, parts), start : start + LANES] = value[
                index * each : (index + 1) * each
            ]

    shifted_pre, sizes, rate = step_sizes(pre_other_ref[:, step_at : step_at + LANES], step_row_ref)
    running = summed_rows(sizes * rate, False)
    running_t = running.T
    expand = head_columns(LANES, wide, head_width)
    rr = sides_ref[:, 0:1]
    pull = rr * rr * rr * sides_ref[:, 1:2] * (1.0 / inner_all)
    for start in range(0, wide, LANES):
        columns = slice(start, start + LANES)
        gate = pre_ref[:, columns]
        y = y_ref[:, columns]
        grad = grad_ref[:, columns]
        gain = wide_row_ref[0:1, columns]
        sigma = sigmoid(gate)
        silu = gate * sigma
        gated = y * silu
        normed = gated * rr
        wide_grad_ref[0:1, columns] = jnp.sum(grad * normed, axis=0, keepdims=True)
        grad_gated = rr * gain * grad - gated * pull
        slope = sigma * (1.0 + gate * (1.0 - sigma))
        put(grad_pre_ref, (grad_gated * y * slope).astype(HALF), start)
        dy = grad_gated * silu
        dy_ref[:, columns] = dy
        conv = conv_rows(
            pre_other_ref[:, columns], conv_input_ref, columns, marks_ref
        )
        sigma = sigmoid(conv)
        x = conv * sigma
        x_ref[:, columns] = x
        slope_ref[:, columns] = sigma * (1.0 + conv * (1.0 - sigma))
        dose = jnp.dot(sizes, expand[:, columns], precision=HIGH, preferred_element_type=FLOAT)
        dose_ref[:, columns] = dose
        dosed_ref[:, columns] = (x * dose).astype(HALF)
        wide_grad_ref[1:2, columns] = jnp.sum(dy * x, axis=0, keepdims=True)
    for start in range(0, 2 * states, LANES):
        columns = slice(start, start + LANES)
        conv = conv_rows(
            pre_ref[:, state_at + start : state_at + start + LANES],
            conv_state_ref,
            columns,
            marks_ref,
        )
        sigma = sigmoid(conv)
        bc_ref[:, columns] = (conv * sigma).astype(HALF)
        bc_slope_ref[:, columns] = sigma * (1.0 + conv * (1.0 - sigma))
    block = min(length, CHUNK)
    place = lax.broadcasted_iota(jnp.int32, (block, block), 0)
    other = lax.broadcasted_iota(jnp.int32, (block, block), 1)
    z_ref[...] = jnp.zeros(z_ref.shape, FLOAT)
    bc_grad_ref[...] = jnp.zeros(bc_grad_ref.shape, FLOAT)
    for late in range(length // block):
        rows = slice(late * block, (late + 1) * block)
        for early in range(late + 1):
            past = slice(early * block, (early + 1) * block)
            same = marks_ref[past, 0:1] == labels_ref[:, rows]
            if late == early:
                same = same & (place <= other)
            mask = jnp.where(same, 0.0, -1e30)
            keys = bc_ref[past, :states]
            queries = bc_ref[rows, states:]
            scores = lax.dot_general(
                keys, queries, (((1,), (1,)), ((), ())), preferred_element_type=FLOAT
            )
            mixed = jnp.zeros((block, block), FLOAT)
            for head in range(heads):
                columns = slice(head * head_width, (head + 1) * head_width)
                spread_log = running_t[head : head + 1, rows] - running[past, head : head + 1]
                decay = jnp.exp(spread_log + mask)
                mixing = (decay * scores).astype(HALF)
                dy = dy_ref[rows, columns].astype(HALF)
                z_ref[past, columns] += jnp.dot(mixing, dy, preferred_element_type=FLOAT)
                along = lax.dot_general(
                    dosed_ref[past, columns],
                    dy,
                    (((1,), (1,)), ((), ())),
                    preferred_element_type=FLOAT,
                )
                mixed = mixed + decay * along
            mixed = mixed.astype(HALF)
            bc_grad_ref[past, :states] += jnp.dot(mixed, queries, preferred_element_type=FLOAT)
            bc_grad_ref[rows, states:] += lax.dot_general(
                mixed, keys, (((0,), (0,)), ((), ())), preferred_element_type=FLOAT
            )
    direct = jnp.zeros((length, LANES), FLOAT)
    balance = jnp.zeros((length, LANES), FLOAT)
    for start in range(0, wide, LANES):
        columns = slice(start, start + LANES)
        x, z, dy = x_ref[:, columns], z_ref[:, columns], dy_ref[:, columns]
        skip = wide_row_ref[1:2, columns]
        collapse = (((1,), (1,)), ((), ()))
        both = dy.astype(HALF).astype(FLOAT) * (y_ref[:, columns] - skip * x)
        both = both - dosed_ref[:, columns].astype(FLOAT) * z
        heads_of = expand[:, columns]
        direct = direct + lax.dot_general(
            x * z, heads_of, collapse, precision=HIGH, preferred_element_type=FLOAT
        )
        balance = balance + lax.dot_general(
            both, heads_of, collapse, precision=HIGH, preferred_element_type=FLOAT
        )
        grad_conv = (dose_ref[:, columns] * z + skip * dy) * slope_ref[:, columns]
        grad_in = conv_rows_back(
            grad_conv,
            pre_other_ref[:, columns],
            conv_input_ref,
            columns,
            marks_ref,
            conv_input_grad_ref,
        )
        put(grad_pre_other_ref, grad_in.astype(HALF), start)
    for start in range(0, 2 * states, LANES):
        columns = slice(start, start + LANES)
        grad_in = conv_rows_back(
            bc_grad_ref[:, columns] * bc_slope_ref[:, columns],
            pre_ref[:, state_at + start : state_at + start + LANES],
            conv_state_ref,
            columns,
            marks_ref,
            conv_state_grad_ref,
        )
        put(grad_pre_ref, grad_in.astype(HALF), state_at + start)
    crossing = summed_rows(balance, True)
    grad_step = (direct + rate * crossing) * sigmoid(shifted_pre)
    put(grad_pre_other_ref, grad_step.astype(HALF), step_at)
    for start in range(step_at + LANES, grad_pre_other_ref.shape[1], LANES):
        put(grad_pre_other_ref, jnp.zeros((length, LANES), HALF), start)
    step_grad_ref[0:1, :] = jnp.sum(grad_step, axis=0, keepdims=True)
    step_grad_ref[1:2, :] = rate * jnp.sum(sizes * crossing, axis=0, keepdims=True)


def ordered_copy(shape):
    return pltpu.VMEM(shape if groups() > 1 else (8, LANES), FLOAT)


def whole_call(kernel, inputs, results, scratch, name):
    whole = pl.BlockSpec(memory_space=pltpu.VMEM)
    place = pl.BlockSpec(memory_space=pltpu.SMEM)
    return pl.pallas_call(
        kernel,
        in_specs=[whole] * (inputs - 1) + [place],
        out_shape=results,
        scratch_shapes=scratch,
        compiler_params=pltpu.CompilerParams(vmem_limit_bytes=VMEM_BYTES),
        name=name,
    )


def mixer_forward(pre, heads, wide, mixer):
    length = pre[0].shape[0]
    kernel = functools.partial(mixer_forward_kernel, heads, groups())
    states = mixer[1].shape[1] // 2
    return whole_call(
        kernel,
        2 + len(mixer),
        (
            jax.ShapeDtypeStruct((length, wide), FLOAT),
            jax.ShapeDtypeStruct((length, wide), HALF),
            jax.ShapeDtypeStruct((length, 1), FLOAT),
        ),
        [
            ordered_copy(pre[0].shape),
            ordered_copy(pre[1].shape),
            pltpu.VMEM((length, wide), FLOAT),
            pltpu.VMEM((length, wide), HALF),
            pltpu.VMEM((length, states), HALF),
            pltpu.VMEM((length, states), HALF),
        ],
        "mixer_forward",
    )(*pre, *mixer)


def mixer_backward(pre, y, grad, sides, heads, mixer):
    length, wide = y.shape
    kernel = functools.partial(mixer_backward_kernel, heads, groups(), DI)
    double = mixer[1].shape[1]
    square = pltpu.VMEM((length, wide), FLOAT)
    return whole_call(
        kernel,
        5 + len(mixer),
        (
            jax.ShapeDtypeStruct(pre[0].shape, HALF),
            jax.ShapeDtypeStruct(pre[1].shape, HALF),
            jax.ShapeDtypeStruct((2, wide), FLOAT),
            jax.ShapeDtypeStruct((4, wide), FLOAT),
            jax.ShapeDtypeStruct((4, double), FLOAT),
            jax.ShapeDtypeStruct((2, LANES), FLOAT),
        ),
        [
            ordered_copy(pre[0].shape),
            ordered_copy(pre[1].shape),
            ordered_copy(y.shape),
            ordered_copy(sides.shape),
            square,
            pltpu.VMEM((length, wide), HALF),
            square,
            square,
            square,
            square,
            pltpu.VMEM((length, double), HALF),
            pltpu.VMEM((length, double), FLOAT),
            pltpu.VMEM((length, double), FLOAT),
        ],
        "mixer_backward",
    )(*pre, y, grad, sides, *mixer)


def to_blocks(per_chunk):
    parts = [None] * groups()
    for chunk, part in zip(chunks(), per_chunk):
        rows_each = part.shape[0] // len(chunk)
        for at, back in enumerate(chunk):
            parts[back] = part[at * rows_each : (at + 1) * rows_each]
    return parts


def through_experts(block, tables, expert, beside):
    if groups() < 4:
        blocks = spread(block)
        tokens = [joined([blocks[back] for back in chunk]) for chunk in chunks()]
        arrived = [to_experts(project(table, each)) for table, each in zip(tables, tokens)]
        answers = [to_experts(expert(index, rows)) for index, rows in enumerate(arrived)]
        made = [beside(*each) for each in zip(range(len(tokens)), tokens, answers)]
        return to_blocks(made), arrived, tokens
    near, far = shifted(block, "col", 1), shifted(block, "col", 3)
    rows = to_experts(project(tables[0], block))
    answer = expert(0, rows)
    answered = to_experts(answer)
    near, far = after(near, answer), after(far, answer)
    last = shifted(after(block, near, far), "col", 2)
    near = jnp.concatenate([near, far], axis=0)
    sent = project(tables[1], near).astype(HALF)
    rows_near = to_experts(sent)
    part = beside(0, block, answered)
    last = after(last, sent, part)
    sent = project(tables[2], last).astype(HALF)
    rows_last = to_experts(sent)
    answer = expert(1, after(rows_near, sent))
    answered = to_experts(answer)
    answer = expert(2, after(rows_last, answer))
    answered_last = to_experts(answer)
    part_near = beside(1, near, after(answered, answer))
    part_last = beside(2, last, answered_last)
    parts = to_blocks([part, part_near, part_last])
    return parts, [rows, rows_near, rows_last], [block, near, last]


def line_shares(values, weights):
    whole = sum(project_back(value, weight) for value, weight in zip(values, weights)).astype(HALF)
    return gathered_sum([block_of(whole, back) for back in range(groups())]), whole


def expert_forward(rows, experts):
    gate_e = project(rows, experts[0])
    lift_e = project(rows, experts[1])
    act_e = (jax.nn.silu(gate_e) * lift_e).astype(HALF)
    return (gate_e, lift_e, act_e), project(act_e, experts[2]).astype(HALF)


def expert_backward(rows, kept, experts):
    gate_e, lift_e, _ = kept
    grad_act = project_back(rows, experts[2])
    grad_gate = (grad_act * lift_e * silu_slope(gate_e)).astype(HALF)
    grad_lift = (grad_act * jax.nn.silu(gate_e)).astype(HALF)
    back = project_back(grad_gate, experts[0]) + project_back(grad_lift, experts[1])
    return (grad_gate, grad_lift), back.astype(HALF)


def shared_forward(tokens, shared):
    hidden = shared.shape[1] // 3
    gate_s = project(tokens, shared[:, :hidden])
    lift_s = project(tokens, shared[:, hidden : 2 * hidden])
    return gate_s, lift_s, (jax.nn.silu(gate_s) * lift_s).astype(HALF)


def shared_backward(tokens, kept, shared):
    hidden = shared.shape[1] // 3
    gate_s, lift_s, _ = kept
    grad_act = project(tokens, shared[:, 2 * hidden :])
    grad_gate = (grad_act * lift_s * silu_slope(gate_s)).astype(HALF)
    grad_lift = (grad_act * jax.nn.silu(gate_s)).astype(HALF)
    part = project_back(grad_gate, shared[:, :hidden])
    part = part + project_back(grad_lift, shared[:, hidden : 2 * hidden])
    return (grad_gate, grad_lift), part


def home_part(table, result, act_s, shared):
    hidden = shared.shape[1] // 3
    return (outer(table, result) + project_back(act_s, shared[:, 2 * hidden :])).astype(HALF)


def weight_sums(rows_in, rows_out, kept, grads, tokens_in, tokens_out, kept_s, grads_s):
    rows_in, rows_out = joined(rows_in), joined(rows_out)
    experts = (
        outer(rows_in, joined([each[0] for each in grads])),
        outer(rows_in, joined([each[1] for each in grads])),
        outer(joined([each[2] for each in kept]), rows_out),
    )
    tokens_in, tokens_out = joined(tokens_in), joined(tokens_out)
    pairs = [joined([each[at] for each in grads_s]) for at in range(2)]
    act_s = joined([each[2] for each in kept_s])
    shared = (section_half(tokens_in, *pairs), section_half(tokens_out, *two_halves(act_s)))
    return experts, shared


def middle_backward(grad_normed, grad_out, middle, mixed, norm_mid):
    _, pull_mid = jax.vjp(rms_norm, middle, norm_mid)
    grad_middle, grad_norm_mid = pull_mid(grad_normed)
    grad_middle = grad_middle + grad_out
    along = jnp.sum(grad_middle * mixed, axis=1, keepdims=True)
    return grad_middle, along, grad_norm_mid


def two_halves(values):
    middle = values.shape[1] // 2
    return values[:, :middle], values[:, middle:]


def half_to_give(left, first_right, second_right):
    first = lax.axis_index("section") == 0
    return outer(left, jnp.where(first, second_right, first_right)).astype(HALF)


def half_to_keep(left, first_right, second_right, given):
    first = lax.axis_index("section") == 0
    keep = outer(left, jnp.where(first, first_right, second_right))
    return (keep + swapped(given).astype(FLOAT)).astype(HALF)


def section_half(left, first_right, second_right):
    given = half_to_give(left, first_right, second_right)
    return half_to_keep(left, first_right, second_right, given)


def row_share(values):
    n_row = lax.axis_size("row")
    rows = values.shape[0] // n_row
    total = None
    for ahead in range(n_row):
        index = lax.rem(lax.axis_index("row") + ahead, n_row)
        part = lax.dynamic_slice_in_dim(values, index * rows, rows, axis=0)
        part = shifted(part, "row", ahead).astype(FLOAT)
        total = part if total is None else total + part
    return total.astype(HALF)


def col_sum(values):
    n_col = lax.axis_size("col")
    if groups() == 1:
        return lax.psum(values, "col")
    rows = values.shape[0] // n_col
    total = None
    for ahead in range(n_col):
        index = lax.rem(lax.axis_index("col") + ahead, n_col)
        part = lax.dynamic_slice_in_dim(values, index * rows, rows, axis=0)
        part = shifted(part, "col", ahead).astype(FLOAT)
        total = part if total is None else total + part
    total = total.astype(values.dtype)
    return in_order([shifted(total, "col", back) for back in range(n_col)], "col")


def flat(parts):
    return jnp.concatenate([part.reshape(-1) for part in parts])


def unflat(vector, shapes):
    result, start = [], 0
    for shape in shapes:
        size = 1
        for entry in shape:
            size *= entry
        result.append(vector[start : start + size].reshape(shape))
        start += size
    return result


def widened(value, columns):
    return jnp.pad(value, ((0, 0), (0, columns - value.shape[1])))


def shards(
    tokens,
    cotangent,
    doc_lengths,
    routes,
    gates,
    norm_in,
    proj_gate,
    proj_input,
    proj_state,
    proj_step,
    step_bias,
    decay_log,
    skip_gain,
    conv_input,
    conv_state,
    gate_norm,
    proj_output,
    norm_mid,
    expert_gate,
    expert_up,
    expert_down,
    shared_gate,
    shared_up,
    shared_down,
):
    section_now = lax.axis_index("section")
    first = section_now == 0
    row_now = lax.axis_index("row")
    n_row, n_col = lax.axis_size("row"), lax.axis_size("col")
    count = tokens.shape[1]
    top = routes.shape[3]
    capacity = count * top * 4 // (3 * n_row * n_col)
    width = tokens.shape[2]
    heads = step_bias.shape[1]
    inner = gate_norm.shape[1]
    state = conv_state.shape[2]
    wide = -(-inner // LANES) * LANES
    layers = range(2)

    def pair(own, other):
        return (jnp.where(first, own, other), jnp.where(first, other, own))

    tokens_now = lax.dynamic_index_in_dim(tokens, section_now, 0, keepdims=False)
    grad_now = lax.dynamic_index_in_dim(cotangent, section_now, 0, keepdims=False)
    wide_tokens = joined(spread(tokens_now.astype(HALF)))

    halves = (
        jnp.concatenate([widened(proj_gate[0], wide), proj_state[0]], axis=1),
        jnp.concatenate([widened(proj_input[0], wide), widened(proj_step[0], state)], axis=1),
    )
    keep, give = jnp.where(first, *halves), jnp.where(first, *halves[::-1])
    mine = pair(keep, swapped(give))
    mine = [lax.all_gather(half, "row", axis=0, tiled=True) for half in mine]
    proj = [pair(half, swapped(half)) for half in mine]

    def both_layers(weight):
        whole = lax.all_gather(weight, ("section", "row"), axis=0, tiled=True)
        return whole.reshape(2, n_row * weight.shape[0], weight.shape[1])

    proj_out = both_layers(widened(proj_output[0], wide))
    gate_all = lax.all_gather(expert_gate[0, 0], "section")
    up_all = lax.all_gather(expert_up[0, 0], "section")
    down_all = lax.all_gather(expert_down[0, 0], "section")
    shared = both_layers(jnp.concatenate([shared_gate[0], shared_up[0], shared_down[0]], axis=1))
    experts = [(gate_all[s], up_all[s], down_all[s]) for s in layers]

    small_in = (
        norm_in[0],
        norm_mid[0],
        widened(conv_input[0], wide),
        conv_state[0],
        widened(jnp.concatenate([step_bias, decay_log], axis=0), LANES),
        widened(jnp.concatenate([gate_norm, jnp.repeat(skip_gain, HEAD, axis=1)], axis=0), wide),
    )
    vector = flat(small_in)
    small_all = [unflat(part, [v.shape for v in small_in]) for part in pair(vector, swapped(vector))]
    norm_ins = [part[0] for part in small_all]
    norm_mids = [part[1] for part in small_all]

    meta = jnp.concatenate([routes.astype(FLOAT), gates], axis=3)[0]
    keep = lax.dynamic_index_in_dim(meta, section_now, 0, keepdims=False)
    give = lax.dynamic_index_in_dim(meta, 1 - section_now, 0, keepdims=False)
    meta = jnp.concatenate(pair(keep, swapped(give)), axis=1)

    lengths = lax.dynamic_slice(
        doc_lengths, (section_now, row_now, 0), (1, 1, doc_lengths.shape[2])
    )
    labels = local_docs(lengths[0, 0], row_now, n_col * count)
    marks = [labels.astype(FLOAT)]
    for back in range(1, conv_input.shape[1]):
        prior = jnp.pad(labels, (back, 0), constant_values=-1)[:-back]
        marks.append((prior == labels).astype(FLOAT))
    marks = jnp.stack(marks, axis=1)
    label_row = labels.astype(FLOAT)[None]
    place = turn()
    mixers = [
        (conv_in, conv_st, step_row, wide_row, marks, label_row, place)
        for _, _, conv_in, conv_st, step_row, wide_row in small_all
    ]

    def mix_in(s, wide_in):
        pre = [project(wide_in, half) for half in proj[s]]
        return pre, *mixer_forward(pre, heads, wide, mixers[s])

    def mix_out(s, resid, scaled, total_part):
        mixed, _ = line_shares([scaled], [proj_out[s]])
        total = gathered_sum([block_of(total_part, back) for back in range(groups())])
        rr = lax.rsqrt(total / DI + EPS)
        return resid + mixed * rr, mixed, rr

    wide_in_0 = rms_norm(wide_tokens.astype(FLOAT), norm_ins[0]).astype(HALF)
    pre_0, y_0, scaled_0, total_0 = mix_in(0, wide_in_0)
    grad_blocks = spread(after(grad_now.astype(HALF), wide_in_0))
    tables = route_tables(spread(after(meta, scaled_0)), top, capacity, 2)
    plain = [[table[0] for table in tables[s]] for s in layers]
    scaling = [[table[1] for table in tables[s]] for s in layers]
    middle_0, mixed_0, rr_0 = mix_out(0, tokens_now, scaled_0, total_0)
    kept_0, kept_s_0 = {}, {}

    def expert_0(index, rows):
        kept_0[index], answer = expert_forward(rows, experts[0])
        return answer

    def beside_0(index, block, result):
        kept_s_0[index] = shared_forward(block, shared[0])
        return home_part(scaling[0][index], result, kept_s_0[index][2], shared[0])

    parts, rows_0, mids_0 = through_experts(
        rms_norm(middle_0, norm_mids[0]).astype(HALF), plain[0], expert_0, beside_0
    )
    out_0 = middle_0 + gathered_sum(parts)

    wide_in_1 = joined(spread(rms_norm(out_0, norm_ins[1]).astype(HALF)))
    grad_tokens = [joined([grad_blocks[back] for back in chunk]) for chunk in chunks()]
    grad_rows_1 = [
        to_experts(project(table, after(block, out_0)))
        for table, block in zip(scaling[1], grad_tokens)
    ]
    pre_1, y_1, scaled_1, total_1 = mix_in(1, wide_in_1)
    scaled_1 = after(scaled_1, *grad_rows_1)
    middle_1, mixed_1, rr_1 = mix_out(1, out_0, scaled_1, total_1)

    kept_1, kept_s_1, grads_1, grads_s_1, answers_1 = {}, {}, {}, {}, {}

    def expert_1(index, rows):
        kept_1[index], answers_1[index] = expert_forward(rows, experts[1])
        grads_1[index], back = expert_backward(grad_rows_1[index], kept_1[index], experts[1])
        return back

    def beside_1(index, block, result):
        kept_s_1[index] = shared_forward(block, shared[1])
        grads_s_1[index], part = shared_backward(grad_tokens[index], kept_s_1[index], shared[1])
        return (part + outer(plain[1][index], result)).astype(HALF)

    parts, rows_1, mids_1 = through_experts(
        rms_norm(middle_1, norm_mids[1]).astype(HALF), plain[1], expert_1, beside_1
    )
    order = range(len(chunks()))
    answers = [to_experts(after(answers_1[index], parts[-1])) for index in order]

    def listed(kept):
        return [kept[index] for index in order]

    def mixer_back(s, grad_middle, along, rr, saved, weight_grads, last):
        wide_in, pre, y, scaled = saved
        wide_mix = joined(spread(grad_middle.astype(HALF)))
        sides = joined(spread(jnp.concatenate([rr, along], axis=1)))
        wide_mix = after(wide_mix, weight_grads)
        grad_scaled = project(wide_mix, proj_out[s])
        *grad_pre, wide_grads, grad_conv_input, grad_conv_state, step_grads = mixer_backward(
            pre, y, grad_scaled, sides, heads, mixers[s]
        )
        ends = [part[:, :wide] for part in grad_pre]
        if last:
            given = half_to_give(wide_in, *ends)
            grad_in, whole = line_shares([after(part, given) for part in grad_pre], proj[s])
        else:
            grad_in, whole = line_shares(grad_pre, proj[s])
            given = half_to_give(after(wide_in, whole), *ends)
        grad_proj = half_to_keep(after(wide_in, whole), *ends, given)
        mix_rr = (after(wide_mix, grad_proj) * sides[:, :1]).astype(HALF)
        grad_proj_out = section_half(mix_rr, *two_halves(scaled))
        tail = jnp.concatenate([grad_pre[0][:, wide:], grad_pre[1][:, wide : wide + LANES]], axis=1)
        grad_tail = outer(after(wide_in, grad_proj), tail).astype(HALF)
        rest = (grad_conv_state, grad_conv_input, wide_grads, step_grads)
        return wide_mix, grad_in, grad_proj, grad_proj_out, grad_tail, rest

    def resid_back(resid, norm, grad_normed, grad_middle):
        _, pull_in = jax.vjp(rms_norm, resid, norm)
        grad_resid, grad_norm = pull_in(grad_normed)
        return grad_resid + grad_middle, grad_norm

    def row_sums(value):
        return lax.psum_scatter(value, "row", scatter_dimension=0, tiled=True)

    def own_layer(first_value, second_value):
        keep = jnp.where(first, first_value, second_value)
        give = jnp.where(first, second_value, first_value).astype(HALF)
        return keep.astype(FLOAT) + swapped(give).astype(FLOAT)

    grad_middle, along, grad_norm_mid_1 = middle_backward(
        gathered_sum(parts), grad_now, middle_1, mixed_1, norm_mids[1]
    )
    expert_grads_1, shared_grads_1 = weight_sums(
        rows_1,
        grad_rows_1,
        listed(kept_1),
        listed(grads_1),
        mids_1,
        grad_tokens,
        listed(kept_s_1),
        listed(grads_s_1),
    )
    expert_grads_1 = [grad.astype(HALF) for grad in expert_grads_1]
    wide_mix, grad_in, grad_proj_1, grad_out_1, grad_tail_1, rest_1 = mixer_back(
        1,
        grad_middle,
        along,
        rr_1,
        (wide_in_1, pre_1, y_1, scaled_1),
        (expert_grads_1, shared_grads_1),
        False,
    )
    grad_1, grad_norm_in_1 = resid_back(out_0, norm_ins[1], grad_in, grad_middle)
    home = [
        home_part(scaling[1][index], answers[index], kept_s_1[index][2], shared[1])
        for index in order
    ]
    home = [after(part, wide_mix) for part in home]
    out_1 = middle_1 + gathered_sum(to_blocks(home))
    sums_1 = [row_sums(value) for value in (*shared_grads_1, grad_out_1, grad_proj_1)]

    grads_0, grads_s_0 = {}, {}

    def expert_back_0(index, rows):
        grads_0[index], back = expert_backward(rows, kept_0[index], experts[0])
        return back

    def beside_back_0(index, block, result):
        grads_s_0[index], part = shared_backward(block, kept_s_0[index], shared[0])
        return (part + outer(plain[0][index], result)).astype(HALF)

    parts, grad_rows_0, grad_tokens_0 = through_experts(
        grad_1.astype(HALF), scaling[0], expert_back_0, beside_back_0
    )
    grad_middle, along, grad_norm_mid_0 = middle_backward(
        gathered_sum(parts), grad_1, middle_0, mixed_0, norm_mids[0]
    )
    expert_grads_0, shared_grads_0 = weight_sums(
        rows_0,
        grad_rows_0,
        listed(kept_0),
        listed(grads_0),
        mids_0,
        grad_tokens_0,
        listed(kept_s_0),
        listed(grads_s_0),
    )
    expert_out = [
        own_layer(a.astype(HALF), b) for a, b in zip(expert_grads_0, expert_grads_1)
    ]
    sums_0 = [row_sums(value) for value in shared_grads_0]
    wide_mix, grad_in, grad_proj_0, grad_out_0, grad_tail_0, rest_0 = mixer_back(
        0,
        grad_middle,
        along,
        rr_0,
        (wide_in_0, pre_0, y_0, scaled_0),
        (expert_out, shared_grads_0),
        True,
    )
    grad_0, grad_norm_in_0 = resid_back(tokens_now, norm_ins[0], grad_in, grad_middle)
    sums_0 = [*sums_0, row_sums(grad_out_0), row_share(grad_proj_0)]

    def own_halves(first_value, second_value):
        keep = jnp.where(first, first_value, second_value)
        give = jnp.where(first, second_value, first_value)
        return pair(keep, swapped(give))

    tail = row_share(own_layer(grad_tail_0, grad_tail_1).astype(HALF))
    state_grad = col_sum(tail[:, :state])
    grad_shared, grad_down, grad_out, grad_ends = [own_halves(a, b) for a, b in zip(sums_0, sums_1)]
    grad_out, grad_down = [jnp.concatenate(both, axis=1) for both in (grad_out, grad_down)]

    smalls = (
        (grad_norm_in_0, grad_norm_mid_0, *rest_0),
        (grad_norm_in_1, grad_norm_mid_1, *rest_1),
    )
    shapes = [part.shape for part in smalls[0]]
    vector = own_layer(flat(smalls[0]), flat(smalls[1]))
    lines = [shifted(vector[None], "row", back) for back in range(n_row)]
    vector = jnp.sum(in_order(lines, "row"), axis=0)
    common = 2 * width + conv_state.shape[1] * state
    if groups() > 1:
        lines = [shifted(vector[None, :common], "col", back) for back in range(n_col)]
        shared_sum = jnp.sum(in_order(lines, "col"), axis=0)
    else:
        shared_sum = lax.psum(vector[:common], "col")
    (
        out_norm_in,
        out_norm_mid,
        out_conv_state,
        out_conv_input,
        out_wide,
        out_step,
    ) = unflat(jnp.concatenate([shared_sum, vector[common:]]), shapes)

    def per_micro(first_value, second_value):
        keep = jnp.where(first, first_value, second_value)
        other = swapped(jnp.where(first, second_value, first_value).astype(HALF)).astype(FLOAT)
        return jnp.stack(pair(keep, other))[None]

    def out(value):
        return value.astype(FLOAT)[None]

    return (
        per_micro(out_0, out_1),
        per_micro(grad_0, grad_1),
        out_norm_in[None],
        out(grad_ends[0][:, :inner]),
        out(grad_ends[1][:, :inner]),
        out(state_grad),
        out(tail[:, state : state + heads]),
        out_step[:1, :heads],
        out_step[1:, :heads],
        jnp.sum(out_wide[1, :inner].reshape(heads, HEAD), axis=1)[None],
        out_conv_input[None, :, :inner],
        out_conv_state[None],
        out_wide[:1, :inner],
        out(grad_out[:, :inner]),
        out_norm_mid[None],
        expert_out[0][None, None],
        expert_out[1][None, None],
        expert_out[2][None, None],
        out(grad_shared[0]),
        out(grad_shared[1]),
        out(grad_down),
    )


def solution(mesh):
    in_specs = (
        P(None, ("row", "col"), None),
        P(None, ("row", "col"), None),
        P(),
        P("section", None, ("row", "col"), None),
        P("section", None, ("row", "col"), None),
        P("section", None),
        P("section", "row", "col"),
        P("section", "row", "col"),
        P("section", "row", None),
        P("section", "row", "col"),
        P("section", "col"),
        P("section", "col"),
        P("section", "col"),
        P("section", None, "col"),
        P("section", None, None),
        P("section", "col"),
        P("section", "row", "col"),
        P("section", None),
        P("section", ("row", "col"), None, None),
        P("section", ("row", "col"), None, None),
        P("section", ("row", "col"), None, None),
        P("section", "row", "col"),
        P("section", "row", "col"),
        P("section", "row", "col"),
    )
    out_specs = (
        P("section", None, ("row", "col"), None),
        P("section", None, ("row", "col"), None),
        P("section", None),
        P("section", "row", "col"),
        P("section", "row", "col"),
        P("section", "row", None),
        P("section", "row", "col"),
        P("section", "col"),
        P("section", "col"),
        P("section", "col"),
        P("section", None, "col"),
        P("section", None, None),
        P("section", "col"),
        P("section", "row", "col"),
        P("section", None),
        P("section", ("row", "col"), None, None),
        P("section", ("row", "col"), None, None),
        P("section", ("row", "col"), None, None),
        P("section", "row", "col"),
        P("section", "row", "col"),
        P("section", "row", "col"),
    )
    return jax.shard_map(shards, mesh=mesh, in_specs=in_specs, out_specs=out_specs, check_vma=False)
```

```python
import functools

import jax
import jax.numpy as jnp
from jax import lax
from jax.experimental import pallas as pl
from jax.experimental.pallas import tpu as pltpu
from jax.sharding import PartitionSpec as P

DI = 3072
HEAD = 64
LANES = 128
CHUNK = 256
VMEM_BYTES = 48 * 2**20

EPS = 1e-05
HIGH = lax.Precision.HIGHEST
FLOAT = jnp.float32
HALF = jnp.bfloat16


def shifted(block, axis, distance):
    count = lax.axis_size(axis)
    if distance % count == 0:
        return block
    return lax.ppermute(block, axis, [(i, (i + distance) % count) for i in range(count)])


def swapped(block):
    return lax.ppermute(block, "section", [(0, 1), (1, 0)])


def after(value, *others):
    return lax.optimization_barrier((value, *others))[0]


def rms_norm(value, gain):
    return value * lax.rsqrt(jnp.mean(value * value, axis=-1, keepdims=True) + EPS) * gain


def local_docs(lengths, row_now, length):
    bounds = jnp.cumsum(lengths)[:-1]
    place = jnp.arange(length, dtype=jnp.int32)
    inner = jnp.sum((place[:, None] >= bounds[None, :]).astype(jnp.int32), axis=1)
    return inner + row_now * lengths.shape[0]


def project(left, right):
    return jnp.dot(left, right, preferred_element_type=FLOAT)


def project_back(left, right):
    return lax.dot_general(left, right, (((1,), (1,)), ((), ())), preferred_element_type=FLOAT)


def outer(left, right):
    return lax.dot_general(left, right, (((0,), (0,)), ((), ())), preferred_element_type=FLOAT)


def silu_slope(value):
    sigma = jax.nn.sigmoid(value)
    return sigma * (1.0 + value * (1.0 - sigma))


def groups():
    count = lax.axis_size("col")
    return count if count <= 4 else 1


def chunks():
    return [tuple(range(groups()))]


def spread(block, meanwhile=()):
    if groups() == 1:
        return [lax.all_gather(block, "col", axis=0, tiled=True)]
    received = [shifted(block, "col", back) for back in range(1, groups())]
    return [block, *after(received, meanwhile)]


def joined(blocks):
    return blocks[0] if len(blocks) == 1 else jnp.concatenate(blocks, axis=0)


def in_order(blocks, axis):
    count = len(blocks)
    if count == 1:
        return blocks[0]
    rows = blocks[0].shape[0]
    line = jnp.concatenate(blocks[::-1] + blocks[:0:-1], axis=0)
    start = (count - 1 - lax.axis_index(axis)) * rows
    return lax.dynamic_slice_in_dim(line, start, count * rows, axis=0)


def gathered_sum(parts, meanwhile=()):
    if len(parts) == 1:
        return lax.psum_scatter(parts[0], "col", scatter_dimension=0, tiled=True).astype(FLOAT)
    received = [shifted(part, "col", -back) for back, part in enumerate(parts) if back]
    received = after(received, meanwhile)
    return sum([part.astype(FLOAT) for part in received], parts[0].astype(FLOAT))


def gathered_sum_in_turn(parts, meanwhile=()):
    count = len(parts)
    if count == 1:
        return gathered_sum(parts)

    def sent(values, section):
        at = section * count
        return [
            lax.ppermute(
                value,
                ("section", "col"),
                [(at + i, at + (i - back) % count) for i in range(count)],
            )
            for back, value in enumerate(values, 1)
        ]

    first = after(sent(parts[1:], 0), meanwhile)
    done = sum(part[:8, :LANES] for part in first)
    go = lax.ppermute(done, "section", [(0, 1)])
    second = sent(after(parts[1:], go), 1)
    return sum([part.astype(FLOAT) for part in (*first, *second)], parts[0].astype(FLOAT))


def block_of(values, back):
    rows = values.shape[0] // groups()
    return values[back * rows : (back + 1) * rows]


def turn():
    place = lax.axis_index("col") if groups() > 1 else jnp.int32(0)
    return place.astype(jnp.int32).reshape(1)


def route_tables(blocks, top, capacity, layers):
    n_row, n_col = lax.axis_size("row"), lax.axis_size("col")
    experts = (jnp.arange(n_row) * n_col + lax.axis_index("col")).astype(FLOAT)
    tables = [[] for _ in range(layers)]
    for chunk in chunks():
        now = joined([blocks[back] for back in chunk])
        count = now.shape[0]
        slots = len(chunk) * (n_col // groups()) * capacity
        now = now.reshape(count, layers, 2, top).transpose(1, 2, 3, 0)
        match = now[:, None, 0] == experts[None, :, None, None]
        hit = jnp.any(match, axis=2)
        weight = jnp.sum(jnp.where(match, now[:, None, 1], 0.0), axis=2)
        order = jnp.arange(count, dtype=jnp.int32)
        triangle = (order[:, None] <= order[None, :]).astype(HALF)
        place = project(hit.astype(HALF).reshape(-1, count), triangle).reshape(hit.shape)
        slot = jnp.arange(1, slots + 1, dtype=jnp.int32).astype(FLOAT)
        chosen = (place[:, :, None, :] == slot[:, None]) & hit[:, :, None, :]
        shape = (layers, n_row * slots, count)
        plain = chosen.astype(HALF).reshape(shape)
        scaled = jnp.where(chosen, weight[:, :, None, :], 0.0).astype(HALF).reshape(shape)
        for s in range(layers):
            tables[s].append((plain[s], scaled[s]))
    return tables


def to_experts(rows):
    return lax.all_to_all(rows.astype(HALF), "row", split_axis=0, concat_axis=0, tiled=True)


def summed_rows(values, reverse):
    step = min(values.shape[0], CHUNK)
    count = values.shape[0] // step
    place = lax.broadcasted_iota(jnp.int32, (step, step), 0)
    other = lax.broadcasted_iota(jnp.int32, (step, step), 1)
    before = (place <= other) if reverse else (place >= other)
    triangle = before.astype(FLOAT)
    carry = jnp.zeros((1, values.shape[1]), FLOAT)
    parts = [None] * count
    for index in reversed(range(count)) if reverse else range(count):
        part = values[index * step : (index + 1) * step]
        run = jnp.dot(triangle, part, precision=HIGH, preferred_element_type=FLOAT) + carry
        carry = run[:1] if reverse else run[step - 1 :]
        parts[index] = run
    return parts[0] if count == 1 else jnp.concatenate(parts, axis=0)


def head_columns(rows, columns, head_width):
    head = lax.broadcasted_iota(jnp.int32, (rows, columns), 0) * head_width
    column = lax.broadcasted_iota(jnp.int32, (rows, columns), 1)
    return ((column >= head) & (column < head + head_width)).astype(FLOAT)


def sigmoid(value):
    return 1.0 / (1.0 + jnp.exp(-value))


def step_sizes(step_pre, step_row_ref):
    shifted_pre = step_pre + step_row_ref[0:1, :]
    sizes = jnp.maximum(shifted_pre, 0.0) + jnp.log1p(jnp.exp(-jnp.abs(shifted_pre)))
    return shifted_pre, sizes, -jnp.exp(step_row_ref[1:2, :])


def conv_rows(values, weight_ref, columns, marks_ref):
    width = weight_ref.shape[0]
    result = values * weight_ref[width - 1 : width, columns]
    for back in range(1, width):
        moved = pltpu.roll(values, back, 0) * marks_ref[:, back : back + 1]
        result = result + moved * weight_ref[width - 1 - back : width - back, columns]
    return result


def conv_rows_back(grad, values, weight_ref, columns, marks_ref, weight_grad_ref):
    width = weight_ref.shape[0]
    rows = values.shape[0]
    result = grad * weight_ref[width - 1 : width, columns]
    weight_grad_ref[width - 1 : width, columns] = jnp.sum(grad * values, axis=0, keepdims=True)
    for back in range(1, width):
        kept = grad * marks_ref[:, back : back + 1]
        taps = jnp.sum(kept * pltpu.roll(values, back, 0), axis=0, keepdims=True)
        weight_grad_ref[width - 1 - back : width - back, columns] = taps
        moved = pltpu.roll(kept, rows - back, 0)
        result = result + moved * weight_ref[width - 1 - back : width - back, columns]
    return result


def copy_in_order(source_ref, target_ref, place_ref, parts):
    if parts == 1:
        return source_ref
    rows = source_ref.shape[0] // parts
    for index in range(parts):
        target_ref[index * rows : (index + 1) * rows, :] = source_ref[
            block_rows(index, rows, place_ref, parts), :
        ]
    return target_ref


def block_rows(index, rows, place_ref, parts):
    if parts == 1:
        return slice(0, rows)
    back = lax.rem(place_ref[0] - index + parts, parts)
    return pl.ds(pl.multiple_of(back * rows, rows), rows)


def mixer_forward_kernel(
    heads,
    parts,
    pre_in_ref,
    pre_other_in_ref,
    conv_input_ref,
    conv_state_ref,
    step_row_ref,
    wide_row_ref,
    marks_ref,
    labels_ref,
    place_ref,
    y_ref,
    scaled_ref,
    total_ref,
    pre_ref,
    pre_other_ref,
    x_ref,
    dosed_ref,
    keys_ref,
    queries_ref,
):
    length, wide = y_ref.shape
    states = conv_state_ref.shape[1] // 2
    state_at, step_at = wide, wide
    head_width = HEAD
    pre_ref = copy_in_order(pre_in_ref, pre_ref, place_ref, parts)
    pre_other_ref = copy_in_order(pre_other_in_ref, pre_other_ref, place_ref, parts)
    _, sizes, rate = step_sizes(pre_other_ref[:, step_at : step_at + LANES], step_row_ref)
    running = summed_rows(sizes * rate, False)
    running_t = running.T
    expand = head_columns(LANES, wide, head_width)
    for start in range(0, wide, LANES):
        columns = slice(start, start + LANES)
        conv = conv_rows(
            pre_other_ref[:, columns], conv_input_ref, columns, marks_ref
        )
        x = conv * sigmoid(conv)
        x_ref[:, columns] = x
        dose = jnp.dot(sizes, expand[:, columns], precision=HIGH, preferred_element_type=FLOAT)
        dosed_ref[:, columns] = (x * dose).astype(HALF)
    for part, target in ((0, keys_ref), (1, queries_ref)):
        columns = slice(part * states, (part + 1) * states)
        conv = conv_rows(
            pre_ref[:, state_at + part * states : state_at + (part + 1) * states],
            conv_state_ref,
            columns,
            marks_ref,
        )
        target[...] = (conv * sigmoid(conv)).astype(HALF)
    block = min(length, CHUNK)
    place = lax.broadcasted_iota(jnp.int32, (block, block), 0)
    other = lax.broadcasted_iota(jnp.int32, (block, block), 1)
    for late in range(length // block):
        rows = slice(late * block, (late + 1) * block)
        for early in range(late + 1):
            past = slice(early * block, (early + 1) * block)
            same = marks_ref[rows, 0:1] == labels_ref[:, past]
            if late == early:
                same = same & (place >= other)
            mask = jnp.where(same, 0.0, -1e30)
            scores = lax.dot_general(
                queries_ref[rows, :],
                keys_ref[past, :],
                (((1,), (1,)), ((), ())),
                preferred_element_type=FLOAT,
            )
            for head in range(heads):
                columns = slice(head * head_width, (head + 1) * head_width)
                spread_log = running[rows, head : head + 1] - running_t[head : head + 1, past]
                mixing = (jnp.exp(spread_log + mask) * scores).astype(HALF)
                inner = jnp.dot(mixing, dosed_ref[past, columns], preferred_element_type=FLOAT)
                if early == 0:
                    y_ref[rows, columns] = inner
                else:
                    y_ref[rows, columns] += inner
    total = jnp.zeros((length, 1), FLOAT)
    for start in range(0, wide, LANES):
        columns = slice(start, start + LANES)
        y = y_ref[:, columns]
        if heads * head_width < start + LANES:
            lane = lax.broadcasted_iota(jnp.int32, y.shape, 1) + start
            y = jnp.where(lane < heads * head_width, y, 0.0)
        y = y + wide_row_ref[1:2, columns] * x_ref[:, columns]
        gate = pre_ref[:, columns]
        gated = y * gate * sigmoid(gate)
        y_ref[:, columns] = y
        scaled = (gated * wide_row_ref[0:1, columns]).astype(HALF)
        each = length // parts
        for index in range(parts):
            block_at = block_rows(index, each, place_ref, parts)
            scaled_ref[block_at, columns] = scaled[index * each : (index + 1) * each]
        total = total + jnp.sum(gated * gated, axis=1, keepdims=True)
    each = length // parts
    for index in range(parts):
        block_at = block_rows(index, each, place_ref, parts)
        total_ref[block_at, :] = total[index * each : (index + 1) * each]


def mixer_backward_kernel(
    heads,
    parts,
    inner_all,
    pre_in_ref,
    pre_other_in_ref,
    y_ref,
    grad_in_ref,
    sides_in_ref,
    conv_input_ref,
    conv_state_ref,
    step_row_ref,
    wide_row_ref,
    marks_ref,
    labels_ref,
    place_ref,
    grad_pre_ref,
    grad_pre_other_ref,
    wide_grad_ref,
    conv_input_grad_ref,
    conv_state_grad_ref,
    step_grad_ref,
    pre_ref,
    pre_other_ref,
    grad_ref,
    sides_ref,
    x_ref,
    dosed_ref,
    dose_ref,
    slope_ref,
    dy_ref,
    z_ref,
    bc_ref,
    bc_slope_ref,
    bc_grad_ref,
):
    length, wide = y_ref.shape
    states = conv_state_ref.shape[1] // 2
    state_at, step_at = wide, wide
    head_width = HEAD
    each = length // parts
    pre_ref = copy_in_order(pre_in_ref, pre_ref, place_ref, parts)
    pre_other_ref = copy_in_order(pre_other_in_ref, pre_other_ref, place_ref, parts)
    grad_ref = copy_in_order(grad_in_ref, grad_ref, place_ref, parts)
    sides_ref = copy_in_order(sides_in_ref, sides_ref, place_ref, parts)

    def put(target_ref, value, start):
        for index in range(parts):
            target_ref[block_rows(index, each, place_ref, parts), start : start + LANES] = value[
                index * each : (index + 1) * each
            ]

    shifted_pre, sizes, rate = step_sizes(pre_other_ref[:, step_at : step_at + LANES], step_row_ref)
    running = summed_rows(sizes * rate, False)
    running_t = running.T
    expand = head_columns(LANES, wide, head_width)
    rr = sides_ref[:, 0:1]
    pull = rr * rr * rr * sides_ref[:, 1:2] * (1.0 / inner_all)
    for start in range(0, wide, LANES):
        columns = slice(start, start + LANES)
        gate = pre_ref[:, columns]
        y = y_ref[:, columns]
        grad = grad_ref[:, columns]
        gain = wide_row_ref[0:1, columns]
        sigma = sigmoid(gate)
        silu = gate * sigma
        gated = y * silu
        normed = gated * rr
        wide_grad_ref[0:1, columns] = jnp.sum(grad * normed, axis=0, keepdims=True)
        grad_gated = rr * gain * grad - gated * pull
        slope = sigma * (1.0 + gate * (1.0 - sigma))
        put(grad_pre_ref, (grad_gated * y * slope).astype(HALF), start)
        dy = grad_gated * silu
        dy_ref[:, columns] = dy
        conv = conv_rows(
            pre_other_ref[:, columns], conv_input_ref, columns, marks_ref
        )
        sigma = sigmoid(conv)
        x = conv * sigma
        x_ref[:, columns] = x
        slope_ref[:, columns] = sigma * (1.0 + conv * (1.0 - sigma))
        dose = jnp.dot(sizes, expand[:, columns], precision=HIGH, preferred_element_type=FLOAT)
        dose_ref[:, columns] = dose
        dosed_ref[:, columns] = (x * dose).astype(HALF)
        wide_grad_ref[1:2, columns] = jnp.sum(dy * x, axis=0, keepdims=True)
    for start in range(0, 2 * states, LANES):
        columns = slice(start, start + LANES)
        conv = conv_rows(
            pre_ref[:, state_at + start : state_at + start + LANES],
            conv_state_ref,
            columns,
            marks_ref,
        )
        sigma = sigmoid(conv)
        bc_ref[:, columns] = (conv * sigma).astype(HALF)
        bc_slope_ref[:, columns] = sigma * (1.0 + conv * (1.0 - sigma))
    block = min(length, CHUNK)
    place = lax.broadcasted_iota(jnp.int32, (block, block), 0)
    other = lax.broadcasted_iota(jnp.int32, (block, block), 1)
    z_ref[...] = jnp.zeros(z_ref.shape, FLOAT)
    bc_grad_ref[...] = jnp.zeros(bc_grad_ref.shape, FLOAT)
    for late in range(length // block):
        rows = slice(late * block, (late + 1) * block)
        for early in range(late + 1):
            past = slice(early * block, (early + 1) * block)
            same = marks_ref[past, 0:1] == labels_ref[:, rows]
            if late == early:
                same = same & (place <= other)
            mask = jnp.where(same, 0.0, -1e30)
            keys = bc_ref[past, :states]
            queries = bc_ref[rows, states:]
            scores = lax.dot_general(
                keys, queries, (((1,), (1,)), ((), ())), preferred_element_type=FLOAT
            )
            mixed = jnp.zeros((block, block), FLOAT)
            for head in range(heads):
                columns = slice(head * head_width, (head + 1) * head_width)
                spread_log = running_t[head : head + 1, rows] - running[past, head : head + 1]
                decay = jnp.exp(spread_log + mask)
                mixing = (decay * scores).astype(HALF)
                dy = dy_ref[rows, columns].astype(HALF)
                z_ref[past, columns] += jnp.dot(mixing, dy, preferred_element_type=FLOAT)
                along = lax.dot_general(
                    dosed_ref[past, columns],
                    dy,
                    (((1,), (1,)), ((), ())),
                    preferred_element_type=FLOAT,
                )
                mixed = mixed + decay * along
            mixed = mixed.astype(HALF)
            bc_grad_ref[past, :states] += jnp.dot(mixed, queries, preferred_element_type=FLOAT)
            bc_grad_ref[rows, states:] += lax.dot_general(
                mixed, keys, (((0,), (0,)), ((), ())), preferred_element_type=FLOAT
            )
    direct = jnp.zeros((length, LANES), FLOAT)
    balance = jnp.zeros((length, LANES), FLOAT)
    for start in range(0, wide, LANES):
        columns = slice(start, start + LANES)
        x, z, dy = x_ref[:, columns], z_ref[:, columns], dy_ref[:, columns]
        skip = wide_row_ref[1:2, columns]
        collapse = (((1,), (1,)), ((), ()))
        both = dy.astype(HALF).astype(FLOAT) * (y_ref[:, columns] - skip * x)
        both = both - dosed_ref[:, columns].astype(FLOAT) * z
        heads_of = expand[:, columns]
        direct = direct + lax.dot_general(
            x * z, heads_of, collapse, precision=HIGH, preferred_element_type=FLOAT
        )
        balance = balance + lax.dot_general(
            both, heads_of, collapse, precision=HIGH, preferred_element_type=FLOAT
        )
        grad_conv = (dose_ref[:, columns] * z + skip * dy) * slope_ref[:, columns]
        grad_in = conv_rows_back(
            grad_conv,
            pre_other_ref[:, columns],
            conv_input_ref,
            columns,
            marks_ref,
            conv_input_grad_ref,
        )
        put(grad_pre_other_ref, grad_in.astype(HALF), start)
    for start in range(0, 2 * states, LANES):
        columns = slice(start, start + LANES)
        grad_in = conv_rows_back(
            bc_grad_ref[:, columns] * bc_slope_ref[:, columns],
            pre_ref[:, state_at + start : state_at + start + LANES],
            conv_state_ref,
            columns,
            marks_ref,
            conv_state_grad_ref,
        )
        put(grad_pre_ref, grad_in.astype(HALF), state_at + start)
    crossing = summed_rows(balance, True)
    grad_step = (direct + rate * crossing) * sigmoid(shifted_pre)
    put(grad_pre_other_ref, grad_step.astype(HALF), step_at)
    for start in range(step_at + LANES, grad_pre_other_ref.shape[1], LANES):
        put(grad_pre_other_ref, jnp.zeros((length, LANES), HALF), start)
    step_grad_ref[0:1, :] = jnp.sum(grad_step, axis=0, keepdims=True)
    step_grad_ref[1:2, :] = rate * jnp.sum(sizes * crossing, axis=0, keepdims=True)


def ordered_copy(shape):
    return pltpu.VMEM(shape if groups() > 1 else (8, LANES), FLOAT)


def whole_call(kernel, inputs, results, scratch, name):
    whole = pl.BlockSpec(memory_space=pltpu.VMEM)
    place = pl.BlockSpec(memory_space=pltpu.SMEM)
    return pl.pallas_call(
        kernel,
        in_specs=[whole] * (inputs - 1) + [place],
        out_shape=results,
        scratch_shapes=scratch,
        compiler_params=pltpu.CompilerParams(vmem_limit_bytes=VMEM_BYTES),
        name=name,
    )


def mixer_forward(pre, heads, wide, mixer):
    length = pre[0].shape[0]
    kernel = functools.partial(mixer_forward_kernel, heads, groups())
    states = mixer[1].shape[1] // 2
    return whole_call(
        kernel,
        2 + len(mixer),
        (
            jax.ShapeDtypeStruct((length, wide), FLOAT),
            jax.ShapeDtypeStruct((length, wide), HALF),
            jax.ShapeDtypeStruct((length, 1), FLOAT),
        ),
        [
            ordered_copy(pre[0].shape),
            ordered_copy(pre[1].shape),
            pltpu.VMEM((length, wide), FLOAT),
            pltpu.VMEM((length, wide), HALF),
            pltpu.VMEM((length, states), HALF),
            pltpu.VMEM((length, states), HALF),
        ],
        "mixer_forward",
    )(*pre, *mixer)


def mixer_backward(pre, y, grad, sides, heads, mixer):
    length, wide = y.shape
    kernel = functools.partial(mixer_backward_kernel, heads, groups(), DI)
    double = mixer[1].shape[1]
    square = pltpu.VMEM((length, wide), FLOAT)
    return whole_call(
        kernel,
        5 + len(mixer),
        (
            jax.ShapeDtypeStruct(pre[0].shape, HALF),
            jax.ShapeDtypeStruct(pre[1].shape, HALF),
            jax.ShapeDtypeStruct((2, wide), FLOAT),
            jax.ShapeDtypeStruct((4, wide), FLOAT),
            jax.ShapeDtypeStruct((4, double), FLOAT),
            jax.ShapeDtypeStruct((2, LANES), FLOAT),
        ),
        [
            ordered_copy(pre[0].shape),
            ordered_copy(pre[1].shape),
            ordered_copy(y.shape),
            ordered_copy(sides.shape),
            square,
            pltpu.VMEM((length, wide), HALF),
            square,
            square,
            square,
            square,
            pltpu.VMEM((length, double), HALF),
            pltpu.VMEM((length, double), FLOAT),
            pltpu.VMEM((length, double), FLOAT),
        ],
        "mixer_backward",
    )(*pre, y, grad, sides, *mixer)


def to_blocks(per_chunk):
    parts = [None] * groups()
    for chunk, part in zip(chunks(), per_chunk):
        rows_each = part.shape[0] // len(chunk)
        for at, back in enumerate(chunk):
            parts[back] = part[at * rows_each : (at + 1) * rows_each]
    return parts


def through_experts(block, tables, expert, beside):
    blocks = spread(block)
    tokens = [joined([blocks[back] for back in chunk]) for chunk in chunks()]
    arrived = [to_experts(project(table, each)) for table, each in zip(tables, tokens)]
    answers = [to_experts(expert(index, rows)) for index, rows in enumerate(arrived)]
    made = [beside(*each) for each in zip(range(len(tokens)), tokens, answers)]
    return to_blocks(made), arrived, tokens


def line_product(values, weights):
    return sum(project_back(value, weight) for value, weight in zip(values, weights)).astype(HALF)


def line_blocks(whole):
    return [block_of(whole, back) for back in range(groups())]


def expert_forward(rows, experts):
    gate_e = project(rows, experts[0])
    lift_e = project(rows, experts[1])
    act_e = (jax.nn.silu(gate_e) * lift_e).astype(HALF)
    return (gate_e, lift_e, act_e), project(act_e, experts[2]).astype(HALF)


def expert_backward(rows, kept, experts):
    gate_e, lift_e, _ = kept
    grad_act = project_back(rows, experts[2])
    grad_gate = (grad_act * lift_e * silu_slope(gate_e)).astype(HALF)
    grad_lift = (grad_act * jax.nn.silu(gate_e)).astype(HALF)
    back = project_back(grad_gate, experts[0]) + project_back(grad_lift, experts[1])
    return (grad_gate, grad_lift), back.astype(HALF)


def shared_forward(tokens, shared):
    hidden = shared.shape[1] // 3
    gate_s = project(tokens, shared[:, :hidden])
    lift_s = project(tokens, shared[:, hidden : 2 * hidden])
    return gate_s, lift_s, (jax.nn.silu(gate_s) * lift_s).astype(HALF)


def shared_backward(tokens, kept, shared):
    hidden = shared.shape[1] // 3
    gate_s, lift_s, _ = kept
    grad_act = project(tokens, shared[:, 2 * hidden :])
    grad_gate = (grad_act * lift_s * silu_slope(gate_s)).astype(HALF)
    grad_lift = (grad_act * jax.nn.silu(gate_s)).astype(HALF)
    part = project_back(grad_gate, shared[:, :hidden])
    part = part + project_back(grad_lift, shared[:, hidden : 2 * hidden])
    return (grad_gate, grad_lift), part


def home_part(table, result, act_s, shared):
    hidden = shared.shape[1] // 3
    return (outer(table, result) + project_back(act_s, shared[:, 2 * hidden :])).astype(HALF)


def weight_sums(rows_in, rows_out, kept, grads, tokens_in, tokens_out, kept_s, grads_s):
    rows_in, rows_out = joined(rows_in), joined(rows_out)
    experts = (
        outer(rows_in, joined([each[0] for each in grads])).astype(HALF),
        outer(rows_in, joined([each[1] for each in grads])).astype(HALF),
        outer(joined([each[2] for each in kept]), rows_out).astype(HALF),
    )
    tokens_in, tokens_out = joined(tokens_in), joined(tokens_out)
    pairs = [joined([each[at] for each in grads_s]) for at in range(2)]
    act_s = joined([each[2] for each in kept_s])
    shared = ((tokens_in, *pairs), (tokens_out, *two_halves(act_s)))
    return experts, [(*each, swapped(half_to_give(*each))) for each in shared]


def middle_backward(grad_normed, grad_out, middle, mixed, norm_mid):
    _, pull_mid = jax.vjp(rms_norm, middle, norm_mid)
    grad_middle, grad_norm_mid = pull_mid(grad_normed)
    grad_middle = grad_middle + grad_out
    along = jnp.sum(grad_middle * mixed, axis=1, keepdims=True)
    return grad_middle, along, grad_norm_mid


def two_halves(values):
    middle = values.shape[1] // 2
    return values[:, :middle], values[:, middle:]


def half_to_give(left, first_right, second_right):
    first = lax.axis_index("section") == 0
    return outer(left, jnp.where(first, second_right, first_right)).astype(HALF)


def half_to_keep(left, first_right, second_right, given):
    first = lax.axis_index("section") == 0
    keep = outer(left, jnp.where(first, first_right, second_right))
    return (keep + given.astype(FLOAT)).astype(HALF)


def row_pieces(values):
    n_row = lax.axis_size("row")
    rows = values.shape[0] // n_row
    index = [lax.rem(lax.axis_index("row") + ahead, n_row) * rows for ahead in range(n_row)]
    return [lax.dynamic_slice_in_dim(values, at, rows, axis=0) for at in index]


def row_total(pieces, meanwhile=()):
    received = [shifted(piece, "row", ahead) for ahead, piece in enumerate(pieces) if ahead]
    received = after(received, meanwhile)
    total = sum([piece.astype(FLOAT) for piece in received], pieces[0].astype(FLOAT))
    return total.astype(HALF)


def col_sum(values):
    n_col = lax.axis_size("col")
    if groups() == 1:
        return lax.psum(values, "col")
    rows = values.shape[0] // n_col
    total = None
    for ahead in range(n_col):
        index = lax.rem(lax.axis_index("col") + ahead, n_col)
        part = lax.dynamic_slice_in_dim(values, index * rows, rows, axis=0)
        part = shifted(part, "col", ahead).astype(FLOAT)
        total = part if total is None else total + part
    total = total.astype(values.dtype)
    return in_order([shifted(total, "col", back) for back in range(n_col)], "col")


def flat(parts):
    return jnp.concatenate([part.reshape(-1) for part in parts])


def unflat(vector, shapes):
    result, start = [], 0
    for shape in shapes:
        size = 1
        for entry in shape:
            size *= entry
        result.append(vector[start : start + size].reshape(shape))
        start += size
    return result


def widened(value, columns):
    return jnp.pad(value, ((0, 0), (0, columns - value.shape[1])))


def shards(
    tokens,
    cotangent,
    doc_lengths,
    routes,
    gates,
    norm_in,
    proj_gate,
    proj_input,
    proj_state,
    proj_step,
    step_bias,
    decay_log,
    skip_gain,
    conv_input,
    conv_state,
    gate_norm,
    proj_output,
    norm_mid,
    expert_gate,
    expert_up,
    expert_down,
    shared_gate,
    shared_up,
    shared_down,
):
    section_now = lax.axis_index("section")
    first = section_now == 0
    row_now = lax.axis_index("row")
    n_row, n_col = lax.axis_size("row"), lax.axis_size("col")
    count = tokens.shape[1]
    top = routes.shape[3]
    capacity = count * top * 4 // (3 * n_row * n_col)
    width = tokens.shape[2]
    heads = step_bias.shape[1]
    inner = gate_norm.shape[1]
    state = conv_state.shape[2]
    wide = -(-inner // LANES) * LANES
    layers = range(2)

    def pair(own, other):
        return (jnp.where(first, own, other), jnp.where(first, other, own))

    tokens_now = lax.dynamic_index_in_dim(tokens, section_now, 0, keepdims=False)
    grad_now = lax.dynamic_index_in_dim(cotangent, section_now, 0, keepdims=False)
    wide_tokens = joined(spread(tokens_now.astype(HALF)))

    halves = (
        jnp.concatenate([widened(proj_gate[0], wide), proj_state[0]], axis=1),
        jnp.concatenate([widened(proj_input[0], wide), widened(proj_step[0], state)], axis=1),
    )
    keep, give = jnp.where(first, *halves), jnp.where(first, *halves[::-1])
    mine = pair(keep, swapped(give))

    def both_halves(half):
        whole = lax.all_gather(half, ("section", "row"), axis=0, tiled=True)
        return whole.reshape(2, n_row * half.shape[0], half.shape[1])

    proj = [both_halves(mine[0])]

    def both_layers(weight):
        whole = lax.all_gather(weight, ("section", "row"), axis=0, tiled=True)
        return whole.reshape(2, n_row * weight.shape[0], weight.shape[1])

    proj_out = both_layers(widened(proj_output[0], wide))
    gate_all = lax.all_gather(expert_gate[0, 0], "section")
    up_all = lax.all_gather(expert_up[0, 0], "section")
    down_all = lax.all_gather(expert_down[0, 0], "section")
    shared = both_layers(jnp.concatenate([shared_gate[0], shared_up[0], shared_down[0]], axis=1))
    experts = [(gate_all[s], up_all[s], down_all[s]) for s in layers]

    small_in = (
        norm_in[0],
        norm_mid[0],
        widened(conv_input[0], wide),
        conv_state[0],
        widened(jnp.concatenate([step_bias, decay_log], axis=0), LANES),
        widened(jnp.concatenate([gate_norm, jnp.repeat(skip_gain, HEAD, axis=1)], axis=0), wide),
    )
    vector = flat(small_in)
    small_all = [unflat(part, [v.shape for v in small_in]) for part in pair(vector, swapped(vector))]
    norm_ins = [part[0] for part in small_all]
    norm_mids = [part[1] for part in small_all]

    meta = jnp.concatenate([routes.astype(FLOAT), gates], axis=3)[0]
    keep = lax.dynamic_index_in_dim(meta, section_now, 0, keepdims=False)
    give = lax.dynamic_index_in_dim(meta, 1 - section_now, 0, keepdims=False)
    meta = jnp.concatenate(pair(keep, swapped(give)), axis=1)

    lengths = lax.dynamic_slice(
        doc_lengths, (section_now, row_now, 0), (1, 1, doc_lengths.shape[2])
    )
    labels = local_docs(lengths[0, 0], row_now, n_col * count)
    marks = [labels.astype(FLOAT)]
    for back in range(1, conv_input.shape[1]):
        prior = jnp.pad(labels, (back, 0), constant_values=-1)[:-back]
        marks.append((prior == labels).astype(FLOAT))
    marks = jnp.stack(marks, axis=1)
    label_row = labels.astype(FLOAT)[None]
    place = turn()
    mixers = [
        (conv_in, conv_st, step_row, wide_row, marks, label_row, place)
        for _, _, conv_in, conv_st, step_row, wide_row in small_all
    ]

    def mix_in(s, wide_in):
        pre = [project(wide_in, half) for half in proj[s]]
        return pre, *mixer_forward(pre, heads, wide, mixers[s])

    def mix_out(s, resid, scaled, total_part, meanwhile, gathered):
        parts = line_blocks(line_product([scaled], [proj_out[s]]))
        mixed = gathered(parts, meanwhile)
        total = gathered_sum(line_blocks(total_part), meanwhile)
        rr = lax.rsqrt(total / DI + EPS)
        return resid + mixed * rr, mixed, rr

    wide_in_0 = rms_norm(wide_tokens.astype(FLOAT), norm_ins[0]).astype(HALF)
    pre_0, y_0, scaled_0, total_0 = mix_in(0, wide_in_0)
    grad_blocks = spread(after(grad_now.astype(HALF), wide_in_0))
    tables = route_tables(spread(after(meta, scaled_0)), top, capacity, 2)
    plain = [[table[0] for table in tables[s]] for s in layers]
    scaling = [[table[1] for table in tables[s]] for s in layers]
    proj.append(both_halves(after(mine[1], scaled_0)))
    middle_0, mixed_0, rr_0 = mix_out(
        0, tokens_now, scaled_0, total_0, tables, gathered_sum_in_turn
    )
    kept_0, kept_s_0 = {}, {}

    def expert_0(index, rows):
        kept_0[index], answer = expert_forward(rows, experts[0])
        return answer

    def beside_0(index, block, result):
        kept_s_0[index] = shared_forward(block, shared[0])
        return home_part(scaling[0][index], result, kept_s_0[index][2], shared[0])

    parts, rows_0, mids_0 = through_experts(
        rms_norm(middle_0, norm_mids[0]).astype(HALF), plain[0], expert_0, beside_0
    )
    out_0 = middle_0 + gathered_sum(parts)

    wide_in_1 = joined(spread(rms_norm(out_0, norm_ins[1]).astype(HALF)))
    grad_blocks = after(grad_blocks, out_0)
    grad_tokens = [joined([grad_blocks[back] for back in chunk]) for chunk in chunks()]
    grad_rows_1 = [
        to_experts(project(table, block)) for table, block in zip(scaling[1], grad_tokens)
    ]
    pre_1, y_1, scaled_1, total_1 = mix_in(1, wide_in_1)
    scaled_1 = after(scaled_1, *grad_rows_1)
    middle_1, mixed_1, rr_1 = mix_out(1, out_0, scaled_1, total_1, (), gathered_sum)

    kept_1, kept_s_1, grads_1, grads_s_1, answers_1 = {}, {}, {}, {}, {}

    def expert_1(index, rows):
        kept_1[index], answers_1[index] = expert_forward(rows, experts[1])
        grads_1[index], back = expert_backward(grad_rows_1[index], kept_1[index], experts[1])
        return back

    def beside_1(index, block, result):
        kept_s_1[index] = shared_forward(block, shared[1])
        grads_s_1[index], part = shared_backward(grad_tokens[index], kept_s_1[index], shared[1])
        return (part + outer(plain[1][index], result)).astype(HALF)

    parts, rows_1, mids_1 = through_experts(
        rms_norm(middle_1, norm_mids[1]).astype(HALF), plain[1], expert_1, beside_1
    )
    order = range(len(chunks()))
    answers = [to_experts(after(answers_1[index], parts[-1])) for index in order]

    def listed(kept):
        return [kept[index] for index in order]

    def mixer_back(s, grad_middle, along, rr, saved, meanwhile, last):
        wide_in, pre, y, scaled = saved
        wide_mix = joined(spread(grad_middle.astype(HALF), meanwhile))
        sides = joined(spread(jnp.concatenate([rr, along], axis=1), meanwhile))
        grad_scaled = project(wide_mix, proj_out[s])
        *grad_pre, wide_grads, grad_conv_input, grad_conv_state, step_grads = mixer_backward(
            pre, y, grad_scaled, sides, heads, mixers[s]
        )
        ends = [part[:, :wide] for part in grad_pre]
        if last:
            given = half_to_give(wide_in, *ends)
            whole = line_product([after(part, given) for part in grad_pre], proj[s])
        else:
            whole = line_product(grad_pre, proj[s])
            given = half_to_give(after(wide_in, whole), *ends)
        grad_proj = (after(wide_in, whole), *ends, swapped(given))
        mix_rr = (after(wide_mix, whole, given) * sides[:, :1]).astype(HALF)
        halves = two_halves(scaled)
        given_out = half_to_give(mix_rr, *halves)
        grad_proj_out = (mix_rr, *halves, swapped(given_out))
        tail = jnp.concatenate([grad_pre[0][:, wide:], grad_pre[1][:, wide : wide + LANES]], axis=1)
        grad_tail = outer(after(wide_in, given_out), tail).astype(HALF)
        rest = (grad_conv_state, grad_conv_input, wide_grads, step_grads)
        if last:
            grad_proj = half_to_keep(*grad_proj)
            meanwhile = row_pieces(grad_proj)
            grad_proj_out = half_to_keep(*after(grad_proj_out, meanwhile))
            grad_proj = row_total(meanwhile)
            meanwhile = (meanwhile, grad_proj_out, grad_tail)
        else:
            meanwhile = (given, given_out, grad_tail)
        grad_in = gathered_sum(line_blocks(whole), meanwhile)
        return wide_mix, grad_in, grad_proj, grad_proj_out, grad_tail, rest

    def resid_back(resid, norm, grad_normed, grad_middle):
        _, pull_in = jax.vjp(rms_norm, resid, norm)
        grad_resid, grad_norm = pull_in(grad_normed)
        return grad_resid + grad_middle, grad_norm

    def row_sums(value):
        return lax.psum_scatter(value, "row", scatter_dimension=0, tiled=True)

    def own_layer(first_value, second_value, *ahead):
        keep = jnp.where(first, first_value, second_value)
        give = jnp.where(first, second_value, first_value).astype(HALF)
        return keep.astype(FLOAT) + after(swapped(give), *ahead).astype(FLOAT)

    grad_middle, along, grad_norm_mid_1 = middle_backward(
        gathered_sum(parts), grad_now, middle_1, mixed_1, norm_mids[1]
    )
    expert_grads_1, shared_grads_1 = weight_sums(
        rows_1,
        grad_rows_1,
        listed(kept_1),
        listed(grads_1),
        mids_1,
        grad_tokens,
        listed(kept_s_1),
        listed(grads_s_1),
    )
    wide_mix, grad_in, grad_proj_1, grad_out_1, grad_tail_1, rest_1 = mixer_back(
        1,
        grad_middle,
        along,
        rr_1,
        (wide_in_1, pre_1, y_1, scaled_1),
        expert_grads_1,
        False,
    )
    grad_1, grad_norm_in_1 = resid_back(out_0, norm_ins[1], grad_in, grad_middle)
    home = [
        home_part(scaling[1][index], answers[index], kept_s_1[index][2], shared[1])
        for index in order
    ]
    home = [after(part, wide_mix) for part in home]
    out_1 = middle_1 + gathered_sum(to_blocks(home), grad_in)
    sums_1 = [half_to_keep(*after(made, grad_1)) for made in shared_grads_1]

    grads_0, grads_s_0 = {}, {}

    def expert_back_0(index, rows):
        grads_0[index], back = expert_backward(rows, kept_0[index], experts[0])
        return back

    def beside_back_0(index, block, result):
        grads_s_0[index], part = shared_backward(block, kept_s_0[index], shared[0])
        return (part + outer(plain[0][index], result)).astype(HALF)

    parts, grad_rows_0, grad_tokens_0 = through_experts(
        grad_1.astype(HALF), scaling[0], expert_back_0, beside_back_0
    )
    sums_1 = [
        *sums_1,
        half_to_keep(*after(grad_out_1, parts)),
        half_to_keep(*after(grad_proj_1, parts)),
    ]
    grad_middle, along, grad_norm_mid_0 = middle_backward(
        gathered_sum(parts, sums_1), grad_1, middle_0, mixed_0, norm_mids[0]
    )
    sums_1 = [row_sums(value) for value in sums_1]
    expert_grads_0, shared_grads_0 = weight_sums(
        rows_0,
        grad_rows_0,
        listed(kept_0),
        listed(grads_0),
        mids_0,
        grad_tokens_0,
        listed(kept_s_0),
        listed(grads_s_0),
    )
    wide_mix, grad_in, grad_proj_0, grad_out_0, grad_tail_0, rest_0 = mixer_back(
        0,
        grad_middle,
        along,
        rr_0,
        (wide_in_0, pre_0, y_0, scaled_0),
        expert_grads_0,
        True,
    )
    sums_0 = [row_sums(half_to_keep(*after(made, wide_mix))) for made in shared_grads_0]
    grad_0, grad_norm_in_0 = resid_back(tokens_now, norm_ins[0], grad_in, grad_middle)
    sums_0 = [*sums_0, row_sums(grad_out_0), grad_proj_0]
    expert_out = [
        own_layer(a, b, grad_out_0) for a, b in zip(expert_grads_0, expert_grads_1)
    ]

    def own_halves(first_value, second_value):
        keep = jnp.where(first, first_value, second_value)
        give = jnp.where(first, second_value, first_value)
        return pair(keep, swapped(give))

    tail = row_total(row_pieces(own_layer(grad_tail_0, grad_tail_1).astype(HALF)))
    state_grad = col_sum(tail[:, :state])
    grad_shared, grad_down, grad_out, grad_ends = [own_halves(a, b) for a, b in zip(sums_0, sums_1)]
    grad_out, grad_down = [jnp.concatenate(both, axis=1) for both in (grad_out, grad_down)]

    smalls = (
        (grad_norm_in_0, grad_norm_mid_0, *rest_0),
        (grad_norm_in_1, grad_norm_mid_1, *rest_1),
    )
    shapes = [part.shape for part in smalls[0]]
    vector = own_layer(flat(smalls[0]), flat(smalls[1]))
    lines = [shifted(vector[None], "row", back) for back in range(n_row)]
    vector = jnp.sum(in_order(lines, "row"), axis=0)
    common = 2 * width + conv_state.shape[1] * state
    if groups() > 1:
        lines = [shifted(vector[None, :common], "col", back) for back in range(n_col)]
        shared_sum = jnp.sum(in_order(lines, "col"), axis=0)
    else:
        shared_sum = lax.psum(vector[:common], "col")
    (
        out_norm_in,
        out_norm_mid,
        out_conv_state,
        out_conv_input,
        out_wide,
        out_step,
    ) = unflat(jnp.concatenate([shared_sum, vector[common:]]), shapes)

    def per_micro(first_value, second_value, *ahead):
        keep = jnp.where(first, first_value, second_value)
        other = swapped(jnp.where(first, second_value, first_value).astype(HALF))
        return jnp.stack(pair(keep, after(other, *ahead).astype(FLOAT)))[None]

    def out(value):
        return value.astype(FLOAT)[None]

    return (
        per_micro(out_0, out_1, grad_out_0),
        per_micro(grad_0, grad_1),
        out_norm_in[None],
        out(grad_ends[0][:, :inner]),
        out(grad_ends[1][:, :inner]),
        out(state_grad),
        out(tail[:, state : state + heads]),
        out_step[:1, :heads],
        out_step[1:, :heads],
        jnp.sum(out_wide[1, :inner].reshape(heads, HEAD), axis=1)[None],
        out_conv_input[None, :, :inner],
        out_conv_state[None],
        out_wide[:1, :inner],
        out(grad_out[:, :inner]),
        out_norm_mid[None],
        expert_out[0][None, None],
        expert_out[1][None, None],
        expert_out[2][None, None],
        out(grad_shared[0]),
        out(grad_shared[1]),
        out(grad_down),
    )


def solution(mesh):
    in_specs = (
        P(None, ("row", "col"), None),
        P(None, ("row", "col"), None),
        P(),
        P("section", None, ("row", "col"), None),
        P("section", None, ("row", "col"), None),
        P("section", None),
        P("section", "row", "col"),
        P("section", "row", "col"),
        P("section", "row", None),
        P("section", "row", "col"),
        P("section", "col"),
        P("section", "col"),
        P("section", "col"),
        P("section", None, "col"),
        P("section", None, None),
        P("section", "col"),
        P("section", "row", "col"),
        P("section", None),
        P("section", ("row", "col"), None, None),
        P("section", ("row", "col"), None, None),
        P("section", ("row", "col"), None, None),
        P("section", "row", "col"),
        P("section", "row", "col"),
        P("section", "row", "col"),
    )
    out_specs = (
        P("section", None, ("row", "col"), None),
        P("section", None, ("row", "col"), None),
        P("section", None),
        P("section", "row", "col"),
        P("section", "row", "col"),
        P("section", "row", None),
        P("section", "row", "col"),
        P("section", "col"),
        P("section", "col"),
        P("section", "col"),
        P("section", None, "col"),
        P("section", None, None),
        P("section", "col"),
        P("section", "row", "col"),
        P("section", None),
        P("section", ("row", "col"), None, None),
        P("section", ("row", "col"), None, None),
        P("section", ("row", "col"), None, None),
        P("section", "row", "col"),
        P("section", "row", "col"),
        P("section", "row", "col"),
    )
    return jax.shard_map(shards, mesh=mesh, in_specs=in_specs, out_specs=out_specs, check_vma=False)
```

```python
import functools

import jax
import jax.numpy as jnp
from jax import lax
from jax.experimental import pallas as pl
from jax.experimental.pallas import tpu as pltpu
from jax.sharding import PartitionSpec as P

DI = 3072
HEAD = 64
LANES = 128
CHUNK = 256
VMEM_BYTES = 48 * 2**20

EPS = 1e-05
HIGH = lax.Precision.HIGHEST
FLOAT = jnp.float32
HALF = jnp.bfloat16


def shifted(block, axis, distance):
    count = lax.axis_size(axis)
    if distance % count == 0:
        return block
    return lax.ppermute(block, axis, [(i, (i + distance) % count) for i in range(count)])


def swapped(block):
    return lax.ppermute(block, "section", [(0, 1), (1, 0)])


def after(value, *others):
    return lax.optimization_barrier((value, *others))[0]


def rms_norm(value, gain):
    return value * lax.rsqrt(jnp.mean(value * value, axis=-1, keepdims=True) + EPS) * gain


def local_docs(lengths, row_now, length):
    bounds = jnp.cumsum(lengths)[:-1]
    place = jnp.arange(length, dtype=jnp.int32)
    inner = jnp.sum((place[:, None] >= bounds[None, :]).astype(jnp.int32), axis=1)
    return inner + row_now * lengths.shape[0]


def project(left, right):
    return jnp.dot(left, right, preferred_element_type=FLOAT)


def project_back(left, right):
    return lax.dot_general(left, right, (((1,), (1,)), ((), ())), preferred_element_type=FLOAT)


def outer(left, right):
    return lax.dot_general(left, right, (((0,), (0,)), ((), ())), preferred_element_type=FLOAT)


def silu_slope(value):
    sigma = jax.nn.sigmoid(value)
    return sigma * (1.0 + value * (1.0 - sigma))


def groups():
    count = lax.axis_size("col")
    return count if count <= 4 else 1


def chunks():
    return [tuple(range(groups()))]


def spread(block, meanwhile=()):
    if groups() == 1:
        return [lax.all_gather(block, "col", axis=0, tiled=True)]
    received = [shifted(block, "col", back) for back in range(1, groups())]
    return [block, *after(received, meanwhile)]


def joined(blocks):
    return blocks[0] if len(blocks) == 1 else jnp.concatenate(blocks, axis=0)


def in_order(blocks, axis):
    count = len(blocks)
    if count == 1:
        return blocks[0]
    rows = blocks[0].shape[0]
    line = jnp.concatenate(blocks[::-1] + blocks[:0:-1], axis=0)
    start = (count - 1 - lax.axis_index(axis)) * rows
    return lax.dynamic_slice_in_dim(line, start, count * rows, axis=0)


def sent_home(parts):
    return [shifted(part, "col", -back) for back, part in enumerate(parts) if back]


def gathered_sum(parts, meanwhile=()):
    if len(parts) == 1:
        return lax.psum_scatter(parts[0], "col", scatter_dimension=0, tiled=True).astype(FLOAT)
    return total_of(parts[0], after(sent_home(parts), meanwhile))


def total_of(own, received):
    return sum([part.astype(FLOAT) for part in received], own.astype(FLOAT))


def block_of(values, back):
    rows = values.shape[0] // groups()
    return values[back * rows : (back + 1) * rows]


def turn():
    place = lax.axis_index("col") if groups() > 1 else jnp.int32(0)
    return place.astype(jnp.int32).reshape(1)


def route_tables(blocks, top, capacity, layers):
    n_row, n_col = lax.axis_size("row"), lax.axis_size("col")
    experts = (jnp.arange(n_row) * n_col + lax.axis_index("col")).astype(FLOAT)
    tables = [[] for _ in range(layers)]
    for chunk in chunks():
        now = joined([blocks[back] for back in chunk])
        count = now.shape[0]
        slots = len(chunk) * (n_col // groups()) * capacity
        now = now.reshape(count, layers, 2, top).transpose(1, 2, 3, 0)
        match = now[:, None, 0] == experts[None, :, None, None]
        hit = jnp.any(match, axis=2)
        weight = jnp.sum(jnp.where(match, now[:, None, 1], 0.0), axis=2)
        order = jnp.arange(count, dtype=jnp.int32)
        triangle = (order[:, None] <= order[None, :]).astype(HALF)
        place = project(hit.astype(HALF).reshape(-1, count), triangle).reshape(hit.shape)
        slot = jnp.arange(1, slots + 1, dtype=jnp.int32).astype(FLOAT)
        chosen = (place[:, :, None, :] == slot[:, None]) & hit[:, :, None, :]
        shape = (layers, n_row * slots, count)
        plain = chosen.astype(HALF).reshape(shape)
        scaled = jnp.where(chosen, weight[:, :, None, :], 0.0).astype(HALF).reshape(shape)
        for s in range(layers):
            tables[s].append((plain[s], scaled[s]))
    return tables


def to_experts(rows):
    return lax.all_to_all(rows.astype(HALF), "row", split_axis=0, concat_axis=0, tiled=True)


def summed_rows(values, reverse):
    step = min(values.shape[0], CHUNK)
    count = values.shape[0] // step
    place = lax.broadcasted_iota(jnp.int32, (step, step), 0)
    other = lax.broadcasted_iota(jnp.int32, (step, step), 1)
    before = (place <= other) if reverse else (place >= other)
    triangle = before.astype(FLOAT)
    carry = jnp.zeros((1, values.shape[1]), FLOAT)
    parts = [None] * count
    for index in reversed(range(count)) if reverse else range(count):
        part = values[index * step : (index + 1) * step]
        run = jnp.dot(triangle, part, precision=HIGH, preferred_element_type=FLOAT) + carry
        carry = run[:1] if reverse else run[step - 1 :]
        parts[index] = run
    return parts[0] if count == 1 else jnp.concatenate(parts, axis=0)


def head_columns(rows, columns, head_width):
    head = lax.broadcasted_iota(jnp.int32, (rows, columns), 0) * head_width
    column = lax.broadcasted_iota(jnp.int32, (rows, columns), 1)
    return ((column >= head) & (column < head + head_width)).astype(FLOAT)


def sigmoid(value):
    return 1.0 / (1.0 + jnp.exp(-value))


def step_sizes(step_pre, step_row_ref):
    shifted_pre = step_pre + step_row_ref[0:1, :]
    sizes = jnp.maximum(shifted_pre, 0.0) + jnp.log1p(jnp.exp(-jnp.abs(shifted_pre)))
    return shifted_pre, sizes, -jnp.exp(step_row_ref[1:2, :])


def conv_rows(values, weight_ref, columns, marks_ref):
    width = weight_ref.shape[0]
    result = values * weight_ref[width - 1 : width, columns]
    for back in range(1, width):
        moved = pltpu.roll(values, back, 0) * marks_ref[:, back : back + 1]
        result = result + moved * weight_ref[width - 1 - back : width - back, columns]
    return result


def conv_rows_back(grad, values, weight_ref, columns, marks_ref, weight_grad_ref):
    width = weight_ref.shape[0]
    rows = values.shape[0]
    result = grad * weight_ref[width - 1 : width, columns]
    weight_grad_ref[width - 1 : width, columns] = jnp.sum(grad * values, axis=0, keepdims=True)
    for back in range(1, width):
        kept = grad * marks_ref[:, back : back + 1]
        taps = jnp.sum(kept * pltpu.roll(values, back, 0), axis=0, keepdims=True)
        weight_grad_ref[width - 1 - back : width - back, columns] = taps
        moved = pltpu.roll(kept, rows - back, 0)
        result = result + moved * weight_ref[width - 1 - back : width - back, columns]
    return result


def copy_in_order(source_ref, target_ref, place_ref, parts):
    if parts == 1:
        return source_ref
    rows = source_ref.shape[0] // parts
    for index in range(parts):
        target_ref[index * rows : (index + 1) * rows, :] = source_ref[
            block_rows(index, rows, place_ref, parts), :
        ]
    return target_ref


def block_rows(index, rows, place_ref, parts):
    if parts == 1:
        return slice(0, rows)
    back = lax.rem(place_ref[0] - index + parts, parts)
    return pl.ds(pl.multiple_of(back * rows, rows), rows)


def mixer_forward_kernel(
    heads,
    parts,
    pre_in_ref,
    pre_other_in_ref,
    conv_input_ref,
    conv_state_ref,
    step_row_ref,
    wide_row_ref,
    marks_ref,
    labels_ref,
    place_ref,
    y_ref,
    scaled_ref,
    total_ref,
    pre_ref,
    pre_other_ref,
    x_ref,
    dosed_ref,
    keys_ref,
    queries_ref,
):
    length, wide = y_ref.shape
    states = conv_state_ref.shape[1] // 2
    state_at, step_at = wide, wide
    head_width = HEAD
    pre_ref = copy_in_order(pre_in_ref, pre_ref, place_ref, parts)
    pre_other_ref = copy_in_order(pre_other_in_ref, pre_other_ref, place_ref, parts)
    _, sizes, rate = step_sizes(pre_other_ref[:, step_at : step_at + LANES], step_row_ref)
    running = summed_rows(sizes * rate, False)
    running_t = running.T
    expand = head_columns(LANES, wide, head_width)
    for start in range(0, wide, LANES):
        columns = slice(start, start + LANES)
        conv = conv_rows(
            pre_other_ref[:, columns], conv_input_ref, columns, marks_ref
        )
        x = conv * sigmoid(conv)
        x_ref[:, columns] = x
        dose = jnp.dot(sizes, expand[:, columns], precision=HIGH, preferred_element_type=FLOAT)
        dosed_ref[:, columns] = (x * dose).astype(HALF)
    for part, target in ((0, keys_ref), (1, queries_ref)):
        columns = slice(part * states, (part + 1) * states)
        conv = conv_rows(
            pre_ref[:, state_at + part * states : state_at + (part + 1) * states],
            conv_state_ref,
            columns,
            marks_ref,
        )
        target[...] = (conv * sigmoid(conv)).astype(HALF)
    block = min(length, CHUNK)
    place = lax.broadcasted_iota(jnp.int32, (block, block), 0)
    other = lax.broadcasted_iota(jnp.int32, (block, block), 1)
    for late in range(length // block):
        rows = slice(late * block, (late + 1) * block)
        for early in range(late + 1):
            past = slice(early * block, (early + 1) * block)
            same = marks_ref[rows, 0:1] == labels_ref[:, past]
            if late == early:
                same = same & (place >= other)
            mask = jnp.where(same, 0.0, -1e30)
            scores = lax.dot_general(
                queries_ref[rows, :],
                keys_ref[past, :],
                (((1,), (1,)), ((), ())),
                preferred_element_type=FLOAT,
            )
            for head in range(heads):
                columns = slice(head * head_width, (head + 1) * head_width)
                spread_log = running[rows, head : head + 1] - running_t[head : head + 1, past]
                mixing = (jnp.exp(spread_log + mask) * scores).astype(HALF)
                inner = jnp.dot(mixing, dosed_ref[past, columns], preferred_element_type=FLOAT)
                if early == 0:
                    y_ref[rows, columns] = inner
                else:
                    y_ref[rows, columns] += inner
    total = jnp.zeros((length, 1), FLOAT)
    for start in range(0, wide, LANES):
        columns = slice(start, start + LANES)
        y = y_ref[:, columns]
        if heads * head_width < start + LANES:
            lane = lax.broadcasted_iota(jnp.int32, y.shape, 1) + start
            y = jnp.where(lane < heads * head_width, y, 0.0)
        y = y + wide_row_ref[1:2, columns] * x_ref[:, columns]
        gate = pre_ref[:, columns]
        gated = y * gate * sigmoid(gate)
        y_ref[:, columns] = y
        scaled = (gated * wide_row_ref[0:1, columns]).astype(HALF)
        each = length // parts
        for index in range(parts):
            block_at = block_rows(index, each, place_ref, parts)
            scaled_ref[block_at, columns] = scaled[index * each : (index + 1) * each]
        total = total + jnp.sum(gated * gated, axis=1, keepdims=True)
    each = length // parts
    for index in range(parts):
        block_at = block_rows(index, each, place_ref, parts)
        total_ref[block_at, :] = total[index * each : (index + 1) * each]


def mixer_backward_kernel(
    heads,
    parts,
    inner_all,
    pre_in_ref,
    pre_other_in_ref,
    y_ref,
    grad_in_ref,
    sides_in_ref,
    conv_input_ref,
    conv_state_ref,
    step_row_ref,
    wide_row_ref,
    marks_ref,
    labels_ref,
    place_ref,
    grad_pre_ref,
    grad_pre_other_ref,
    wide_grad_ref,
    conv_input_grad_ref,
    conv_state_grad_ref,
    step_grad_ref,
    pre_ref,
    pre_other_ref,
    grad_ref,
    sides_ref,
    x_ref,
    dosed_ref,
    dose_ref,
    slope_ref,
    dy_ref,
    z_ref,
    bc_ref,
    bc_slope_ref,
    bc_grad_ref,
):
    length, wide = y_ref.shape
    states = conv_state_ref.shape[1] // 2
    state_at, step_at = wide, wide
    head_width = HEAD
    each = length // parts
    pre_ref = copy_in_order(pre_in_ref, pre_ref, place_ref, parts)
    pre_other_ref = copy_in_order(pre_other_in_ref, pre_other_ref, place_ref, parts)
    grad_ref = copy_in_order(grad_in_ref, grad_ref, place_ref, parts)
    sides_ref = copy_in_order(sides_in_ref, sides_ref, place_ref, parts)

    def put(target_ref, value, start):
        for index in range(parts):
            target_ref[block_rows(index, each, place_ref, parts), start : start + LANES] = value[
                index * each : (index + 1) * each
            ]

    shifted_pre, sizes, rate = step_sizes(pre_other_ref[:, step_at : step_at + LANES], step_row_ref)
    running = summed_rows(sizes * rate, False)
    running_t = running.T
    expand = head_columns(LANES, wide, head_width)
    rr = sides_ref[:, 0:1]
    pull = rr * rr * rr * sides_ref[:, 1:2] * (1.0 / inner_all)
    for start in range(0, wide, LANES):
        columns = slice(start, start + LANES)
        gate = pre_ref[:, columns]
        y = y_ref[:, columns]
        grad = grad_ref[:, columns]
        gain = wide_row_ref[0:1, columns]
        sigma = sigmoid(gate)
        silu = gate * sigma
        gated = y * silu
        normed = gated * rr
        wide_grad_ref[0:1, columns] = jnp.sum(grad * normed, axis=0, keepdims=True)
        grad_gated = rr * gain * grad - gated * pull
        slope = sigma * (1.0 + gate * (1.0 - sigma))
        put(grad_pre_ref, (grad_gated * y * slope).astype(HALF), start)
        dy = grad_gated * silu
        dy_ref[:, columns] = dy
        conv = conv_rows(
            pre_other_ref[:, columns], conv_input_ref, columns, marks_ref
        )
        sigma = sigmoid(conv)
        x = conv * sigma
        x_ref[:, columns] = x
        slope_ref[:, columns] = sigma * (1.0 + conv * (1.0 - sigma))
        dose = jnp.dot(sizes, expand[:, columns], precision=HIGH, preferred_element_type=FLOAT)
        dose_ref[:, columns] = dose
        dosed_ref[:, columns] = (x * dose).astype(HALF)
        wide_grad_ref[1:2, columns] = jnp.sum(dy * x, axis=0, keepdims=True)
    for start in range(0, 2 * states, LANES):
        columns = slice(start, start + LANES)
        conv = conv_rows(
            pre_ref[:, state_at + start : state_at + start + LANES],
            conv_state_ref,
            columns,
            marks_ref,
        )
        sigma = sigmoid(conv)
        bc_ref[:, columns] = (conv * sigma).astype(HALF)
        bc_slope_ref[:, columns] = sigma * (1.0 + conv * (1.0 - sigma))
    block = min(length, CHUNK)
    place = lax.broadcasted_iota(jnp.int32, (block, block), 0)
    other = lax.broadcasted_iota(jnp.int32, (block, block), 1)
    z_ref[...] = jnp.zeros(z_ref.shape, FLOAT)
    bc_grad_ref[...] = jnp.zeros(bc_grad_ref.shape, FLOAT)
    for late in range(length // block):
        rows = slice(late * block, (late + 1) * block)
        for early in range(late + 1):
            past = slice(early * block, (early + 1) * block)
            same = marks_ref[past, 0:1] == labels_ref[:, rows]
            if late == early:
                same = same & (place <= other)
            mask = jnp.where(same, 0.0, -1e30)
            keys = bc_ref[past, :states]
            queries = bc_ref[rows, states:]
            scores = lax.dot_general(
                keys, queries, (((1,), (1,)), ((), ())), preferred_element_type=FLOAT
            )
            mixed = jnp.zeros((block, block), FLOAT)
            for head in range(heads):
                columns = slice(head * head_width, (head + 1) * head_width)
                spread_log = running_t[head : head + 1, rows] - running[past, head : head + 1]
                decay = jnp.exp(spread_log + mask)
                mixing = (decay * scores).astype(HALF)
                dy = dy_ref[rows, columns].astype(HALF)
                z_ref[past, columns] += jnp.dot(mixing, dy, preferred_element_type=FLOAT)
                along = lax.dot_general(
                    dosed_ref[past, columns],
                    dy,
                    (((1,), (1,)), ((), ())),
                    preferred_element_type=FLOAT,
                )
                mixed = mixed + decay * along
            mixed = mixed.astype(HALF)
            bc_grad_ref[past, :states] += jnp.dot(mixed, queries, preferred_element_type=FLOAT)
            bc_grad_ref[rows, states:] += lax.dot_general(
                mixed, keys, (((0,), (0,)), ((), ())), preferred_element_type=FLOAT
            )
    direct = jnp.zeros((length, LANES), FLOAT)
    balance = jnp.zeros((length, LANES), FLOAT)
    for start in range(0, wide, LANES):
        columns = slice(start, start + LANES)
        x, z, dy = x_ref[:, columns], z_ref[:, columns], dy_ref[:, columns]
        skip = wide_row_ref[1:2, columns]
        collapse = (((1,), (1,)), ((), ()))
        both = dy.astype(HALF).astype(FLOAT) * (y_ref[:, columns] - skip * x)
        both = both - dosed_ref[:, columns].astype(FLOAT) * z
        heads_of = expand[:, columns]
        direct = direct + lax.dot_general(
            x * z, heads_of, collapse, precision=HIGH, preferred_element_type=FLOAT
        )
        balance = balance + lax.dot_general(
            both, heads_of, collapse, precision=HIGH, preferred_element_type=FLOAT
        )
        grad_conv = (dose_ref[:, columns] * z + skip * dy) * slope_ref[:, columns]
        grad_in = conv_rows_back(
            grad_conv,
            pre_other_ref[:, columns],
            conv_input_ref,
            columns,
            marks_ref,
            conv_input_grad_ref,
        )
        put(grad_pre_other_ref, grad_in.astype(HALF), start)
    for start in range(0, 2 * states, LANES):
        columns = slice(start, start + LANES)
        grad_in = conv_rows_back(
            bc_grad_ref[:, columns] * bc_slope_ref[:, columns],
            pre_ref[:, state_at + start : state_at + start + LANES],
            conv_state_ref,
            columns,
            marks_ref,
            conv_state_grad_ref,
        )
        put(grad_pre_ref, grad_in.astype(HALF), state_at + start)
    crossing = summed_rows(balance, True)
    grad_step = (direct + rate * crossing) * sigmoid(shifted_pre)
    put(grad_pre_other_ref, grad_step.astype(HALF), step_at)
    for start in range(step_at + LANES, grad_pre_other_ref.shape[1], LANES):
        put(grad_pre_other_ref, jnp.zeros((length, LANES), HALF), start)
    step_grad_ref[0:1, :] = jnp.sum(grad_step, axis=0, keepdims=True)
    step_grad_ref[1:2, :] = rate * jnp.sum(sizes * crossing, axis=0, keepdims=True)


def ordered_copy(shape):
    return pltpu.VMEM(shape if groups() > 1 else (8, LANES), FLOAT)


def whole_call(kernel, inputs, results, scratch, name):
    whole = pl.BlockSpec(memory_space=pltpu.VMEM)
    place = pl.BlockSpec(memory_space=pltpu.SMEM)
    return pl.pallas_call(
        kernel,
        in_specs=[whole] * (inputs - 1) + [place],
        out_shape=results,
        scratch_shapes=scratch,
        compiler_params=pltpu.CompilerParams(vmem_limit_bytes=VMEM_BYTES),
        name=name,
    )


def mixer_forward(pre, heads, wide, mixer):
    length = pre[0].shape[0]
    kernel = functools.partial(mixer_forward_kernel, heads, groups())
    states = mixer[1].shape[1] // 2
    return whole_call(
        kernel,
        2 + len(mixer),
        (
            jax.ShapeDtypeStruct((length, wide), FLOAT),
            jax.ShapeDtypeStruct((length, wide), HALF),
            jax.ShapeDtypeStruct((length, 1), FLOAT),
        ),
        [
            ordered_copy(pre[0].shape),
            ordered_copy(pre[1].shape),
            pltpu.VMEM((length, wide), FLOAT),
            pltpu.VMEM((length, wide), HALF),
            pltpu.VMEM((length, states), HALF),
            pltpu.VMEM((length, states), HALF),
        ],
        "mixer_forward",
    )(*pre, *mixer)


def mixer_backward(pre, y, grad, sides, heads, mixer):
    length, wide = y.shape
    kernel = functools.partial(mixer_backward_kernel, heads, groups(), DI)
    double = mixer[1].shape[1]
    square = pltpu.VMEM((length, wide), FLOAT)
    return whole_call(
        kernel,
        5 + len(mixer),
        (
            jax.ShapeDtypeStruct(pre[0].shape, HALF),
            jax.ShapeDtypeStruct(pre[1].shape, HALF),
            jax.ShapeDtypeStruct((2, wide), FLOAT),
            jax.ShapeDtypeStruct((4, wide), FLOAT),
            jax.ShapeDtypeStruct((4, double), FLOAT),
            jax.ShapeDtypeStruct((2, LANES), FLOAT),
        ),
        [
            ordered_copy(pre[0].shape),
            ordered_copy(pre[1].shape),
            ordered_copy(y.shape),
            ordered_copy(sides.shape),
            square,
            pltpu.VMEM((length, wide), HALF),
            square,
            square,
            square,
            square,
            pltpu.VMEM((length, double), HALF),
            pltpu.VMEM((length, double), FLOAT),
            pltpu.VMEM((length, double), FLOAT),
        ],
        "mixer_backward",
    )(*pre, y, grad, sides, *mixer)


def to_blocks(per_chunk):
    parts = [None] * groups()
    for chunk, part in zip(chunks(), per_chunk):
        rows_each = part.shape[0] // len(chunk)
        for at, back in enumerate(chunk):
            parts[back] = part[at * rows_each : (at + 1) * rows_each]
    return parts


def through_experts(block, tables, expert, beside, aside=None):
    blocks = spread(block)
    tokens = [joined([blocks[back] for back in chunk]) for chunk in chunks()]
    arrived = [to_experts(project(table, each)) for table, each in zip(tables, tokens)]
    answers = [expert(index, rows) for index, rows in enumerate(arrived)]
    if aside is not None:
        answers = after(answers, aside(tokens))
    answers = [to_experts(rows) for rows in answers]
    made = [beside(*each) for each in zip(range(len(tokens)), tokens, answers)]
    return to_blocks(made), arrived, tokens, answers


def line_product(values, weights):
    return sum(project_back(value, weight) for value, weight in zip(values, weights)).astype(HALF)


def line_blocks(whole):
    return [block_of(whole, back) for back in range(groups())]


def expert_forward(rows, experts):
    gate_e = project(rows, experts[0])
    lift_e = project(rows, experts[1])
    act_e = (jax.nn.silu(gate_e) * lift_e).astype(HALF)
    return (gate_e, lift_e, act_e), project(act_e, experts[2]).astype(HALF)


def expert_backward(rows, kept, experts):
    gate_e, lift_e, _ = kept
    grad_act = project_back(rows, experts[2])
    grad_gate = (grad_act * lift_e * silu_slope(gate_e)).astype(HALF)
    grad_lift = (grad_act * jax.nn.silu(gate_e)).astype(HALF)
    back = project_back(grad_gate, experts[0]) + project_back(grad_lift, experts[1])
    return (grad_gate, grad_lift), back.astype(HALF)


def shared_forward(tokens, shared):
    hidden = shared.shape[1] // 3
    gate_s = project(tokens, shared[:, :hidden])
    lift_s = project(tokens, shared[:, hidden : 2 * hidden])
    return gate_s, lift_s, (jax.nn.silu(gate_s) * lift_s).astype(HALF)


def shared_backward(tokens, kept, shared):
    hidden = shared.shape[1] // 3
    gate_s, lift_s, _ = kept
    grad_act = project(tokens, shared[:, 2 * hidden :])
    grad_gate = (grad_act * lift_s * silu_slope(gate_s)).astype(HALF)
    grad_lift = (grad_act * jax.nn.silu(gate_s)).astype(HALF)
    part = project_back(grad_gate, shared[:, :hidden])
    part = part + project_back(grad_lift, shared[:, hidden : 2 * hidden])
    return (grad_gate, grad_lift), part


def home_part(table, result, act_s, shared):
    hidden = shared.shape[1] // 3
    return (outer(table, result) + project_back(act_s, shared[:, 2 * hidden :])).astype(HALF)


def weight_sums(rows_in, rows_out, kept, grads, tokens_in, tokens_out, kept_s, grads_s):
    rows_in, rows_out = joined(rows_in), joined(rows_out)
    experts = (
        outer(rows_in, joined([each[0] for each in grads])).astype(HALF),
        outer(rows_in, joined([each[1] for each in grads])).astype(HALF),
        outer(joined([each[2] for each in kept]), rows_out).astype(HALF),
    )
    tokens_in, tokens_out = joined(tokens_in), joined(tokens_out)
    pairs = [joined([each[at] for each in grads_s]) for at in range(2)]
    act_s = joined([each[2] for each in kept_s])
    shared = ((tokens_in, *pairs), (tokens_out, *two_halves(act_s)))
    return experts, [(*each, swapped(half_to_give(*each))) for each in shared]


def middle_backward(grad_normed, grad_out, middle, mixed, norm_mid):
    _, pull_mid = jax.vjp(rms_norm, middle, norm_mid)
    grad_middle, grad_norm_mid = pull_mid(grad_normed)
    grad_middle = grad_middle + grad_out
    along = jnp.sum(grad_middle * mixed, axis=1, keepdims=True)
    return grad_middle, along, grad_norm_mid


def two_halves(values):
    middle = values.shape[1] // 2
    return values[:, :middle], values[:, middle:]


def half_to_give(left, first_right, second_right):
    first = lax.axis_index("section") == 0
    return outer(left, jnp.where(first, second_right, first_right)).astype(HALF)


def half_to_keep(left, first_right, second_right, given):
    first = lax.axis_index("section") == 0
    keep = outer(left, jnp.where(first, first_right, second_right))
    return (keep + given.astype(FLOAT)).astype(HALF)


def row_pieces(values, axis="row"):
    count = lax.axis_size(axis)
    rows = values.shape[0] // count
    index = [lax.rem(lax.axis_index(axis) + ahead, count) * rows for ahead in range(count)]
    return [lax.dynamic_slice_in_dim(values, at, rows, axis=0) for at in index]


def row_received(pieces, axis="row"):
    return [shifted(piece, axis, ahead) for ahead, piece in enumerate(pieces) if ahead]


def flat(parts):
    return jnp.concatenate([part.reshape(-1) for part in parts])


def unflat(vector, shapes):
    result, start = [], 0
    for shape in shapes:
        size = 1
        for entry in shape:
            size *= entry
        result.append(vector[start : start + size].reshape(shape))
        start += size
    return result


def widened(value, columns):
    return jnp.pad(value, ((0, 0), (0, columns - value.shape[1])))


def shards(
    tokens,
    cotangent,
    doc_lengths,
    routes,
    gates,
    norm_in,
    proj_gate,
    proj_input,
    proj_state,
    proj_step,
    step_bias,
    decay_log,
    skip_gain,
    conv_input,
    conv_state,
    gate_norm,
    proj_output,
    norm_mid,
    expert_gate,
    expert_up,
    expert_down,
    shared_gate,
    shared_up,
    shared_down,
):
    section_now = lax.axis_index("section")
    first = section_now == 0
    row_now = lax.axis_index("row")
    n_row, n_col = lax.axis_size("row"), lax.axis_size("col")
    count = tokens.shape[1]
    top = routes.shape[3]
    capacity = count * top * 4 // (3 * n_row * n_col)
    width = tokens.shape[2]
    heads = step_bias.shape[1]
    inner = gate_norm.shape[1]
    state = conv_state.shape[2]
    wide = -(-inner // LANES) * LANES
    layers = range(2)

    def pair(own, other):
        return (jnp.where(first, own, other), jnp.where(first, other, own))

    tokens_now = lax.dynamic_index_in_dim(tokens, section_now, 0, keepdims=False)
    grad_now = lax.dynamic_index_in_dim(cotangent, section_now, 0, keepdims=False)
    wide_tokens = joined(spread(tokens_now.astype(HALF)))

    halves = (
        jnp.concatenate([widened(proj_gate[0], wide), proj_state[0]], axis=1),
        jnp.concatenate([widened(proj_input[0], wide), widened(proj_step[0], state)], axis=1),
    )
    keep, give = jnp.where(first, *halves), jnp.where(first, *halves[::-1])
    mine = pair(keep, swapped(give))

    def both_halves(half):
        whole = lax.all_gather(half, ("section", "row"), axis=0, tiled=True)
        return whole.reshape(2, n_row * half.shape[0], half.shape[1])

    proj = [both_halves(mine[0])]

    def both_layers(weight):
        whole = lax.all_gather(weight, ("section", "row"), axis=0, tiled=True)
        return whole.reshape(2, n_row * weight.shape[0], weight.shape[1])

    proj_out = both_layers(widened(proj_output[0], wide))
    gate_all = lax.all_gather(expert_gate[0, 0], "section")
    up_all = lax.all_gather(expert_up[0, 0], "section")
    down_all = lax.all_gather(expert_down[0, 0], "section")
    shared = both_layers(jnp.concatenate([shared_gate[0], shared_up[0], shared_down[0]], axis=1))
    experts = [(gate_all[s], up_all[s], down_all[s]) for s in layers]

    small_in = (
        norm_in[0],
        norm_mid[0],
        widened(conv_input[0], wide),
        conv_state[0],
        widened(jnp.concatenate([step_bias, decay_log], axis=0), LANES),
        widened(jnp.concatenate([gate_norm, jnp.repeat(skip_gain, HEAD, axis=1)], axis=0), wide),
    )
    vector = flat(small_in)
    small_all = [unflat(part, [v.shape for v in small_in]) for part in pair(vector, swapped(vector))]
    norm_ins = [part[0] for part in small_all]
    norm_mids = [part[1] for part in small_all]

    meta = jnp.concatenate([routes.astype(FLOAT), gates], axis=3)[0]
    keep = lax.dynamic_index_in_dim(meta, section_now, 0, keepdims=False)
    give = lax.dynamic_index_in_dim(meta, 1 - section_now, 0, keepdims=False)
    meta = jnp.concatenate(pair(keep, swapped(give)), axis=1)

    lengths = lax.dynamic_slice(
        doc_lengths, (section_now, row_now, 0), (1, 1, doc_lengths.shape[2])
    )
    labels = local_docs(lengths[0, 0], row_now, n_col * count)
    marks = [labels.astype(FLOAT)]
    for back in range(1, conv_input.shape[1]):
        prior = jnp.pad(labels, (back, 0), constant_values=-1)[:-back]
        marks.append((prior == labels).astype(FLOAT))
    marks = jnp.stack(marks, axis=1)
    label_row = labels.astype(FLOAT)[None]
    place = turn()
    mixers = [
        (conv_in, conv_st, step_row, wide_row, marks, label_row, place)
        for _, _, conv_in, conv_st, step_row, wide_row in small_all
    ]

    def mix_in(s, wide_in):
        pre = [project(wide_in, half) for half in proj[s]]
        return pre, *mixer_forward(pre, heads, wide, mixers[s])

    def mix_out(s, resid, scaled, total_part, meanwhile):
        total = gathered_sum(line_blocks(total_part))
        whole = after(line_product([scaled], [proj_out[s]]), total)
        mixed = gathered_sum(line_blocks(whole), meanwhile)
        rr = lax.rsqrt(total / DI + EPS)
        return resid + mixed * rr, mixed, rr

    wide_in_0 = rms_norm(wide_tokens.astype(FLOAT), norm_ins[0]).astype(HALF)
    pre_0, y_0, scaled_0, total_0 = mix_in(0, wide_in_0)
    tables = route_tables(spread(after(meta, scaled_0)), top, capacity, 2)
    plain = [[table[0] for table in tables[s]] for s in layers]
    scaling = [[table[1] for table in tables[s]] for s in layers]
    middle_0, mixed_0, rr_0 = mix_out(0, tokens_now, scaled_0, total_0, tables)
    kept_0, kept_s_0, grad_blocks = {}, {}, []

    def expert_0(index, rows):
        kept_0[index], answer = expert_forward(rows, experts[0])
        return answer

    def beside_0(index, block, result):
        kept_s_0[index] = shared_forward(block, shared[0])
        return home_part(scaling[0][index], result, kept_s_0[index][2], shared[0])

    def aside_0(blocks):
        grad_blocks.extend(spread(after(grad_now.astype(HALF), blocks)))
        return grad_blocks

    parts, rows_0, mids_0, answers = through_experts(
        rms_norm(middle_0, norm_mids[0]).astype(HALF), plain[0], expert_0, beside_0, aside_0
    )
    proj.append(both_halves(after(mine[1], answers)))
    out_0 = middle_0 + gathered_sum(parts)

    wide_in_1 = joined(spread(rms_norm(out_0, norm_ins[1]).astype(HALF)))
    grad_blocks = after(grad_blocks, out_0)
    grad_tokens = [joined([grad_blocks[back] for back in chunk]) for chunk in chunks()]
    grad_rows_1 = [
        to_experts(project(table, block)) for table, block in zip(scaling[1], grad_tokens)
    ]
    pre_1, y_1, scaled_1, total_1 = mix_in(1, wide_in_1)
    scaled_1 = after(scaled_1, *grad_rows_1)
    middle_1, mixed_1, rr_1 = mix_out(1, out_0, scaled_1, total_1, ())

    kept_1, kept_s_1, grads_1, grads_s_1, answers_1 = {}, {}, {}, {}, {}

    def expert_1(index, rows):
        kept_1[index], answers_1[index] = expert_forward(rows, experts[1])
        grads_1[index], back = expert_backward(grad_rows_1[index], kept_1[index], experts[1])
        return back

    def beside_1(index, block, result):
        kept_s_1[index] = shared_forward(block, shared[1])
        grads_s_1[index], part = shared_backward(grad_tokens[index], kept_s_1[index], shared[1])
        return (part + outer(plain[1][index], result)).astype(HALF)

    parts, rows_1, mids_1, _ = through_experts(
        rms_norm(middle_1, norm_mids[1]).astype(HALF), plain[1], expert_1, beside_1
    )
    order = range(len(chunks()))
    answers = [to_experts(after(answers_1[index], parts[-1])) for index in order]

    def listed(kept):
        return [kept[index] for index in order]

    def mixer_back(s, grad_middle, along, rr, saved, meanwhile):
        wide_in, pre, y, scaled = saved
        sides = joined(spread(jnp.concatenate([rr, along], axis=1), meanwhile))
        wide_mix = joined(spread(grad_middle.astype(HALF), meanwhile))
        grad_scaled = project(wide_mix, proj_out[s])
        *grad_pre, wide_grads, grad_conv_input, grad_conv_state, step_grads = mixer_backward(
            pre, y, grad_scaled, sides, heads, mixers[s]
        )
        ends = [part[:, :wide] for part in grad_pre]
        tail = jnp.concatenate([grad_pre[0][:, wide:], grad_pre[1][:, wide : wide + LANES]], axis=1)
        mix_rr = (wide_mix * sides[:, :1]).astype(HALF)
        rest = (grad_conv_state, grad_conv_input, wide_grads, step_grads)
        return wide_mix, grad_pre, (wide_in, *ends), (mix_rr, *two_halves(scaled)), tail, rest

    def resid_back(resid, norm, grad_normed, grad_middle):
        _, pull_in = jax.vjp(rms_norm, resid, norm)
        grad_resid, grad_norm = pull_in(grad_normed)
        return grad_resid + grad_middle, grad_norm

    def row_sums(value):
        return lax.psum_scatter(value, "row", scatter_dimension=0, tiled=True)

    def own_layer(first_value, second_value):
        keep = jnp.where(first, first_value, second_value)
        give = jnp.where(first, second_value, first_value).astype(HALF)
        return keep.astype(FLOAT), swapped(give)

    grad_middle, along, grad_norm_mid_1 = middle_backward(
        gathered_sum(parts, answers), grad_now, middle_1, mixed_1, norm_mids[1]
    )
    expert_grads_1, shared_grads_1 = weight_sums(
        rows_1,
        grad_rows_1,
        listed(kept_1),
        listed(grads_1),
        mids_1,
        grad_tokens,
        listed(kept_s_1),
        listed(grads_s_1),
    )
    home = [
        home_part(scaling[1][index], answers[index], kept_s_1[index][2], shared[1])
        for index in order
    ]
    _, grad_pre, to_proj, to_out, tail, rest_1 = mixer_back(
        1,
        grad_middle,
        along,
        rr_1,
        (wide_in_1, pre_1, y_1, scaled_1),
        (expert_grads_1, home),
    )
    whole = line_product(grad_pre, proj[1])
    given = half_to_give(*after(to_proj, whole))
    given_out = half_to_give(*after(to_out, given))
    grad_proj_1 = (*to_proj, swapped(given))
    grad_out_1 = (*to_out, swapped(given_out))
    grad_tail_1 = outer(after(wide_in_1, given_out), tail).astype(HALF)
    grad_in = gathered_sum(line_blocks(whole), (given, given_out, grad_tail_1))
    grad_1, grad_norm_in_1 = resid_back(out_0, norm_ins[1], grad_in, grad_middle)
    sums_1 = [half_to_keep(*after(made, grad_1)) for made in shared_grads_1]

    grads_0, grads_s_0, out_parts = {}, {}, []

    def expert_back_0(index, rows):
        grads_0[index], back = expert_backward(rows, kept_0[index], experts[0])
        return back

    def beside_back_0(index, block, result):
        grads_s_0[index], part = shared_backward(block, kept_s_0[index], shared[0])
        return (part + outer(plain[0][index], result)).astype(HALF)

    def aside_back_0(blocks):
        sums_1.extend(half_to_keep(*after(made, blocks)) for made in (grad_out_1, grad_proj_1))
        out_parts.extend(to_blocks(after(home, blocks)))
        if groups() > 1:
            out_parts[1:] = after(sent_home(out_parts), sums_1)
        return out_parts[1:]

    parts, grad_rows_0, grad_tokens_0, _ = through_experts(
        grad_1.astype(HALF), scaling[0], expert_back_0, beside_back_0, aside_back_0
    )
    if groups() > 1:
        out_1 = middle_1 + total_of(out_parts[0], out_parts[1:])
    else:
        out_1 = middle_1 + gathered_sum(out_parts)
    sums_1 = [row_sums(value) for value in sums_1]
    grad_middle, along, grad_norm_mid_0 = middle_backward(
        gathered_sum(parts, out_1), grad_1, middle_0, mixed_0, norm_mids[0]
    )
    expert_grads_0, shared_grads_0 = weight_sums(
        rows_0,
        grad_rows_0,
        listed(kept_0),
        listed(grads_0),
        mids_0,
        grad_tokens_0,
        listed(kept_s_0),
        listed(grads_s_0),
    )
    expert_out = [own_layer(a, b) for a, b in zip(expert_grads_0, expert_grads_1)]
    wide_mix, grad_pre, to_proj, to_out, tail, rest_0 = mixer_back(
        0,
        grad_middle,
        along,
        rr_0,
        (wide_in_0, pre_0, y_0, scaled_0),
        [part[0] for part in expert_out],
    )
    sums_0 = [row_sums(half_to_keep(*after(made, wide_mix))) for made in shared_grads_0]

    given = half_to_give(*to_proj)
    whole = line_product(after(grad_pre, given), proj[0])
    given_out = half_to_give(*after(to_out, whole))
    grad_tail_0 = outer(after(wide_in_0, given_out), tail).astype(HALF)
    tail_keep, tail_other = own_layer(grad_tail_0, grad_tail_1)
    wide_x = wide_tokens.astype(FLOAT)
    wide_r = lax.rsqrt(jnp.mean(wide_x * wide_x, axis=1, keepdims=True) + EPS)
    grad_norm_in_0 = jnp.sum(whole.astype(FLOAT) * wide_x * wide_r, axis=0)
    smalls = (
        (grad_norm_in_0, grad_norm_mid_0, *rest_0),
        (grad_norm_in_1, grad_norm_mid_1, *rest_1),
    )
    shapes = [part.shape for part in smalls[0]]
    small_keep, small_other = own_layer(flat(smalls[0]), flat(smalls[1]))
    line_parts = line_blocks(whole)
    if groups() > 1:
        line_received = sent_home(line_parts)
    to_proj, to_out, tail_own, small_own = after(
        (
            (*to_proj, swapped(given)),
            (*to_out, swapped(given_out)),
            (tail_keep, tail_other),
            (small_keep, small_other),
        ),
        grad_tail_0,
    )
    proj_pieces = row_pieces(half_to_keep(*to_proj))
    out_pieces = row_pieces(half_to_keep(*to_out))
    tail_pieces = row_pieces((tail_own[0] + tail_own[1].astype(FLOAT)).astype(HALF))
    vector = small_own[0] + small_own[1].astype(FLOAT)
    proj_received, out_received, tail_received = [
        row_received(pieces) for pieces in (proj_pieces, out_pieces, tail_pieces)
    ]
    lines = [shifted(vector[None], "row", back) for back in range(n_row)]
    expert_out = [keep + other.astype(FLOAT) for keep, other in after(expert_out, proj_pieces)]
    if groups() > 1:
        line_received, proj_received, out_received, tail_received, lines, sums_0 = after(
            (line_received, proj_received, out_received, tail_received, lines, sums_0), expert_out
        )
        grad_in = total_of(line_parts[0], line_received)
    else:
        grad_in = gathered_sum(line_parts)
    grad_proj_0 = total_of(proj_pieces[0], proj_received).astype(HALF)
    grad_out_0 = total_of(out_pieces[0], out_received).astype(HALF)
    tail = total_of(tail_pieces[0], tail_received).astype(HALF)
    vector = jnp.sum(in_order(lines, "row"), axis=0)
    grad_0, _ = resid_back(tokens_now, norm_ins[0], grad_in, grad_middle)
    sums_0 = [*sums_0, grad_out_0, grad_proj_0]

    def own_halves(first_value, second_value):
        keep = jnp.where(first, first_value, second_value)
        give = jnp.where(first, second_value, first_value)
        return keep, swapped(give)

    def per_micro(first_value, second_value):
        keep = jnp.where(first, first_value, second_value)
        return keep, swapped(jnp.where(first, second_value, first_value).astype(HALF))

    halves = [own_halves(a, b) for a, b in zip(sums_0, sums_1)]
    outs, in_grads = per_micro(out_0, after(out_1, grad_in)), per_micro(grad_0, grad_1)
    common = 2 * width + conv_state.shape[1] * state
    state_grad = tail[:, :state]
    if groups() > 1:
        state_pieces = row_pieces(state_grad, "col")
        state_received = row_received(state_pieces, "col")
        lines = [shifted(vector[None, :common], "col", back) for back in range(n_col)]
        state_received, lines, halves, outs, in_grads = after(
            (state_received, lines, halves, outs, in_grads)
        )
        state_grad = total_of(state_pieces[0], state_received).astype(HALF)
        state_grad = in_order([shifted(state_grad, "col", back) for back in range(n_col)], "col")
        shared_sum = jnp.sum(in_order(lines, "col"), axis=0)
    else:
        state_grad = lax.psum(state_grad, "col")
        shared_sum = lax.psum(vector[:common], "col")
    halves = [pair(*half) for half in halves]
    grad_shared, grad_down, grad_out, grad_ends = halves
    grad_out, grad_down = [jnp.concatenate(both, axis=1) for both in (grad_out, grad_down)]
    (
        out_norm_in,
        out_norm_mid,
        out_conv_state,
        out_conv_input,
        out_wide,
        out_step,
    ) = unflat(jnp.concatenate([shared_sum, vector[common:]]), shapes)

    def stacked(keep, other):
        return jnp.stack(pair(keep, other.astype(FLOAT)))[None]

    def out(value):
        return value.astype(FLOAT)[None]

    return (
        stacked(*outs),
        stacked(*in_grads),
        out_norm_in[None],
        out(grad_ends[0][:, :inner]),
        out(grad_ends[1][:, :inner]),
        out(state_grad),
        out(tail[:, state : state + heads]),
        out_step[:1, :heads],
        out_step[1:, :heads],
        jnp.sum(out_wide[1, :inner].reshape(heads, HEAD), axis=1)[None],
        out_conv_input[None, :, :inner],
        out_conv_state[None],
        out_wide[:1, :inner],
        out(grad_out[:, :inner]),
        out_norm_mid[None],
        expert_out[0][None, None],
        expert_out[1][None, None],
        expert_out[2][None, None],
        out(grad_shared[0]),
        out(grad_shared[1]),
        out(grad_down),
    )


def solution(mesh):
    in_specs = (
        P(None, ("row", "col"), None),
        P(None, ("row", "col"), None),
        P(),
        P("section", None, ("row", "col"), None),
        P("section", None, ("row", "col"), None),
        P("section", None),
        P("section", "row", "col"),
        P("section", "row", "col"),
        P("section", "row", None),
        P("section", "row", "col"),
        P("section", "col"),
        P("section", "col"),
        P("section", "col"),
        P("section", None, "col"),
        P("section", None, None),
        P("section", "col"),
        P("section", "row", "col"),
        P("section", None),
        P("section", ("row", "col"), None, None),
        P("section", ("row", "col"), None, None),
        P("section", ("row", "col"), None, None),
        P("section", "row", "col"),
        P("section", "row", "col"),
        P("section", "row", "col"),
    )
    out_specs = (
        P("section", None, ("row", "col"), None),
        P("section", None, ("row", "col"), None),
        P("section", None),
        P("section", "row", "col"),
        P("section", "row", "col"),
        P("section", "row", None),
        P("section", "row", "col"),
        P("section", "col"),
        P("section", "col"),
        P("section", "col"),
        P("section", None, "col"),
        P("section", None, None),
        P("section", "col"),
        P("section", "row", "col"),
        P("section", None),
        P("section", ("row", "col"), None, None),
        P("section", ("row", "col"), None, None),
        P("section", ("row", "col"), None, None),
        P("section", "row", "col"),
        P("section", "row", "col"),
        P("section", "row", "col"),
    )
    return jax.shard_map(shards, mesh=mesh, in_specs=in_specs, out_specs=out_specs, check_vma=False)
```

```python
import functools

import jax
import jax.numpy as jnp
from jax import lax
from jax.experimental import pallas as pl
from jax.experimental.pallas import tpu as pltpu
from jax.sharding import PartitionSpec as P

DI = 3072
HEAD = 64
LANES = 128
CHUNK = 256
VMEM_BYTES = 48 * 2**20

EPS = 1e-05
HIGH = lax.Precision.HIGHEST
FLOAT = jnp.float32
HALF = jnp.bfloat16


def shifted(block, axis, distance):
    count = lax.axis_size(axis)
    if distance % count == 0:
        return block
    return lax.ppermute(block, axis, [(i, (i + distance) % count) for i in range(count)])


def swapped(block):
    return lax.ppermute(block, "section", [(0, 1), (1, 0)])


def after(value, *others):
    return lax.optimization_barrier((value, *others))[0]


def rms_norm(value, gain):
    return value * lax.rsqrt(jnp.mean(value * value, axis=-1, keepdims=True) + EPS) * gain


def local_docs(lengths, row_now, length):
    bounds = jnp.cumsum(lengths)[:-1]
    place = jnp.arange(length, dtype=jnp.int32)
    inner = jnp.sum((place[:, None] >= bounds[None, :]).astype(jnp.int32), axis=1)
    return inner + row_now * lengths.shape[0]


def project(left, right):
    return jnp.dot(left, right, preferred_element_type=FLOAT)


def project_back(left, right):
    return lax.dot_general(left, right, (((1,), (1,)), ((), ())), preferred_element_type=FLOAT)


def outer(left, right):
    return lax.dot_general(left, right, (((0,), (0,)), ((), ())), preferred_element_type=FLOAT)


def silu_slope(value):
    sigma = jax.nn.sigmoid(value)
    return sigma * (1.0 + value * (1.0 - sigma))


def spread(block):
    count = lax.axis_size("col")
    if count > 4:
        return lax.all_gather(block, "col", axis=0, tiled=True)
    return exchanged(jnp.tile(block, (count, 1)), "col")


def exchanged(rows, axis):
    return lax.all_to_all(rows, axis, split_axis=0, concat_axis=0, tiled=True)


def summed(rows, axis):
    count = lax.axis_size(axis)
    rows = rows.reshape(count, rows.shape[0] // count, rows.shape[1])
    return sum(rows[index].astype(FLOAT) for index in range(count))


def sent_home(rows):
    if lax.axis_size("col") > 4:
        return lax.psum_scatter(rows, "col", scatter_dimension=0, tiled=True)
    return exchanged(rows, "col")


def added_up(received):
    if lax.axis_size("col") > 4:
        return received.astype(FLOAT)
    return summed(received, "col")


def gathered_sum(rows, meanwhile=()):
    return added_up(after(sent_home(rows), meanwhile))


def as_halves(columns):
    high = lax.reduce_precision(columns, 8, 7)
    both = jnp.concatenate([high, columns - high], axis=1).astype(HALF)
    return jnp.pad(both, ((0, 0), (0, LANES - both.shape[1])))


def from_halves(tile, count):
    return tile[:, :count].astype(FLOAT) + tile[:, count : 2 * count].astype(FLOAT)


def route_tables(meta, top, capacity, layers):
    n_row, n_col = lax.axis_size("row"), lax.axis_size("col")
    experts = (jnp.arange(n_row) * n_col + lax.axis_index("col")).astype(FLOAT)
    count = meta.shape[0]
    slots = n_col * capacity
    meta = meta.reshape(count, layers, 2, top).transpose(1, 2, 3, 0)
    match = meta[:, None, 0] == experts[None, :, None, None]
    hit = jnp.any(match, axis=2)
    weight = jnp.sum(jnp.where(match, meta[:, None, 1], 0.0), axis=2)
    order = jnp.arange(count, dtype=jnp.int32)
    triangle = (order[:, None] <= order[None, :]).astype(HALF)
    place = project(hit.astype(HALF).reshape(-1, count), triangle).reshape(hit.shape)
    slot = jnp.arange(1, slots + 1, dtype=jnp.int32).astype(FLOAT)
    chosen = (place[:, :, None, :] == slot[:, None]) & hit[:, :, None, :]
    shape = (layers, n_row * slots, count)
    plain = chosen.astype(HALF).reshape(shape)
    scaled = jnp.where(chosen, weight[:, :, None, :], 0.0).astype(HALF).reshape(shape)
    return [(plain[s], scaled[s]) for s in range(layers)]


def to_experts(rows):
    return exchanged(rows.astype(HALF), "row")


def summed_rows(values, reverse):
    step = min(values.shape[0], CHUNK)
    count = values.shape[0] // step
    place = lax.broadcasted_iota(jnp.int32, (step, step), 0)
    other = lax.broadcasted_iota(jnp.int32, (step, step), 1)
    before = (place <= other) if reverse else (place >= other)
    triangle = before.astype(FLOAT)
    carry = jnp.zeros((1, values.shape[1]), FLOAT)
    parts = [None] * count
    for index in reversed(range(count)) if reverse else range(count):
        part = values[index * step : (index + 1) * step]
        run = jnp.dot(triangle, part, precision=HIGH, preferred_element_type=FLOAT) + carry
        carry = run[:1] if reverse else run[step - 1 :]
        parts[index] = run
    return parts[0] if count == 1 else jnp.concatenate(parts, axis=0)


def head_columns(rows, columns, head_width):
    head = lax.broadcasted_iota(jnp.int32, (rows, columns), 0) * head_width
    column = lax.broadcasted_iota(jnp.int32, (rows, columns), 1)
    return ((column >= head) & (column < head + head_width)).astype(FLOAT)


def sigmoid(value):
    return 1.0 / (1.0 + jnp.exp(-value))


def step_sizes(step_pre, step_row_ref):
    shifted_pre = step_pre + step_row_ref[0:1, :]
    sizes = jnp.maximum(shifted_pre, 0.0) + jnp.log1p(jnp.exp(-jnp.abs(shifted_pre)))
    return shifted_pre, sizes, -jnp.exp(step_row_ref[1:2, :])


def conv_rows(values, weight_ref, columns, marks_ref):
    width = weight_ref.shape[0]
    result = values * weight_ref[width - 1 : width, columns]
    for back in range(1, width):
        moved = pltpu.roll(values, back, 0) * marks_ref[:, back : back + 1]
        result = result + moved * weight_ref[width - 1 - back : width - back, columns]
    return result


def conv_rows_back(grad, values, weight_ref, columns, marks_ref, weight_grad_ref):
    width = weight_ref.shape[0]
    rows = values.shape[0]
    result = grad * weight_ref[width - 1 : width, columns]
    weight_grad_ref[width - 1 : width, columns] = jnp.sum(grad * values, axis=0, keepdims=True)
    for back in range(1, width):
        kept = grad * marks_ref[:, back : back + 1]
        taps = jnp.sum(kept * pltpu.roll(values, back, 0), axis=0, keepdims=True)
        weight_grad_ref[width - 1 - back : width - back, columns] = taps
        moved = pltpu.roll(kept, rows - back, 0)
        result = result + moved * weight_ref[width - 1 - back : width - back, columns]
    return result


def mixer_forward_kernel(
    heads,
    pre_ref,
    pre_other_ref,
    conv_input_ref,
    conv_state_ref,
    step_row_ref,
    wide_row_ref,
    marks_ref,
    labels_ref,
    y_ref,
    scaled_ref,
    total_ref,
    x_ref,
    dosed_ref,
    keys_ref,
    queries_ref,
):
    length, wide = y_ref.shape
    states = conv_state_ref.shape[1] // 2
    state_at, step_at = wide, wide
    head_width = HEAD
    _, sizes, rate = step_sizes(pre_other_ref[:, step_at : step_at + LANES], step_row_ref)
    running = summed_rows(sizes * rate, False)
    running_t = running.T
    expand = head_columns(LANES, wide, head_width)
    for start in range(0, wide, LANES):
        columns = slice(start, start + LANES)
        conv = conv_rows(
            pre_other_ref[:, columns], conv_input_ref, columns, marks_ref
        )
        x = conv * sigmoid(conv)
        x_ref[:, columns] = x
        dose = jnp.dot(sizes, expand[:, columns], precision=HIGH, preferred_element_type=FLOAT)
        dosed_ref[:, columns] = (x * dose).astype(HALF)
    for part, target in ((0, keys_ref), (1, queries_ref)):
        columns = slice(part * states, (part + 1) * states)
        conv = conv_rows(
            pre_ref[:, state_at + part * states : state_at + (part + 1) * states],
            conv_state_ref,
            columns,
            marks_ref,
        )
        target[...] = (conv * sigmoid(conv)).astype(HALF)
    block = min(length, CHUNK)
    place = lax.broadcasted_iota(jnp.int32, (block, block), 0)
    other = lax.broadcasted_iota(jnp.int32, (block, block), 1)
    for late in range(length // block):
        rows = slice(late * block, (late + 1) * block)
        for early in range(late + 1):
            past = slice(early * block, (early + 1) * block)
            same = marks_ref[rows, 0:1] == labels_ref[:, past]
            if late == early:
                same = same & (place >= other)
            mask = jnp.where(same, 0.0, -1e30)
            scores = lax.dot_general(
                queries_ref[rows, :],
                keys_ref[past, :],
                (((1,), (1,)), ((), ())),
                preferred_element_type=FLOAT,
            )
            for head in range(heads):
                columns = slice(head * head_width, (head + 1) * head_width)
                spread_log = running[rows, head : head + 1] - running_t[head : head + 1, past]
                mixing = (jnp.exp(spread_log + mask) * scores).astype(HALF)
                inner = jnp.dot(mixing, dosed_ref[past, columns], preferred_element_type=FLOAT)
                if early == 0:
                    y_ref[rows, columns] = inner
                else:
                    y_ref[rows, columns] += inner
    total = jnp.zeros((length, 1), FLOAT)
    for start in range(0, wide, LANES):
        columns = slice(start, start + LANES)
        y = y_ref[:, columns]
        if heads * head_width < start + LANES:
            lane = lax.broadcasted_iota(jnp.int32, y.shape, 1) + start
            y = jnp.where(lane < heads * head_width, y, 0.0)
        y = y + wide_row_ref[1:2, columns] * x_ref[:, columns]
        gate = pre_ref[:, columns]
        gated = y * gate * sigmoid(gate)
        y_ref[:, columns] = y
        scaled_ref[:, columns] = (gated * wide_row_ref[0:1, columns]).astype(HALF)
        total = total + jnp.sum(gated * gated, axis=1, keepdims=True)
    total_ref[...] = total


def mixer_backward_kernel(
    heads,
    inner_all,
    pre_ref,
    pre_other_ref,
    y_ref,
    grad_ref,
    sides_ref,
    conv_input_ref,
    conv_state_ref,
    step_row_ref,
    wide_row_ref,
    marks_ref,
    labels_ref,
    grad_pre_ref,
    grad_pre_other_ref,
    wide_grad_ref,
    conv_input_grad_ref,
    conv_state_grad_ref,
    step_grad_ref,
    x_ref,
    dosed_ref,
    dose_ref,
    slope_ref,
    dy_ref,
    z_ref,
    bc_ref,
    bc_slope_ref,
    bc_grad_ref,
):
    length, wide = y_ref.shape
    states = conv_state_ref.shape[1] // 2
    state_at, step_at = wide, wide
    head_width = HEAD
    shifted_pre, sizes, rate = step_sizes(pre_other_ref[:, step_at : step_at + LANES], step_row_ref)
    running = summed_rows(sizes * rate, False)
    running_t = running.T
    expand = head_columns(LANES, wide, head_width)
    rr = sides_ref[:, 0:1]
    pull = rr * rr * rr * sides_ref[:, 1:2] * (1.0 / inner_all)
    for start in range(0, wide, LANES):
        columns = slice(start, start + LANES)
        gate = pre_ref[:, columns]
        y = y_ref[:, columns]
        grad = grad_ref[:, columns]
        gain = wide_row_ref[0:1, columns]
        sigma = sigmoid(gate)
        silu = gate * sigma
        gated = y * silu
        normed = gated * rr
        wide_grad_ref[0:1, columns] = jnp.sum(grad * normed, axis=0, keepdims=True)
        grad_gated = rr * gain * grad - gated * pull
        slope = sigma * (1.0 + gate * (1.0 - sigma))
        grad_pre_ref[:, start : start + LANES] = (grad_gated * y * slope).astype(HALF)
        dy = grad_gated * silu
        dy_ref[:, columns] = dy
        conv = conv_rows(
            pre_other_ref[:, columns], conv_input_ref, columns, marks_ref
        )
        sigma = sigmoid(conv)
        x = conv * sigma
        x_ref[:, columns] = x
        slope_ref[:, columns] = sigma * (1.0 + conv * (1.0 - sigma))
        dose = jnp.dot(sizes, expand[:, columns], precision=HIGH, preferred_element_type=FLOAT)
        dose_ref[:, columns] = dose
        dosed_ref[:, columns] = (x * dose).astype(HALF)
        wide_grad_ref[1:2, columns] = jnp.sum(dy * x, axis=0, keepdims=True)
    for start in range(0, 2 * states, LANES):
        columns = slice(start, start + LANES)
        conv = conv_rows(
            pre_ref[:, state_at + start : state_at + start + LANES],
            conv_state_ref,
            columns,
            marks_ref,
        )
        sigma = sigmoid(conv)
        bc_ref[:, columns] = (conv * sigma).astype(HALF)
        bc_slope_ref[:, columns] = sigma * (1.0 + conv * (1.0 - sigma))
    block = min(length, CHUNK)
    place = lax.broadcasted_iota(jnp.int32, (block, block), 0)
    other = lax.broadcasted_iota(jnp.int32, (block, block), 1)
    z_ref[...] = jnp.zeros(z_ref.shape, FLOAT)
    bc_grad_ref[...] = jnp.zeros(bc_grad_ref.shape, FLOAT)
    for late in range(length // block):
        rows = slice(late * block, (late + 1) * block)
        for early in range(late + 1):
            past = slice(early * block, (early + 1) * block)
            same = marks_ref[past, 0:1] == labels_ref[:, rows]
            if late == early:
                same = same & (place <= other)
            mask = jnp.where(same, 0.0, -1e30)
            keys = bc_ref[past, :states]
            queries = bc_ref[rows, states:]
            scores = lax.dot_general(
                keys, queries, (((1,), (1,)), ((), ())), preferred_element_type=FLOAT
            )
            mixed = jnp.zeros((block, block), FLOAT)
            for head in range(heads):
                columns = slice(head * head_width, (head + 1) * head_width)
                spread_log = running_t[head : head + 1, rows] - running[past, head : head + 1]
                decay = jnp.exp(spread_log + mask)
                mixing = (decay * scores).astype(HALF)
                dy = dy_ref[rows, columns].astype(HALF)
                z_ref[past, columns] += jnp.dot(mixing, dy, preferred_element_type=FLOAT)
                along = lax.dot_general(
                    dosed_ref[past, columns],
                    dy,
                    (((1,), (1,)), ((), ())),
                    preferred_element_type=FLOAT,
                )
                mixed = mixed + decay * along
            mixed = mixed.astype(HALF)
            bc_grad_ref[past, :states] += jnp.dot(mixed, queries, preferred_element_type=FLOAT)
            bc_grad_ref[rows, states:] += lax.dot_general(
                mixed, keys, (((0,), (0,)), ((), ())), preferred_element_type=FLOAT
            )
    direct = jnp.zeros((length, LANES), FLOAT)
    balance = jnp.zeros((length, LANES), FLOAT)
    for start in range(0, wide, LANES):
        columns = slice(start, start + LANES)
        x, z, dy = x_ref[:, columns], z_ref[:, columns], dy_ref[:, columns]
        skip = wide_row_ref[1:2, columns]
        collapse = (((1,), (1,)), ((), ()))
        both = dy.astype(HALF).astype(FLOAT) * (y_ref[:, columns] - skip * x)
        both = both - dosed_ref[:, columns].astype(FLOAT) * z
        heads_of = expand[:, columns]
        direct = direct + lax.dot_general(
            x * z, heads_of, collapse, precision=HIGH, preferred_element_type=FLOAT
        )
        balance = balance + lax.dot_general(
            both, heads_of, collapse, precision=HIGH, preferred_element_type=FLOAT
        )
        grad_conv = (dose_ref[:, columns] * z + skip * dy) * slope_ref[:, columns]
        grad_in = conv_rows_back(
            grad_conv,
            pre_other_ref[:, columns],
            conv_input_ref,
            columns,
            marks_ref,
            conv_input_grad_ref,
        )
        grad_pre_other_ref[:, start : start + LANES] = grad_in.astype(HALF)
    for start in range(0, 2 * states, LANES):
        columns = slice(start, start + LANES)
        grad_in = conv_rows_back(
            bc_grad_ref[:, columns] * bc_slope_ref[:, columns],
            pre_ref[:, state_at + start : state_at + start + LANES],
            conv_state_ref,
            columns,
            marks_ref,
            conv_state_grad_ref,
        )
        grad_pre_ref[:, state_at + start : state_at + start + LANES] = grad_in.astype(HALF)
    crossing = summed_rows(balance, True)
    grad_step = (direct + rate * crossing) * sigmoid(shifted_pre)
    grad_pre_other_ref[:, step_at : step_at + LANES] = grad_step.astype(HALF)
    for start in range(step_at + LANES, grad_pre_other_ref.shape[1], LANES):
        grad_pre_other_ref[:, start : start + LANES] = jnp.zeros((length, LANES), HALF)
    step_grad_ref[0:1, :] = jnp.sum(grad_step, axis=0, keepdims=True)
    step_grad_ref[1:2, :] = rate * jnp.sum(sizes * crossing, axis=0, keepdims=True)


def whole_call(kernel, results, scratch, name):
    return pl.pallas_call(
        kernel,
        out_shape=results,
        scratch_shapes=scratch,
        compiler_params=pltpu.CompilerParams(vmem_limit_bytes=VMEM_BYTES),
        name=name,
    )


def mixer_forward(pre, heads, wide, mixer):
    length = pre[0].shape[0]
    kernel = functools.partial(mixer_forward_kernel, heads)
    states = mixer[1].shape[1] // 2
    return whole_call(
        kernel,
        (
            jax.ShapeDtypeStruct((length, wide), FLOAT),
            jax.ShapeDtypeStruct((length, wide), HALF),
            jax.ShapeDtypeStruct((length, 1), FLOAT),
        ),
        [
            pltpu.VMEM((length, wide), FLOAT),
            pltpu.VMEM((length, wide), HALF),
            pltpu.VMEM((length, states), HALF),
            pltpu.VMEM((length, states), HALF),
        ],
        "mixer_forward",
    )(*pre, *mixer)


def mixer_backward(pre, y, grad, sides, heads, mixer):
    length, wide = y.shape
    kernel = functools.partial(mixer_backward_kernel, heads, DI)
    double = mixer[1].shape[1]
    square = pltpu.VMEM((length, wide), FLOAT)
    return whole_call(
        kernel,
        (
            jax.ShapeDtypeStruct(pre[0].shape, HALF),
            jax.ShapeDtypeStruct(pre[1].shape, HALF),
            jax.ShapeDtypeStruct((2, wide), FLOAT),
            jax.ShapeDtypeStruct((4, wide), FLOAT),
            jax.ShapeDtypeStruct((4, double), FLOAT),
            jax.ShapeDtypeStruct((2, LANES), FLOAT),
        ),
        [
            square,
            pltpu.VMEM((length, wide), HALF),
            square,
            square,
            square,
            square,
            pltpu.VMEM((length, double), HALF),
            pltpu.VMEM((length, double), FLOAT),
            pltpu.VMEM((length, double), FLOAT),
        ],
        "mixer_backward",
    )(*pre, y, grad, sides, *mixer)


def through_experts(block, table, expert, beside, aside=None):
    tokens = spread(block)
    arrived = to_experts(project(table, tokens))
    answer = expert(arrived)
    if aside is not None:
        answer = after(answer, aside(tokens))
    answer = to_experts(answer)
    return beside(tokens, answer), arrived, tokens


def line_product(values, weights):
    return sum(project_back(value, weight) for value, weight in zip(values, weights)).astype(HALF)


def expert_forward(rows, experts):
    gate_e = project(rows, experts[0])
    lift_e = project(rows, experts[1])
    act_e = (jax.nn.silu(gate_e) * lift_e).astype(HALF)
    return (gate_e, lift_e, act_e), project(act_e, experts[2]).astype(HALF)


def expert_backward(rows, kept, experts):
    gate_e, lift_e, _ = kept
    grad_act = project_back(rows, experts[2])
    grad_gate = (grad_act * lift_e * silu_slope(gate_e)).astype(HALF)
    grad_lift = (grad_act * jax.nn.silu(gate_e)).astype(HALF)
    back = project_back(grad_gate, experts[0]) + project_back(grad_lift, experts[1])
    return (grad_gate, grad_lift), back.astype(HALF)


def shared_forward(tokens, shared):
    hidden = shared.shape[1] // 3
    gate_s = project(tokens, shared[:, :hidden])
    lift_s = project(tokens, shared[:, hidden : 2 * hidden])
    return gate_s, lift_s, (jax.nn.silu(gate_s) * lift_s).astype(HALF)


def shared_backward(tokens, kept, shared):
    hidden = shared.shape[1] // 3
    gate_s, lift_s, _ = kept
    grad_act = project(tokens, shared[:, 2 * hidden :])
    grad_gate = (grad_act * lift_s * silu_slope(gate_s)).astype(HALF)
    grad_lift = (grad_act * jax.nn.silu(gate_s)).astype(HALF)
    part = project_back(grad_gate, shared[:, :hidden])
    part = part + project_back(grad_lift, shared[:, hidden : 2 * hidden])
    return (grad_gate, grad_lift), part


def home_part(table, result, act_s, shared):
    hidden = shared.shape[1] // 3
    return (outer(table, result) + project_back(act_s, shared[:, 2 * hidden :])).astype(HALF)


def weight_sums(rows_in, rows_out, kept, grads, tokens_in, tokens_out, kept_s, grads_s):
    experts = (
        outer(rows_in, grads[0]).astype(HALF),
        outer(rows_in, grads[1]).astype(HALF),
        outer(kept[2], rows_out).astype(HALF),
    )
    shared = ((tokens_in, *grads_s), (tokens_out, *two_halves(kept_s[2])))
    return experts, [(*each, swapped(half_to_give(*each))) for each in shared]


def middle_backward(grad_normed, grad_out, middle, mixed, norm_mid):
    _, pull_mid = jax.vjp(rms_norm, middle, norm_mid)
    grad_middle, grad_norm_mid = pull_mid(grad_normed)
    grad_middle = grad_middle + grad_out
    along = jnp.sum(grad_middle * mixed, axis=1, keepdims=True)
    return grad_middle, along, grad_norm_mid


def two_halves(values):
    middle = values.shape[1] // 2
    return values[:, :middle], values[:, middle:]


def half_to_give(left, first_right, second_right):
    first = lax.axis_index("section") == 0
    return outer(left, jnp.where(first, second_right, first_right)).astype(HALF)


def half_to_keep(left, first_right, second_right, given):
    first = lax.axis_index("section") == 0
    keep = outer(left, jnp.where(first, first_right, second_right))
    return (keep + given.astype(FLOAT)).astype(HALF)


def flat(parts):
    return jnp.concatenate([part.reshape(-1) for part in parts])


def unflat(vector, shapes):
    result, start = [], 0
    for shape in shapes:
        size = 1
        for entry in shape:
            size *= entry
        result.append(vector[start : start + size].reshape(shape))
        start += size
    return result


def widened(value, columns):
    return jnp.pad(value, ((0, 0), (0, columns - value.shape[1])))


def shards(
    tokens,
    cotangent,
    doc_lengths,
    routes,
    gates,
    norm_in,
    proj_gate,
    proj_input,
    proj_state,
    proj_step,
    step_bias,
    decay_log,
    skip_gain,
    conv_input,
    conv_state,
    gate_norm,
    proj_output,
    norm_mid,
    expert_gate,
    expert_up,
    expert_down,
    shared_gate,
    shared_up,
    shared_down,
):
    section_now = lax.axis_index("section")
    first = section_now == 0
    row_now = lax.axis_index("row")
    n_row, n_col = lax.axis_size("row"), lax.axis_size("col")
    count = tokens.shape[1]
    top = routes.shape[3]
    capacity = count * top * 4 // (3 * n_row * n_col)
    width = tokens.shape[2]
    heads = step_bias.shape[1]
    inner = gate_norm.shape[1]
    state = conv_state.shape[2]
    wide = -(-inner // LANES) * LANES
    layers = range(2)

    def pair(own, other):
        return (jnp.where(first, own, other), jnp.where(first, other, own))

    tokens_now = lax.dynamic_index_in_dim(tokens, section_now, 0, keepdims=False)
    grad_now = lax.dynamic_index_in_dim(cotangent, section_now, 0, keepdims=False)
    wide_tokens = spread(tokens_now.astype(HALF))

    halves = (
        jnp.concatenate([widened(proj_gate[0], wide), proj_state[0]], axis=1),
        jnp.concatenate([widened(proj_input[0], wide), widened(proj_step[0], state)], axis=1),
    )
    keep, give = jnp.where(first, *halves), jnp.where(first, *halves[::-1])
    mine = pair(keep, swapped(give))

    def both_halves(half):
        whole = lax.all_gather(half, ("section", "row"), axis=0, tiled=True)
        return whole.reshape(2, n_row * half.shape[0], half.shape[1])

    proj = [both_halves(mine[0])]

    def both_layers(weight):
        whole = lax.all_gather(weight, ("section", "row"), axis=0, tiled=True)
        return whole.reshape(2, n_row * weight.shape[0], weight.shape[1])

    proj_out = both_layers(widened(proj_output[0], wide))
    gate_all = lax.all_gather(expert_gate[0, 0], "section")
    up_all = lax.all_gather(expert_up[0, 0], "section")
    down_all = lax.all_gather(expert_down[0, 0], "section")
    shared = both_layers(jnp.concatenate([shared_gate[0], shared_up[0], shared_down[0]], axis=1))
    experts = [(gate_all[s], up_all[s], down_all[s]) for s in layers]

    small_in = (
        norm_in[0],
        norm_mid[0],
        widened(conv_input[0], wide),
        conv_state[0],
        widened(jnp.concatenate([step_bias, decay_log], axis=0), LANES),
        widened(jnp.concatenate([gate_norm, jnp.repeat(skip_gain, HEAD, axis=1)], axis=0), wide),
    )
    vector = flat(small_in)
    small_all = [unflat(part, [v.shape for v in small_in]) for part in pair(vector, swapped(vector))]
    norm_ins = [part[0] for part in small_all]
    norm_mids = [part[1] for part in small_all]

    meta = jnp.concatenate([routes.astype(FLOAT), gates], axis=3)[0]
    keep = lax.dynamic_index_in_dim(meta, section_now, 0, keepdims=False)
    give = lax.dynamic_index_in_dim(meta, 1 - section_now, 0, keepdims=False)
    meta = jnp.concatenate(pair(keep, swapped(give)), axis=1)

    lengths = lax.dynamic_slice(
        doc_lengths, (section_now, row_now, 0), (1, 1, doc_lengths.shape[2])
    )
    labels = local_docs(lengths[0, 0], row_now, n_col * count)
    marks = [labels.astype(FLOAT)]
    for back in range(1, conv_input.shape[1]):
        prior = jnp.pad(labels, (back, 0), constant_values=-1)[:-back]
        marks.append((prior == labels).astype(FLOAT))
    marks = jnp.stack(marks, axis=1)
    label_row = labels.astype(FLOAT)[None]
    mixers = [
        (conv_in, conv_st, step_row, wide_row, marks, label_row)
        for _, _, conv_in, conv_st, step_row, wide_row in small_all
    ]

    def mix_in(s, wide_in):
        pre = [project(wide_in, half) for half in proj[s]]
        return pre, *mixer_forward(pre, heads, wide, mixers[s])

    def mix_out(s, resid, scaled, total_part, meanwhile):
        whole = line_product([scaled], [proj_out[s]])
        sums = gathered_sum(jnp.concatenate([whole, as_halves(total_part)], axis=1), meanwhile)
        mixed, total = sums[:, :width], from_halves(sums[:, width:], 1)
        rr = lax.rsqrt(total / DI + EPS)
        return resid + mixed * rr, mixed, rr

    wide_in_0 = rms_norm(wide_tokens.astype(FLOAT), norm_ins[0]).astype(HALF)
    pre_0, y_0, scaled_0, total_0 = mix_in(0, wide_in_0)
    tables = route_tables(spread(after(meta, scaled_0)), top, capacity, 2)
    plain = [table[0] for table in tables]
    scaling = [table[1] for table in tables]
    middle_0, mixed_0, rr_0 = mix_out(0, tokens_now, scaled_0, total_0, tables)
    kept = {}

    def expert_0(rows):
        kept["rows 0"], answer = expert_forward(rows, experts[0])
        return answer

    def beside_0(block, result):
        kept["shared 0"] = shared_forward(block, shared[0])
        return home_part(scaling[0], result, kept["shared 0"][2], shared[0])

    def aside_0(blocks):
        kept["grads"] = spread(after(grad_now.astype(HALF), blocks))
        return kept["grads"]

    parts, rows_0, mids_0 = through_experts(
        rms_norm(middle_0, norm_mids[0]).astype(HALF), plain[0], expert_0, beside_0, aside_0
    )
    proj.append(both_halves(after(mine[1], parts)))
    out_0 = middle_0 + gathered_sum(parts)

    wide_in_1 = spread(rms_norm(out_0, norm_ins[1]).astype(HALF))
    grad_tokens_1 = after(kept["grads"], out_0)
    grad_rows_1 = to_experts(project(scaling[1], grad_tokens_1))
    pre_1, y_1, scaled_1, total_1 = mix_in(1, wide_in_1)
    scaled_1 = after(scaled_1, grad_rows_1)
    middle_1, mixed_1, rr_1 = mix_out(1, out_0, scaled_1, total_1, ())

    def expert_1(rows):
        kept["rows 1"], kept["answer 1"] = expert_forward(rows, experts[1])
        kept["grads 1"], back = expert_backward(grad_rows_1, kept["rows 1"], experts[1])
        return back

    def beside_1(block, result):
        kept["shared 1"] = shared_forward(block, shared[1])
        kept["shared grads 1"], part = shared_backward(grad_tokens_1, kept["shared 1"], shared[1])
        return (part + outer(plain[1], result)).astype(HALF)

    parts, rows_1, mids_1 = through_experts(
        rms_norm(middle_1, norm_mids[1]).astype(HALF), plain[1], expert_1, beside_1
    )
    answer_1 = to_experts(after(kept["answer 1"], parts))

    def mixer_back(s, grad_middle, along, rr, saved, meanwhile):
        wide_in, pre, y, scaled = saved
        sides = as_halves(jnp.concatenate([rr, along], axis=1))
        payload = spread(jnp.concatenate([grad_middle.astype(HALF), sides], axis=1))
        payload = after(payload, meanwhile)
        wide_mix, sides = payload[:, :width], from_halves(payload[:, width:], 2)
        grad_scaled = project(wide_mix, proj_out[s])
        *grad_pre, wide_grads, grad_conv_input, grad_conv_state, step_grads = mixer_backward(
            pre, y, grad_scaled, sides, heads, mixers[s]
        )
        ends = [part[:, :wide] for part in grad_pre]
        tail = jnp.concatenate([grad_pre[0][:, wide:], grad_pre[1][:, wide : wide + LANES]], axis=1)
        mix_rr = (wide_mix * sides[:, :1]).astype(HALF)
        rest = (grad_conv_state, grad_conv_input, wide_grads, step_grads)
        return grad_pre, (wide_in, *ends), (mix_rr, *two_halves(scaled)), tail, rest

    def resid_back(resid, norm, grad_normed, grad_middle):
        _, pull_in = jax.vjp(rms_norm, resid, norm)
        grad_resid, grad_norm = pull_in(grad_normed)
        return grad_resid + grad_middle, grad_norm

    def own_layer(first_value, second_value):
        keep = jnp.where(first, first_value, second_value)
        give = jnp.where(first, second_value, first_value).astype(HALF)
        return keep.astype(FLOAT), swapped(give)

    def row_sent(values):
        return exchanged(values, "row")

    def row_total(received):
        return summed(received, "row").astype(HALF)

    grad_middle, along, grad_norm_mid_1 = middle_backward(
        gathered_sum(parts, answer_1), grad_now, middle_1, mixed_1, norm_mids[1]
    )
    expert_grads_1, shared_grads_1 = weight_sums(
        rows_1,
        grad_rows_1,
        kept["rows 1"],
        kept["grads 1"],
        mids_1,
        grad_tokens_1,
        kept["shared 1"],
        kept["shared grads 1"],
    )
    home = home_part(scaling[1], answer_1, kept["shared 1"][2], shared[1])
    grad_pre, to_proj, to_out, tail, rest_1 = mixer_back(
        1,
        grad_middle,
        along,
        rr_1,
        (wide_in_1, pre_1, y_1, scaled_1),
        (expert_grads_1, home, [made[-1] for made in shared_grads_1]),
    )
    whole = line_product(grad_pre, proj[1])
    given = half_to_give(*after(to_proj, whole))
    given_out = half_to_give(*after(to_out, given))
    grad_proj_1 = (*to_proj, swapped(given))
    grad_out_1 = (*to_out, swapped(given_out))
    grad_tail_1 = outer(after(wide_in_1, given_out), tail).astype(HALF)
    shared_sent_1 = [row_sent(half_to_keep(*after(made, whole))) for made in shared_grads_1]
    grad_in = gathered_sum(whole, (given, given_out, grad_tail_1, shared_sent_1))
    grad_1, grad_norm_in_1 = resid_back(out_0, norm_ins[1], grad_in, grad_middle)

    def expert_back_0(rows):
        kept["grads 0"], back = expert_backward(rows, kept["rows 0"], experts[0])
        return back

    def beside_back_0(block, result):
        kept["shared grads 0"], part = shared_backward(block, kept["shared 0"], shared[0])
        return (part + outer(plain[0], result)).astype(HALF)

    def aside_back_0(blocks):
        sums = [half_to_keep(*after(made, blocks)) for made in (grad_out_1, grad_proj_1)]
        kept["sums 1"] = sums
        kept["home"] = after(sent_home(after(home, blocks)), sums)
        return kept["home"]

    parts, grad_rows_0, grad_tokens_0 = through_experts(
        grad_1.astype(HALF), scaling[0], expert_back_0, beside_back_0, aside_back_0
    )
    out_1 = middle_1 + added_up(kept["home"])
    mixer_sent_1 = [row_sent(after(made, parts)) for made in kept["sums 1"]]
    grad_middle, along, grad_norm_mid_0 = middle_backward(
        gathered_sum(parts, (out_1, mixer_sent_1)), grad_1, middle_0, mixed_0, norm_mids[0]
    )
    expert_grads_0, shared_grads_0 = weight_sums(
        rows_0,
        grad_rows_0,
        kept["rows 0"],
        kept["grads 0"],
        mids_0,
        grad_tokens_0,
        kept["shared 0"],
        kept["shared grads 0"],
    )
    expert_out = [own_layer(a, b) for a, b in zip(expert_grads_0, expert_grads_1)]
    sums_1 = [row_total(received) for received in (*shared_sent_1, *mixer_sent_1)]
    grad_pre, to_proj, to_out, tail, rest_0 = mixer_back(
        0,
        grad_middle,
        along,
        rr_0,
        (wide_in_0, pre_0, y_0, scaled_0),
        ([part[0] for part in expert_out], [made[-1] for made in shared_grads_0], sums_1),
    )

    def row_sums(value):
        return lax.psum_scatter(value, "row", scatter_dimension=0, tiled=True)

    sums_0 = [row_sums(half_to_keep(*after(made, to_out[0]))) for made in shared_grads_0]
    given = half_to_give(*to_proj)
    whole = line_product(after(grad_pre, given), proj[0])
    line_received = sent_home(whole)
    proj_sent = row_sent(half_to_keep(*after((*to_proj, swapped(given)), whole)))
    given_out = half_to_give(*after(to_out, whole))
    sums_0.append(row_sums(half_to_keep(*after((*to_out, swapped(given_out)), proj_sent[:8]))))
    grad_tail_0 = outer(after(wide_in_0, given_out), tail).astype(HALF)
    tail_keep, tail_other = own_layer(grad_tail_0, grad_tail_1)
    tail_sent = row_sent((tail_keep + tail_other.astype(FLOAT)).astype(HALF))
    wide_x = wide_tokens.astype(FLOAT)
    wide_r = lax.rsqrt(jnp.mean(wide_x * wide_x, axis=1, keepdims=True) + EPS)
    grad_norm_in_0 = jnp.sum(whole.astype(FLOAT) * wide_x * wide_r, axis=0)
    smalls = (
        (grad_norm_in_0, grad_norm_mid_0, *rest_0),
        (grad_norm_in_1, grad_norm_mid_1, *rest_1),
    )
    shapes = [part.shape for part in smalls[0]]
    small_keep, small_other = own_layer(flat(smalls[0]), flat(smalls[1]))
    vector = small_keep + small_other.astype(FLOAT)
    lines = row_sent(jnp.tile(vector[None], (n_row, 1)))
    expert_out = [keep + other.astype(FLOAT) for keep, other in after(expert_out, given_out)]
    line_received, proj_sent, tail_sent, lines = after(
        (line_received, proj_sent, tail_sent, lines), expert_out
    )
    grad_in = added_up(line_received)
    sums_0.append(row_total(proj_sent))
    tail = row_total(tail_sent)
    vector = jnp.sum(lines, axis=0)
    grad_0, _ = resid_back(tokens_now, norm_ins[0], grad_in, grad_middle)

    def own_halves(first_value, second_value):
        keep = jnp.where(first, first_value, second_value)
        give = jnp.where(first, second_value, first_value)
        return keep, swapped(give)

    def per_micro(first_value, second_value):
        keep = jnp.where(first, first_value, second_value)
        return keep, swapped(jnp.where(first, second_value, first_value).astype(HALF))

    halves = [own_halves(a, b) for a, b in zip(sums_0, sums_1)]
    outs, in_grads = per_micro(out_0, after(out_1, grad_in)), per_micro(grad_0, grad_1)
    common = 2 * width + conv_state.shape[1] * state
    state_grad = tail[:, :state]
    if n_col <= 4:
        state_sent = exchanged(state_grad, "col")
        lines = exchanged(jnp.tile(vector[None, :common], (n_col, 1)), "col")
        state_sent, lines, halves, outs, in_grads = after(
            (state_sent, lines, halves, outs, in_grads)
        )
        state_grad = spread(summed(state_sent, "col").astype(HALF))
        shared_sum = jnp.sum(lines, axis=0)
    else:
        state_grad = lax.psum(state_grad, "col")
        shared_sum = lax.psum(vector[:common], "col")
    halves = [pair(*half) for half in halves]
    grad_shared, grad_down, grad_out, grad_ends = halves
    grad_out, grad_down = [jnp.concatenate(both, axis=1) for both in (grad_out, grad_down)]
    (
        out_norm_in,
        out_norm_mid,
        out_conv_state,
        out_conv_input,
        out_wide,
        out_step,
    ) = unflat(jnp.concatenate([shared_sum, vector[common:]]), shapes)

    def stacked(keep, other):
        return jnp.stack(pair(keep, other.astype(FLOAT)))[None]

    def out(value):
        return value.astype(FLOAT)[None]

    return (
        stacked(*outs),
        stacked(*in_grads),
        out_norm_in[None],
        out(grad_ends[0][:, :inner]),
        out(grad_ends[1][:, :inner]),
        out(state_grad),
        out(tail[:, state : state + heads]),
        out_step[:1, :heads],
        out_step[1:, :heads],
        jnp.sum(out_wide[1, :inner].reshape(heads, HEAD), axis=1)[None],
        out_conv_input[None, :, :inner],
        out_conv_state[None],
        out_wide[:1, :inner],
        out(grad_out[:, :inner]),
        out_norm_mid[None],
        expert_out[0][None, None],
        expert_out[1][None, None],
        expert_out[2][None, None],
        out(grad_shared[0]),
        out(grad_shared[1]),
        out(grad_down),
    )


def solution(mesh):
    in_specs = (
        P(None, ("row", "col"), None),
        P(None, ("row", "col"), None),
        P(),
        P("section", None, ("row", "col"), None),
        P("section", None, ("row", "col"), None),
        P("section", None),
        P("section", "row", "col"),
        P("section", "row", "col"),
        P("section", "row", None),
        P("section", "row", "col"),
        P("section", "col"),
        P("section", "col"),
        P("section", "col"),
        P("section", None, "col"),
        P("section", None, None),
        P("section", "col"),
        P("section", "row", "col"),
        P("section", None),
        P("section", ("row", "col"), None, None),
        P("section", ("row", "col"), None, None),
        P("section", ("row", "col"), None, None),
        P("section", "row", "col"),
        P("section", "row", "col"),
        P("section", "row", "col"),
    )
    out_specs = (
        P("section", None, ("row", "col"), None),
        P("section", None, ("row", "col"), None),
        P("section", None),
        P("section", "row", "col"),
        P("section", "row", "col"),
        P("section", "row", None),
        P("section", "row", "col"),
        P("section", "col"),
        P("section", "col"),
        P("section", "col"),
        P("section", None, "col"),
        P("section", None, None),
        P("section", "col"),
        P("section", "row", "col"),
        P("section", None),
        P("section", ("row", "col"), None, None),
        P("section", ("row", "col"), None, None),
        P("section", ("row", "col"), None, None),
        P("section", "row", "col"),
        P("section", "row", "col"),
        P("section", "row", "col"),
    )
    return jax.shard_map(shards, mesh=mesh, in_specs=in_specs, out_specs=out_specs, check_vma=False)
```

```python
import functools

import jax
import jax.numpy as jnp
from jax import lax
from jax.experimental import pallas as pl
from jax.experimental.pallas import tpu as pltpu
from jax.sharding import PartitionSpec as P

DI = 3072
HEAD = 64
LANES = 128
CHUNK = 256
VMEM_BYTES = 48 * 2**20

EPS = 1e-05
HIGH = lax.Precision.HIGHEST
FLOAT = jnp.float32
HALF = jnp.bfloat16


def shifted(block, axis, distance):
    count = lax.axis_size(axis)
    if distance % count == 0:
        return block
    return lax.ppermute(block, axis, [(i, (i + distance) % count) for i in range(count)])


def swapped(block):
    return lax.ppermute(block, "section", [(0, 1), (1, 0)])


def after(value, *others):
    return lax.optimization_barrier((value, *others))[0]


def rms_norm(value, gain):
    return value * lax.rsqrt(jnp.mean(value * value, axis=-1, keepdims=True) + EPS) * gain


def local_docs(lengths, row_now, length):
    bounds = jnp.cumsum(lengths)[:-1]
    place = jnp.arange(length, dtype=jnp.int32)
    inner = jnp.sum((place[:, None] >= bounds[None, :]).astype(jnp.int32), axis=1)
    return inner + row_now * lengths.shape[0]


def project(left, right):
    return jnp.dot(left, right, preferred_element_type=FLOAT)


def project_back(left, right):
    return lax.dot_general(left, right, (((1,), (1,)), ((), ())), preferred_element_type=FLOAT)


def outer(left, right):
    return lax.dot_general(left, right, (((0,), (0,)), ((), ())), preferred_element_type=FLOAT)


def silu_slope(value):
    sigma = jax.nn.sigmoid(value)
    return sigma * (1.0 + value * (1.0 - sigma))


def groups():
    count = lax.axis_size("col")
    return count if count <= 4 else 1


def spread(block, meanwhile=()):
    if groups() == 1:
        return lax.all_gather(block, "col", axis=0, tiled=True)
    received = [shifted(block, "col", back) for back in range(1, groups())]
    return jnp.concatenate([block, *after(received, meanwhile)], axis=0)


def in_order(blocks, axis):
    count = len(blocks)
    if count == 1:
        return blocks[0]
    rows = blocks[0].shape[0]
    line = jnp.concatenate(blocks[::-1] + blocks[:0:-1], axis=0)
    start = (count - 1 - lax.axis_index(axis)) * rows
    return lax.dynamic_slice_in_dim(line, start, count * rows, axis=0)


def sent_home(rows):
    if groups() == 1:
        return lax.psum_scatter(rows, "col", scatter_dimension=0, tiled=True)
    return [shifted(block_of(rows, back), "col", -back) for back in range(1, groups())]


def added_up(rows, received):
    if groups() == 1:
        return received.astype(FLOAT)
    return sum([part.astype(FLOAT) for part in received], block_of(rows, 0).astype(FLOAT))


def gathered_sum(rows, meanwhile=()):
    return added_up(rows, after(sent_home(rows), meanwhile))


def exchanged(rows, axis):
    return lax.all_to_all(rows, axis, split_axis=0, concat_axis=0, tiled=True)


def as_halves(columns):
    high = lax.reduce_precision(columns, 8, 7)
    both = jnp.concatenate([high, columns - high], axis=1).astype(HALF)
    return jnp.pad(both, ((0, 0), (0, LANES - both.shape[1])))


def from_halves(tile, count):
    return tile[:, :count].astype(FLOAT) + tile[:, count : 2 * count].astype(FLOAT)


def block_of(values, back):
    rows = values.shape[0] // groups()
    return values[back * rows : (back + 1) * rows]


def turn():
    place = lax.axis_index("col") if groups() > 1 else jnp.int32(0)
    return place.astype(jnp.int32).reshape(1)


def route_tables(meta, top, capacity, layers):
    n_row, n_col = lax.axis_size("row"), lax.axis_size("col")
    experts = (jnp.arange(n_row) * n_col + lax.axis_index("col")).astype(FLOAT)
    count = meta.shape[0]
    slots = n_col * capacity
    meta = meta.reshape(count, layers, 2, top).transpose(1, 2, 3, 0)
    match = meta[:, None, 0] == experts[None, :, None, None]
    hit = jnp.any(match, axis=2)
    weight = jnp.sum(jnp.where(match, meta[:, None, 1], 0.0), axis=2)
    order = jnp.arange(count, dtype=jnp.int32)
    triangle = (order[:, None] <= order[None, :]).astype(HALF)
    place = project(hit.astype(HALF).reshape(-1, count), triangle).reshape(hit.shape)
    slot = jnp.arange(1, slots + 1, dtype=jnp.int32).astype(FLOAT)
    chosen = (place[:, :, None, :] == slot[:, None]) & hit[:, :, None, :]
    shape = (layers, n_row * slots, count)
    plain = chosen.astype(HALF).reshape(shape)
    scaled = jnp.where(chosen, weight[:, :, None, :], 0.0).astype(HALF).reshape(shape)
    return [(plain[s], scaled[s]) for s in range(layers)]


def to_experts(rows):
    return exchanged(rows.astype(HALF), "row")


def summed_rows(values, reverse):
    step = min(values.shape[0], CHUNK)
    count = values.shape[0] // step
    place = lax.broadcasted_iota(jnp.int32, (step, step), 0)
    other = lax.broadcasted_iota(jnp.int32, (step, step), 1)
    before = (place <= other) if reverse else (place >= other)
    triangle = before.astype(FLOAT)
    carry = jnp.zeros((1, values.shape[1]), FLOAT)
    parts = [None] * count
    for index in reversed(range(count)) if reverse else range(count):
        part = values[index * step : (index + 1) * step]
        run = jnp.dot(triangle, part, precision=HIGH, preferred_element_type=FLOAT) + carry
        carry = run[:1] if reverse else run[step - 1 :]
        parts[index] = run
    return parts[0] if count == 1 else jnp.concatenate(parts, axis=0)


def head_columns(rows, columns, head_width):
    head = lax.broadcasted_iota(jnp.int32, (rows, columns), 0) * head_width
    column = lax.broadcasted_iota(jnp.int32, (rows, columns), 1)
    return ((column >= head) & (column < head + head_width)).astype(FLOAT)


def sigmoid(value):
    return 1.0 / (1.0 + jnp.exp(-value))


def step_sizes(step_pre, step_row_ref):
    shifted_pre = step_pre + step_row_ref[0:1, :]
    sizes = jnp.maximum(shifted_pre, 0.0) + jnp.log1p(jnp.exp(-jnp.abs(shifted_pre)))
    return shifted_pre, sizes, -jnp.exp(step_row_ref[1:2, :])


def conv_rows(values, weight_ref, columns, marks_ref):
    width = weight_ref.shape[0]
    result = values * weight_ref[width - 1 : width, columns]
    for back in range(1, width):
        moved = pltpu.roll(values, back, 0) * marks_ref[:, back : back + 1]
        result = result + moved * weight_ref[width - 1 - back : width - back, columns]
    return result


def conv_rows_back(grad, values, weight_ref, columns, marks_ref, weight_grad_ref):
    width = weight_ref.shape[0]
    rows = values.shape[0]
    result = grad * weight_ref[width - 1 : width, columns]
    weight_grad_ref[width - 1 : width, columns] = jnp.sum(grad * values, axis=0, keepdims=True)
    for back in range(1, width):
        kept = grad * marks_ref[:, back : back + 1]
        taps = jnp.sum(kept * pltpu.roll(values, back, 0), axis=0, keepdims=True)
        weight_grad_ref[width - 1 - back : width - back, columns] = taps
        moved = pltpu.roll(kept, rows - back, 0)
        result = result + moved * weight_ref[width - 1 - back : width - back, columns]
    return result


def copy_in_order(source_ref, target_ref, place_ref, parts):
    if parts == 1:
        return source_ref
    rows = source_ref.shape[0] // parts
    for index in range(parts):
        target_ref[index * rows : (index + 1) * rows, :] = source_ref[
            block_rows(index, rows, place_ref, parts), :
        ]
    return target_ref


def block_rows(index, rows, place_ref, parts):
    if parts == 1:
        return slice(0, rows)
    back = lax.rem(place_ref[0] - index + parts, parts)
    return pl.ds(pl.multiple_of(back * rows, rows), rows)


def mixer_forward_kernel(
    heads,
    parts,
    pre_in_ref,
    pre_other_in_ref,
    conv_input_ref,
    conv_state_ref,
    step_row_ref,
    wide_row_ref,
    marks_ref,
    labels_ref,
    place_ref,
    y_ref,
    scaled_ref,
    total_ref,
    pre_ref,
    pre_other_ref,
    x_ref,
    dosed_ref,
    keys_ref,
    queries_ref,
):
    length, wide = y_ref.shape
    states = conv_state_ref.shape[1] // 2
    state_at, step_at = wide, wide
    head_width = HEAD
    pre_ref = copy_in_order(pre_in_ref, pre_ref, place_ref, parts)
    pre_other_ref = copy_in_order(pre_other_in_ref, pre_other_ref, place_ref, parts)
    _, sizes, rate = step_sizes(pre_other_ref[:, step_at : step_at + LANES], step_row_ref)
    running = summed_rows(sizes * rate, False)
    running_t = running.T
    expand = head_columns(LANES, wide, head_width)
    for start in range(0, wide, LANES):
        columns = slice(start, start + LANES)
        conv = conv_rows(
            pre_other_ref[:, columns], conv_input_ref, columns, marks_ref
        )
        x = conv * sigmoid(conv)
        x_ref[:, columns] = x
        dose = jnp.dot(sizes, expand[:, columns], precision=HIGH, preferred_element_type=FLOAT)
        dosed_ref[:, columns] = (x * dose).astype(HALF)
    for part, target in ((0, keys_ref), (1, queries_ref)):
        columns = slice(part * states, (part + 1) * states)
        conv = conv_rows(
            pre_ref[:, state_at + part * states : state_at + (part + 1) * states],
            conv_state_ref,
            columns,
            marks_ref,
        )
        target[...] = (conv * sigmoid(conv)).astype(HALF)
    block = min(length, CHUNK)
    place = lax.broadcasted_iota(jnp.int32, (block, block), 0)
    other = lax.broadcasted_iota(jnp.int32, (block, block), 1)
    for late in range(length // block):
        rows = slice(late * block, (late + 1) * block)
        for early in range(late + 1):
            past = slice(early * block, (early + 1) * block)
            same = marks_ref[rows, 0:1] == labels_ref[:, past]
            if late == early:
                same = same & (place >= other)
            mask = jnp.where(same, 0.0, -1e30)
            scores = lax.dot_general(
                queries_ref[rows, :],
                keys_ref[past, :],
                (((1,), (1,)), ((), ())),
                preferred_element_type=FLOAT,
            )
            for head in range(heads):
                columns = slice(head * head_width, (head + 1) * head_width)
                spread_log = running[rows, head : head + 1] - running_t[head : head + 1, past]
                mixing = (jnp.exp(spread_log + mask) * scores).astype(HALF)
                inner = jnp.dot(mixing, dosed_ref[past, columns], preferred_element_type=FLOAT)
                if early == 0:
                    y_ref[rows, columns] = inner
                else:
                    y_ref[rows, columns] += inner
    total = jnp.zeros((length, 1), FLOAT)
    for start in range(0, wide, LANES):
        columns = slice(start, start + LANES)
        y = y_ref[:, columns]
        if heads * head_width < start + LANES:
            lane = lax.broadcasted_iota(jnp.int32, y.shape, 1) + start
            y = jnp.where(lane < heads * head_width, y, 0.0)
        y = y + wide_row_ref[1:2, columns] * x_ref[:, columns]
        gate = pre_ref[:, columns]
        gated = y * gate * sigmoid(gate)
        y_ref[:, columns] = y
        scaled = (gated * wide_row_ref[0:1, columns]).astype(HALF)
        each = length // parts
        for index in range(parts):
            block_at = block_rows(index, each, place_ref, parts)
            scaled_ref[block_at, columns] = scaled[index * each : (index + 1) * each]
        total = total + jnp.sum(gated * gated, axis=1, keepdims=True)
    each = length // parts
    for index in range(parts):
        block_at = block_rows(index, each, place_ref, parts)
        total_ref[block_at, :] = total[index * each : (index + 1) * each]


def mixer_backward_kernel(
    heads,
    parts,
    inner_all,
    pre_in_ref,
    pre_other_in_ref,
    y_ref,
    grad_in_ref,
    sides_in_ref,
    conv_input_ref,
    conv_state_ref,
    step_row_ref,
    wide_row_ref,
    marks_ref,
    labels_ref,
    place_ref,
    grad_pre_ref,
    grad_pre_other_ref,
    wide_grad_ref,
    conv_input_grad_ref,
    conv_state_grad_ref,
    step_grad_ref,
    pre_ref,
    pre_other_ref,
    grad_ref,
    sides_ref,
    x_ref,
    dosed_ref,
    dose_ref,
    slope_ref,
    dy_ref,
    z_ref,
    bc_ref,
    bc_slope_ref,
    bc_grad_ref,
):
    length, wide = y_ref.shape
    states = conv_state_ref.shape[1] // 2
    state_at, step_at = wide, wide
    head_width = HEAD
    each = length // parts
    pre_ref = copy_in_order(pre_in_ref, pre_ref, place_ref, parts)
    pre_other_ref = copy_in_order(pre_other_in_ref, pre_other_ref, place_ref, parts)
    grad_ref = copy_in_order(grad_in_ref, grad_ref, place_ref, parts)
    sides_ref = copy_in_order(sides_in_ref, sides_ref, place_ref, parts)

    def put(target_ref, value, start):
        for index in range(parts):
            target_ref[block_rows(index, each, place_ref, parts), start : start + LANES] = value[
                index * each : (index + 1) * each
            ]

    shifted_pre, sizes, rate = step_sizes(pre_other_ref[:, step_at : step_at + LANES], step_row_ref)
    running = summed_rows(sizes * rate, False)
    running_t = running.T
    expand = head_columns(LANES, wide, head_width)
    rr = sides_ref[:, 0:1]
    pull = rr * rr * rr * sides_ref[:, 1:2] * (1.0 / inner_all)
    for start in range(0, wide, LANES):
        columns = slice(start, start + LANES)
        gate = pre_ref[:, columns]
        y = y_ref[:, columns]
        grad = grad_ref[:, columns]
        gain = wide_row_ref[0:1, columns]
        sigma = sigmoid(gate)
        silu = gate * sigma
        gated = y * silu
        normed = gated * rr
        wide_grad_ref[0:1, columns] = jnp.sum(grad * normed, axis=0, keepdims=True)
        grad_gated = rr * gain * grad - gated * pull
        slope = sigma * (1.0 + gate * (1.0 - sigma))
        put(grad_pre_ref, (grad_gated * y * slope).astype(HALF), start)
        dy = grad_gated * silu
        dy_ref[:, columns] = dy
        conv = conv_rows(
            pre_other_ref[:, columns], conv_input_ref, columns, marks_ref
        )
        sigma = sigmoid(conv)
        x = conv * sigma
        x_ref[:, columns] = x
        slope_ref[:, columns] = sigma * (1.0 + conv * (1.0 - sigma))
        dose = jnp.dot(sizes, expand[:, columns], precision=HIGH, preferred_element_type=FLOAT)
        dose_ref[:, columns] = dose
        dosed_ref[:, columns] = (x * dose).astype(HALF)
        wide_grad_ref[1:2, columns] = jnp.sum(dy * x, axis=0, keepdims=True)
    for start in range(0, 2 * states, LANES):
        columns = slice(start, start + LANES)
        conv = conv_rows(
            pre_ref[:, state_at + start : state_at + start + LANES],
            conv_state_ref,
            columns,
            marks_ref,
        )
        sigma = sigmoid(conv)
        bc_ref[:, columns] = (conv * sigma).astype(HALF)
        bc_slope_ref[:, columns] = sigma * (1.0 + conv * (1.0 - sigma))
    block = min(length, CHUNK)
    place = lax.broadcasted_iota(jnp.int32, (block, block), 0)
    other = lax.broadcasted_iota(jnp.int32, (block, block), 1)
    z_ref[...] = jnp.zeros(z_ref.shape, FLOAT)
    bc_grad_ref[...] = jnp.zeros(bc_grad_ref.shape, FLOAT)
    for late in range(length // block):
        rows = slice(late * block, (late + 1) * block)
        for early in range(late + 1):
            past = slice(early * block, (early + 1) * block)
            same = marks_ref[past, 0:1] == labels_ref[:, rows]
            if late == early:
                same = same & (place <= other)
            mask = jnp.where(same, 0.0, -1e30)
            keys = bc_ref[past, :states]
            queries = bc_ref[rows, states:]
            scores = lax.dot_general(
                keys, queries, (((1,), (1,)), ((), ())), preferred_element_type=FLOAT
            )
            mixed = jnp.zeros((block, block), FLOAT)
            for head in range(heads):
                columns = slice(head * head_width, (head + 1) * head_width)
                spread_log = running_t[head : head + 1, rows] - running[past, head : head + 1]
                decay = jnp.exp(spread_log + mask)
                mixing = (decay * scores).astype(HALF)
                dy = dy_ref[rows, columns].astype(HALF)
                z_ref[past, columns] += jnp.dot(mixing, dy, preferred_element_type=FLOAT)
                along = lax.dot_general(
                    dosed_ref[past, columns],
                    dy,
                    (((1,), (1,)), ((), ())),
                    preferred_element_type=FLOAT,
                )
                mixed = mixed + decay * along
            mixed = mixed.astype(HALF)
            bc_grad_ref[past, :states] += jnp.dot(mixed, queries, preferred_element_type=FLOAT)
            bc_grad_ref[rows, states:] += lax.dot_general(
                mixed, keys, (((0,), (0,)), ((), ())), preferred_element_type=FLOAT
            )
    direct = jnp.zeros((length, LANES), FLOAT)
    balance = jnp.zeros((length, LANES), FLOAT)
    for start in range(0, wide, LANES):
        columns = slice(start, start + LANES)
        x, z, dy = x_ref[:, columns], z_ref[:, columns], dy_ref[:, columns]
        skip = wide_row_ref[1:2, columns]
        collapse = (((1,), (1,)), ((), ()))
        both = dy.astype(HALF).astype(FLOAT) * (y_ref[:, columns] - skip * x)
        both = both - dosed_ref[:, columns].astype(FLOAT) * z
        heads_of = expand[:, columns]
        direct = direct + lax.dot_general(
            x * z, heads_of, collapse, precision=HIGH, preferred_element_type=FLOAT
        )
        balance = balance + lax.dot_general(
            both, heads_of, collapse, precision=HIGH, preferred_element_type=FLOAT
        )
        grad_conv = (dose_ref[:, columns] * z + skip * dy) * slope_ref[:, columns]
        grad_in = conv_rows_back(
            grad_conv,
            pre_other_ref[:, columns],
            conv_input_ref,
            columns,
            marks_ref,
            conv_input_grad_ref,
        )
        put(grad_pre_other_ref, grad_in.astype(HALF), start)
    for start in range(0, 2 * states, LANES):
        columns = slice(start, start + LANES)
        grad_in = conv_rows_back(
            bc_grad_ref[:, columns] * bc_slope_ref[:, columns],
            pre_ref[:, state_at + start : state_at + start + LANES],
            conv_state_ref,
            columns,
            marks_ref,
            conv_state_grad_ref,
        )
        put(grad_pre_ref, grad_in.astype(HALF), state_at + start)
    crossing = summed_rows(balance, True)
    grad_step = (direct + rate * crossing) * sigmoid(shifted_pre)
    put(grad_pre_other_ref, grad_step.astype(HALF), step_at)
    for start in range(step_at + LANES, grad_pre_other_ref.shape[1], LANES):
        put(grad_pre_other_ref, jnp.zeros((length, LANES), HALF), start)
    step_grad_ref[0:1, :] = jnp.sum(grad_step, axis=0, keepdims=True)
    step_grad_ref[1:2, :] = rate * jnp.sum(sizes * crossing, axis=0, keepdims=True)


def ordered_copy(shape):
    return pltpu.VMEM(shape if groups() > 1 else (8, LANES), FLOAT)


def whole_call(kernel, inputs, results, scratch, name):
    whole = pl.BlockSpec(memory_space=pltpu.VMEM)
    place = pl.BlockSpec(memory_space=pltpu.SMEM)
    return pl.pallas_call(
        kernel,
        in_specs=[whole] * (inputs - 1) + [place],
        out_shape=results,
        scratch_shapes=scratch,
        compiler_params=pltpu.CompilerParams(vmem_limit_bytes=VMEM_BYTES),
        name=name,
    )


def mixer_forward(pre, heads, wide, mixer):
    length = pre[0].shape[0]
    kernel = functools.partial(mixer_forward_kernel, heads, groups())
    states = mixer[1].shape[1] // 2
    return whole_call(
        kernel,
        2 + len(mixer),
        (
            jax.ShapeDtypeStruct((length, wide), FLOAT),
            jax.ShapeDtypeStruct((length, wide), HALF),
            jax.ShapeDtypeStruct((length, 1), FLOAT),
        ),
        [
            ordered_copy(pre[0].shape),
            ordered_copy(pre[1].shape),
            pltpu.VMEM((length, wide), FLOAT),
            pltpu.VMEM((length, wide), HALF),
            pltpu.VMEM((length, states), HALF),
            pltpu.VMEM((length, states), HALF),
        ],
        "mixer_forward",
    )(*pre, *mixer)


def mixer_backward(pre, y, grad, sides, heads, mixer):
    length, wide = y.shape
    kernel = functools.partial(mixer_backward_kernel, heads, groups(), DI)
    double = mixer[1].shape[1]
    square = pltpu.VMEM((length, wide), FLOAT)
    return whole_call(
        kernel,
        5 + len(mixer),
        (
            jax.ShapeDtypeStruct(pre[0].shape, HALF),
            jax.ShapeDtypeStruct(pre[1].shape, HALF),
            jax.ShapeDtypeStruct((2, wide), FLOAT),
            jax.ShapeDtypeStruct((4, wide), FLOAT),
            jax.ShapeDtypeStruct((4, double), FLOAT),
            jax.ShapeDtypeStruct((2, LANES), FLOAT),
        ),
        [
            ordered_copy(pre[0].shape),
            ordered_copy(pre[1].shape),
            ordered_copy(y.shape),
            ordered_copy(sides.shape),
            square,
            pltpu.VMEM((length, wide), HALF),
            square,
            square,
            square,
            square,
            pltpu.VMEM((length, double), HALF),
            pltpu.VMEM((length, double), FLOAT),
            pltpu.VMEM((length, double), FLOAT),
        ],
        "mixer_backward",
    )(*pre, y, grad, sides, *mixer)


def through_experts(block, table, expert, own, beside, aside=None):
    tokens = spread(block)
    arrived = to_experts(project(table, tokens))
    answer = expert(arrived)
    if aside is not None:
        answer = after(answer, aside(tokens))
    answered = to_experts(answer)
    answered = after(answered, own(after(tokens, answer), after(arrived, answer)))
    return beside(answered), arrived, tokens


def line_product(values, weights):
    return sum(project_back(value, weight) for value, weight in zip(values, weights)).astype(HALF)


def expert_forward(rows, experts):
    gate_e = project(rows, experts[0])
    lift_e = project(rows, experts[1])
    act_e = (jax.nn.silu(gate_e) * lift_e).astype(HALF)
    return (gate_e, lift_e, act_e), project(act_e, experts[2]).astype(HALF)


def expert_backward(rows, kept, experts):
    gate_e, lift_e, _ = kept
    grad_act = project_back(rows, experts[2])
    grad_gate = (grad_act * lift_e * silu_slope(gate_e)).astype(HALF)
    grad_lift = (grad_act * jax.nn.silu(gate_e)).astype(HALF)
    back = project_back(grad_gate, experts[0]) + project_back(grad_lift, experts[1])
    return (grad_gate, grad_lift), back.astype(HALF)


def shared_forward(tokens, shared):
    hidden = shared.shape[1] // 3
    gate_s = project(tokens, shared[:, :hidden])
    lift_s = project(tokens, shared[:, hidden : 2 * hidden])
    return gate_s, lift_s, (jax.nn.silu(gate_s) * lift_s).astype(HALF)


def shared_backward(tokens, kept, shared):
    hidden = shared.shape[1] // 3
    gate_s, lift_s, _ = kept
    grad_act = project(tokens, shared[:, 2 * hidden :])
    grad_gate = (grad_act * lift_s * silu_slope(gate_s)).astype(HALF)
    grad_lift = (grad_act * jax.nn.silu(gate_s)).astype(HALF)
    part = project_back(grad_gate, shared[:, :hidden])
    part = part + project_back(grad_lift, shared[:, hidden : 2 * hidden])
    return (grad_gate, grad_lift), part


def home_part(table, result, act_s, shared):
    hidden = shared.shape[1] // 3
    return (outer(table, result) + project_back(act_s, shared[:, 2 * hidden :])).astype(HALF)


def weight_sums(rows_in, rows_out, kept, grads, tokens_in, tokens_out, kept_s, grads_s):
    experts = (
        outer(rows_in, grads[0]).astype(HALF),
        outer(rows_in, grads[1]).astype(HALF),
        outer(kept[2], rows_out).astype(HALF),
    )
    shared = ((tokens_in, *grads_s), (tokens_out, *two_halves(kept_s[2])))
    return experts, [(*each, swapped(half_to_give(*each))) for each in shared]


def middle_backward(grad_normed, grad_out, middle, mixed, norm_mid):
    _, pull_mid = jax.vjp(rms_norm, middle, norm_mid)
    grad_middle, grad_norm_mid = pull_mid(grad_normed)
    grad_middle = grad_middle + grad_out
    along = jnp.sum(grad_middle * mixed, axis=1, keepdims=True)
    return grad_middle, along, grad_norm_mid


def two_halves(values):
    middle = values.shape[1] // 2
    return values[:, :middle], values[:, middle:]


def half_to_give(left, first_right, second_right):
    first = lax.axis_index("section") == 0
    return outer(left, jnp.where(first, second_right, first_right)).astype(HALF)


def half_to_keep(left, first_right, second_right, given):
    first = lax.axis_index("section") == 0
    keep = outer(left, jnp.where(first, first_right, second_right))
    return (keep + given.astype(FLOAT)).astype(HALF)


def row_pieces(values, axis="row"):
    count = lax.axis_size(axis)
    rows = values.shape[0] // count
    index = [lax.rem(lax.axis_index(axis) + ahead, count) * rows for ahead in range(count)]
    return [lax.dynamic_slice_in_dim(values, at, rows, axis=0) for at in index]


def total_of(own, received):
    return sum([part.astype(FLOAT) for part in received], own.astype(FLOAT))


def row_received(pieces, axis="row"):
    return [shifted(piece, axis, ahead) for ahead, piece in enumerate(pieces) if ahead]


def flat(parts):
    return jnp.concatenate([part.reshape(-1) for part in parts])


def unflat(vector, shapes):
    result, start = [], 0
    for shape in shapes:
        size = 1
        for entry in shape:
            size *= entry
        result.append(vector[start : start + size].reshape(shape))
        start += size
    return result


def widened(value, columns):
    return jnp.pad(value, ((0, 0), (0, columns - value.shape[1])))


def shards(
    tokens,
    cotangent,
    doc_lengths,
    routes,
    gates,
    norm_in,
    proj_gate,
    proj_input,
    proj_state,
    proj_step,
    step_bias,
    decay_log,
    skip_gain,
    conv_input,
    conv_state,
    gate_norm,
    proj_output,
    norm_mid,
    expert_gate,
    expert_up,
    expert_down,
    shared_gate,
    shared_up,
    shared_down,
):
    section_now = lax.axis_index("section")
    first = section_now == 0
    row_now = lax.axis_index("row")
    n_row, n_col = lax.axis_size("row"), lax.axis_size("col")
    count = tokens.shape[1]
    top = routes.shape[3]
    capacity = count * top * 4 // (3 * n_row * n_col)
    width = tokens.shape[2]
    heads = step_bias.shape[1]
    inner = gate_norm.shape[1]
    state = conv_state.shape[2]
    wide = -(-inner // LANES) * LANES
    layers = range(2)

    def pair(own, other):
        return (jnp.where(first, own, other), jnp.where(first, other, own))

    tokens_now = lax.dynamic_index_in_dim(tokens, section_now, 0, keepdims=False)
    grad_now = lax.dynamic_index_in_dim(cotangent, section_now, 0, keepdims=False)
    wide_tokens = spread(tokens_now.astype(HALF))

    halves = (
        jnp.concatenate([widened(proj_gate[0], wide), proj_state[0]], axis=1),
        jnp.concatenate([widened(proj_input[0], wide), widened(proj_step[0], state)], axis=1),
    )
    keep, give = jnp.where(first, *halves), jnp.where(first, *halves[::-1])
    mine = pair(keep, swapped(give))

    def both_halves(half):
        whole = lax.all_gather(half, ("section", "row"), axis=0, tiled=True)
        return whole.reshape(2, n_row * half.shape[0], half.shape[1])

    proj = [both_halves(mine[0])]

    def both_layers(weight):
        whole = lax.all_gather(weight, ("section", "row"), axis=0, tiled=True)
        return whole.reshape(2, n_row * weight.shape[0], weight.shape[1])

    proj_out = both_layers(widened(proj_output[0], wide))
    gate_all = lax.all_gather(expert_gate[0, 0], "section")
    up_all = lax.all_gather(expert_up[0, 0], "section")
    down_all = lax.all_gather(expert_down[0, 0], "section")
    shared = both_layers(jnp.concatenate([shared_gate[0], shared_up[0], shared_down[0]], axis=1))
    experts = [(gate_all[s], up_all[s], down_all[s]) for s in layers]

    small_in = (
        norm_in[0],
        norm_mid[0],
        widened(conv_input[0], wide),
        conv_state[0],
        widened(jnp.concatenate([step_bias, decay_log], axis=0), LANES),
        widened(jnp.concatenate([gate_norm, jnp.repeat(skip_gain, HEAD, axis=1)], axis=0), wide),
    )
    vector = flat(small_in)
    small_all = [unflat(part, [v.shape for v in small_in]) for part in pair(vector, swapped(vector))]
    norm_ins = [part[0] for part in small_all]
    norm_mids = [part[1] for part in small_all]

    meta = jnp.concatenate([routes.astype(FLOAT), gates], axis=3)[0]
    keep = lax.dynamic_index_in_dim(meta, section_now, 0, keepdims=False)
    give = lax.dynamic_index_in_dim(meta, 1 - section_now, 0, keepdims=False)
    meta = jnp.concatenate(pair(keep, swapped(give)), axis=1)

    lengths = lax.dynamic_slice(
        doc_lengths, (section_now, row_now, 0), (1, 1, doc_lengths.shape[2])
    )
    labels = local_docs(lengths[0, 0], row_now, n_col * count)
    marks = [labels.astype(FLOAT)]
    for back in range(1, conv_input.shape[1]):
        prior = jnp.pad(labels, (back, 0), constant_values=-1)[:-back]
        marks.append((prior == labels).astype(FLOAT))
    marks = jnp.stack(marks, axis=1)
    label_row = labels.astype(FLOAT)[None]
    place = turn()
    mixers = [
        (conv_in, conv_st, step_row, wide_row, marks, label_row, place)
        for _, _, conv_in, conv_st, step_row, wide_row in small_all
    ]

    def mix_in(s, wide_in):
        pre = [project(wide_in, half) for half in proj[s]]
        return pre, *mixer_forward(pre, heads, wide, mixers[s])

    def mix_out(s, resid, scaled, total_part, meanwhile):
        whole = line_product([scaled], [proj_out[s]])
        sums = gathered_sum(jnp.concatenate([whole, as_halves(total_part)], axis=1), meanwhile)
        mixed, total = sums[:, :width], from_halves(sums[:, width:], 1)
        rr = lax.rsqrt(total / DI + EPS)
        return resid + mixed * rr, mixed, rr

    wide_in_0 = rms_norm(wide_tokens.astype(FLOAT), norm_ins[0]).astype(HALF)
    pre_0, y_0, scaled_0, total_0 = mix_in(0, wide_in_0)
    tables = route_tables(spread(after(meta, scaled_0)), top, capacity, 2)
    plain = [table[0] for table in tables]
    scaling = [table[1] for table in tables]
    middle_0, mixed_0, rr_0 = mix_out(0, tokens_now, scaled_0, total_0, tables)
    kept = {}

    def expert_0(rows):
        kept["rows 0"], answer = expert_forward(rows, experts[0])
        return answer

    def own_0(block, rows):
        kept["shared 0"] = shared_forward(block, shared[0])
        return kept["shared 0"]

    def beside_0(result):
        return home_part(scaling[0], result, kept["shared 0"][2], shared[0])

    def aside_0(blocks):
        kept["grads"] = spread(after(grad_now.astype(HALF), blocks))
        return kept["grads"]

    parts, rows_0, mids_0 = through_experts(
        rms_norm(middle_0, norm_mids[0]).astype(HALF), plain[0], expert_0, own_0, beside_0, aside_0
    )
    proj.append(both_halves(after(mine[1], parts)))
    out_0 = middle_0 + gathered_sum(parts)

    wide_in_1 = spread(rms_norm(out_0, norm_ins[1]).astype(HALF))
    grad_tokens_1 = after(kept["grads"], out_0)
    grad_rows_1 = to_experts(project(scaling[1], grad_tokens_1))
    pre_1, y_1, scaled_1, total_1 = mix_in(1, wide_in_1)
    scaled_1 = after(scaled_1, grad_rows_1)
    middle_1, mixed_1, rr_1 = mix_out(1, out_0, scaled_1, total_1, ())

    def expert_1(rows):
        kept["rows 1"], kept["answer 1"] = expert_forward(rows, experts[1])
        kept["grads 1"], back = expert_backward(grad_rows_1, kept["rows 1"], experts[1])
        return back

    def own_1(block, rows):
        kept["shared 1"] = shared_forward(block, shared[1])
        kept["shared grads 1"], kept["part 1"] = shared_backward(
            grad_tokens_1, kept["shared 1"], shared[1]
        )
        kept["sums 1"] = weight_sums(
            rows,
            grad_rows_1,
            kept["rows 1"],
            kept["grads 1"],
            block,
            grad_tokens_1,
            kept["shared 1"],
            kept["shared grads 1"],
        )
        experts_1, shared_1 = kept["sums 1"]
        return experts_1, [made[-1] for made in shared_1]

    def beside_1(result):
        return (kept["part 1"] + outer(plain[1], result)).astype(HALF)

    parts, rows_1, mids_1 = through_experts(
        rms_norm(middle_1, norm_mids[1]).astype(HALF), plain[1], expert_1, own_1, beside_1
    )
    answer_1 = to_experts(after(kept["answer 1"], parts))

    def mixer_back(s, grad_middle, along, rr, saved, meanwhile):
        wide_in, pre, y, scaled = saved
        sides = as_halves(jnp.concatenate([rr, along], axis=1))
        payload = spread(
            jnp.concatenate([grad_middle.astype(HALF), sides], axis=1), meanwhile
        )
        wide_mix, sides = payload[:, :width], from_halves(payload[:, width:], 2)
        grad_scaled = project(wide_mix, proj_out[s])
        *grad_pre, wide_grads, grad_conv_input, grad_conv_state, step_grads = mixer_backward(
            pre, y, grad_scaled, sides, heads, mixers[s]
        )
        ends = [part[:, :wide] for part in grad_pre]
        tail = jnp.concatenate([grad_pre[0][:, wide:], grad_pre[1][:, wide : wide + LANES]], axis=1)
        mix_rr = (wide_mix * sides[:, :1]).astype(HALF)
        rest = (grad_conv_state, grad_conv_input, wide_grads, step_grads)
        return grad_pre, (wide_in, *ends), (mix_rr, *two_halves(scaled)), tail, rest

    def resid_back(resid, norm, grad_normed, grad_middle):
        _, pull_in = jax.vjp(rms_norm, resid, norm)
        grad_resid, grad_norm = pull_in(grad_normed)
        return grad_resid + grad_middle, grad_norm

    def own_layer(first_value, second_value):
        keep = jnp.where(first, first_value, second_value)
        give = jnp.where(first, second_value, first_value).astype(HALF)
        return keep.astype(FLOAT), swapped(give)

    def row_sums(value):
        return lax.psum_scatter(value, "row", scatter_dimension=0, tiled=True)

    grad_middle, along, grad_norm_mid_1 = middle_backward(
        gathered_sum(parts, answer_1), grad_now, middle_1, mixed_1, norm_mids[1]
    )
    expert_grads_1, shared_grads_1 = kept["sums 1"]
    home = home_part(scaling[1], answer_1, kept["shared 1"][2], shared[1])
    grad_pre, to_proj, to_out, tail, rest_1 = mixer_back(
        1,
        grad_middle,
        along,
        rr_1,
        (wide_in_1, pre_1, y_1, scaled_1),
        home,
    )
    whole = line_product(grad_pre, proj[1])
    grad_in = gathered_sum(whole)
    grad_1, grad_norm_in_1 = resid_back(out_0, norm_ins[1], grad_in, grad_middle)

    def aside_back_0(blocks):
        own_proj, own_out, own_tail = after((to_proj, to_out, tail), blocks)
        given, given_out = half_to_give(*own_proj), half_to_give(*own_out)
        made = (*shared_grads_1, (*own_out, swapped(given_out)), (*own_proj, swapped(given)))
        made = [half_to_keep(*each) for each in after(made, (given, given_out))]
        kept["sent 1"] = [row_sums(each) for each in made]
        kept["tail 1"] = outer(own_proj[0], own_tail).astype(HALF)
        kept["home"] = home
        if groups() > 1:
            kept["home"] = in_order([block_of(home, back) for back in range(groups())], "col")
        kept["home"] = lax.psum_scatter(
            after(kept["home"], made), "col", scatter_dimension=0, tiled=True
        )
        return made, kept["tail 1"]

    def expert_back_0(rows):
        kept["grads 0"], back = expert_backward(rows, kept["rows 0"], experts[0])
        return back

    def own_back_0(block, rows):
        kept["shared grads 0"], kept["part 0"] = shared_backward(block, kept["shared 0"], shared[0])
        kept["sums 0"] = weight_sums(
            rows_0,
            rows,
            kept["rows 0"],
            kept["grads 0"],
            mids_0,
            block,
            kept["shared 0"],
            kept["shared grads 0"],
        )
        experts_0, shared_0 = kept["sums 0"]
        return experts_0, [made[-1] for made in shared_0]

    def beside_back_0(result):
        return (kept["part 0"] + outer(plain[0], result)).astype(HALF)

    parts, grad_rows_0, grad_tokens_0 = through_experts(
        grad_1.astype(HALF), scaling[0], expert_back_0, own_back_0, beside_back_0, aside_back_0
    )
    sums_1, grad_tail_1 = kept["sent 1"], kept["tail 1"]
    grad_middle, along, grad_norm_mid_0 = middle_backward(
        gathered_sum(parts), grad_1, middle_0, mixed_0, norm_mids[0]
    )
    expert_grads_0, shared_grads_0 = kept["sums 0"]
    shared_sums_0 = [half_to_keep(*after(made, parts)) for made in shared_grads_0]
    sums_0 = [row_sums(made) for made in shared_sums_0]
    expert_out = [own_layer(a, b) for a, b in zip(expert_grads_0, expert_grads_1)]
    grad_pre, to_proj, to_out, tail, rest_0 = mixer_back(
        0,
        grad_middle,
        along,
        rr_0,
        (wide_in_0, pre_0, y_0, scaled_0),
        ([part[0] for part in expert_out], shared_sums_0, sums_1),
    )

    given = half_to_give(*to_proj)
    whole = line_product(after(grad_pre, given), proj[0])
    line_received = sent_home(whole)
    proj_half = half_to_keep(*after((*to_proj, swapped(given)), whole))
    proj_sums = row_sums(proj_half)
    given_out = half_to_give(*after(to_out, proj_half))
    grad_tail_0 = outer(after(wide_in_0, given_out), tail).astype(HALF)
    out_half = half_to_keep(*after((*to_out, swapped(given_out)), grad_tail_0))
    sums_0.append(row_sums(out_half))
    tail_keep, tail_other = own_layer(grad_tail_0, grad_tail_1)
    tail_pieces = row_pieces((tail_keep + tail_other.astype(FLOAT)).astype(HALF))
    tail_received = row_received(tail_pieces)
    wide_x = wide_tokens.astype(FLOAT)
    wide_r = lax.rsqrt(jnp.mean(wide_x * wide_x, axis=1, keepdims=True) + EPS)
    grad_norm_in_0 = jnp.sum(whole.astype(FLOAT) * wide_x * wide_r, axis=0)
    smalls = (
        (grad_norm_in_0, grad_norm_mid_0, *rest_0),
        (grad_norm_in_1, grad_norm_mid_1, *rest_1),
    )
    shapes = [part.shape for part in smalls[0]]
    small_keep, small_other = own_layer(flat(smalls[0]), flat(smalls[1]))
    vector = small_keep + small_other.astype(FLOAT)
    lines = [shifted(vector[None], "row", back) for back in range(n_row)]
    expert_out = [keep + other.astype(FLOAT) for keep, other in after(expert_out, out_half)]
    line_received, tail_received, lines = after((line_received, tail_received, lines), expert_out)
    grad_in = added_up(whole, line_received)
    sums_0.append(proj_sums)
    tail = total_of(tail_pieces[0], tail_received).astype(HALF)
    vector = jnp.sum(in_order(lines, "row"), axis=0)
    grad_0, _ = resid_back(tokens_now, norm_ins[0], grad_in, grad_middle)
    out_1 = middle_1 + kept["home"].astype(FLOAT)

    def own_halves(first_value, second_value):
        keep = jnp.where(first, first_value, second_value)
        give = jnp.where(first, second_value, first_value)
        return keep, swapped(give)

    def per_micro(first_value, second_value):
        keep = jnp.where(first, first_value, second_value)
        return keep, swapped(jnp.where(first, second_value, first_value).astype(HALF))

    halves = [own_halves(a, b) for a, b in zip(sums_0, sums_1)]
    outs, in_grads = per_micro(out_0, after(out_1, grad_in)), per_micro(grad_0, grad_1)
    common = 2 * width + conv_state.shape[1] * state
    state_grad = tail[:, :state]
    if groups() > 1:
        state_pieces = row_pieces(state_grad, "col")
        state_received = row_received(state_pieces, "col")
        lines = [shifted(vector[None, :common], "col", back) for back in range(n_col)]
        state_received, lines, outs, in_grads = after((state_received, lines, outs, in_grads))
        state_grad = total_of(state_pieces[0], state_received).astype(HALF)
        state_grad = in_order([shifted(state_grad, "col", back) for back in range(n_col)], "col")
        shared_sum = jnp.sum(in_order(lines, "col"), axis=0)
    else:
        state_grad = lax.psum(state_grad, "col")
        shared_sum = lax.psum(vector[:common], "col")
    halves = [pair(*half) for half in halves]
    grad_shared, grad_down, grad_out, grad_ends = halves
    grad_out, grad_down = [jnp.concatenate(both, axis=1) for both in (grad_out, grad_down)]
    (
        out_norm_in,
        out_norm_mid,
        out_conv_state,
        out_conv_input,
        out_wide,
        out_step,
    ) = unflat(jnp.concatenate([shared_sum, vector[common:]]), shapes)

    def stacked(keep, other):
        return jnp.stack(pair(keep, other.astype(FLOAT)))[None]

    def out(value):
        return value.astype(FLOAT)[None]

    return (
        stacked(*outs),
        stacked(*in_grads),
        out_norm_in[None],
        out(grad_ends[0][:, :inner]),
        out(grad_ends[1][:, :inner]),
        out(state_grad),
        out(tail[:, state : state + heads]),
        out_step[:1, :heads],
        out_step[1:, :heads],
        jnp.sum(out_wide[1, :inner].reshape(heads, HEAD), axis=1)[None],
        out_conv_input[None, :, :inner],
        out_conv_state[None],
        out_wide[:1, :inner],
        out(grad_out[:, :inner]),
        out_norm_mid[None],
        expert_out[0][None, None],
        expert_out[1][None, None],
        expert_out[2][None, None],
        out(grad_shared[0]),
        out(grad_shared[1]),
        out(grad_down),
    )


def solution(mesh):
    in_specs = (
        P(None, ("row", "col"), None),
        P(None, ("row", "col"), None),
        P(),
        P("section", None, ("row", "col"), None),
        P("section", None, ("row", "col"), None),
        P("section", None),
        P("section", "row", "col"),
        P("section", "row", "col"),
        P("section", "row", None),
        P("section", "row", "col"),
        P("section", "col"),
        P("section", "col"),
        P("section", "col"),
        P("section", None, "col"),
        P("section", None, None),
        P("section", "col"),
        P("section", "row", "col"),
        P("section", None),
        P("section", ("row", "col"), None, None),
        P("section", ("row", "col"), None, None),
        P("section", ("row", "col"), None, None),
        P("section", "row", "col"),
        P("section", "row", "col"),
        P("section", "row", "col"),
    )
    out_specs = (
        P("section", None, ("row", "col"), None),
        P("section", None, ("row", "col"), None),
        P("section", None),
        P("section", "row", "col"),
        P("section", "row", "col"),
        P("section", "row", None),
        P("section", "row", "col"),
        P("section", "col"),
        P("section", "col"),
        P("section", "col"),
        P("section", None, "col"),
        P("section", None, None),
        P("section", "col"),
        P("section", "row", "col"),
        P("section", None),
        P("section", ("row", "col"), None, None),
        P("section", ("row", "col"), None, None),
        P("section", ("row", "col"), None, None),
        P("section", "row", "col"),
        P("section", "row", "col"),
        P("section", "row", "col"),
    )
    return jax.shard_map(shards, mesh=mesh, in_specs=in_specs, out_specs=out_specs, check_vma=False)
```

```python
import functools

import jax
import jax.numpy as jnp
from jax import lax
from jax.experimental import pallas as pl
from jax.experimental.pallas import tpu as pltpu
from jax.sharding import PartitionSpec as P

DI = 3072
HEAD = 64
LANES = 128
CHUNK = 256
VMEM_BYTES = 48 * 2**20

EPS = 1e-05
HIGH = lax.Precision.HIGHEST
FLOAT = jnp.float32
HALF = jnp.bfloat16


def shifted(block, axis, distance):
    count = lax.axis_size(axis)
    if distance % count == 0:
        return block
    return lax.ppermute(block, axis, [(i, (i + distance) % count) for i in range(count)])


def swapped(block):
    return lax.ppermute(block, "section", [(0, 1), (1, 0)])


def after(value, *others):
    return lax.optimization_barrier((value, *others))[0]


def rms_norm(value, gain):
    return value * lax.rsqrt(jnp.mean(value * value, axis=-1, keepdims=True) + EPS) * gain


def local_docs(lengths, row_now, length):
    bounds = jnp.cumsum(lengths)[:-1]
    place = jnp.arange(length, dtype=jnp.int32)
    inner = jnp.sum((place[:, None] >= bounds[None, :]).astype(jnp.int32), axis=1)
    return inner + row_now * lengths.shape[0]


def project(left, right):
    return jnp.dot(left, right, preferred_element_type=FLOAT)


def project_back(left, right):
    return lax.dot_general(left, right, (((1,), (1,)), ((), ())), preferred_element_type=FLOAT)


def outer(left, right):
    return lax.dot_general(left, right, (((0,), (0,)), ((), ())), preferred_element_type=FLOAT)


def silu_slope(value):
    sigma = jax.nn.sigmoid(value)
    return sigma * (1.0 + value * (1.0 - sigma))


def groups():
    count = lax.axis_size("col")
    return count if count <= 4 else 1


def spread(block, meanwhile=()):
    if groups() == 1:
        return lax.all_gather(block, "col", axis=0, tiled=True)
    received = [shifted(block, "col", back) for back in range(1, groups())]
    return jnp.concatenate([block, *after(received, meanwhile)], axis=0)


def in_order(blocks, axis):
    count = len(blocks)
    if count == 1:
        return blocks[0]
    rows = blocks[0].shape[0]
    line = jnp.concatenate(blocks[::-1] + blocks[:0:-1], axis=0)
    start = (count - 1 - lax.axis_index(axis)) * rows
    return lax.dynamic_slice_in_dim(line, start, count * rows, axis=0)


def sent_home(rows):
    if groups() == 1:
        return lax.psum_scatter(rows, "col", scatter_dimension=0, tiled=True)
    return [shifted(block_of(rows, back), "col", -back) for back in range(1, groups())]


def added_up(rows, received):
    if groups() == 1:
        return received.astype(FLOAT)
    return sum([part.astype(FLOAT) for part in received], block_of(rows, 0).astype(FLOAT))


def gathered_sum(rows, meanwhile=()):
    return added_up(rows, after(sent_home(rows), meanwhile))


def exchanged(rows, axis):
    return lax.all_to_all(rows, axis, split_axis=0, concat_axis=0, tiled=True)


def as_halves(columns):
    high = lax.reduce_precision(columns, 8, 7)
    both = jnp.concatenate([high, columns - high], axis=1).astype(HALF)
    return jnp.pad(both, ((0, 0), (0, LANES - both.shape[1])))


def from_halves(tile, count):
    return tile[:, :count].astype(FLOAT) + tile[:, count : 2 * count].astype(FLOAT)


def block_of(values, back):
    rows = values.shape[0] // groups()
    return values[back * rows : (back + 1) * rows]


def turn():
    place = lax.axis_index("col") if groups() > 1 else jnp.int32(0)
    return place.astype(jnp.int32).reshape(1)


def chunk_of(rows, index):
    if groups() == 1:
        return rows
    own = rows.shape[0] // groups()
    return rows[own:] if index else rows[:own]


def route_tables(meta, top, capacity, layers):
    n_row, n_col = lax.axis_size("row"), lax.axis_size("col")
    place = jnp.arange(n_row)
    tables = [[] for _ in range(layers)]
    for index in range(min(groups(), 2)):
        now = chunk_of(meta, index)
        count = now.shape[0]
        slots = count * n_col * capacity // meta.shape[0]
        rows = place
        if groups() > 1 and index == 0:
            rows = lax.rem(lax.axis_index("row") + place, n_row)
        experts = (rows * n_col + lax.axis_index("col")).astype(FLOAT)
        now = now.reshape(count, layers, 2, top).transpose(1, 2, 3, 0)
        match = now[:, None, 0] == experts[None, :, None, None]
        hit = jnp.any(match, axis=2)
        weight = jnp.sum(jnp.where(match, now[:, None, 1], 0.0), axis=2)
        order = jnp.arange(count, dtype=jnp.int32)
        triangle = (order[:, None] <= order[None, :]).astype(HALF)
        rank = project(hit.astype(HALF).reshape(-1, count), triangle).reshape(hit.shape)
        slot = jnp.arange(1, slots + 1, dtype=jnp.int32).astype(FLOAT)
        chosen = (rank[:, :, None, :] == slot[:, None]) & hit[:, :, None, :]
        shape = (layers, n_row * slots, count)
        plain = chosen.astype(HALF).reshape(shape)
        scaled = jnp.where(chosen, weight[:, :, None, :], 0.0).astype(HALF).reshape(shape)
        for s in range(layers):
            tables[s].append((plain[s], scaled[s]))
    return tables


def to_experts(rows):
    return exchanged(rows.astype(HALF), "row")


def summed_rows(values, reverse):
    step = min(values.shape[0], CHUNK)
    count = values.shape[0] // step
    place = lax.broadcasted_iota(jnp.int32, (step, step), 0)
    other = lax.broadcasted_iota(jnp.int32, (step, step), 1)
    before = (place <= other) if reverse else (place >= other)
    triangle = before.astype(FLOAT)
    carry = jnp.zeros((1, values.shape[1]), FLOAT)
    parts = [None] * count
    for index in reversed(range(count)) if reverse else range(count):
        part = values[index * step : (index + 1) * step]
        run = jnp.dot(triangle, part, precision=HIGH, preferred_element_type=FLOAT) + carry
        carry = run[:1] if reverse else run[step - 1 :]
        parts[index] = run
    return parts[0] if count == 1 else jnp.concatenate(parts, axis=0)


def head_columns(rows, columns, head_width):
    head = lax.broadcasted_iota(jnp.int32, (rows, columns), 0) * head_width
    column = lax.broadcasted_iota(jnp.int32, (rows, columns), 1)
    return ((column >= head) & (column < head + head_width)).astype(FLOAT)


def sigmoid(value):
    return 1.0 / (1.0 + jnp.exp(-value))


def step_sizes(step_pre, step_row_ref):
    shifted_pre = step_pre + step_row_ref[0:1, :]
    sizes = jnp.maximum(shifted_pre, 0.0) + jnp.log1p(jnp.exp(-jnp.abs(shifted_pre)))
    return shifted_pre, sizes, -jnp.exp(step_row_ref[1:2, :])


def conv_rows(values, weight_ref, columns, marks_ref):
    width = weight_ref.shape[0]
    result = values * weight_ref[width - 1 : width, columns]
    for back in range(1, width):
        moved = pltpu.roll(values, back, 0) * marks_ref[:, back : back + 1]
        result = result + moved * weight_ref[width - 1 - back : width - back, columns]
    return result


def conv_rows_back(grad, values, weight_ref, columns, marks_ref, weight_grad_ref):
    width = weight_ref.shape[0]
    rows = values.shape[0]
    result = grad * weight_ref[width - 1 : width, columns]
    weight_grad_ref[width - 1 : width, columns] = jnp.sum(grad * values, axis=0, keepdims=True)
    for back in range(1, width):
        kept = grad * marks_ref[:, back : back + 1]
        taps = jnp.sum(kept * pltpu.roll(values, back, 0), axis=0, keepdims=True)
        weight_grad_ref[width - 1 - back : width - back, columns] = taps
        moved = pltpu.roll(kept, rows - back, 0)
        result = result + moved * weight_ref[width - 1 - back : width - back, columns]
    return result


def copy_in_order(source_ref, target_ref, place_ref, parts):
    if parts == 1:
        return source_ref
    rows = source_ref.shape[0] // parts
    for index in range(parts):
        target_ref[index * rows : (index + 1) * rows, :] = source_ref[
            block_rows(index, rows, place_ref, parts), :
        ]
    return target_ref


def block_rows(index, rows, place_ref, parts):
    if parts == 1:
        return slice(0, rows)
    back = lax.rem(place_ref[0] - index + parts, parts)
    return pl.ds(pl.multiple_of(back * rows, rows), rows)


def mixer_forward_kernel(
    heads,
    parts,
    pre_in_ref,
    pre_other_in_ref,
    conv_input_ref,
    conv_state_ref,
    step_row_ref,
    wide_row_ref,
    marks_ref,
    labels_ref,
    place_ref,
    y_ref,
    scaled_ref,
    total_ref,
    pre_ref,
    pre_other_ref,
    x_ref,
    dosed_ref,
    keys_ref,
    queries_ref,
):
    length, wide = y_ref.shape
    states = conv_state_ref.shape[1] // 2
    state_at, step_at = wide, wide
    head_width = HEAD
    pre_ref = copy_in_order(pre_in_ref, pre_ref, place_ref, parts)
    pre_other_ref = copy_in_order(pre_other_in_ref, pre_other_ref, place_ref, parts)
    _, sizes, rate = step_sizes(pre_other_ref[:, step_at : step_at + LANES], step_row_ref)
    running = summed_rows(sizes * rate, False)
    running_t = running.T
    expand = head_columns(LANES, wide, head_width)
    for start in range(0, wide, LANES):
        columns = slice(start, start + LANES)
        conv = conv_rows(
            pre_other_ref[:, columns], conv_input_ref, columns, marks_ref
        )
        x = conv * sigmoid(conv)
        x_ref[:, columns] = x
        dose = jnp.dot(sizes, expand[:, columns], precision=HIGH, preferred_element_type=FLOAT)
        dosed_ref[:, columns] = (x * dose).astype(HALF)
    for part, target in ((0, keys_ref), (1, queries_ref)):
        columns = slice(part * states, (part + 1) * states)
        conv = conv_rows(
            pre_ref[:, state_at + part * states : state_at + (part + 1) * states],
            conv_state_ref,
            columns,
            marks_ref,
        )
        target[...] = (conv * sigmoid(conv)).astype(HALF)
    block = min(length, CHUNK)
    place = lax.broadcasted_iota(jnp.int32, (block, block), 0)
    other = lax.broadcasted_iota(jnp.int32, (block, block), 1)
    for late in range(length // block):
        rows = slice(late * block, (late + 1) * block)
        for early in range(late + 1):
            past = slice(early * block, (early + 1) * block)
            same = marks_ref[rows, 0:1] == labels_ref[:, past]
            if late == early:
                same = same & (place >= other)
            mask = jnp.where(same, 0.0, -1e30)
            scores = lax.dot_general(
                queries_ref[rows, :],
                keys_ref[past, :],
                (((1,), (1,)), ((), ())),
                preferred_element_type=FLOAT,
            )
            for head in range(heads):
                columns = slice(head * head_width, (head + 1) * head_width)
                spread_log = running[rows, head : head + 1] - running_t[head : head + 1, past]
                mixing = (jnp.exp(spread_log + mask) * scores).astype(HALF)
                inner = jnp.dot(mixing, dosed_ref[past, columns], preferred_element_type=FLOAT)
                if early == 0:
                    y_ref[rows, columns] = inner
                else:
                    y_ref[rows, columns] += inner
    total = jnp.zeros((length, 1), FLOAT)
    for start in range(0, wide, LANES):
        columns = slice(start, start + LANES)
        y = y_ref[:, columns]
        if heads * head_width < start + LANES:
            lane = lax.broadcasted_iota(jnp.int32, y.shape, 1) + start
            y = jnp.where(lane < heads * head_width, y, 0.0)
        y = y + wide_row_ref[1:2, columns] * x_ref[:, columns]
        gate = pre_ref[:, columns]
        gated = y * gate * sigmoid(gate)
        y_ref[:, columns] = y
        scaled = (gated * wide_row_ref[0:1, columns]).astype(HALF)
        each = length // parts
        for index in range(parts):
            block_at = block_rows(index, each, place_ref, parts)
            scaled_ref[block_at, columns] = scaled[index * each : (index + 1) * each]
        total = total + jnp.sum(gated * gated, axis=1, keepdims=True)
    each = length // parts
    for index in range(parts):
        block_at = block_rows(index, each, place_ref, parts)
        total_ref[block_at, :] = total[index * each : (index + 1) * each]


def mixer_backward_kernel(
    heads,
    parts,
    inner_all,
    pre_in_ref,
    pre_other_in_ref,
    y_ref,
    grad_in_ref,
    sides_in_ref,
    conv_input_ref,
    conv_state_ref,
    step_row_ref,
    wide_row_ref,
    marks_ref,
    labels_ref,
    place_ref,
    grad_pre_ref,
    grad_pre_other_ref,
    wide_grad_ref,
    conv_input_grad_ref,
    conv_state_grad_ref,
    step_grad_ref,
    pre_ref,
    pre_other_ref,
    grad_ref,
    sides_ref,
    x_ref,
    dosed_ref,
    dose_ref,
    slope_ref,
    dy_ref,
    z_ref,
    bc_ref,
    bc_slope_ref,
    bc_grad_ref,
):
    length, wide = y_ref.shape
    states = conv_state_ref.shape[1] // 2
    state_at, step_at = wide, wide
    head_width = HEAD
    each = length // parts
    pre_ref = copy_in_order(pre_in_ref, pre_ref, place_ref, parts)
    pre_other_ref = copy_in_order(pre_other_in_ref, pre_other_ref, place_ref, parts)
    grad_ref = copy_in_order(grad_in_ref, grad_ref, place_ref, parts)
    sides_ref = copy_in_order(sides_in_ref, sides_ref, place_ref, parts)

    def put(target_ref, value, start):
        for index in range(parts):
            target_ref[block_rows(index, each, place_ref, parts), start : start + LANES] = value[
                index * each : (index + 1) * each
            ]

    shifted_pre, sizes, rate = step_sizes(pre_other_ref[:, step_at : step_at + LANES], step_row_ref)
    running = summed_rows(sizes * rate, False)
    running_t = running.T
    expand = head_columns(LANES, wide, head_width)
    rr = sides_ref[:, 0:1]
    pull = rr * rr * rr * sides_ref[:, 1:2] * (1.0 / inner_all)
    for start in range(0, wide, LANES):
        columns = slice(start, start + LANES)
        gate = pre_ref[:, columns]
        y = y_ref[:, columns]
        grad = grad_ref[:, columns]
        gain = wide_row_ref[0:1, columns]
        sigma = sigmoid(gate)
        silu = gate * sigma
        gated = y * silu
        normed = gated * rr
        wide_grad_ref[0:1, columns] = jnp.sum(grad * normed, axis=0, keepdims=True)
        grad_gated = rr * gain * grad - gated * pull
        slope = sigma * (1.0 + gate * (1.0 - sigma))
        put(grad_pre_ref, (grad_gated * y * slope).astype(HALF), start)
        dy = grad_gated * silu
        dy_ref[:, columns] = dy
        conv = conv_rows(
            pre_other_ref[:, columns], conv_input_ref, columns, marks_ref
        )
        sigma = sigmoid(conv)
        x = conv * sigma
        x_ref[:, columns] = x
        slope_ref[:, columns] = sigma * (1.0 + conv * (1.0 - sigma))
        dose = jnp.dot(sizes, expand[:, columns], precision=HIGH, preferred_element_type=FLOAT)
        dose_ref[:, columns] = dose
        dosed_ref[:, columns] = (x * dose).astype(HALF)
        wide_grad_ref[1:2, columns] = jnp.sum(dy * x, axis=0, keepdims=True)
    for start in range(0, 2 * states, LANES):
        columns = slice(start, start + LANES)
        conv = conv_rows(
            pre_ref[:, state_at + start : state_at + start + LANES],
            conv_state_ref,
            columns,
            marks_ref,
        )
        sigma = sigmoid(conv)
        bc_ref[:, columns] = (conv * sigma).astype(HALF)
        bc_slope_ref[:, columns] = sigma * (1.0 + conv * (1.0 - sigma))
    block = min(length, CHUNK)
    place = lax.broadcasted_iota(jnp.int32, (block, block), 0)
    other = lax.broadcasted_iota(jnp.int32, (block, block), 1)
    z_ref[...] = jnp.zeros(z_ref.shape, FLOAT)
    bc_grad_ref[...] = jnp.zeros(bc_grad_ref.shape, FLOAT)
    for late in range(length // block):
        rows = slice(late * block, (late + 1) * block)
        for early in range(late + 1):
            past = slice(early * block, (early + 1) * block)
            same = marks_ref[past, 0:1] == labels_ref[:, rows]
            if late == early:
                same = same & (place <= other)
            mask = jnp.where(same, 0.0, -1e30)
            keys = bc_ref[past, :states]
            queries = bc_ref[rows, states:]
            scores = lax.dot_general(
                keys, queries, (((1,), (1,)), ((), ())), preferred_element_type=FLOAT
            )
            mixed = jnp.zeros((block, block), FLOAT)
            for head in range(heads):
                columns = slice(head * head_width, (head + 1) * head_width)
                spread_log = running_t[head : head + 1, rows] - running[past, head : head + 1]
                decay = jnp.exp(spread_log + mask)
                mixing = (decay * scores).astype(HALF)
                dy = dy_ref[rows, columns].astype(HALF)
                z_ref[past, columns] += jnp.dot(mixing, dy, preferred_element_type=FLOAT)
                along = lax.dot_general(
                    dosed_ref[past, columns],
                    dy,
                    (((1,), (1,)), ((), ())),
                    preferred_element_type=FLOAT,
                )
                mixed = mixed + decay * along
            mixed = mixed.astype(HALF)
            bc_grad_ref[past, :states] += jnp.dot(mixed, queries, preferred_element_type=FLOAT)
            bc_grad_ref[rows, states:] += lax.dot_general(
                mixed, keys, (((0,), (0,)), ((), ())), preferred_element_type=FLOAT
            )
    direct = jnp.zeros((length, LANES), FLOAT)
    balance = jnp.zeros((length, LANES), FLOAT)
    for start in range(0, wide, LANES):
        columns = slice(start, start + LANES)
        x, z, dy = x_ref[:, columns], z_ref[:, columns], dy_ref[:, columns]
        skip = wide_row_ref[1:2, columns]
        collapse = (((1,), (1,)), ((), ()))
        both = dy.astype(HALF).astype(FLOAT) * (y_ref[:, columns] - skip * x)
        both = both - dosed_ref[:, columns].astype(FLOAT) * z
        heads_of = expand[:, columns]
        direct = direct + lax.dot_general(
            x * z, heads_of, collapse, precision=HIGH, preferred_element_type=FLOAT
        )
        balance = balance + lax.dot_general(
            both, heads_of, collapse, precision=HIGH, preferred_element_type=FLOAT
        )
        grad_conv = (dose_ref[:, columns] * z + skip * dy) * slope_ref[:, columns]
        grad_in = conv_rows_back(
            grad_conv,
            pre_other_ref[:, columns],
            conv_input_ref,
            columns,
            marks_ref,
            conv_input_grad_ref,
        )
        put(grad_pre_other_ref, grad_in.astype(HALF), start)
    for start in range(0, 2 * states, LANES):
        columns = slice(start, start + LANES)
        grad_in = conv_rows_back(
            bc_grad_ref[:, columns] * bc_slope_ref[:, columns],
            pre_ref[:, state_at + start : state_at + start + LANES],
            conv_state_ref,
            columns,
            marks_ref,
            conv_state_grad_ref,
        )
        put(grad_pre_ref, grad_in.astype(HALF), state_at + start)
    crossing = summed_rows(balance, True)
    grad_step = (direct + rate * crossing) * sigmoid(shifted_pre)
    put(grad_pre_other_ref, grad_step.astype(HALF), step_at)
    for start in range(step_at + LANES, grad_pre_other_ref.shape[1], LANES):
        put(grad_pre_other_ref, jnp.zeros((length, LANES), HALF), start)
    step_grad_ref[0:1, :] = jnp.sum(grad_step, axis=0, keepdims=True)
    step_grad_ref[1:2, :] = rate * jnp.sum(sizes * crossing, axis=0, keepdims=True)


def ordered_copy(shape):
    return pltpu.VMEM(shape if groups() > 1 else (8, LANES), FLOAT)


def whole_call(kernel, inputs, results, scratch, name):
    whole = pl.BlockSpec(memory_space=pltpu.VMEM)
    place = pl.BlockSpec(memory_space=pltpu.SMEM)
    return pl.pallas_call(
        kernel,
        in_specs=[whole] * (inputs - 1) + [place],
        out_shape=results,
        scratch_shapes=scratch,
        compiler_params=pltpu.CompilerParams(vmem_limit_bytes=VMEM_BYTES),
        name=name,
    )


def mixer_forward(pre, heads, wide, mixer):
    length = pre[0].shape[0]
    kernel = functools.partial(mixer_forward_kernel, heads, groups())
    states = mixer[1].shape[1] // 2
    return whole_call(
        kernel,
        2 + len(mixer),
        (
            jax.ShapeDtypeStruct((length, wide), FLOAT),
            jax.ShapeDtypeStruct((length, wide), HALF),
            jax.ShapeDtypeStruct((length, 1), FLOAT),
        ),
        [
            ordered_copy(pre[0].shape),
            ordered_copy(pre[1].shape),
            pltpu.VMEM((length, wide), FLOAT),
            pltpu.VMEM((length, wide), HALF),
            pltpu.VMEM((length, states), HALF),
            pltpu.VMEM((length, states), HALF),
        ],
        "mixer_forward",
    )(*pre, *mixer)


def mixer_backward(pre, y, grad, sides, heads, mixer):
    length, wide = y.shape
    kernel = functools.partial(mixer_backward_kernel, heads, groups(), DI)
    double = mixer[1].shape[1]
    square = pltpu.VMEM((length, wide), FLOAT)
    return whole_call(
        kernel,
        5 + len(mixer),
        (
            jax.ShapeDtypeStruct(pre[0].shape, HALF),
            jax.ShapeDtypeStruct(pre[1].shape, HALF),
            jax.ShapeDtypeStruct((2, wide), FLOAT),
            jax.ShapeDtypeStruct((4, wide), FLOAT),
            jax.ShapeDtypeStruct((4, double), FLOAT),
            jax.ShapeDtypeStruct((2, LANES), FLOAT),
        ),
        [
            ordered_copy(pre[0].shape),
            ordered_copy(pre[1].shape),
            ordered_copy(y.shape),
            ordered_copy(sides.shape),
            square,
            pltpu.VMEM((length, wide), HALF),
            square,
            square,
            square,
            square,
            pltpu.VMEM((length, double), HALF),
            pltpu.VMEM((length, double), FLOAT),
            pltpu.VMEM((length, double), FLOAT),
        ],
        "mixer_backward",
    )(*pre, y, grad, sides, *mixer)


def joined(parts):
    return parts[0] if len(parts) == 1 else jnp.concatenate(parts, axis=0)


def row_slices(rows):
    count = lax.axis_size("row")
    each = rows.shape[0] // count
    return [rows[index * each : (index + 1) * each] for index in range(count)]


def sent_ahead(rows):
    shares = row_slices(rows)
    return shares[0], [shifted(share, "row", ahead) for ahead, share in enumerate(shares) if ahead]


def sent_back(rows):
    shares = row_slices(rows)
    return shares[0], [shifted(share, "row", -ahead) for ahead, share in enumerate(shares) if ahead]


def through_experts(block, tables, expert, own, beside, aside=None):
    if groups() == 1:
        tokens = spread(block)
        sent = project(tables[0], tokens).astype(HALF)
        arrived = to_experts(sent)
        answer = expert(0, arrived)
        if aside is not None:
            answer = after(answer, aside(after(tokens, sent)))
        answered = to_experts(answer)
        answered = after(answered, own(after(tokens, answer), after([arrived], answer)))
        return gathered_sum(beside(0, answered)), [arrived], tokens
    count = block.shape[0]
    first, others = sent_ahead(project(tables[0], block).astype(HALF))
    line = [shifted(block, "col", back) for back in range(1, groups())]
    others, line = after((others, line))
    tokens = jnp.concatenate([block, *line], axis=0)
    rows_own = jnp.concatenate([first, *others], axis=0)
    sent = project(tables[1], chunk_of(tokens, 1)).astype(HALF)
    arrived = to_experts(sent)
    answer_own = expert(0, after(rows_own, sent))
    held = () if aside is None else aside(after(tokens, sent))
    answer = after(expert(1, arrived), answer_own, held)
    answered = to_experts(answer)
    answered = after(answered, own(after(tokens, answer), after([rows_own, arrived], answer)))
    part = beside(1, answered)
    first, others = sent_back(answer_own)
    line = [
        shifted(part[at * count : (at + 1) * count], "col", -at - 1) for at in range(groups() - 1)
    ]
    others, line = after((others, line))
    total = beside(0, jnp.concatenate([first, *others], axis=0)).astype(FLOAT)
    return sum([each.astype(FLOAT) for each in line], total), [rows_own, arrived], tokens


def line_product(values, weights):
    return sum(project_back(value, weight) for value, weight in zip(values, weights)).astype(HALF)


def expert_forward(rows, experts):
    gate_e = project(rows, experts[0])
    lift_e = project(rows, experts[1])
    act_e = (jax.nn.silu(gate_e) * lift_e).astype(HALF)
    return (gate_e, lift_e, act_e), project(act_e, experts[2]).astype(HALF)


def expert_backward(rows, kept, experts):
    gate_e, lift_e, _ = kept
    grad_act = project_back(rows, experts[2])
    grad_gate = (grad_act * lift_e * silu_slope(gate_e)).astype(HALF)
    grad_lift = (grad_act * jax.nn.silu(gate_e)).astype(HALF)
    back = project_back(grad_gate, experts[0]) + project_back(grad_lift, experts[1])
    return (grad_gate, grad_lift), back.astype(HALF)


def shared_forward(tokens, shared):
    hidden = shared.shape[1] // 3
    gate_s = project(tokens, shared[:, :hidden])
    lift_s = project(tokens, shared[:, hidden : 2 * hidden])
    return gate_s, lift_s, (jax.nn.silu(gate_s) * lift_s).astype(HALF)


def shared_backward(tokens, kept, shared):
    hidden = shared.shape[1] // 3
    gate_s, lift_s, _ = kept
    grad_act = project(tokens, shared[:, 2 * hidden :])
    grad_gate = (grad_act * lift_s * silu_slope(gate_s)).astype(HALF)
    grad_lift = (grad_act * jax.nn.silu(gate_s)).astype(HALF)
    part = project_back(grad_gate, shared[:, :hidden])
    part = part + project_back(grad_lift, shared[:, hidden : 2 * hidden])
    return (grad_gate, grad_lift), part


def home_part(act_s, shared):
    return project_back(act_s, shared[:, 2 * (shared.shape[1] // 3) :])


def weight_sums(rows_in, rows_out, kept, grads, tokens_in, tokens_out, kept_s, grads_s):
    rows_in, rows_out = joined(rows_in), joined(rows_out)
    experts = (
        outer(rows_in, joined([grads[index][0] for index in grads])).astype(HALF),
        outer(rows_in, joined([grads[index][1] for index in grads])).astype(HALF),
        outer(joined([kept[index][2] for index in kept]), rows_out).astype(HALF),
    )
    shared = ((tokens_in, *grads_s), (tokens_out, *two_halves(kept_s[2])))
    return experts, [(*each, swapped(half_to_give(*each))) for each in shared]


def middle_backward(grad_normed, grad_out, middle, mixed, norm_mid):
    _, pull_mid = jax.vjp(rms_norm, middle, norm_mid)
    grad_middle, grad_norm_mid = pull_mid(grad_normed)
    grad_middle = grad_middle + grad_out
    along = jnp.sum(grad_middle * mixed, axis=1, keepdims=True)
    return grad_middle, along, grad_norm_mid


def two_halves(values):
    middle = values.shape[1] // 2
    return values[:, :middle], values[:, middle:]


def half_to_give(left, first_right, second_right):
    first = lax.axis_index("section") == 0
    return outer(left, jnp.where(first, second_right, first_right)).astype(HALF)


def half_to_keep(left, first_right, second_right, given):
    first = lax.axis_index("section") == 0
    keep = outer(left, jnp.where(first, first_right, second_right))
    return (keep + given.astype(FLOAT)).astype(HALF)


def row_pieces(values, axis="row"):
    count = lax.axis_size(axis)
    rows = values.shape[0] // count
    index = [lax.rem(lax.axis_index(axis) + ahead, count) * rows for ahead in range(count)]
    return [lax.dynamic_slice_in_dim(values, at, rows, axis=0) for at in index]


def total_of(own, received):
    return sum([part.astype(FLOAT) for part in received], own.astype(FLOAT))


def row_received(pieces, axis="row"):
    return [shifted(piece, axis, ahead) for ahead, piece in enumerate(pieces) if ahead]


def flat(parts):
    return jnp.concatenate([part.reshape(-1) for part in parts])


def unflat(vector, shapes):
    result, start = [], 0
    for shape in shapes:
        size = 1
        for entry in shape:
            size *= entry
        result.append(vector[start : start + size].reshape(shape))
        start += size
    return result


def widened(value, columns):
    return jnp.pad(value, ((0, 0), (0, columns - value.shape[1])))


def shards(
    tokens,
    cotangent,
    doc_lengths,
    routes,
    gates,
    norm_in,
    proj_gate,
    proj_input,
    proj_state,
    proj_step,
    step_bias,
    decay_log,
    skip_gain,
    conv_input,
    conv_state,
    gate_norm,
    proj_output,
    norm_mid,
    expert_gate,
    expert_up,
    expert_down,
    shared_gate,
    shared_up,
    shared_down,
):
    section_now = lax.axis_index("section")
    first = section_now == 0
    row_now = lax.axis_index("row")
    n_row, n_col = lax.axis_size("row"), lax.axis_size("col")
    count = tokens.shape[1]
    top = routes.shape[3]
    capacity = count * top * 4 // (3 * n_row * n_col)
    width = tokens.shape[2]
    heads = step_bias.shape[1]
    inner = gate_norm.shape[1]
    state = conv_state.shape[2]
    wide = -(-inner // LANES) * LANES
    layers = range(2)

    def pair(own, other):
        return (jnp.where(first, own, other), jnp.where(first, other, own))

    tokens_now = lax.dynamic_index_in_dim(tokens, section_now, 0, keepdims=False)
    grad_now = lax.dynamic_index_in_dim(cotangent, section_now, 0, keepdims=False)
    wide_tokens = spread(tokens_now.astype(HALF))

    halves = (
        jnp.concatenate([widened(proj_gate[0], wide), proj_state[0]], axis=1),
        jnp.concatenate([widened(proj_input[0], wide), widened(proj_step[0], state)], axis=1),
    )
    keep, give = jnp.where(first, *halves), jnp.where(first, *halves[::-1])
    mine = pair(keep, swapped(give))

    def both_halves(half):
        whole = lax.all_gather(half, ("section", "row"), axis=0, tiled=True)
        return whole.reshape(2, n_row * half.shape[0], half.shape[1])

    def both_layers(weight):
        whole = lax.all_gather(weight, ("section", "row"), axis=0, tiled=True)
        return whole.reshape(2, n_row * weight.shape[0], weight.shape[1])

    proj = [both_halves(mine[0])]
    halves = two_halves(widened(proj_output[0], wide))
    keep, give = jnp.where(first, *halves), jnp.where(first, *halves[::-1])
    mine_out = pair(keep, swapped(give))
    proj_out = [both_halves(mine_out[0])]
    gate_all = lax.all_gather(expert_gate[0, 0], "section")
    up_all = lax.all_gather(expert_up[0, 0], "section")
    down_all = lax.all_gather(expert_down[0, 0], "section")
    shared = both_layers(jnp.concatenate([shared_gate[0], shared_up[0], shared_down[0]], axis=1))
    experts = [(gate_all[s], up_all[s], down_all[s]) for s in layers]

    small_in = (
        norm_in[0],
        norm_mid[0],
        widened(conv_input[0], wide),
        conv_state[0],
        widened(jnp.concatenate([step_bias, decay_log], axis=0), LANES),
        widened(jnp.concatenate([gate_norm, jnp.repeat(skip_gain, HEAD, axis=1)], axis=0), wide),
    )
    vector = flat(small_in)
    small_all = [unflat(part, [v.shape for v in small_in]) for part in pair(vector, swapped(vector))]
    norm_ins = [part[0] for part in small_all]
    norm_mids = [part[1] for part in small_all]

    meta = jnp.concatenate([routes.astype(FLOAT), gates], axis=3)[0]
    keep = lax.dynamic_index_in_dim(meta, section_now, 0, keepdims=False)
    give = lax.dynamic_index_in_dim(meta, 1 - section_now, 0, keepdims=False)
    meta = jnp.concatenate(pair(keep, swapped(give)), axis=1)

    lengths = lax.dynamic_slice(
        doc_lengths, (section_now, row_now, 0), (1, 1, doc_lengths.shape[2])
    )
    labels = local_docs(lengths[0, 0], row_now, n_col * count)
    marks = [labels.astype(FLOAT)]
    for back in range(1, conv_input.shape[1]):
        prior = jnp.pad(labels, (back, 0), constant_values=-1)[:-back]
        marks.append((prior == labels).astype(FLOAT))
    marks = jnp.stack(marks, axis=1)
    label_row = labels.astype(FLOAT)[None]
    place = turn()
    mixers = [
        (conv_in, conv_st, step_row, wide_row, marks, label_row, place)
        for _, _, conv_in, conv_st, step_row, wide_row in small_all
    ]

    def mix_in(s, wide_in):
        pre = [project(wide_in, half) for half in proj[s]]
        return pre, *mixer_forward(pre, heads, wide, mixers[s])

    def mix_out(s, resid, scaled, total_part, meanwhile):
        whole = line_product(two_halves(scaled), proj_out[s])
        sums = gathered_sum(jnp.concatenate([whole, as_halves(total_part)], axis=1), meanwhile)
        mixed, total = sums[:, :width], from_halves(sums[:, width:], 1)
        rr = lax.rsqrt(total / DI + EPS)
        return resid + mixed * rr, mixed, rr

    wide_in_0 = rms_norm(wide_tokens.astype(FLOAT), norm_ins[0]).astype(HALF)
    pre_0, y_0, scaled_0, total_0 = mix_in(0, wide_in_0)
    tables = route_tables(spread(after(meta, scaled_0)), top, capacity, 2)
    plain = [[table[0] for table in tables[s]] for s in layers]
    scaling = [[table[1] for table in tables[s]] for s in layers]
    middle_0, mixed_0, rr_0 = mix_out(0, tokens_now, scaled_0, total_0, tables)
    kept = {name: {} for name in ("rows 0", "rows 1", "answer 1", "grads 0", "grads 1")}

    def expert_0(index, rows):
        kept["rows 0"][index], answer = expert_forward(rows, experts[0])
        return answer

    def own_0(tokens_all, rows):
        kept["shared 0"] = shared_forward(tokens_all, shared[0])
        kept["part 0"] = home_part(kept["shared 0"][2], shared[0])
        return kept["part 0"]

    def beside_0(index, result):
        part = outer(scaling[0][index], result) + chunk_of(kept["part 0"], index)
        return part.astype(HALF)

    def aside_0(tokens_all):
        kept["grads"] = spread(after(grad_now.astype(HALF), tokens_all))
        return kept["grads"]

    total, rows_0, mids_0 = through_experts(
        rms_norm(middle_0, norm_mids[0]).astype(HALF), plain[0], expert_0, own_0, beside_0, aside_0
    )
    proj.append(both_halves(after(mine[1], kept["part 0"])))
    proj_out.append(both_halves(after(mine_out[1], kept["part 0"])))
    out_0 = middle_0 + total

    wide_in_1 = spread(rms_norm(out_0, norm_ins[1]).astype(HALF))
    grad_tokens_1 = after(kept["grads"], out_0)
    grad_sent = [
        project(table, chunk_of(grad_tokens_1, index)).astype(HALF)
        for index, table in enumerate(scaling[1])
    ]
    grad_rows_1 = [to_experts(grad_sent[-1])]
    if groups() > 1:
        own_rows, others = sent_ahead(grad_sent[0])
        grad_rows_1 = [jnp.concatenate([own_rows, *others], axis=0), *grad_rows_1]
    pre_1, y_1, scaled_1, total_1 = mix_in(1, wide_in_1)
    scaled_1 = after(scaled_1, grad_rows_1)
    middle_1, mixed_1, rr_1 = mix_out(1, out_0, scaled_1, total_1, ())

    def expert_1(index, rows):
        kept["rows 1"][index], kept["answer 1"][index] = expert_forward(rows, experts[1])
        kept["grads 1"][index], back = expert_backward(
            grad_rows_1[index], kept["rows 1"][index], experts[1]
        )
        return back

    def own_1(tokens_all, rows):
        kept["shared 1"] = shared_forward(tokens_all, shared[1])
        kept["shared grads 1"], kept["part 1"] = shared_backward(
            grad_tokens_1, kept["shared 1"], shared[1]
        )
        kept["sums 1"] = weight_sums(
            rows,
            grad_rows_1,
            kept["rows 1"],
            kept["grads 1"],
            tokens_all,
            grad_tokens_1,
            kept["shared 1"],
            kept["shared grads 1"],
        )
        experts_1, shared_1 = kept["sums 1"]
        return experts_1, kept["part 1"], [made[-1] for made in shared_1]

    def beside_1(index, result):
        part = outer(plain[1][index], result) + chunk_of(kept["part 1"], index)
        return part.astype(HALF)

    total, rows_1, mids_1 = through_experts(
        rms_norm(middle_1, norm_mids[1]).astype(HALF), plain[1], expert_1, own_1, beside_1
    )

    def mixer_back(s, grad_middle, along, rr, saved, meanwhile):
        wide_in, pre, y, scaled = saved
        sides = as_halves(jnp.concatenate([rr, along], axis=1))
        payload = spread(
            jnp.concatenate([grad_middle.astype(HALF), sides], axis=1), meanwhile
        )
        wide_mix, sides = payload[:, :width], from_halves(payload[:, width:], 2)
        grad_scaled = [project(wide_mix, half) for half in proj_out[s]]
        grad_scaled = jnp.concatenate(grad_scaled, axis=1)
        *grad_pre, wide_grads, grad_conv_input, grad_conv_state, step_grads = mixer_backward(
            pre, y, grad_scaled, sides, heads, mixers[s]
        )
        ends = [part[:, :wide] for part in grad_pre]
        tail = jnp.concatenate([grad_pre[0][:, wide:], grad_pre[1][:, wide : wide + LANES]], axis=1)
        mix_rr = (wide_mix * sides[:, :1]).astype(HALF)
        rest = (grad_conv_state, grad_conv_input, wide_grads, step_grads)
        return grad_pre, (wide_in, *ends), (mix_rr, *two_halves(scaled)), tail, rest

    def resid_back(resid, norm, grad_normed, grad_middle):
        _, pull_in = jax.vjp(rms_norm, resid, norm)
        grad_resid, grad_norm = pull_in(grad_normed)
        return grad_resid + grad_middle, grad_norm

    def own_layer(first_value, second_value):
        keep = jnp.where(first, first_value, second_value)
        give = jnp.where(first, second_value, first_value).astype(HALF)
        return keep.astype(FLOAT), swapped(give)

    def row_sums(value):
        return lax.psum_scatter(value, "row", scatter_dimension=0, tiled=True)

    grad_middle, along, grad_norm_mid_1 = middle_backward(
        total, grad_now, middle_1, mixed_1, norm_mids[1]
    )
    expert_grads_1, shared_grads_1 = kept["sums 1"]
    answers = after([kept["answer 1"][index] for index in kept["answer 1"]], grad_middle)
    answers_back = [to_experts(answers[-1])]
    if groups() > 1:
        own_rows, others = sent_back(answers[0])
        answers_back = [jnp.concatenate([own_rows, *others], axis=0), *answers_back]
    shared_made_1 = [half_to_keep(*made) for made in shared_grads_1]
    grad_pre, to_proj, to_out, tail, rest_1 = mixer_back(
        1,
        grad_middle,
        along,
        rr_1,
        (wide_in_1, pre_1, y_1, scaled_1),
        shared_made_1,
    )
    shared_sent_1 = [row_sums(each) for each in shared_made_1]
    whole = line_product(grad_pre, proj[1])
    grad_in = gathered_sum(whole)
    grad_1, grad_norm_in_1 = resid_back(out_0, norm_ins[1], grad_in, grad_middle)

    def aside_back_0(tokens_all):
        own_proj, own_out, own_tail = after((to_proj, to_out, tail), tokens_all)
        given, given_out = half_to_give(*own_proj), half_to_give(*own_out)
        made = ((*own_out, swapped(given_out)), (*own_proj, swapped(given)))
        made = [half_to_keep(*each) for each in after(made, (given, given_out))]
        kept["sent 1"] = [*shared_sent_1, *[row_sums(each) for each in made]]
        kept["tail 1"] = outer(own_proj[0], own_tail).astype(HALF)
        home = home_part(after(kept["shared 1"][2], made), shared[1])
        home = [
            (outer(scaling[1][index], answer) + chunk_of(home, index)).astype(HALF)
            for index, answer in enumerate(answers_back)
        ]
        home = joined(home)
        if groups() > 1:
            home = in_order([block_of(home, back) for back in range(groups())], "col")
        kept["home"] = lax.psum_scatter(home, "col", scatter_dimension=0, tiled=True)
        return made, kept["tail 1"], home

    def expert_back_0(index, rows):
        kept["grads 0"][index], back = expert_backward(rows, kept["rows 0"][index], experts[0])
        return back

    def own_back_0(tokens_all, rows):
        kept["shared grads 0"], kept["part 0"] = shared_backward(
            tokens_all, kept["shared 0"], shared[0]
        )
        kept["sums 0"] = weight_sums(
            rows_0,
            rows,
            kept["rows 0"],
            kept["grads 0"],
            mids_0,
            tokens_all,
            kept["shared 0"],
            kept["shared grads 0"],
        )
        experts_0, shared_0 = kept["sums 0"]
        return experts_0, kept["part 0"], [made[-1] for made in shared_0]

    def beside_back_0(index, result):
        part = outer(plain[0][index], result) + chunk_of(kept["part 0"], index)
        return part.astype(HALF)

    total, grad_rows_0, grad_tokens_0 = through_experts(
        grad_1.astype(HALF), scaling[0], expert_back_0, own_back_0, beside_back_0, aside_back_0
    )
    sums_1, grad_tail_1 = kept["sent 1"], kept["tail 1"]
    grad_middle, along, grad_norm_mid_0 = middle_backward(
        total, grad_1, middle_0, mixed_0, norm_mids[0]
    )
    expert_grads_0, shared_grads_0 = kept["sums 0"]
    shared_sums_0 = [half_to_keep(*after(made, total)) for made in shared_grads_0]
    sums_0 = [row_sums(made) for made in shared_sums_0]
    expert_out = [own_layer(a, b) for a, b in zip(expert_grads_0, expert_grads_1)]
    grad_pre, to_proj, to_out, tail, rest_0 = mixer_back(
        0,
        grad_middle,
        along,
        rr_0,
        (wide_in_0, pre_0, y_0, scaled_0),
        ([part[0] for part in expert_out], shared_sums_0, sums_1),
    )

    given = half_to_give(*to_proj)
    whole = line_product(after(grad_pre, given), proj[0])
    proj_half = half_to_keep(*after((*to_proj, swapped(given)), whole))
    proj_pieces = row_pieces(proj_half)
    proj_received = row_received(proj_pieces)
    line_received = sent_home(after(whole, proj_half))
    given_out = half_to_give(*after(to_out, proj_half))
    grad_tail_0 = outer(after(wide_in_0, given_out), tail).astype(HALF)
    out_half = half_to_keep(*after((*to_out, swapped(given_out)), grad_tail_0))
    out_pieces = row_pieces(out_half)
    out_received = row_received(out_pieces)
    tail_keep, tail_other = own_layer(grad_tail_0, grad_tail_1)
    tail_pieces = row_pieces((tail_keep + tail_other.astype(FLOAT)).astype(HALF))
    tail_received = row_received(tail_pieces)
    wide_x = wide_tokens.astype(FLOAT)
    wide_r = lax.rsqrt(jnp.mean(wide_x * wide_x, axis=1, keepdims=True) + EPS)
    grad_norm_in_0 = jnp.sum(whole.astype(FLOAT) * wide_x * wide_r, axis=0)
    smalls = (
        (grad_norm_in_0, grad_norm_mid_0, *rest_0),
        (grad_norm_in_1, grad_norm_mid_1, *rest_1),
    )
    shapes = [part.shape for part in smalls[0]]
    small_keep, small_other = own_layer(flat(smalls[0]), flat(smalls[1]))
    vector = small_keep + small_other.astype(FLOAT)
    lines = [shifted(vector[None], "row", back) for back in range(n_row)]
    line_received, proj_received, out_received, tail_received, lines = after(
        (line_received, proj_received, out_received, tail_received, lines)
    )
    grad_in = added_up(whole, line_received)
    sums_0.append(total_of(out_pieces[0], out_received).astype(HALF))
    sums_0.append(total_of(proj_pieces[0], proj_received).astype(HALF))
    sums_0, sums_1 = after((sums_0, sums_1), grad_in)
    expert_out = [keep + other.astype(FLOAT) for keep, other in after(expert_out, grad_in)]
    tail = total_of(tail_pieces[0], tail_received).astype(HALF)
    vector = jnp.sum(in_order(lines, "row"), axis=0)
    grad_0, _ = resid_back(tokens_now, norm_ins[0], grad_in, grad_middle)
    out_1 = middle_1 + kept["home"].astype(FLOAT)

    def own_halves(first_value, second_value):
        keep = jnp.where(first, first_value, second_value)
        give = jnp.where(first, second_value, first_value)
        return keep, swapped(give)

    def per_micro(first_value, second_value):
        keep = jnp.where(first, first_value, second_value)
        return keep, swapped(jnp.where(first, second_value, first_value).astype(HALF))

    halves = [own_halves(a, b) for a, b in zip(sums_0, sums_1)]
    outs, in_grads = per_micro(out_0, after(out_1, grad_in)), per_micro(grad_0, grad_1)
    common = 2 * width + conv_state.shape[1] * state
    state_grad = tail[:, :state]
    if groups() > 1:
        state_pieces = row_pieces(state_grad, "col")
        state_received = row_received(state_pieces, "col")
        lines = [shifted(vector[None, :common], "col", back) for back in range(n_col)]
        state_received, lines, outs, in_grads = after((state_received, lines, outs, in_grads))
        state_grad = total_of(state_pieces[0], state_received).astype(HALF)
        state_grad = in_order([shifted(state_grad, "col", back) for back in range(n_col)], "col")
        shared_sum = jnp.sum(in_order(lines, "col"), axis=0)
    else:
        state_grad = lax.psum(state_grad, "col")
        shared_sum = lax.psum(vector[:common], "col")
    halves = [pair(*half) for half in halves]
    grad_shared, grad_down, grad_out, grad_ends = halves
    grad_out, grad_down = [jnp.concatenate(both, axis=1) for both in (grad_out, grad_down)]
    (
        out_norm_in,
        out_norm_mid,
        out_conv_state,
        out_conv_input,
        out_wide,
        out_step,
    ) = unflat(jnp.concatenate([shared_sum, vector[common:]]), shapes)

    def stacked(keep, other):
        return jnp.stack(pair(keep, other.astype(FLOAT)))[None]

    def out(value):
        return value.astype(FLOAT)[None]

    return (
        stacked(*outs),
        stacked(*in_grads),
        out_norm_in[None],
        out(grad_ends[0][:, :inner]),
        out(grad_ends[1][:, :inner]),
        out(state_grad),
        out(tail[:, state : state + heads]),
        out_step[:1, :heads],
        out_step[1:, :heads],
        jnp.sum(out_wide[1, :inner].reshape(heads, HEAD), axis=1)[None],
        out_conv_input[None, :, :inner],
        out_conv_state[None],
        out_wide[:1, :inner],
        out(grad_out[:, :inner]),
        out_norm_mid[None],
        expert_out[0][None, None],
        expert_out[1][None, None],
        expert_out[2][None, None],
        out(grad_shared[0]),
        out(grad_shared[1]),
        out(grad_down),
    )


def solution(mesh):
    in_specs = (
        P(None, ("row", "col"), None),
        P(None, ("row", "col"), None),
        P(),
        P("section", None, ("row", "col"), None),
        P("section", None, ("row", "col"), None),
        P("section", None),
        P("section", "row", "col"),
        P("section", "row", "col"),
        P("section", "row", None),
        P("section", "row", "col"),
        P("section", "col"),
        P("section", "col"),
        P("section", "col"),
        P("section", None, "col"),
        P("section", None, None),
        P("section", "col"),
        P("section", "row", "col"),
        P("section", None),
        P("section", ("row", "col"), None, None),
        P("section", ("row", "col"), None, None),
        P("section", ("row", "col"), None, None),
        P("section", "row", "col"),
        P("section", "row", "col"),
        P("section", "row", "col"),
    )
    out_specs = (
        P("section", None, ("row", "col"), None),
        P("section", None, ("row", "col"), None),
        P("section", None),
        P("section", "row", "col"),
        P("section", "row", "col"),
        P("section", "row", None),
        P("section", "row", "col"),
        P("section", "col"),
        P("section", "col"),
        P("section", "col"),
        P("section", None, "col"),
        P("section", None, None),
        P("section", "col"),
        P("section", "row", "col"),
        P("section", None),
        P("section", ("row", "col"), None, None),
        P("section", ("row", "col"), None, None),
        P("section", ("row", "col"), None, None),
        P("section", "row", "col"),
        P("section", "row", "col"),
        P("section", "row", "col"),
    )
    return jax.shard_map(shards, mesh=mesh, in_specs=in_specs, out_specs=out_specs, check_vma=False)
```

```python
import functools

import jax
import jax.numpy as jnp
from jax import lax
from jax.experimental import pallas as pl
from jax.experimental.pallas import tpu as pltpu
from jax.sharding import PartitionSpec as P

DI = 3072
HEAD = 64
LANES = 128
CHUNK = 256
VMEM_BYTES = 48 * 2**20

EPS = 1e-05
HIGH = lax.Precision.HIGHEST
FLOAT = jnp.float32
HALF = jnp.bfloat16


def shifted(block, axis, distance):
    count = lax.axis_size(axis)
    if distance % count == 0:
        return block
    return lax.ppermute(block, axis, [(i, (i + distance) % count) for i in range(count)])


def swapped(block):
    return lax.ppermute(block, "section", [(0, 1), (1, 0)])


def after(value, *others):
    return lax.optimization_barrier((value, *others))[0]


def rms_norm(value, gain):
    return value * lax.rsqrt(jnp.mean(value * value, axis=-1, keepdims=True) + EPS) * gain


def local_docs(lengths, row_now, length):
    bounds = jnp.cumsum(lengths)[:-1]
    place = jnp.arange(length, dtype=jnp.int32)
    inner = jnp.sum((place[:, None] >= bounds[None, :]).astype(jnp.int32), axis=1)
    return inner + row_now * lengths.shape[0]


def project(left, right):
    return jnp.dot(left, right, preferred_element_type=FLOAT)


def project_back(left, right):
    return lax.dot_general(left, right, (((1,), (1,)), ((), ())), preferred_element_type=FLOAT)


def outer(left, right):
    return lax.dot_general(left, right, (((0,), (0,)), ((), ())), preferred_element_type=FLOAT)


def silu_slope(value):
    sigma = jax.nn.sigmoid(value)
    return sigma * (1.0 + value * (1.0 - sigma))


def groups():
    count = lax.axis_size("col")
    return count if count <= 4 else 1


def spread(block, meanwhile=()):
    if groups() == 1:
        return lax.all_gather(block, "col", axis=0, tiled=True)
    received = [shifted(block, "col", back) for back in range(1, groups())]
    return jnp.concatenate([block, *after(received, meanwhile)], axis=0)


def in_order(blocks, axis):
    count = len(blocks)
    if count == 1:
        return blocks[0]
    rows = blocks[0].shape[0]
    line = jnp.concatenate(blocks[::-1] + blocks[:0:-1], axis=0)
    start = (count - 1 - lax.axis_index(axis)) * rows
    return lax.dynamic_slice_in_dim(line, start, count * rows, axis=0)


def sent_home(rows):
    if groups() == 1:
        return lax.psum_scatter(rows, "col", scatter_dimension=0, tiled=True)
    return [shifted(block_of(rows, back), "col", -back) for back in range(1, groups())]


def added_up(rows, received):
    if groups() == 1:
        return received.astype(FLOAT)
    return sum([part.astype(FLOAT) for part in received], block_of(rows, 0).astype(FLOAT))


def gathered_sum(rows, meanwhile=()):
    return added_up(rows, after(sent_home(rows), meanwhile))


def exchanged(rows, axis):
    return lax.all_to_all(rows, axis, split_axis=0, concat_axis=0, tiled=True)


def as_halves(columns):
    high = lax.reduce_precision(columns, 8, 7)
    both = jnp.concatenate([high, columns - high], axis=1).astype(HALF)
    return jnp.pad(both, ((0, 0), (0, LANES - both.shape[1])))


def from_halves(tile, count):
    return tile[:, :count].astype(FLOAT) + tile[:, count : 2 * count].astype(FLOAT)


def block_of(values, back):
    rows = values.shape[0] // groups()
    return values[back * rows : (back + 1) * rows]


def turn():
    place = lax.axis_index("col") if groups() > 1 else jnp.int32(0)
    return place.astype(jnp.int32).reshape(1)


def chunk_of(rows, index):
    if groups() == 1:
        return rows
    own = rows.shape[0] // groups()
    return rows[own:] if index else rows[:own]


def route_tables(meta, top, capacity, layers):
    n_row, n_col = lax.axis_size("row"), lax.axis_size("col")
    place = jnp.arange(n_row)
    tables = [[] for _ in range(layers)]
    for index in range(min(groups(), 2)):
        now = chunk_of(meta, index)
        count = now.shape[0]
        slots = count * n_col * capacity // meta.shape[0]
        rows = place
        if groups() > 1 and index == 0:
            rows = lax.rem(lax.axis_index("row") + place, n_row)
        experts = (rows * n_col + lax.axis_index("col")).astype(FLOAT)
        now = now.reshape(count, layers, 2, top).transpose(1, 2, 3, 0)
        match = now[:, None, 0] == experts[None, :, None, None]
        hit = jnp.any(match, axis=2)
        weight = jnp.sum(jnp.where(match, now[:, None, 1], 0.0), axis=2)
        order = jnp.arange(count, dtype=jnp.int32)
        triangle = (order[:, None] <= order[None, :]).astype(HALF)
        rank = project(hit.astype(HALF).reshape(-1, count), triangle).reshape(hit.shape)
        slot = jnp.arange(1, slots + 1, dtype=jnp.int32).astype(FLOAT)
        chosen = (rank[:, :, None, :] == slot[:, None]) & hit[:, :, None, :]
        shape = (layers, n_row * slots, count)
        plain = chosen.astype(HALF).reshape(shape)
        scaled = jnp.where(chosen, weight[:, :, None, :], 0.0).astype(HALF).reshape(shape)
        for s in range(layers):
            tables[s].append((plain[s], scaled[s]))
    return tables


def to_experts(rows):
    return exchanged(rows.astype(HALF), "row")


def summed_rows(values, reverse):
    step = min(values.shape[0], CHUNK)
    count = values.shape[0] // step
    place = lax.broadcasted_iota(jnp.int32, (step, step), 0)
    other = lax.broadcasted_iota(jnp.int32, (step, step), 1)
    before = (place <= other) if reverse else (place >= other)
    triangle = before.astype(FLOAT)
    carry = jnp.zeros((1, values.shape[1]), FLOAT)
    parts = [None] * count
    for index in reversed(range(count)) if reverse else range(count):
        part = values[index * step : (index + 1) * step]
        run = jnp.dot(triangle, part, precision=HIGH, preferred_element_type=FLOAT) + carry
        carry = run[:1] if reverse else run[step - 1 :]
        parts[index] = run
    return parts[0] if count == 1 else jnp.concatenate(parts, axis=0)


def head_columns(rows, columns, head_width):
    head = lax.broadcasted_iota(jnp.int32, (rows, columns), 0) * head_width
    column = lax.broadcasted_iota(jnp.int32, (rows, columns), 1)
    return ((column >= head) & (column < head + head_width)).astype(FLOAT)


def sigmoid(value):
    return 1.0 / (1.0 + jnp.exp(-value))


def step_sizes(step_pre, step_row_ref):
    shifted_pre = step_pre + step_row_ref[0:1, :]
    sizes = jnp.maximum(shifted_pre, 0.0) + jnp.log1p(jnp.exp(-jnp.abs(shifted_pre)))
    return shifted_pre, sizes, -jnp.exp(step_row_ref[1:2, :])


def conv_rows(values, weight_ref, columns, marks_ref):
    width = weight_ref.shape[0]
    result = values * weight_ref[width - 1 : width, columns]
    for back in range(1, width):
        moved = pltpu.roll(values, back, 0) * marks_ref[:, back : back + 1]
        result = result + moved * weight_ref[width - 1 - back : width - back, columns]
    return result


def conv_rows_back(grad, values, weight_ref, columns, marks_ref, weight_grad_ref):
    width = weight_ref.shape[0]
    rows = values.shape[0]
    result = grad * weight_ref[width - 1 : width, columns]
    weight_grad_ref[width - 1 : width, columns] = jnp.sum(grad * values, axis=0, keepdims=True)
    for back in range(1, width):
        kept = grad * marks_ref[:, back : back + 1]
        taps = jnp.sum(kept * pltpu.roll(values, back, 0), axis=0, keepdims=True)
        weight_grad_ref[width - 1 - back : width - back, columns] = taps
        moved = pltpu.roll(kept, rows - back, 0)
        result = result + moved * weight_ref[width - 1 - back : width - back, columns]
    return result


def copy_in_order(source_ref, target_ref, place_ref, parts):
    if parts == 1:
        return source_ref
    rows = source_ref.shape[0] // parts
    for index in range(parts):
        target_ref[index * rows : (index + 1) * rows, :] = source_ref[
            block_rows(index, rows, place_ref, parts), :
        ]
    return target_ref


def block_rows(index, rows, place_ref, parts):
    if parts == 1:
        return slice(0, rows)
    back = lax.rem(place_ref[0] - index + parts, parts)
    return pl.ds(pl.multiple_of(back * rows, rows), rows)


def mixer_forward_kernel(
    heads,
    parts,
    pre_in_ref,
    pre_other_in_ref,
    conv_input_ref,
    conv_state_ref,
    step_row_ref,
    wide_row_ref,
    marks_ref,
    labels_ref,
    place_ref,
    y_ref,
    scaled_ref,
    total_ref,
    pre_ref,
    pre_other_ref,
    x_ref,
    dosed_ref,
    keys_ref,
    queries_ref,
):
    length, wide = y_ref.shape
    states = conv_state_ref.shape[1] // 2
    state_at, step_at = wide, wide
    head_width = HEAD
    pre_ref = copy_in_order(pre_in_ref, pre_ref, place_ref, parts)
    pre_other_ref = copy_in_order(pre_other_in_ref, pre_other_ref, place_ref, parts)
    _, sizes, rate = step_sizes(pre_other_ref[:, step_at : step_at + LANES], step_row_ref)
    running = summed_rows(sizes * rate, False)
    running_t = running.T
    expand = head_columns(LANES, wide, head_width)
    for start in range(0, wide, LANES):
        columns = slice(start, start + LANES)
        conv = conv_rows(
            pre_other_ref[:, columns], conv_input_ref, columns, marks_ref
        )
        x = conv * sigmoid(conv)
        x_ref[:, columns] = x
        dose = jnp.dot(sizes, expand[:, columns], precision=HIGH, preferred_element_type=FLOAT)
        dosed_ref[:, columns] = (x * dose).astype(HALF)
    for part, target in ((0, keys_ref), (1, queries_ref)):
        columns = slice(part * states, (part + 1) * states)
        conv = conv_rows(
            pre_ref[:, state_at + part * states : state_at + (part + 1) * states],
            conv_state_ref,
            columns,
            marks_ref,
        )
        target[...] = (conv * sigmoid(conv)).astype(HALF)
    block = min(length, CHUNK)
    place = lax.broadcasted_iota(jnp.int32, (block, block), 0)
    other = lax.broadcasted_iota(jnp.int32, (block, block), 1)
    for late in range(length // block):
        rows = slice(late * block, (late + 1) * block)
        for early in range(late + 1):
            past = slice(early * block, (early + 1) * block)
            same = marks_ref[rows, 0:1] == labels_ref[:, past]
            if late == early:
                same = same & (place >= other)
            mask = jnp.where(same, 0.0, -1e30)
            scores = lax.dot_general(
                queries_ref[rows, :],
                keys_ref[past, :],
                (((1,), (1,)), ((), ())),
                preferred_element_type=FLOAT,
            )
            for head in range(heads):
                columns = slice(head * head_width, (head + 1) * head_width)
                spread_log = running[rows, head : head + 1] - running_t[head : head + 1, past]
                mixing = (jnp.exp(spread_log + mask) * scores).astype(HALF)
                inner = jnp.dot(mixing, dosed_ref[past, columns], preferred_element_type=FLOAT)
                if early == 0:
                    y_ref[rows, columns] = inner
                else:
                    y_ref[rows, columns] += inner
    total = jnp.zeros((length, 1), FLOAT)
    for start in range(0, wide, LANES):
        columns = slice(start, start + LANES)
        y = y_ref[:, columns]
        if heads * head_width < start + LANES:
            lane = lax.broadcasted_iota(jnp.int32, y.shape, 1) + start
            y = jnp.where(lane < heads * head_width, y, 0.0)
        y = y + wide_row_ref[1:2, columns] * x_ref[:, columns]
        gate = pre_ref[:, columns]
        gated = y * gate * sigmoid(gate)
        y_ref[:, columns] = y
        scaled = (gated * wide_row_ref[0:1, columns]).astype(HALF)
        each = length // parts
        for index in range(parts):
            block_at = block_rows(index, each, place_ref, parts)
            scaled_ref[block_at, columns] = scaled[index * each : (index + 1) * each]
        total = total + jnp.sum(gated * gated, axis=1, keepdims=True)
    each = length // parts
    for index in range(parts):
        block_at = block_rows(index, each, place_ref, parts)
        total_ref[block_at, :] = total[index * each : (index + 1) * each]


def mixer_backward_kernel(
    heads,
    parts,
    inner_all,
    pre_in_ref,
    pre_other_in_ref,
    y_ref,
    grad_in_ref,
    sides_in_ref,
    conv_input_ref,
    conv_state_ref,
    step_row_ref,
    wide_row_ref,
    marks_ref,
    labels_ref,
    place_ref,
    grad_pre_ref,
    grad_pre_other_ref,
    wide_grad_ref,
    conv_input_grad_ref,
    conv_state_grad_ref,
    step_grad_ref,
    pre_ref,
    pre_other_ref,
    grad_ref,
    sides_ref,
    x_ref,
    dosed_ref,
    dose_ref,
    slope_ref,
    dy_ref,
    z_ref,
    bc_ref,
    bc_slope_ref,
    bc_grad_ref,
):
    length, wide = y_ref.shape
    states = conv_state_ref.shape[1] // 2
    state_at, step_at = wide, wide
    head_width = HEAD
    each = length // parts
    pre_ref = copy_in_order(pre_in_ref, pre_ref, place_ref, parts)
    pre_other_ref = copy_in_order(pre_other_in_ref, pre_other_ref, place_ref, parts)
    grad_ref = copy_in_order(grad_in_ref, grad_ref, place_ref, parts)
    sides_ref = copy_in_order(sides_in_ref, sides_ref, place_ref, parts)

    def put(target_ref, value, start):
        for index in range(parts):
            target_ref[block_rows(index, each, place_ref, parts), start : start + LANES] = value[
                index * each : (index + 1) * each
            ]

    shifted_pre, sizes, rate = step_sizes(pre_other_ref[:, step_at : step_at + LANES], step_row_ref)
    running = summed_rows(sizes * rate, False)
    running_t = running.T
    expand = head_columns(LANES, wide, head_width)
    rr = sides_ref[:, 0:1]
    pull = rr * rr * rr * sides_ref[:, 1:2] * (1.0 / inner_all)
    for start in range(0, wide, LANES):
        columns = slice(start, start + LANES)
        gate = pre_ref[:, columns]
        y = y_ref[:, columns]
        grad = grad_ref[:, columns]
        gain = wide_row_ref[0:1, columns]
        sigma = sigmoid(gate)
        silu = gate * sigma
        gated = y * silu
        normed = gated * rr
        wide_grad_ref[0:1, columns] = jnp.sum(grad * normed, axis=0, keepdims=True)
        grad_gated = rr * gain * grad - gated * pull
        slope = sigma * (1.0 + gate * (1.0 - sigma))
        put(grad_pre_ref, (grad_gated * y * slope).astype(HALF), start)
        dy = grad_gated * silu
        dy_ref[:, columns] = dy
        conv = conv_rows(
            pre_other_ref[:, columns], conv_input_ref, columns, marks_ref
        )
        sigma = sigmoid(conv)
        x = conv * sigma
        x_ref[:, columns] = x
        slope_ref[:, columns] = sigma * (1.0 + conv * (1.0 - sigma))
        dose = jnp.dot(sizes, expand[:, columns], precision=HIGH, preferred_element_type=FLOAT)
        dose_ref[:, columns] = dose
        dosed_ref[:, columns] = (x * dose).astype(HALF)
        wide_grad_ref[1:2, columns] = jnp.sum(dy * x, axis=0, keepdims=True)
    for start in range(0, 2 * states, LANES):
        columns = slice(start, start + LANES)
        conv = conv_rows(
            pre_ref[:, state_at + start : state_at + start + LANES],
            conv_state_ref,
            columns,
            marks_ref,
        )
        sigma = sigmoid(conv)
        bc_ref[:, columns] = (conv * sigma).astype(HALF)
        bc_slope_ref[:, columns] = sigma * (1.0 + conv * (1.0 - sigma))
    block = min(length, CHUNK)
    place = lax.broadcasted_iota(jnp.int32, (block, block), 0)
    other = lax.broadcasted_iota(jnp.int32, (block, block), 1)
    z_ref[...] = jnp.zeros(z_ref.shape, FLOAT)
    bc_grad_ref[...] = jnp.zeros(bc_grad_ref.shape, FLOAT)
    for late in range(length // block):
        rows = slice(late * block, (late + 1) * block)
        for early in range(late + 1):
            past = slice(early * block, (early + 1) * block)
            same = marks_ref[past, 0:1] == labels_ref[:, rows]
            if late == early:
                same = same & (place <= other)
            mask = jnp.where(same, 0.0, -1e30)
            keys = bc_ref[past, :states]
            queries = bc_ref[rows, states:]
            scores = lax.dot_general(
                keys, queries, (((1,), (1,)), ((), ())), preferred_element_type=FLOAT
            )
            mixed = jnp.zeros((block, block), FLOAT)
            for head in range(heads):
                columns = slice(head * head_width, (head + 1) * head_width)
                spread_log = running_t[head : head + 1, rows] - running[past, head : head + 1]
                decay = jnp.exp(spread_log + mask)
                mixing = (decay * scores).astype(HALF)
                dy = dy_ref[rows, columns].astype(HALF)
                z_ref[past, columns] += jnp.dot(mixing, dy, preferred_element_type=FLOAT)
                along = lax.dot_general(
                    dosed_ref[past, columns],
                    dy,
                    (((1,), (1,)), ((), ())),
                    preferred_element_type=FLOAT,
                )
                mixed = mixed + decay * along
            mixed = mixed.astype(HALF)
            bc_grad_ref[past, :states] += jnp.dot(mixed, queries, preferred_element_type=FLOAT)
            bc_grad_ref[rows, states:] += lax.dot_general(
                mixed, keys, (((0,), (0,)), ((), ())), preferred_element_type=FLOAT
            )
    direct = jnp.zeros((length, LANES), FLOAT)
    balance = jnp.zeros((length, LANES), FLOAT)
    for start in range(0, wide, LANES):
        columns = slice(start, start + LANES)
        x, z, dy = x_ref[:, columns], z_ref[:, columns], dy_ref[:, columns]
        skip = wide_row_ref[1:2, columns]
        collapse = (((1,), (1,)), ((), ()))
        both = dy.astype(HALF).astype(FLOAT) * (y_ref[:, columns] - skip * x)
        both = both - dosed_ref[:, columns].astype(FLOAT) * z
        heads_of = expand[:, columns]
        direct = direct + lax.dot_general(
            x * z, heads_of, collapse, precision=HIGH, preferred_element_type=FLOAT
        )
        balance = balance + lax.dot_general(
            both, heads_of, collapse, precision=HIGH, preferred_element_type=FLOAT
        )
        grad_conv = (dose_ref[:, columns] * z + skip * dy) * slope_ref[:, columns]
        grad_in = conv_rows_back(
            grad_conv,
            pre_other_ref[:, columns],
            conv_input_ref,
            columns,
            marks_ref,
            conv_input_grad_ref,
        )
        put(grad_pre_other_ref, grad_in.astype(HALF), start)
    for start in range(0, 2 * states, LANES):
        columns = slice(start, start + LANES)
        grad_in = conv_rows_back(
            bc_grad_ref[:, columns] * bc_slope_ref[:, columns],
            pre_ref[:, state_at + start : state_at + start + LANES],
            conv_state_ref,
            columns,
            marks_ref,
            conv_state_grad_ref,
        )
        put(grad_pre_ref, grad_in.astype(HALF), state_at + start)
    crossing = summed_rows(balance, True)
    grad_step = (direct + rate * crossing) * sigmoid(shifted_pre)
    put(grad_pre_other_ref, grad_step.astype(HALF), step_at)
    for start in range(step_at + LANES, grad_pre_other_ref.shape[1], LANES):
        put(grad_pre_other_ref, jnp.zeros((length, LANES), HALF), start)
    step_grad_ref[0:1, :] = jnp.sum(grad_step, axis=0, keepdims=True)
    step_grad_ref[1:2, :] = rate * jnp.sum(sizes * crossing, axis=0, keepdims=True)


def ordered_copy(shape):
    return pltpu.VMEM(shape if groups() > 1 else (8, LANES), FLOAT)


def whole_call(kernel, inputs, results, scratch, name):
    whole = pl.BlockSpec(memory_space=pltpu.VMEM)
    place = pl.BlockSpec(memory_space=pltpu.SMEM)
    return pl.pallas_call(
        kernel,
        in_specs=[whole] * (inputs - 1) + [place],
        out_shape=results,
        scratch_shapes=scratch,
        compiler_params=pltpu.CompilerParams(vmem_limit_bytes=VMEM_BYTES),
        name=name,
    )


def mixer_forward(pre, heads, wide, mixer):
    length = pre[0].shape[0]
    kernel = functools.partial(mixer_forward_kernel, heads, groups())
    states = mixer[1].shape[1] // 2
    return whole_call(
        kernel,
        2 + len(mixer),
        (
            jax.ShapeDtypeStruct((length, wide), FLOAT),
            jax.ShapeDtypeStruct((length, wide), HALF),
            jax.ShapeDtypeStruct((length, 1), FLOAT),
        ),
        [
            ordered_copy(pre[0].shape),
            ordered_copy(pre[1].shape),
            pltpu.VMEM((length, wide), FLOAT),
            pltpu.VMEM((length, wide), HALF),
            pltpu.VMEM((length, states), HALF),
            pltpu.VMEM((length, states), HALF),
        ],
        "mixer_forward",
    )(*pre, *mixer)


def mixer_backward(pre, y, grad, sides, heads, mixer):
    length, wide = y.shape
    kernel = functools.partial(mixer_backward_kernel, heads, groups(), DI)
    double = mixer[1].shape[1]
    square = pltpu.VMEM((length, wide), FLOAT)
    return whole_call(
        kernel,
        5 + len(mixer),
        (
            jax.ShapeDtypeStruct(pre[0].shape, HALF),
            jax.ShapeDtypeStruct(pre[1].shape, HALF),
            jax.ShapeDtypeStruct((2, wide), FLOAT),
            jax.ShapeDtypeStruct((4, wide), FLOAT),
            jax.ShapeDtypeStruct((4, double), FLOAT),
            jax.ShapeDtypeStruct((2, LANES), FLOAT),
        ),
        [
            ordered_copy(pre[0].shape),
            ordered_copy(pre[1].shape),
            ordered_copy(y.shape),
            ordered_copy(sides.shape),
            square,
            pltpu.VMEM((length, wide), HALF),
            square,
            square,
            square,
            square,
            pltpu.VMEM((length, double), HALF),
            pltpu.VMEM((length, double), FLOAT),
            pltpu.VMEM((length, double), FLOAT),
        ],
        "mixer_backward",
    )(*pre, y, grad, sides, *mixer)


def joined(parts):
    return parts[0] if len(parts) == 1 else jnp.concatenate(parts, axis=0)


def row_slices(rows):
    count = lax.axis_size("row")
    each = rows.shape[0] // count
    return [rows[index * each : (index + 1) * each] for index in range(count)]


def sent_ahead(rows):
    shares = row_slices(rows)
    return shares[0], [shifted(share, "row", ahead) for ahead, share in enumerate(shares) if ahead]


def sent_back(rows):
    shares = row_slices(rows)
    return shares[0], [shifted(share, "row", -ahead) for ahead, share in enumerate(shares) if ahead]


def through_experts(block, tables, expert, own, beside, aside=None):
    if groups() == 1:
        tokens = spread(block)
        sent = project(tables[0], tokens).astype(HALF)
        arrived = to_experts(sent)
        answer = expert(0, arrived)
        if aside is not None:
            answer = after(answer, aside(after(tokens, sent)))
        answered = to_experts(answer)
        answered = after(answered, own(after(tokens, answer), after([arrived], answer)))
        return gathered_sum(beside(0, answered)), [arrived], tokens
    count = block.shape[0]
    first, others = sent_ahead(project(tables[0], block).astype(HALF))
    line = [shifted(block, "col", back) for back in range(1, groups())]
    line = after(line, others)
    tokens = jnp.concatenate([block, *line], axis=0)
    rows_own = jnp.concatenate([first, *others], axis=0)
    sent = project(tables[1], chunk_of(tokens, 1)).astype(HALF)
    arrived = to_experts(sent)
    answer_own = expert(0, after(rows_own, sent))
    held = () if aside is None else aside(after(tokens, sent))
    answer = after(expert(1, arrived), answer_own, held)
    answered = to_experts(answer)
    answered = after(answered, own(after(tokens, answer), after([rows_own, arrived], answer)))
    part = beside(1, answered)
    first, others = sent_back(answer_own)
    line = [
        shifted(part[at * count : (at + 1) * count], "col", -at - 1) for at in range(groups() - 1)
    ]
    others, line = after((others, line))
    total = beside(0, jnp.concatenate([first, *others], axis=0)).astype(FLOAT)
    return sum([each.astype(FLOAT) for each in line], total), [rows_own, arrived], tokens


def line_product(values, weights):
    return sum(project_back(value, weight) for value, weight in zip(values, weights)).astype(HALF)


def expert_forward(rows, experts):
    gate_e = project(rows, experts[0])
    lift_e = project(rows, experts[1])
    act_e = (jax.nn.silu(gate_e) * lift_e).astype(HALF)
    return (gate_e, lift_e, act_e), project(act_e, experts[2]).astype(HALF)


def expert_backward(rows, kept, experts):
    gate_e, lift_e, _ = kept
    grad_act = project_back(rows, experts[2])
    grad_gate = (grad_act * lift_e * silu_slope(gate_e)).astype(HALF)
    grad_lift = (grad_act * jax.nn.silu(gate_e)).astype(HALF)
    back = project_back(grad_gate, experts[0]) + project_back(grad_lift, experts[1])
    return (grad_gate, grad_lift), back.astype(HALF)


def shared_forward(tokens, shared):
    hidden = shared.shape[1] // 3
    gate_s = project(tokens, shared[:, :hidden])
    lift_s = project(tokens, shared[:, hidden : 2 * hidden])
    return gate_s, lift_s, (jax.nn.silu(gate_s) * lift_s).astype(HALF)


def shared_backward(tokens, kept, shared):
    hidden = shared.shape[1] // 3
    gate_s, lift_s, _ = kept
    grad_act = project(tokens, shared[:, 2 * hidden :])
    grad_gate = (grad_act * lift_s * silu_slope(gate_s)).astype(HALF)
    grad_lift = (grad_act * jax.nn.silu(gate_s)).astype(HALF)
    part = project_back(grad_gate, shared[:, :hidden])
    part = part + project_back(grad_lift, shared[:, hidden : 2 * hidden])
    return (grad_gate, grad_lift), part


def home_part(act_s, shared):
    return project_back(act_s, shared[:, 2 * (shared.shape[1] // 3) :])


def weight_sums(rows_in, rows_out, kept, grads, tokens_in, tokens_out, kept_s, grads_s):
    rows_in, rows_out = joined(rows_in), joined(rows_out)
    experts = (
        outer(rows_in, joined([grads[index][0] for index in grads])).astype(HALF),
        outer(rows_in, joined([grads[index][1] for index in grads])).astype(HALF),
        outer(joined([kept[index][2] for index in kept]), rows_out).astype(HALF),
    )
    shared = ((tokens_in, *grads_s), (tokens_out, *two_halves(kept_s[2])))
    return experts, [(*each, swapped(half_to_give(*each))) for each in shared]


def middle_backward(grad_normed, grad_out, middle, mixed, norm_mid):
    _, pull_mid = jax.vjp(rms_norm, middle, norm_mid)
    grad_middle, grad_norm_mid = pull_mid(grad_normed)
    grad_middle = grad_middle + grad_out
    along = jnp.sum(grad_middle * mixed, axis=1, keepdims=True)
    return grad_middle, along, grad_norm_mid


def two_halves(values):
    middle = values.shape[1] // 2
    return values[:, :middle], values[:, middle:]


def half_to_give(left, first_right, second_right):
    first = lax.axis_index("section") == 0
    return outer(left, jnp.where(first, second_right, first_right)).astype(HALF)


def half_to_keep(left, first_right, second_right, given):
    first = lax.axis_index("section") == 0
    keep = outer(left, jnp.where(first, first_right, second_right))
    return (keep + given.astype(FLOAT)).astype(HALF)


def row_pieces(values, axis="row"):
    count = lax.axis_size(axis)
    rows = values.shape[0] // count
    index = [lax.rem(lax.axis_index(axis) + ahead, count) * rows for ahead in range(count)]
    return [lax.dynamic_slice_in_dim(values, at, rows, axis=0) for at in index]


def total_of(own, received):
    return sum([part.astype(FLOAT) for part in received], own.astype(FLOAT))


def row_received(pieces, axis="row"):
    return [shifted(piece, axis, ahead) for ahead, piece in enumerate(pieces) if ahead]


class Kept:
    pass


def flat(parts):
    return jnp.concatenate([part.reshape(-1) for part in parts])


def unflat(vector, shapes):
    result, start = [], 0
    for shape in shapes:
        size = 1
        for entry in shape:
            size *= entry
        result.append(vector[start : start + size].reshape(shape))
        start += size
    return result


def widened(value, columns):
    return jnp.pad(value, ((0, 0), (0, columns - value.shape[1])))


def shards(
    tokens,
    cotangent,
    doc_lengths,
    routes,
    gates,
    norm_in,
    proj_gate,
    proj_input,
    proj_state,
    proj_step,
    step_bias,
    decay_log,
    skip_gain,
    conv_input,
    conv_state,
    gate_norm,
    proj_output,
    norm_mid,
    expert_gate,
    expert_up,
    expert_down,
    shared_gate,
    shared_up,
    shared_down,
):
    section_now = lax.axis_index("section")
    first = section_now == 0
    row_now = lax.axis_index("row")
    n_row, n_col = lax.axis_size("row"), lax.axis_size("col")
    count = tokens.shape[1]
    top = routes.shape[3]
    capacity = count * top * 4 // (3 * n_row * n_col)
    width = tokens.shape[2]
    heads = step_bias.shape[1]
    inner = gate_norm.shape[1]
    state = conv_state.shape[2]
    wide = -(-inner // LANES) * LANES
    layers = range(2)

    def pair(own, other):
        return (jnp.where(first, own, other), jnp.where(first, other, own))

    tokens_now = lax.dynamic_index_in_dim(tokens, section_now, 0, keepdims=False)
    grad_now = lax.dynamic_index_in_dim(cotangent, section_now, 0, keepdims=False)

    halves = (
        jnp.concatenate([widened(proj_gate[0], wide), proj_state[0]], axis=1),
        jnp.concatenate([widened(proj_input[0], wide), widened(proj_step[0], state)], axis=1),
    )
    keep, give = jnp.where(first, *halves), jnp.where(first, *halves[::-1])
    mine = pair(keep, swapped(give))

    def both_halves(half):
        whole = lax.all_gather(half, ("section", "row"), axis=0, tiled=True)
        return whole.reshape(2, n_row * half.shape[0], half.shape[1])

    def both_layers(weight):
        whole = lax.all_gather(weight, ("section", "row"), axis=0, tiled=True)
        return whole.reshape(2, n_row * weight.shape[0], weight.shape[1])

    proj = [both_halves(mine[0])]
    halves = two_halves(widened(proj_output[0], wide))
    keep, give = jnp.where(first, *halves), jnp.where(first, *halves[::-1])
    mine_out = pair(keep, swapped(give))
    proj_out = [both_halves(mine_out[0])]
    own_experts = (expert_gate[0, 0], expert_up[0, 0], expert_down[0, 0])
    experts = list(zip(*[pair(weight, swapped(weight)) for weight in own_experts]))
    wide_tokens = spread(tokens_now.astype(HALF), experts)
    shared = both_layers(jnp.concatenate([shared_gate[0], shared_up[0], shared_down[0]], axis=1))

    small_in = (
        norm_in[0],
        norm_mid[0],
        widened(conv_input[0], wide),
        conv_state[0],
        widened(jnp.concatenate([step_bias, decay_log], axis=0), LANES),
        widened(jnp.concatenate([gate_norm, jnp.repeat(skip_gain, HEAD, axis=1)], axis=0), wide),
    )
    vector = flat(small_in)
    small_all = [unflat(part, [v.shape for v in small_in]) for part in pair(vector, swapped(vector))]
    norm_ins = [part[0] for part in small_all]
    norm_mids = [part[1] for part in small_all]

    meta = jnp.concatenate([routes.astype(FLOAT), gates], axis=3)[0]
    keep = lax.dynamic_index_in_dim(meta, section_now, 0, keepdims=False)
    give = lax.dynamic_index_in_dim(meta, 1 - section_now, 0, keepdims=False)
    meta = jnp.concatenate(pair(keep, swapped(give)), axis=1)

    lengths = lax.dynamic_slice(
        doc_lengths, (section_now, row_now, 0), (1, 1, doc_lengths.shape[2])
    )
    labels = local_docs(lengths[0, 0], row_now, n_col * count)
    marks = [labels.astype(FLOAT)]
    for back in range(1, conv_input.shape[1]):
        prior = jnp.pad(labels, (back, 0), constant_values=-1)[:-back]
        marks.append((prior == labels).astype(FLOAT))
    marks = jnp.stack(marks, axis=1)
    label_row = labels.astype(FLOAT)[None]
    place = turn()
    mixers = [
        (conv_in, conv_st, step_row, wide_row, marks, label_row, place)
        for _, _, conv_in, conv_st, step_row, wide_row in small_all
    ]

    def mix_in(s, wide_in):
        pre = [project(wide_in, half) for half in proj[s]]
        return pre, *mixer_forward(pre, heads, wide, mixers[s])

    def mix_out(s, resid, scaled, total_part, meanwhile):
        whole = line_product(two_halves(scaled), proj_out[s])
        sums = gathered_sum(jnp.concatenate([whole, as_halves(total_part)], axis=1), meanwhile)
        mixed, total = sums[:, :width], from_halves(sums[:, width:], 1)
        rr = lax.rsqrt(total / DI + EPS)
        return resid + mixed * rr, mixed, rr

    wide_in_0 = rms_norm(wide_tokens.astype(FLOAT), norm_ins[0]).astype(HALF)
    pre_0, y_0, scaled_0, total_0 = mix_in(0, wide_in_0)
    proj.append(both_halves(after(mine[1], scaled_0)))
    proj_out.append(both_halves(after(mine_out[1], scaled_0)))
    tables = route_tables(spread(after(meta, scaled_0)), top, capacity, 2)
    plain = [[table[0] for table in tables[s]] for s in layers]
    scaling = [[table[1] for table in tables[s]] for s in layers]
    middle_0, mixed_0, rr_0 = mix_out(0, tokens_now, scaled_0, total_0, tables)
    kept = Kept()
    kept.rows_0, kept.rows_1, kept.answer_1, kept.grads_0, kept.grads_1 = {}, {}, {}, {}, {}

    def expert_0(index, rows):
        kept.rows_0[index], answer = expert_forward(rows, experts[0])
        return answer

    def own_0(tokens_all, rows):
        kept.shared_0 = shared_forward(tokens_all, shared[0])
        kept.part_0 = home_part(kept.shared_0[2], shared[0])
        return kept.part_0

    def beside_0(index, result):
        part = outer(scaling[0][index], result) + chunk_of(kept.part_0, index)
        return part.astype(HALF)

    def aside_0(tokens_all):
        kept.grads = spread(after(grad_now.astype(HALF), tokens_all))
        return kept.grads

    total, rows_0, mids_0 = through_experts(
        rms_norm(middle_0, norm_mids[0]).astype(HALF), plain[0], expert_0, own_0, beside_0, aside_0
    )
    out_0 = middle_0 + total

    wide_in_1 = spread(rms_norm(out_0, norm_ins[1]).astype(HALF))
    grad_tokens_1 = after(kept.grads, out_0)
    grad_sent = [
        project(table, chunk_of(grad_tokens_1, index)).astype(HALF)
        for index, table in enumerate(scaling[1])
    ]
    grad_rows_1 = [to_experts(grad_sent[-1])]
    if groups() > 1:
        own_rows, others = sent_ahead(grad_sent[0])
    pre_1, y_1, scaled_1, total_1 = mix_in(1, wide_in_1)
    if groups() > 1:
        own_rows = jnp.concatenate([own_rows, *after(others, scaled_1)], axis=0)
        grad_rows_1 = [own_rows, *after(grad_rows_1, scaled_1)]
    middle_1, mixed_1, rr_1 = mix_out(1, out_0, scaled_1, total_1, ())

    def expert_1(index, rows):
        kept.rows_1[index], kept.answer_1[index] = expert_forward(rows, experts[1])
        kept.grads_1[index], back = expert_backward(
            grad_rows_1[index], kept.rows_1[index], experts[1]
        )
        return back

    def own_1(tokens_all, rows):
        kept.shared_1 = shared_forward(tokens_all, shared[1])
        kept.shared_grads_1, kept.part_1 = shared_backward(
            grad_tokens_1, kept.shared_1, shared[1]
        )
        kept.sums_1 = weight_sums(
            rows,
            grad_rows_1,
            kept.rows_1,
            kept.grads_1,
            tokens_all,
            grad_tokens_1,
            kept.shared_1,
            kept.shared_grads_1,
        )
        experts_1, shared_1 = kept.sums_1
        return experts_1, kept.part_1, [made[-1] for made in shared_1]

    def beside_1(index, result):
        part = outer(plain[1][index], result) + chunk_of(kept.part_1, index)
        return part.astype(HALF)

    total, rows_1, mids_1 = through_experts(
        rms_norm(middle_1, norm_mids[1]).astype(HALF), plain[1], expert_1, own_1, beside_1
    )

    def mixer_back(s, grad_middle, along, rr, saved, meanwhile):
        wide_in, pre, y, scaled = saved
        sides = as_halves(jnp.concatenate([rr, along], axis=1))
        payload = spread(
            jnp.concatenate([grad_middle.astype(HALF), sides], axis=1), meanwhile
        )
        wide_mix, sides = payload[:, :width], from_halves(payload[:, width:], 2)
        grad_scaled = [project(wide_mix, half) for half in proj_out[s]]
        grad_scaled = jnp.concatenate(grad_scaled, axis=1)
        *grad_pre, wide_grads, grad_conv_input, grad_conv_state, step_grads = mixer_backward(
            pre, y, grad_scaled, sides, heads, mixers[s]
        )
        ends = [part[:, :wide] for part in grad_pre]
        tail = jnp.concatenate([grad_pre[0][:, wide:], grad_pre[1][:, wide : wide + LANES]], axis=1)
        mix_rr = (wide_mix * sides[:, :1]).astype(HALF)
        rest = (grad_conv_state, grad_conv_input, wide_grads, step_grads)
        return grad_pre, (wide_in, *ends), (mix_rr, *two_halves(scaled)), tail, rest

    def resid_back(resid, norm, grad_normed, grad_middle):
        _, pull_in = jax.vjp(rms_norm, resid, norm)
        grad_resid, grad_norm = pull_in(grad_normed)
        return grad_resid + grad_middle, grad_norm

    def own_layer(first_value, second_value):
        keep = jnp.where(first, first_value, second_value)
        give = jnp.where(first, second_value, first_value).astype(HALF)
        return keep.astype(FLOAT), swapped(give)

    def row_sums(value):
        return lax.psum_scatter(value, "row", scatter_dimension=0, tiled=True)

    grad_middle, along, grad_norm_mid_1 = middle_backward(
        total, grad_now, middle_1, mixed_1, norm_mids[1]
    )
    expert_grads_1, shared_grads_1 = kept.sums_1
    answers = after([kept.answer_1[index] for index in kept.answer_1], grad_middle)
    answers_back = [to_experts(answers[-1])]
    if groups() > 1:
        own_rows, others = sent_back(answers[0])
        answers_back = [jnp.concatenate([own_rows, *others], axis=0), *answers_back]
    shared_made_1 = [half_to_keep(*made) for made in shared_grads_1]
    grad_pre, to_proj, to_out, tail, rest_1 = mixer_back(
        1,
        grad_middle,
        along,
        rr_1,
        (wide_in_1, pre_1, y_1, scaled_1),
        shared_made_1,
    )
    shared_sent_1 = [row_sums(each) for each in shared_made_1]
    whole = line_product(grad_pre, proj[1])
    grad_in = gathered_sum(whole)
    grad_1, grad_norm_in_1 = resid_back(out_0, norm_ins[1], grad_in, grad_middle)

    def aside_back_0(tokens_all):
        home = home_part(after(kept.shared_1[2], tokens_all), shared[1])
        home = [
            (outer(scaling[1][index], answer) + chunk_of(home, index)).astype(HALF)
            for index, answer in enumerate(answers_back)
        ]
        home = joined(home)
        if groups() > 1:
            home = in_order([block_of(home, back) for back in range(groups())], "col")
        kept.home = lax.psum_scatter(home, "col", scatter_dimension=0, tiled=True)
        own_proj, own_out, own_tail = after((to_proj, to_out, tail), home)
        given, given_out = half_to_give(*own_proj), half_to_give(*own_out)
        made = ((*own_out, swapped(given_out)), (*own_proj, swapped(given)))
        made = [half_to_keep(*each) for each in after(made, (given, given_out))]
        kept.sent_1 = [*shared_sent_1, *[row_sums(each) for each in made]]
        kept.tail_1 = outer(own_proj[0], own_tail).astype(HALF)
        return made, kept.tail_1

    def expert_back_0(index, rows):
        kept.grads_0[index], back = expert_backward(rows, kept.rows_0[index], experts[0])
        return back

    def own_back_0(tokens_all, rows):
        kept.shared_grads_0, kept.part_0 = shared_backward(
            tokens_all, kept.shared_0, shared[0]
        )
        kept.sums_0 = weight_sums(
            rows_0,
            rows,
            kept.rows_0,
            kept.grads_0,
            mids_0,
            tokens_all,
            kept.shared_0,
            kept.shared_grads_0,
        )
        experts_0, shared_0 = kept.sums_0
        return experts_0, kept.part_0, [made[-1] for made in shared_0]

    def beside_back_0(index, result):
        part = outer(plain[0][index], result) + chunk_of(kept.part_0, index)
        return part.astype(HALF)

    total, grad_rows_0, grad_tokens_0 = through_experts(
        grad_1.astype(HALF), scaling[0], expert_back_0, own_back_0, beside_back_0, aside_back_0
    )
    sums_1, grad_tail_1 = kept.sent_1, kept.tail_1
    grad_middle, along, grad_norm_mid_0 = middle_backward(
        total, grad_1, middle_0, mixed_0, norm_mids[0]
    )
    expert_grads_0, shared_grads_0 = kept.sums_0
    shared_sums_0 = [half_to_keep(*after(made, total)) for made in shared_grads_0]
    sums_0 = [row_sums(made) for made in shared_sums_0]
    expert_out = [own_layer(a, b) for a, b in zip(expert_grads_0, expert_grads_1)]
    grad_pre, to_proj, to_out, tail, rest_0 = mixer_back(
        0,
        grad_middle,
        along,
        rr_0,
        (wide_in_0, pre_0, y_0, scaled_0),
        ([part[0] for part in expert_out], shared_sums_0, sums_1),
    )

    grad_tail_0 = outer(wide_in_0, tail).astype(HALF)
    tail_keep, tail_other = own_layer(grad_tail_0, grad_tail_1)
    given = half_to_give(*after(to_proj, grad_tail_0))
    whole = line_product(after(grad_pre, given), proj[0])
    wide_x = wide_tokens.astype(FLOAT)
    wide_r = lax.rsqrt(jnp.mean(wide_x * wide_x, axis=1, keepdims=True) + EPS)
    grad_norm_in_0 = jnp.sum(whole.astype(FLOAT) * wide_x * wide_r, axis=0)
    smalls = (
        (grad_norm_in_0, grad_norm_mid_0, *rest_0),
        (grad_norm_in_1, grad_norm_mid_1, *rest_1),
    )
    shapes = [part.shape for part in smalls[0]]
    small_keep, small_other = own_layer(flat(smalls[0]), flat(smalls[1]))
    tail_pieces = row_pieces((tail_keep + tail_other.astype(FLOAT)).astype(HALF))
    vector = small_keep + small_other.astype(FLOAT)
    lines = [shifted(vector[None], "row", back) for back in range(n_row)]
    tail_received = row_received(tail_pieces)
    proj_half = half_to_keep(*after((*to_proj, swapped(given)), whole))
    given_out = half_to_give(*after(to_out, proj_half))
    tail_received, lines = after((tail_received, lines), (proj_half, given_out))
    tail = total_of(tail_pieces[0], tail_received).astype(HALF)
    vector = jnp.sum(in_order(lines, "row"), axis=0)
    common = 2 * width + conv_state.shape[1] * state
    state_grad = tail[:, :state]
    line_received = sent_home(after(whole, proj_half))
    proj_pieces = row_pieces(after(proj_half, tail))
    proj_received = row_received(proj_pieces)
    out_half = half_to_keep(*after((*to_out, swapped(given_out)), tail))
    out_pieces = row_pieces(out_half)
    out_received = row_received(out_pieces)
    if groups() > 1:
        state_pieces = row_pieces(state_grad, "col")
        state_received = row_received(state_pieces, "col")
        lines = [shifted(vector[None, :common], "col", back) for back in range(n_col)]
        state_received, lines = after((state_received, lines), out_half)
        shared_sum = jnp.sum(in_order(lines, "col"), axis=0)
        state_grad = total_of(state_pieces[0], state_received).astype(HALF)
        state_lines = [shifted(state_grad, "col", back) for back in range(n_col)]
    else:
        state_grad = lax.psum(state_grad, "col")
        state_lines = [state_grad]
        shared_sum = lax.psum(vector[:common], "col")
    expert_out = [keep + other.astype(FLOAT) for keep, other in after(expert_out, out_half)]
    state_lines, line_received, proj_received, out_received = after(
        (state_lines, line_received, proj_received, out_received), expert_out
    )
    state_grad = in_order(state_lines, "col")
    grad_in = added_up(whole, line_received)
    sums_0.append(total_of(out_pieces[0], out_received).astype(HALF))
    sums_0.append(total_of(proj_pieces[0], proj_received).astype(HALF))
    sums_0, sums_1 = after((sums_0, sums_1), grad_in)
    grad_0, _ = resid_back(tokens_now, norm_ins[0], grad_in, grad_middle)
    out_1 = middle_1 + kept.home.astype(FLOAT)

    def own_halves(first_value, second_value):
        keep = jnp.where(first, first_value, second_value)
        give = jnp.where(first, second_value, first_value)
        return keep, swapped(give)

    def per_micro(first_value, second_value):
        keep = jnp.where(first, first_value, second_value)
        return keep, swapped(jnp.where(first, second_value, first_value).astype(HALF))

    halves = [own_halves(a, b) for a, b in zip(sums_0, sums_1)]
    outs, in_grads = per_micro(out_0, after(out_1, grad_in)), per_micro(grad_0, grad_1)
    halves = [pair(*half) for half in halves]
    grad_shared, grad_down, grad_out, grad_ends = halves
    grad_out, grad_down = [jnp.concatenate(both, axis=1) for both in (grad_out, grad_down)]
    (
        out_norm_in,
        out_norm_mid,
        out_conv_state,
        out_conv_input,
        out_wide,
        out_step,
    ) = unflat(jnp.concatenate([shared_sum, vector[common:]]), shapes)

    def stacked(keep, other):
        return jnp.stack(pair(keep, other.astype(FLOAT)))[None]

    def out(value):
        return value.astype(FLOAT)[None]

    return (
        stacked(*outs),
        stacked(*in_grads),
        out_norm_in[None],
        out(grad_ends[0][:, :inner]),
        out(grad_ends[1][:, :inner]),
        out(state_grad),
        out(tail[:, state : state + heads]),
        out_step[:1, :heads],
        out_step[1:, :heads],
        jnp.sum(out_wide[1, :inner].reshape(heads, HEAD), axis=1)[None],
        out_conv_input[None, :, :inner],
        out_conv_state[None],
        out_wide[:1, :inner],
        out(grad_out[:, :inner]),
        out_norm_mid[None],
        expert_out[0][None, None],
        expert_out[1][None, None],
        expert_out[2][None, None],
        out(grad_shared[0]),
        out(grad_shared[1]),
        out(grad_down),
    )


def solution(mesh):
    in_specs = (
        P(None, ("row", "col"), None),
        P(None, ("row", "col"), None),
        P(),
        P("section", None, ("row", "col"), None),
        P("section", None, ("row", "col"), None),
        P("section", None),
        P("section", "row", "col"),
        P("section", "row", "col"),
        P("section", "row", None),
        P("section", "row", "col"),
        P("section", "col"),
        P("section", "col"),
        P("section", "col"),
        P("section", None, "col"),
        P("section", None, None),
        P("section", "col"),
        P("section", "row", "col"),
        P("section", None),
        P("section", ("row", "col"), None, None),
        P("section", ("row", "col"), None, None),
        P("section", ("row", "col"), None, None),
        P("section", "row", "col"),
        P("section", "row", "col"),
        P("section", "row", "col"),
    )
    out_specs = (
        P("section", None, ("row", "col"), None),
        P("section", None, ("row", "col"), None),
        P("section", None),
        P("section", "row", "col"),
        P("section", "row", "col"),
        P("section", "row", None),
        P("section", "row", "col"),
        P("section", "col"),
        P("section", "col"),
        P("section", "col"),
        P("section", None, "col"),
        P("section", None, None),
        P("section", "col"),
        P("section", "row", "col"),
        P("section", None),
        P("section", ("row", "col"), None, None),
        P("section", ("row", "col"), None, None),
        P("section", ("row", "col"), None, None),
        P("section", "row", "col"),
        P("section", "row", "col"),
        P("section", "row", "col"),
    )
    return jax.shard_map(shards, mesh=mesh, in_specs=in_specs, out_specs=out_specs, check_vma=False)
```

```python
import functools

import jax
import jax.numpy as jnp
from jax import lax
from jax.experimental import pallas as pl
from jax.experimental.pallas import tpu as pltpu
from jax.sharding import PartitionSpec as P

DI = 3072
HEAD = 64
LANES = 128
CHUNK = 256
VMEM_BYTES = 48 * 2**20

EPS = 1e-05
HIGH = lax.Precision.HIGHEST
FLOAT = jnp.float32
HALF = jnp.bfloat16


def shifted(block, axis, distance):
    count = lax.axis_size(axis)
    if distance % count == 0:
        return block
    return lax.ppermute(block, axis, [(i, (i + distance) % count) for i in range(count)])


def swapped(block):
    return lax.ppermute(block, "section", [(0, 1), (1, 0)])


def after(value, *others):
    return lax.optimization_barrier((value, *others))[0]


def rms_norm(value, gain):
    return value * lax.rsqrt(jnp.mean(value * value, axis=-1, keepdims=True) + EPS) * gain


def local_docs(lengths, row_now, length):
    bounds = jnp.cumsum(lengths)[:-1]
    place = jnp.arange(length, dtype=jnp.int32)
    inner = jnp.sum((place[:, None] >= bounds[None, :]).astype(jnp.int32), axis=1)
    return inner + row_now * lengths.shape[0]


def project(left, right):
    return jnp.dot(left, right, preferred_element_type=FLOAT)


def project_back(left, right):
    return lax.dot_general(left, right, (((1,), (1,)), ((), ())), preferred_element_type=FLOAT)


def outer(left, right):
    return lax.dot_general(left, right, (((0,), (0,)), ((), ())), preferred_element_type=FLOAT)


def silu_slope(value):
    sigma = jax.nn.sigmoid(value)
    return sigma * (1.0 + value * (1.0 - sigma))


def groups():
    count = lax.axis_size("col")
    return count if count <= 4 else 1


def spread(block, meanwhile=()):
    if groups() == 1:
        return lax.all_gather(block, "col", axis=0, tiled=True)
    received = [shifted(block, "col", back) for back in range(1, groups())]
    return jnp.concatenate([block, *after(received, meanwhile)], axis=0)


def in_order(blocks, axis):
    count = len(blocks)
    if count == 1:
        return blocks[0]
    rows = blocks[0].shape[0]
    line = jnp.concatenate(blocks[::-1] + blocks[:0:-1], axis=0)
    start = (count - 1 - lax.axis_index(axis)) * rows
    return lax.dynamic_slice_in_dim(line, start, count * rows, axis=0)


def sent_home(rows):
    if groups() == 1:
        return lax.psum_scatter(rows, "col", scatter_dimension=0, tiled=True)
    return [shifted(block_of(rows, back), "col", -back) for back in range(1, groups())]


def added_up(rows, received):
    if groups() == 1:
        return received.astype(FLOAT)
    return sum([part.astype(FLOAT) for part in received], block_of(rows, 0).astype(FLOAT))


def gathered_sum(rows, meanwhile=()):
    return added_up(rows, after(sent_home(rows), meanwhile))


def exchanged(rows, axis):
    return lax.all_to_all(rows, axis, split_axis=0, concat_axis=0, tiled=True)


def as_halves(columns):
    high = lax.reduce_precision(columns, 8, 7)
    both = jnp.concatenate([high, columns - high], axis=1).astype(HALF)
    return jnp.pad(both, ((0, 0), (0, LANES - both.shape[1])))


def from_halves(tile, count):
    return tile[:, :count].astype(FLOAT) + tile[:, count : 2 * count].astype(FLOAT)


def block_of(values, back):
    rows = values.shape[0] // groups()
    return values[back * rows : (back + 1) * rows]


def turn():
    place = lax.axis_index("col") if groups() > 1 else jnp.int32(0)
    return place.astype(jnp.int32).reshape(1)


def chunk_of(rows, index):
    if groups() == 1:
        return rows
    own = rows.shape[0] // groups()
    return rows[own:] if index else rows[:own]


def route_tables(meta, top, capacity, layers):
    n_row, n_col = lax.axis_size("row"), lax.axis_size("col")
    place = jnp.arange(n_row)
    tables = [[] for _ in range(layers)]
    for index in range(min(groups(), 2)):
        now = chunk_of(meta, index)
        count = now.shape[0]
        slots = count * n_col * capacity // meta.shape[0]
        rows = place
        if groups() > 1 and index == 0:
            rows = lax.rem(lax.axis_index("row") + place, n_row)
        experts = (rows * n_col + lax.axis_index("col")).astype(FLOAT)
        now = now.reshape(count, layers, 2, top).transpose(1, 2, 3, 0)
        match = now[:, None, 0] == experts[None, :, None, None]
        hit = jnp.any(match, axis=2)
        weight = jnp.sum(jnp.where(match, now[:, None, 1], 0.0), axis=2)
        order = jnp.arange(count, dtype=jnp.int32)
        triangle = (order[:, None] <= order[None, :]).astype(HALF)
        rank = project(hit.astype(HALF).reshape(-1, count), triangle).reshape(hit.shape)
        slot = jnp.arange(1, slots + 1, dtype=jnp.int32).astype(FLOAT)
        chosen = (rank[:, :, None, :] == slot[:, None]) & hit[:, :, None, :]
        shape = (layers, n_row * slots, count)
        plain = chosen.astype(HALF).reshape(shape)
        scaled = jnp.where(chosen, weight[:, :, None, :], 0.0).astype(HALF).reshape(shape)
        for s in range(layers):
            tables[s].append((plain[s], scaled[s]))
    return tables


def to_experts(rows):
    return exchanged(rows.astype(HALF), "row")


def summed_rows(values, reverse):
    step = min(values.shape[0], CHUNK)
    count = values.shape[0] // step
    place = lax.broadcasted_iota(jnp.int32, (step, step), 0)
    other = lax.broadcasted_iota(jnp.int32, (step, step), 1)
    before = (place <= other) if reverse else (place >= other)
    triangle = before.astype(FLOAT)
    carry = jnp.zeros((1, values.shape[1]), FLOAT)
    parts = [None] * count
    for index in reversed(range(count)) if reverse else range(count):
        part = values[index * step : (index + 1) * step]
        run = jnp.dot(triangle, part, precision=HIGH, preferred_element_type=FLOAT) + carry
        carry = run[:1] if reverse else run[step - 1 :]
        parts[index] = run
    return parts[0] if count == 1 else jnp.concatenate(parts, axis=0)


def head_columns(rows, columns, head_width):
    head = lax.broadcasted_iota(jnp.int32, (rows, columns), 0) * head_width
    column = lax.broadcasted_iota(jnp.int32, (rows, columns), 1)
    return ((column >= head) & (column < head + head_width)).astype(FLOAT)


def sigmoid(value):
    return 1.0 / (1.0 + jnp.exp(-value))


def step_sizes(step_pre, step_row_ref):
    shifted_pre = step_pre + step_row_ref[0:1, :]
    sizes = jnp.maximum(shifted_pre, 0.0) + jnp.log1p(jnp.exp(-jnp.abs(shifted_pre)))
    return shifted_pre, sizes, -jnp.exp(step_row_ref[1:2, :])


def conv_rows(values, weight_ref, columns, marks_ref):
    width = weight_ref.shape[0]
    result = values * weight_ref[width - 1 : width, columns]
    for back in range(1, width):
        moved = pltpu.roll(values, back, 0) * marks_ref[:, back : back + 1]
        result = result + moved * weight_ref[width - 1 - back : width - back, columns]
    return result


def conv_rows_back(grad, values, weight_ref, columns, marks_ref, weight_grad_ref):
    width = weight_ref.shape[0]
    rows = values.shape[0]
    result = grad * weight_ref[width - 1 : width, columns]
    weight_grad_ref[width - 1 : width, columns] = jnp.sum(grad * values, axis=0, keepdims=True)
    for back in range(1, width):
        kept = grad * marks_ref[:, back : back + 1]
        taps = jnp.sum(kept * pltpu.roll(values, back, 0), axis=0, keepdims=True)
        weight_grad_ref[width - 1 - back : width - back, columns] = taps
        moved = pltpu.roll(kept, rows - back, 0)
        result = result + moved * weight_ref[width - 1 - back : width - back, columns]
    return result


def copy_in_order(source_ref, target_ref, place_ref, parts):
    if parts == 1:
        return source_ref
    rows = source_ref.shape[0] // parts
    for index in range(parts):
        target_ref[index * rows : (index + 1) * rows, :] = source_ref[
            block_rows(index, rows, place_ref, parts), :
        ]
    return target_ref


def block_rows(index, rows, place_ref, parts):
    if parts == 1:
        return slice(0, rows)
    back = lax.rem(place_ref[0] - index + parts, parts)
    return pl.ds(pl.multiple_of(back * rows, rows), rows)


def mixer_forward_kernel(
    heads,
    parts,
    pre_in_ref,
    pre_other_in_ref,
    conv_input_ref,
    conv_state_ref,
    step_row_ref,
    wide_row_ref,
    marks_ref,
    labels_ref,
    place_ref,
    y_ref,
    scaled_ref,
    total_ref,
    pre_ref,
    pre_other_ref,
    x_ref,
    dosed_ref,
    keys_ref,
    queries_ref,
):
    length, wide = y_ref.shape
    states = conv_state_ref.shape[1] // 2
    state_at, step_at = wide, wide
    head_width = HEAD
    pre_ref = copy_in_order(pre_in_ref, pre_ref, place_ref, parts)
    pre_other_ref = copy_in_order(pre_other_in_ref, pre_other_ref, place_ref, parts)
    _, sizes, rate = step_sizes(pre_other_ref[:, step_at : step_at + LANES], step_row_ref)
    running = summed_rows(sizes * rate, False)
    running_t = running.T
    expand = head_columns(LANES, wide, head_width)
    for start in range(0, wide, LANES):
        columns = slice(start, start + LANES)
        conv = conv_rows(
            pre_other_ref[:, columns], conv_input_ref, columns, marks_ref
        )
        x = conv * sigmoid(conv)
        x_ref[:, columns] = x
        dose = jnp.dot(sizes, expand[:, columns], precision=HIGH, preferred_element_type=FLOAT)
        dosed_ref[:, columns] = (x * dose).astype(HALF)
    for part, target in ((0, keys_ref), (1, queries_ref)):
        columns = slice(part * states, (part + 1) * states)
        conv = conv_rows(
            pre_ref[:, state_at + part * states : state_at + (part + 1) * states],
            conv_state_ref,
            columns,
            marks_ref,
        )
        target[...] = (conv * sigmoid(conv)).astype(HALF)
    block = min(length, CHUNK)
    place = lax.broadcasted_iota(jnp.int32, (block, block), 0)
    other = lax.broadcasted_iota(jnp.int32, (block, block), 1)
    for late in range(length // block):
        rows = slice(late * block, (late + 1) * block)
        for early in range(late + 1):
            past = slice(early * block, (early + 1) * block)
            same = marks_ref[rows, 0:1] == labels_ref[:, past]
            if late == early:
                same = same & (place >= other)
            mask = jnp.where(same, 0.0, -1e30)
            scores = lax.dot_general(
                queries_ref[rows, :],
                keys_ref[past, :],
                (((1,), (1,)), ((), ())),
                preferred_element_type=FLOAT,
            )
            for head in range(heads):
                columns = slice(head * head_width, (head + 1) * head_width)
                spread_log = running[rows, head : head + 1] - running_t[head : head + 1, past]
                mixing = (jnp.exp(spread_log + mask) * scores).astype(HALF)
                inner = jnp.dot(mixing, dosed_ref[past, columns], preferred_element_type=FLOAT)
                if early == 0:
                    y_ref[rows, columns] = inner
                else:
                    y_ref[rows, columns] += inner
    total = jnp.zeros((length, 1), FLOAT)
    for start in range(0, wide, LANES):
        columns = slice(start, start + LANES)
        y = y_ref[:, columns]
        if heads * head_width < start + LANES:
            lane = lax.broadcasted_iota(jnp.int32, y.shape, 1) + start
            y = jnp.where(lane < heads * head_width, y, 0.0)
        y = y + wide_row_ref[1:2, columns] * x_ref[:, columns]
        gate = pre_ref[:, columns]
        gated = y * gate * sigmoid(gate)
        y_ref[:, columns] = y
        scaled = (gated * wide_row_ref[0:1, columns]).astype(HALF)
        each = length // parts
        for index in range(parts):
            block_at = block_rows(index, each, place_ref, parts)
            scaled_ref[block_at, columns] = scaled[index * each : (index + 1) * each]
        total = total + jnp.sum(gated * gated, axis=1, keepdims=True)
    each = length // parts
    for index in range(parts):
        block_at = block_rows(index, each, place_ref, parts)
        total_ref[block_at, :] = total[index * each : (index + 1) * each]


def mixer_backward_kernel(
    heads,
    parts,
    inner_all,
    pre_in_ref,
    pre_other_in_ref,
    y_ref,
    grad_in_ref,
    sides_in_ref,
    conv_input_ref,
    conv_state_ref,
    step_row_ref,
    wide_row_ref,
    marks_ref,
    labels_ref,
    place_ref,
    grad_pre_ref,
    grad_pre_other_ref,
    wide_grad_ref,
    conv_input_grad_ref,
    conv_state_grad_ref,
    step_grad_ref,
    pre_ref,
    pre_other_ref,
    grad_ref,
    sides_ref,
    x_ref,
    dosed_ref,
    dose_ref,
    slope_ref,
    dy_ref,
    z_ref,
    bc_ref,
    bc_slope_ref,
    bc_grad_ref,
):
    length, wide = y_ref.shape
    states = conv_state_ref.shape[1] // 2
    state_at, step_at = wide, wide
    head_width = HEAD
    each = length // parts
    pre_ref = copy_in_order(pre_in_ref, pre_ref, place_ref, parts)
    pre_other_ref = copy_in_order(pre_other_in_ref, pre_other_ref, place_ref, parts)
    grad_ref = copy_in_order(grad_in_ref, grad_ref, place_ref, parts)
    sides_ref = copy_in_order(sides_in_ref, sides_ref, place_ref, parts)

    def put(target_ref, value, start):
        for index in range(parts):
            target_ref[block_rows(index, each, place_ref, parts), start : start + LANES] = value[
                index * each : (index + 1) * each
            ]

    shifted_pre, sizes, rate = step_sizes(pre_other_ref[:, step_at : step_at + LANES], step_row_ref)
    running = summed_rows(sizes * rate, False)
    running_t = running.T
    expand = head_columns(LANES, wide, head_width)
    rr = sides_ref[:, 0:1]
    pull = rr * rr * rr * sides_ref[:, 1:2] * (1.0 / inner_all)
    for start in range(0, wide, LANES):
        columns = slice(start, start + LANES)
        gate = pre_ref[:, columns]
        y = y_ref[:, columns]
        grad = grad_ref[:, columns]
        gain = wide_row_ref[0:1, columns]
        sigma = sigmoid(gate)
        silu = gate * sigma
        gated = y * silu
        normed = gated * rr
        wide_grad_ref[0:1, columns] = jnp.sum(grad * normed, axis=0, keepdims=True)
        grad_gated = rr * gain * grad - gated * pull
        slope = sigma * (1.0 + gate * (1.0 - sigma))
        put(grad_pre_ref, (grad_gated * y * slope).astype(HALF), start)
        dy = grad_gated * silu
        dy_ref[:, columns] = dy
        conv = conv_rows(
            pre_other_ref[:, columns], conv_input_ref, columns, marks_ref
        )
        sigma = sigmoid(conv)
        x = conv * sigma
        x_ref[:, columns] = x
        slope_ref[:, columns] = sigma * (1.0 + conv * (1.0 - sigma))
        dose = jnp.dot(sizes, expand[:, columns], precision=HIGH, preferred_element_type=FLOAT)
        dose_ref[:, columns] = dose
        dosed_ref[:, columns] = (x * dose).astype(HALF)
        wide_grad_ref[1:2, columns] = jnp.sum(dy * x, axis=0, keepdims=True)
    for start in range(0, 2 * states, LANES):
        columns = slice(start, start + LANES)
        conv = conv_rows(
            pre_ref[:, state_at + start : state_at + start + LANES],
            conv_state_ref,
            columns,
            marks_ref,
        )
        sigma = sigmoid(conv)
        bc_ref[:, columns] = (conv * sigma).astype(HALF)
        bc_slope_ref[:, columns] = sigma * (1.0 + conv * (1.0 - sigma))
    block = min(length, CHUNK)
    place = lax.broadcasted_iota(jnp.int32, (block, block), 0)
    other = lax.broadcasted_iota(jnp.int32, (block, block), 1)
    z_ref[...] = jnp.zeros(z_ref.shape, FLOAT)
    bc_grad_ref[...] = jnp.zeros(bc_grad_ref.shape, FLOAT)
    for late in range(length // block):
        rows = slice(late * block, (late + 1) * block)
        for early in range(late + 1):
            past = slice(early * block, (early + 1) * block)
            same = marks_ref[past, 0:1] == labels_ref[:, rows]
            if late == early:
                same = same & (place <= other)
            mask = jnp.where(same, 0.0, -1e30)
            keys = bc_ref[past, :states]
            queries = bc_ref[rows, states:]
            scores = lax.dot_general(
                keys, queries, (((1,), (1,)), ((), ())), preferred_element_type=FLOAT
            )
            mixed = jnp.zeros((block, block), FLOAT)
            for head in range(heads):
                columns = slice(head * head_width, (head + 1) * head_width)
                spread_log = running_t[head : head + 1, rows] - running[past, head : head + 1]
                decay = jnp.exp(spread_log + mask)
                mixing = (decay * scores).astype(HALF)
                dy = dy_ref[rows, columns].astype(HALF)
                z_ref[past, columns] += jnp.dot(mixing, dy, preferred_element_type=FLOAT)
                along = lax.dot_general(
                    dosed_ref[past, columns],
                    dy,
                    (((1,), (1,)), ((), ())),
                    preferred_element_type=FLOAT,
                )
                mixed = mixed + decay * along
            mixed = mixed.astype(HALF)
            bc_grad_ref[past, :states] += jnp.dot(mixed, queries, preferred_element_type=FLOAT)
            bc_grad_ref[rows, states:] += lax.dot_general(
                mixed, keys, (((0,), (0,)), ((), ())), preferred_element_type=FLOAT
            )
    direct = jnp.zeros((length, LANES), FLOAT)
    balance = jnp.zeros((length, LANES), FLOAT)
    for start in range(0, wide, LANES):
        columns = slice(start, start + LANES)
        x, z, dy = x_ref[:, columns], z_ref[:, columns], dy_ref[:, columns]
        skip = wide_row_ref[1:2, columns]
        collapse = (((1,), (1,)), ((), ()))
        both = dy.astype(HALF).astype(FLOAT) * (y_ref[:, columns] - skip * x)
        both = both - dosed_ref[:, columns].astype(FLOAT) * z
        heads_of = expand[:, columns]
        direct = direct + lax.dot_general(
            x * z, heads_of, collapse, precision=HIGH, preferred_element_type=FLOAT
        )
        balance = balance + lax.dot_general(
            both, heads_of, collapse, precision=HIGH, preferred_element_type=FLOAT
        )
        grad_conv = (dose_ref[:, columns] * z + skip * dy) * slope_ref[:, columns]
        grad_in = conv_rows_back(
            grad_conv,
            pre_other_ref[:, columns],
            conv_input_ref,
            columns,
            marks_ref,
            conv_input_grad_ref,
        )
        put(grad_pre_other_ref, grad_in.astype(HALF), start)
    for start in range(0, 2 * states, LANES):
        columns = slice(start, start + LANES)
        grad_in = conv_rows_back(
            bc_grad_ref[:, columns] * bc_slope_ref[:, columns],
            pre_ref[:, state_at + start : state_at + start + LANES],
            conv_state_ref,
            columns,
            marks_ref,
            conv_state_grad_ref,
        )
        put(grad_pre_ref, grad_in.astype(HALF), state_at + start)
    crossing = summed_rows(balance, True)
    grad_step = (direct + rate * crossing) * sigmoid(shifted_pre)
    put(grad_pre_other_ref, grad_step.astype(HALF), step_at)
    for start in range(step_at + LANES, grad_pre_other_ref.shape[1], LANES):
        put(grad_pre_other_ref, jnp.zeros((length, LANES), HALF), start)
    step_grad_ref[0:1, :] = jnp.sum(grad_step, axis=0, keepdims=True)
    step_grad_ref[1:2, :] = rate * jnp.sum(sizes * crossing, axis=0, keepdims=True)


def ordered_copy(shape):
    return pltpu.VMEM(shape if groups() > 1 else (8, LANES), FLOAT)


def whole_call(kernel, inputs, results, scratch, name):
    whole = pl.BlockSpec(memory_space=pltpu.VMEM)
    place = pl.BlockSpec(memory_space=pltpu.SMEM)
    return pl.pallas_call(
        kernel,
        in_specs=[whole] * (inputs - 1) + [place],
        out_shape=results,
        scratch_shapes=scratch,
        compiler_params=pltpu.CompilerParams(vmem_limit_bytes=VMEM_BYTES),
        name=name,
    )


def mixer_forward(pre, heads, wide, mixer):
    length = pre[0].shape[0]
    kernel = functools.partial(mixer_forward_kernel, heads, groups())
    states = mixer[1].shape[1] // 2
    return whole_call(
        kernel,
        2 + len(mixer),
        (
            jax.ShapeDtypeStruct((length, wide), FLOAT),
            jax.ShapeDtypeStruct((length, wide), HALF),
            jax.ShapeDtypeStruct((length, 1), FLOAT),
        ),
        [
            ordered_copy(pre[0].shape),
            ordered_copy(pre[1].shape),
            pltpu.VMEM((length, wide), FLOAT),
            pltpu.VMEM((length, wide), HALF),
            pltpu.VMEM((length, states), HALF),
            pltpu.VMEM((length, states), HALF),
        ],
        "mixer_forward",
    )(*pre, *mixer)


def mixer_backward(pre, y, grad, sides, heads, mixer):
    length, wide = y.shape
    kernel = functools.partial(mixer_backward_kernel, heads, groups(), DI)
    double = mixer[1].shape[1]
    square = pltpu.VMEM((length, wide), FLOAT)
    return whole_call(
        kernel,
        5 + len(mixer),
        (
            jax.ShapeDtypeStruct(pre[0].shape, HALF),
            jax.ShapeDtypeStruct(pre[1].shape, HALF),
            jax.ShapeDtypeStruct((2, wide), FLOAT),
            jax.ShapeDtypeStruct((4, wide), FLOAT),
            jax.ShapeDtypeStruct((4, double), FLOAT),
            jax.ShapeDtypeStruct((2, LANES), FLOAT),
        ),
        [
            ordered_copy(pre[0].shape),
            ordered_copy(pre[1].shape),
            ordered_copy(y.shape),
            ordered_copy(sides.shape),
            square,
            pltpu.VMEM((length, wide), HALF),
            square,
            square,
            square,
            square,
            pltpu.VMEM((length, double), HALF),
            pltpu.VMEM((length, double), FLOAT),
            pltpu.VMEM((length, double), FLOAT),
        ],
        "mixer_backward",
    )(*pre, y, grad, sides, *mixer)


def joined(parts):
    return parts[0] if len(parts) == 1 else jnp.concatenate(parts, axis=0)


def row_slices(rows):
    count = lax.axis_size("row")
    each = rows.shape[0] // count
    return [rows[index * each : (index + 1) * each] for index in range(count)]


def sent_ahead(rows):
    shares = row_slices(rows)
    return shares[0], [shifted(share, "row", ahead) for ahead, share in enumerate(shares) if ahead]


def sent_back(rows):
    shares = row_slices(rows)
    return shares[0], [shifted(share, "row", -ahead) for ahead, share in enumerate(shares) if ahead]


def through_experts(block, tables, expert, own, beside, aside=None):
    if groups() == 1:
        tokens = spread(block)
        sent = project(tables[0], tokens).astype(HALF)
        arrived = to_experts(sent)
        answer = expert(0, arrived)
        if aside is not None:
            answer = after(answer, aside(after(tokens, sent)))
        answered = to_experts(answer)
        answered = after(answered, own(after(tokens, answer), after([arrived], answer)))
        return gathered_sum(beside(0, answered)), [arrived], tokens
    count = block.shape[0]
    first, others = sent_ahead(project(tables[0], block).astype(HALF))
    line = [shifted(block, "col", back) for back in range(1, groups())]
    line = after(line, others)
    tokens = jnp.concatenate([block, *line], axis=0)
    rows_own = jnp.concatenate([first, *others], axis=0)
    sent = project(tables[1], chunk_of(tokens, 1)).astype(HALF)
    arrived = to_experts(sent)
    answer_own = expert(0, after(rows_own, sent))
    held = () if aside is None else aside(after(tokens, sent))
    answer = after(expert(1, arrived), answer_own, held)
    answered = to_experts(answer)
    answered = after(answered, own(after(tokens, answer), after([rows_own, arrived], answer)))
    part = beside(1, answered)
    first, others = sent_back(answer_own)
    line = [
        shifted(part[at * count : (at + 1) * count], "col", -at - 1) for at in range(groups() - 1)
    ]
    others, line = after((others, line))
    total = beside(0, jnp.concatenate([first, *others], axis=0)).astype(FLOAT)
    return sum([each.astype(FLOAT) for each in line], total), [rows_own, arrived], tokens


def line_product(values, weights):
    return sum(project_back(value, weight) for value, weight in zip(values, weights)).astype(HALF)


def expert_forward(rows, experts):
    gate_e = project(rows, experts[0])
    lift_e = project(rows, experts[1])
    act_e = (jax.nn.silu(gate_e) * lift_e).astype(HALF)
    return (gate_e, lift_e, act_e), project(act_e, experts[2]).astype(HALF)


def expert_backward(rows, kept, experts):
    gate_e, lift_e, _ = kept
    grad_act = project_back(rows, experts[2])
    grad_gate = (grad_act * lift_e * silu_slope(gate_e)).astype(HALF)
    grad_lift = (grad_act * jax.nn.silu(gate_e)).astype(HALF)
    back = project_back(grad_gate, experts[0]) + project_back(grad_lift, experts[1])
    return (grad_gate, grad_lift), back.astype(HALF)


def shared_forward(tokens, shared):
    hidden = shared.shape[1] // 3
    gate_s = project(tokens, shared[:, :hidden])
    lift_s = project(tokens, shared[:, hidden : 2 * hidden])
    return gate_s, lift_s, (jax.nn.silu(gate_s) * lift_s).astype(HALF)


def shared_backward(tokens, kept, shared):
    hidden = shared.shape[1] // 3
    gate_s, lift_s, _ = kept
    grad_act = project(tokens, shared[:, 2 * hidden :])
    grad_gate = (grad_act * lift_s * silu_slope(gate_s)).astype(HALF)
    grad_lift = (grad_act * jax.nn.silu(gate_s)).astype(HALF)
    part = project_back(grad_gate, shared[:, :hidden])
    part = part + project_back(grad_lift, shared[:, hidden : 2 * hidden])
    return (grad_gate, grad_lift), part


def home_part(act_s, shared):
    return project_back(act_s, shared[:, 2 * (shared.shape[1] // 3) :])


def weight_sums(rows_in, rows_out, kept, grads, tokens_in, tokens_out, kept_s, grads_s):
    rows_in, rows_out = joined(rows_in), joined(rows_out)
    experts = (
        outer(rows_in, joined([grads[index][0] for index in grads])).astype(HALF),
        outer(rows_in, joined([grads[index][1] for index in grads])).astype(HALF),
        outer(joined([kept[index][2] for index in kept]), rows_out).astype(HALF),
    )
    shared = ((tokens_in, *grads_s), (tokens_out, *two_halves(kept_s[2])))
    return experts, [(*each, swapped(half_to_give(*each))) for each in shared]


def middle_backward(grad_normed, grad_out, middle, mixed, norm_mid):
    _, pull_mid = jax.vjp(rms_norm, middle, norm_mid)
    grad_middle, grad_norm_mid = pull_mid(grad_normed)
    grad_middle = grad_middle + grad_out
    along = jnp.sum(grad_middle * mixed, axis=1, keepdims=True)
    return grad_middle, along, grad_norm_mid


def two_halves(values):
    middle = values.shape[1] // 2
    return values[:, :middle], values[:, middle:]


def half_to_give(left, first_right, second_right):
    first = lax.axis_index("section") == 0
    return outer(left, jnp.where(first, second_right, first_right)).astype(HALF)


def half_to_keep(left, first_right, second_right, given):
    first = lax.axis_index("section") == 0
    keep = outer(left, jnp.where(first, first_right, second_right))
    return (keep + given.astype(FLOAT)).astype(HALF)


def row_pieces(values, axis="row"):
    count = lax.axis_size(axis)
    rows = values.shape[0] // count
    index = [lax.rem(lax.axis_index(axis) + ahead, count) * rows for ahead in range(count)]
    return [lax.dynamic_slice_in_dim(values, at, rows, axis=0) for at in index]


def total_of(own, received):
    return sum([part.astype(FLOAT) for part in received], own.astype(FLOAT))


def row_received(pieces, axis="row"):
    return [shifted(piece, axis, ahead) for ahead, piece in enumerate(pieces) if ahead]


class Kept:
    pass


def flat(parts):
    return jnp.concatenate([part.reshape(-1) for part in parts])


def unflat(vector, shapes):
    result, start = [], 0
    for shape in shapes:
        size = 1
        for entry in shape:
            size *= entry
        result.append(vector[start : start + size].reshape(shape))
        start += size
    return result


def widened(value, columns):
    return jnp.pad(value, ((0, 0), (0, columns - value.shape[1])))


def shards(
    tokens,
    cotangent,
    doc_lengths,
    routes,
    gates,
    norm_in,
    proj_gate,
    proj_input,
    proj_state,
    proj_step,
    step_bias,
    decay_log,
    skip_gain,
    conv_input,
    conv_state,
    gate_norm,
    proj_output,
    norm_mid,
    expert_gate,
    expert_up,
    expert_down,
    shared_gate,
    shared_up,
    shared_down,
):
    section_now = lax.axis_index("section")
    first = section_now == 0
    row_now = lax.axis_index("row")
    n_row, n_col = lax.axis_size("row"), lax.axis_size("col")
    count = tokens.shape[1]
    top = routes.shape[3]
    capacity = count * top * 4 // (3 * n_row * n_col)
    width = tokens.shape[2]
    heads = step_bias.shape[1]
    inner = gate_norm.shape[1]
    state = conv_state.shape[2]
    wide = -(-inner // LANES) * LANES
    layers = range(2)

    def pair(own, other):
        return (jnp.where(first, own, other), jnp.where(first, other, own))

    tokens_now = lax.dynamic_index_in_dim(tokens, section_now, 0, keepdims=False)
    grad_now = lax.dynamic_index_in_dim(cotangent, section_now, 0, keepdims=False)

    halves = (
        jnp.concatenate([widened(proj_gate[0], wide), proj_state[0]], axis=1),
        jnp.concatenate([widened(proj_input[0], wide), widened(proj_step[0], state)], axis=1),
    )
    keep, give = jnp.where(first, *halves), jnp.where(first, *halves[::-1])
    mine = pair(keep, swapped(give))

    def both_halves(half):
        whole = lax.all_gather(half, ("section", "row"), axis=0, tiled=True)
        return whole.reshape(2, n_row * half.shape[0], half.shape[1])

    def both_layers(weight):
        whole = lax.all_gather(weight, ("section", "row"), axis=0, tiled=True)
        return whole.reshape(2, n_row * weight.shape[0], weight.shape[1])

    proj = [both_halves(mine[0])]
    halves = two_halves(widened(proj_output[0], wide))
    keep, give = jnp.where(first, *halves), jnp.where(first, *halves[::-1])
    mine_out = pair(keep, swapped(give))
    proj_out = [both_halves(mine_out[0])]
    own_experts = (expert_gate[0, 0], expert_up[0, 0], expert_down[0, 0])
    experts = list(zip(*[pair(weight, swapped(weight)) for weight in own_experts]))
    wide_tokens = spread(tokens_now.astype(HALF), experts)
    shared = both_layers(jnp.concatenate([shared_gate[0], shared_up[0], shared_down[0]], axis=1))

    small_in = (
        norm_in[0],
        norm_mid[0],
        widened(conv_input[0], wide),
        conv_state[0],
        widened(jnp.concatenate([step_bias, decay_log], axis=0), LANES),
        widened(jnp.concatenate([gate_norm, jnp.repeat(skip_gain, HEAD, axis=1)], axis=0), wide),
    )
    vector = flat(small_in)
    small_all = [unflat(part, [v.shape for v in small_in]) for part in pair(vector, swapped(vector))]
    norm_ins = [part[0] for part in small_all]
    norm_mids = [part[1] for part in small_all]

    meta = jnp.concatenate([routes.astype(FLOAT), gates], axis=3)[0]
    keep = lax.dynamic_index_in_dim(meta, section_now, 0, keepdims=False)
    give = lax.dynamic_index_in_dim(meta, 1 - section_now, 0, keepdims=False)
    meta = jnp.concatenate(pair(keep, swapped(give)), axis=1)

    lengths = lax.dynamic_slice(
        doc_lengths, (section_now, row_now, 0), (1, 1, doc_lengths.shape[2])
    )
    labels = local_docs(lengths[0, 0], row_now, n_col * count)
    marks = [labels.astype(FLOAT)]
    for back in range(1, conv_input.shape[1]):
        prior = jnp.pad(labels, (back, 0), constant_values=-1)[:-back]
        marks.append((prior == labels).astype(FLOAT))
    marks = jnp.stack(marks, axis=1)
    label_row = labels.astype(FLOAT)[None]
    place = turn()
    mixers = [
        (conv_in, conv_st, step_row, wide_row, marks, label_row, place)
        for _, _, conv_in, conv_st, step_row, wide_row in small_all
    ]

    def mix_in(s, wide_in):
        pre = [project(wide_in, half) for half in proj[s]]
        return pre, *mixer_forward(pre, heads, wide, mixers[s])

    def mix_out(s, resid, scaled, total_part, meanwhile):
        whole = line_product(two_halves(scaled), proj_out[s])
        sums = gathered_sum(jnp.concatenate([whole, as_halves(total_part)], axis=1), meanwhile)
        mixed, total = sums[:, :width], from_halves(sums[:, width:], 1)
        rr = lax.rsqrt(total / DI + EPS)
        return resid + mixed * rr, mixed, rr

    wide_in_0 = rms_norm(wide_tokens.astype(FLOAT), norm_ins[0]).astype(HALF)
    pre_0, y_0, scaled_0, total_0 = mix_in(0, wide_in_0)
    proj.append(both_halves(after(mine[1], scaled_0)))
    proj_out.append(both_halves(after(mine_out[1], scaled_0)))
    tables = route_tables(spread(after(meta, scaled_0)), top, capacity, 2)
    plain = [[table[0] for table in tables[s]] for s in layers]
    scaling = [[table[1] for table in tables[s]] for s in layers]
    middle_0, mixed_0, rr_0 = mix_out(0, tokens_now, scaled_0, total_0, tables)
    kept = Kept()
    kept.rows_0, kept.rows_1, kept.answer_1, kept.grads_0, kept.grads_1 = {}, {}, {}, {}, {}

    def expert_0(index, rows):
        kept.rows_0[index], answer = expert_forward(rows, experts[0])
        return answer

    def own_0(tokens_all, rows):
        kept.shared_0 = shared_forward(tokens_all, shared[0])
        kept.part_0 = home_part(kept.shared_0[2], shared[0])
        return kept.part_0

    def beside_0(index, result):
        part = outer(scaling[0][index], result) + chunk_of(kept.part_0, index)
        return part.astype(HALF)

    def aside_0(tokens_all):
        kept.grads = spread(after(grad_now.astype(HALF), tokens_all))
        return kept.grads

    total, rows_0, mids_0 = through_experts(
        rms_norm(middle_0, norm_mids[0]).astype(HALF), plain[0], expert_0, own_0, beside_0, aside_0
    )
    out_0 = middle_0 + total

    wide_in_1 = spread(rms_norm(out_0, norm_ins[1]).astype(HALF))
    grad_tokens_1 = after(kept.grads, out_0)
    grad_sent = [
        project(table, chunk_of(grad_tokens_1, index)).astype(HALF)
        for index, table in enumerate(scaling[1])
    ]
    grad_rows_1 = [to_experts(grad_sent[-1])]
    if groups() > 1:
        own_rows, others = sent_ahead(grad_sent[0])
    pre_1, y_1, scaled_1, total_1 = mix_in(1, wide_in_1)
    if groups() > 1:
        own_rows = jnp.concatenate([own_rows, *after(others, scaled_1)], axis=0)
        grad_rows_1 = [own_rows, *after(grad_rows_1, scaled_1)]
    middle_1, mixed_1, rr_1 = mix_out(1, out_0, scaled_1, total_1, ())

    def expert_1(index, rows):
        kept.rows_1[index], kept.answer_1[index] = expert_forward(rows, experts[1])
        kept.grads_1[index], back = expert_backward(
            grad_rows_1[index], kept.rows_1[index], experts[1]
        )
        return back

    def own_1(tokens_all, rows):
        kept.shared_1 = shared_forward(tokens_all, shared[1])
        kept.shared_grads_1, kept.part_1 = shared_backward(
            grad_tokens_1, kept.shared_1, shared[1]
        )
        kept.sums_1 = weight_sums(
            rows,
            grad_rows_1,
            kept.rows_1,
            kept.grads_1,
            tokens_all,
            grad_tokens_1,
            kept.shared_1,
            kept.shared_grads_1,
        )
        experts_1, shared_1 = kept.sums_1
        return experts_1, kept.part_1, [made[-1] for made in shared_1]

    def beside_1(index, result):
        part = outer(plain[1][index], result) + chunk_of(kept.part_1, index)
        return part.astype(HALF)

    total, rows_1, mids_1 = through_experts(
        rms_norm(middle_1, norm_mids[1]).astype(HALF), plain[1], expert_1, own_1, beside_1
    )

    def mixer_back(s, grad_middle, along, rr, saved, meanwhile):
        wide_in, pre, y, scaled = saved
        sides = as_halves(jnp.concatenate([rr, along], axis=1))
        payload = spread(
            jnp.concatenate([grad_middle.astype(HALF), sides], axis=1), meanwhile
        )
        wide_mix, sides = payload[:, :width], from_halves(payload[:, width:], 2)
        grad_scaled = [project(wide_mix, half) for half in proj_out[s]]
        grad_scaled = jnp.concatenate(grad_scaled, axis=1)
        *grad_pre, wide_grads, grad_conv_input, grad_conv_state, step_grads = mixer_backward(
            pre, y, grad_scaled, sides, heads, mixers[s]
        )
        ends = [part[:, :wide] for part in grad_pre]
        tail = jnp.concatenate([grad_pre[0][:, wide:], grad_pre[1][:, wide : wide + LANES]], axis=1)
        mix_rr = (wide_mix * sides[:, :1]).astype(HALF)
        rest = (grad_conv_state, grad_conv_input, wide_grads, step_grads)
        return grad_pre, (wide_in, *ends), (mix_rr, *two_halves(scaled)), tail, rest

    def resid_back(resid, norm, grad_normed, grad_middle):
        _, pull_in = jax.vjp(rms_norm, resid, norm)
        grad_resid, grad_norm = pull_in(grad_normed)
        return grad_resid + grad_middle, grad_norm

    def own_layer(first_value, second_value):
        keep = jnp.where(first, first_value, second_value)
        give = jnp.where(first, second_value, first_value).astype(HALF)
        return keep.astype(FLOAT), swapped(give)

    def row_sums(value):
        return lax.psum_scatter(value, "row", scatter_dimension=0, tiled=True)

    grad_middle, along, grad_norm_mid_1 = middle_backward(
        total, grad_now, middle_1, mixed_1, norm_mids[1]
    )
    expert_grads_1, shared_grads_1 = kept.sums_1
    answers = after([kept.answer_1[index] for index in kept.answer_1], grad_middle)
    answers_back = [to_experts(answers[-1])]
    if groups() > 1:
        own_rows, others = sent_back(answers[0])
        answers_back = [jnp.concatenate([own_rows, *others], axis=0), *answers_back]
    grad_pre, to_proj, to_out, tail, rest_1 = mixer_back(
        1,
        grad_middle,
        along,
        rr_1,
        (wide_in_1, pre_1, y_1, scaled_1),
        answers_back,
    )
    whole = line_product(grad_pre, proj[1])
    grad_in = gathered_sum(whole)
    grad_1, grad_norm_in_1 = resid_back(out_0, norm_ins[1], grad_in, grad_middle)

    def aside_back_0(tokens_all):
        home = home_part(after(kept.shared_1[2], tokens_all), shared[1])
        home = [
            (outer(scaling[1][index], answer) + chunk_of(home, index)).astype(HALF)
            for index, answer in enumerate(after(answers_back, tokens_all))
        ]
        home = joined(home)
        if groups() > 1:
            home = in_order([block_of(home, back) for back in range(groups())], "col")
        kept.home = lax.psum_scatter(home, "col", scatter_dimension=0, tiled=True)
        own_proj, own_out, own_tail = after((to_proj, to_out, tail), home)
        given, given_out = half_to_give(*own_proj), half_to_give(*own_out)
        made = (*shared_grads_1, (*own_out, swapped(given_out)), (*own_proj, swapped(given)))
        made = [half_to_keep(*each) for each in after(made, (given, given_out))]
        kept.sent_1 = [row_sums(each) for each in made]
        kept.tail_1 = outer(own_proj[0], own_tail).astype(HALF)
        return made, kept.tail_1

    def expert_back_0(index, rows):
        kept.grads_0[index], back = expert_backward(rows, kept.rows_0[index], experts[0])
        return back

    def own_back_0(tokens_all, rows):
        kept.shared_grads_0, kept.part_0 = shared_backward(
            tokens_all, kept.shared_0, shared[0]
        )
        kept.sums_0 = weight_sums(
            rows_0,
            rows,
            kept.rows_0,
            kept.grads_0,
            mids_0,
            tokens_all,
            kept.shared_0,
            kept.shared_grads_0,
        )
        experts_0, shared_0 = kept.sums_0
        return experts_0, kept.part_0, [made[-1] for made in shared_0]

    def beside_back_0(index, result):
        part = outer(plain[0][index], result) + chunk_of(kept.part_0, index)
        return part.astype(HALF)

    total, grad_rows_0, grad_tokens_0 = through_experts(
        grad_1.astype(HALF), scaling[0], expert_back_0, own_back_0, beside_back_0, aside_back_0
    )
    sums_1, grad_tail_1 = kept.sent_1, kept.tail_1
    grad_middle, along, grad_norm_mid_0 = middle_backward(
        total, grad_1, middle_0, mixed_0, norm_mids[0]
    )
    expert_grads_0, shared_grads_0 = kept.sums_0
    shared_sums_0 = [half_to_keep(*after(made, total)) for made in shared_grads_0]
    sums_0 = [row_sums(made) for made in shared_sums_0]
    expert_out = [own_layer(a, b) for a, b in zip(expert_grads_0, expert_grads_1)]
    grad_pre, to_proj, to_out, tail, rest_0 = mixer_back(
        0,
        grad_middle,
        along,
        rr_0,
        (wide_in_0, pre_0, y_0, scaled_0),
        ([part[0] for part in expert_out], shared_sums_0, sums_1),
    )

    grad_tail_0 = outer(wide_in_0, tail).astype(HALF)
    tail_keep, tail_other = own_layer(grad_tail_0, grad_tail_1)
    given = half_to_give(*after(to_proj, grad_tail_0))
    whole = line_product(after(grad_pre, given), proj[0])
    wide_x = wide_tokens.astype(FLOAT)
    wide_r = lax.rsqrt(jnp.mean(wide_x * wide_x, axis=1, keepdims=True) + EPS)
    grad_norm_in_0 = jnp.sum(whole.astype(FLOAT) * wide_x * wide_r, axis=0)
    smalls = (
        (grad_norm_in_0, grad_norm_mid_0, *rest_0),
        (grad_norm_in_1, grad_norm_mid_1, *rest_1),
    )
    shapes = [part.shape for part in smalls[0]]
    small_keep, small_other = own_layer(flat(smalls[0]), flat(smalls[1]))
    tail_pieces = row_pieces((tail_keep + tail_other.astype(FLOAT)).astype(HALF))
    vector = small_keep + small_other.astype(FLOAT)
    lines = [shifted(vector[None], "row", back) for back in range(n_row)]
    tail_received = row_received(tail_pieces)
    proj_half = half_to_keep(*after((*to_proj, swapped(given)), whole))
    given_out = half_to_give(*after(to_out, proj_half))
    line_received = sent_home(after(whole, proj_half))
    proj_pieces = row_pieces(proj_half)
    proj_received = row_received(proj_pieces)
    out_half = half_to_keep(*to_out, swapped(given_out))
    out_pieces = row_pieces(out_half)
    out_received = row_received(out_pieces)
    tail_received, lines, line_received, proj_received, out_received = after(
        (tail_received, lines, line_received, proj_received, out_received)
    )
    tail = total_of(tail_pieces[0], tail_received).astype(HALF)
    vector = jnp.sum(in_order(lines, "row"), axis=0)
    common = 2 * width + conv_state.shape[1] * state
    state_grad = tail[:, :state]
    if groups() > 1:
        state_pieces = row_pieces(state_grad, "col")
        state_received = row_received(state_pieces, "col")
        lines = [shifted(vector[None, :common], "col", back) for back in range(n_col)]
        state_received, lines = after((state_received, lines))
        shared_sum = jnp.sum(in_order(lines, "col"), axis=0)
        state_grad = total_of(state_pieces[0], state_received).astype(HALF)
        state_lines = [shifted(state_grad, "col", back) for back in range(n_col)]
    else:
        state_grad = lax.psum(state_grad, "col")
        state_lines = [state_grad]
        shared_sum = lax.psum(vector[:common], "col")
    expert_out = [keep + other.astype(FLOAT) for keep, other in after(expert_out, tail)]
    state_grad = in_order(after(state_lines, expert_out), "col")
    grad_in = added_up(whole, line_received)
    sums_0.append(total_of(out_pieces[0], out_received).astype(HALF))
    sums_0.append(total_of(proj_pieces[0], proj_received).astype(HALF))
    sums_0, sums_1 = after((sums_0, sums_1), grad_in)
    grad_0, _ = resid_back(tokens_now, norm_ins[0], grad_in, grad_middle)
    out_1 = middle_1 + kept.home.astype(FLOAT)

    def own_halves(first_value, second_value):
        keep = jnp.where(first, first_value, second_value)
        give = jnp.where(first, second_value, first_value)
        return keep, swapped(give)

    def per_micro(first_value, second_value):
        keep = jnp.where(first, first_value, second_value)
        return keep, swapped(jnp.where(first, second_value, first_value).astype(HALF))

    halves = [own_halves(a, b) for a, b in zip(sums_0, sums_1)]
    outs, in_grads = per_micro(out_0, after(out_1, grad_in)), per_micro(grad_0, grad_1)
    halves = [pair(*half) for half in halves]
    grad_shared, grad_down, grad_out, grad_ends = halves
    grad_out, grad_down = [jnp.concatenate(both, axis=1) for both in (grad_out, grad_down)]
    (
        out_norm_in,
        out_norm_mid,
        out_conv_state,
        out_conv_input,
        out_wide,
        out_step,
    ) = unflat(jnp.concatenate([shared_sum, vector[common:]]), shapes)

    def stacked(keep, other):
        return jnp.stack(pair(keep, other.astype(FLOAT)))[None]

    def out(value):
        return value.astype(FLOAT)[None]

    return (
        stacked(*outs),
        stacked(*in_grads),
        out_norm_in[None],
        out(grad_ends[0][:, :inner]),
        out(grad_ends[1][:, :inner]),
        out(state_grad),
        out(tail[:, state : state + heads]),
        out_step[:1, :heads],
        out_step[1:, :heads],
        jnp.sum(out_wide[1, :inner].reshape(heads, HEAD), axis=1)[None],
        out_conv_input[None, :, :inner],
        out_conv_state[None],
        out_wide[:1, :inner],
        out(grad_out[:, :inner]),
        out_norm_mid[None],
        expert_out[0][None, None],
        expert_out[1][None, None],
        expert_out[2][None, None],
        out(grad_shared[0]),
        out(grad_shared[1]),
        out(grad_down),
    )


def solution(mesh):
    in_specs = (
        P(None, ("row", "col"), None),
        P(None, ("row", "col"), None),
        P(),
        P("section", None, ("row", "col"), None),
        P("section", None, ("row", "col"), None),
        P("section", None),
        P("section", "row", "col"),
        P("section", "row", "col"),
        P("section", "row", None),
        P("section", "row", "col"),
        P("section", "col"),
        P("section", "col"),
        P("section", "col"),
        P("section", None, "col"),
        P("section", None, None),
        P("section", "col"),
        P("section", "row", "col"),
        P("section", None),
        P("section", ("row", "col"), None, None),
        P("section", ("row", "col"), None, None),
        P("section", ("row", "col"), None, None),
        P("section", "row", "col"),
        P("section", "row", "col"),
        P("section", "row", "col"),
    )
    out_specs = (
        P("section", None, ("row", "col"), None),
        P("section", None, ("row", "col"), None),
        P("section", None),
        P("section", "row", "col"),
        P("section", "row", "col"),
        P("section", "row", None),
        P("section", "row", "col"),
        P("section", "col"),
        P("section", "col"),
        P("section", "col"),
        P("section", None, "col"),
        P("section", None, None),
        P("section", "col"),
        P("section", "row", "col"),
        P("section", None),
        P("section", ("row", "col"), None, None),
        P("section", ("row", "col"), None, None),
        P("section", ("row", "col"), None, None),
        P("section", "row", "col"),
        P("section", "row", "col"),
        P("section", "row", "col"),
    )
    return jax.shard_map(shards, mesh=mesh, in_specs=in_specs, out_specs=out_specs, check_vma=False)
```
